32 devices in a mesh: ctx: 16 (over z, y, core), fsdp: 2 (over x).
Axes of the slice: x: 2, y: 2, z: 4, core: 2. Of those that a mesh axis runs over, the one named last changes fastest.
Arguments:
- tokens: bfloat16 [6144, 2048], P(('ctx', 'fsdp')), may hold values from -6 to 6
- cotangent: bfloat16 [6144, 2048], P(('ctx', 'fsdp')), may hold values from -6 to 6
- expert_ids: int32 [6144, 8], P(('ctx', 'fsdp')), may hold values from 0 to 15, all different within a row; in each aligned block of 192 rows (0 to 191, 192 to 383, ...) at most 120 rows name the same one
- attention_gain: float32 [2048], replicated, may hold values from 0.5 to 1.5
- ffn_gain: float32 [2048], replicated, may hold values from 0.5 to 1.5
- query_gain: float32 [128], replicated, may hold values from 0.5 to 1.5
- key_gain: float32 [128], replicated, may hold values from 0.5 to 1.5
- w_query: bfloat16 [2048, 4096], P(('ctx', 'fsdp')), may hold values from -0.125 to 0.125
- key_weight: bfloat16 [2048, 512], P(('ctx', 'fsdp')), may hold values from -0.125 to 0.125
- value_weight: bfloat16 [2048, 512], P(('ctx', 'fsdp')), may hold values from -0.125 to 0.125
- w_output: bfloat16 [4096, 2048], P(('ctx', 'fsdp')), may hold values from -2 to 2
- w_router: bfloat16 [2048, 16], P(('ctx', 'fsdp')), may hold values from -0.0625 to 0.0625
- w_gate: bfloat16 [16, 2048, 768], P('ctx', 'fsdp'), may hold values from -0.125 to 0.125
- w_up: bfloat16 [16, 2048, 768], P('ctx', 'fsdp'), may hold values from -0.125 to 0.125
- w_down: bfloat16 [16, 768, 2048], P('ctx', 'fsdp'), may hold values from -1 to 1
Outputs:
- mixed: bfloat16 [6144, 2048], P(('ctx', 'fsdp'))
- d_tokens: bfloat16 [6144, 2048], P(('ctx', 'fsdp'))
- attention_gain_grad: float32 [2048], replicated
- ffn_gain_grad: float32 [2048], replicated
- query_gain_grad: float32 [128], replicated
- key_gain_grad: float32 [128], replicated
- query_grad: float32 [2048, 4096], P(('ctx', 'fsdp'))
- key_grad: float32 [2048, 512], P(('ctx', 'fsdp'))
- value_grad: float32 [2048, 512], P(('ctx', 'fsdp'))
- output_grad: float32 [4096, 2048], P(('ctx', 'fsdp'))
- router_grad: float32 [2048, 16], P(('ctx', 'fsdp'))
- gate_grad: float32 [16, 2048, 768], P('ctx', 'fsdp')
- up_grad: float32 [16, 2048, 768], P('ctx', 'fsdp')
- down_grad: float32 [16, 768, 2048], P('ctx', 'fsdp')
The draws below stay inside these ranges and needn't reach their ends.
Inputs may be any that keep to these rules, and one draw needn't show every extreme that they name: `expert_ids`: among the rows of one device no expert is named more than 120 times, a bound that some block reaches.
All inputs are finite; a program needn't handle non-finite values.
Results may differ from the reference program's by a relative error of at most 0.024.
Values may be sent and summed in bfloat16 or wider, within the bound.
No kernel may reach another device: no remote copies, remote signals or barrier semaphores. Data moves between devices by JAX's collectives and lax.ppermute only.
A program may use at most 320 MiB of HBM per device.

```python
import math
import jax
import jax.numpy as jnp
import numpy as np
from jax import lax

MODEL_WIDTH = 2048
QUERY_HEADS = 32
KEY_VALUE_HEADS = 4
HEAD_SIZE = 128
F = 768
TOP = 8
LOCAL_SEQUENCES = 3
TOK_DEV = 192
SEQUENCE_LENGTH = 1024
TOTAL_SEQUENCES = 6
TOKENS = 6144
EXPERTS = 16
CAP = 120
N_CTX = 16
N_FSDP = 2


def block_scale(stream_key, extent, pieces, smallest, high):
    loudness, own = 1.0, jax.random.fold_in(stream_key, 6)
    for position, parts in pieces:
        heights = jnp.exp(jax.random.uniform(jax.random.fold_in(own, position), (parts,), jnp.float32, smallest / len(pieces), high / len(pieces)))
        loudness = loudness * jnp.repeat(heights, extent[position] // parts).reshape([-1 if axis == position else 1 for axis in range(len(extent))])
    return loudness


def assign_block(rng, own, number, rows, amount, top, most, skew):
    sequence = jax.random.permutation(rng, amount)
    packed, common = shares(amount, rows * top, most, skew, True), shares(amount, rows * top, most, skew, False)
    places = jnp.arange(amount)

    def named(lengths, offset_by):
        used = int((lengths > 0).sum())
        fixed = max(1, used // 4)
        shifted = fixed + (places - fixed + offset_by * (used - fixed)) % max(1, amount - fixed)
        return jnp.zeros((amount,), jnp.int32).at[sequence[jnp.where(places < fixed, places, shifted)]].set(jnp.asarray(lengths, jnp.int32))

    lengths = jnp.where(number % 4 == 0, named(packed, number // 4), named(common, number - number // 4 - 1))
    mixed = jax.random.permutation(jax.random.fold_in(own, 3), amount)
    giver, taker = mixed[0:amount // 2 * 2:2], mixed[1:amount // 2 * 2:2]
    slack = jnp.minimum(lengths[giver] - 1, most - lengths[taker]) // 2
    slack = jnp.where((giver == sequence[0]) | (taker == sequence[0]) | (lengths[taker] == 0), 0, jnp.maximum(slack, 0))
    shifted = jax.random.randint(jax.random.fold_in(own, 4), (amount // 2,), 0, 1 << 20) % (slack + 1)
    lengths = lengths.at[giver].add(-shifted).at[taker].add(shifted)
    items = jnp.searchsorted(jnp.cumsum(lengths), jnp.arange(rows * top), side="right").astype(jnp.int32)
    grid = items.reshape(top, rows).T
    grid = grid[jax.random.permutation(jax.random.fold_in(own, 1), rows)]
    offset_by = jax.random.randint(jax.random.fold_in(own, 2), (rows, 1), 0, top)
    return jnp.take_along_axis(grid, (jnp.arange(top)[None, :] + offset_by) % top, axis=1)


def shares(amount, total, reach, slope, full):
    loads = [(1 << 20) // math.isqrt(rank ** slope) + 1 for rank in range(1, amount + 1)]
    largest = reach if full else min(reach, max(-(-total // amount), total * loads[0] // sum(loads)))
    least = 1 if total - largest >= amount - 1 else 0
    counts, surplus = [largest] + [least] * (amount - 1), total - largest - least * (amount - 1)
    while surplus > 0:
        movable = [i for i in range(1, amount) if counts[i] < largest] or [i for i in range(1, amount) if counts[i] < reach]
        pool, budget = sum([loads[i] for i in movable]), surplus
        for i in movable:
            addition = min(reach - counts[i], max(1, budget * loads[i] // pool), surplus)
            counts[i] = counts[i] + addition
            surplus = surplus - addition
    return np.array(counts)


def scatter_about(rng, extent, scale, bound, shards=(), kind=jnp.bfloat16):
    result = jax.random.normal(rng, extent, jnp.float32) * scale
    if len(shards) > 0:
        result = block_scale(rng, extent, shards, -0.22, 0.18) * result
    return jnp.clip(result, min=-bound, max=bound).astype(kind)


def setup_inputs(seed: int = 0) -> dict:
    keys = jax.random.split(jax.random.key(seed), 16)
    tokens = scatter_about(keys[0], (TOKENS, MODEL_WIDTH), 1.0, 6.0, ((0, 32),))
    cotangent = scatter_about(keys[1], (TOKENS, MODEL_WIDTH), 1.0, 6.0, ((0, 32),))
    expert_ids_keys = jax.random.split(jax.random.fold_in(keys[2], 1), TOKENS // TOK_DEV)
    expert_ids_turns = jax.random.permutation(jax.random.fold_in(keys[2], 3), TOKENS // TOK_DEV)
    expert_ids = jax.vmap(lambda own, number: assign_block(jax.random.fold_in(keys[2], 2), own, number, TOK_DEV, EXPERTS, TOP, CAP, 1))(expert_ids_keys, expert_ids_turns).reshape((TOKENS, TOP))
    attention_gain = jnp.clip(1.0 + 0.1 * jax.random.normal(keys[3], (MODEL_WIDTH,), jnp.float32), 0.5, 1.5)
    ffn_gain = jnp.clip(1.0 + 0.1 * jax.random.normal(keys[4], (MODEL_WIDTH,), jnp.float32), 0.5, 1.5)
    query_gain = jnp.clip(1.0 + 0.1 * jax.random.normal(keys[5], (HEAD_SIZE,), jnp.float32), 0.5, 1.5)
    key_gain = jnp.clip(1.0 + 0.1 * jax.random.normal(keys[6], (HEAD_SIZE,), jnp.float32), 0.5, 1.5)
    w_query = scatter_about(keys[7], (MODEL_WIDTH, QUERY_HEADS * HEAD_SIZE), MODEL_WIDTH ** -0.5, 0.125, ((0, 32),))
    key_weight = scatter_about(keys[8], (MODEL_WIDTH, KEY_VALUE_HEADS * HEAD_SIZE), MODEL_WIDTH ** -0.5, 0.125, ((0, 32),))
    value_weight = scatter_about(keys[9], (MODEL_WIDTH, KEY_VALUE_HEADS * HEAD_SIZE), MODEL_WIDTH ** -0.5, 0.125, ((0, 32),))
    w_output = scatter_about(keys[10], (QUERY_HEADS * HEAD_SIZE, MODEL_WIDTH), (max(QUERY_HEADS * HEAD_SIZE // 512, 2)) ** -0.5, 2.0, ((0, 32),))
    w_router = scatter_about(keys[11], (MODEL_WIDTH, EXPERTS), (4 * MODEL_WIDTH) ** -0.5, 0.0625, ((0, 32),))
    w_gate = scatter_about(keys[12], (EXPERTS, MODEL_WIDTH, F), MODEL_WIDTH ** -0.5, 0.125, ((0, 16), (1, 2)))
    w_up = scatter_about(keys[13], (EXPERTS, MODEL_WIDTH, F), MODEL_WIDTH ** -0.5, 0.125, ((0, 16), (1, 2)))
    w_down = scatter_about(keys[14], (EXPERTS, F, MODEL_WIDTH), (max(F // 24, 2)) ** -0.5, 1.0, ((0, 16), (1, 2)))
    return dict(tokens=tokens, cotangent=cotangent, expert_ids=expert_ids, attention_gain=attention_gain, ffn_gain=ffn_gain, query_gain=query_gain, key_gain=key_gain, w_query=w_query, key_weight=key_weight, value_weight=value_weight, w_output=w_output, w_router=w_router, w_gate=w_gate, w_up=w_up, w_down=w_down)


EPS = 1e-06
THETA = 1000000.0
HIGH = lax.Precision.HIGHEST

@jax.custom_vjp
def low(v):
    return lax.optimization_barrier(v.astype(jnp.bfloat16)).astype(jnp.float32)

@jax.custom_vjp
def lower_backward(v):
    return v

def low_keep(v):
    return (low(v), None)

def low_pass(kept, grad):
    return (grad,)

def back_keep(v):
    return (v, None)

def back_low(kept, grad):
    return (low(grad),)
low.defvjp(low_keep, low_pass)
lower_backward.defvjp(back_keep, back_low)

def matrix_product(left, right):
    return jnp.dot(left, right, precision=HIGH, preferred_element_type=jnp.float32)

def rms_apply(value_rows_list, gain_vec):
    return value_rows_list * lax.rsqrt(lax.optimization_barrier(jnp.mean(value_rows_list * value_rows_list, -1, keepdims=True)) + EPS) * gain_vec

def rotary(positions, head_width):
    half_width = head_width // 2
    frequency = jnp.exp(-math.log(THETA) * (2.0 * jnp.arange(half_width, dtype=jnp.float32)) / head_width)
    angles = positions.astype(jnp.float32)[:, None] * frequency[None, :]
    angles = jnp.concatenate([angles, angles], -1)
    return (jnp.cos(angles)[:, None, :], jnp.sin(angles)[:, None, :])

def rope_apply(value_rows_list, cosine, sine_tab):
    half_width = value_rows_list.shape[-1] // 2
    turned = jnp.concatenate([-value_rows_list[..., half_width:], value_rows_list[..., :half_width]], -1)
    return value_rows_list * cosine + turned * sine_tab

def attend_sequence(queries, key_row_matrix, value_rows, qblock):
    length = key_row_matrix.shape[0]
    heads_kv = key_row_matrix.shape[1]
    groups = queries.shape[1] // heads_kv
    score_scale = 1.0 / math.sqrt(key_row_matrix.shape[2])
    key_pos = jnp.arange(length, dtype=jnp.int32)

    def one_block(query_block, start_row):
        shaped = query_block.reshape(qblock, heads_kv, groups, -1)
        scores = jnp.einsum('qkgd,wkd->kgqw', shaped, key_row_matrix, precision=HIGH, preferred_element_type=jnp.float32)
        scores = lower_backward(scores * score_scale)
        query_pos = start_row + jnp.arange(qblock, dtype=jnp.int32)
        allowed = key_pos[None, :] <= query_pos[:, None]
        masked = jnp.where(allowed, scores, -1e+30)
        weights = low(jax.nn.softmax(masked, -1))
        mixed = jnp.einsum('kgqw,wkd->qkgd', weights, value_rows, precision=HIGH, preferred_element_type=jnp.float32)
        return mixed.reshape(qblock, -1)
    checked = jax.checkpoint(one_block)
    blocks = queries.reshape(length // qblock, qblock, queries.shape[1], queries.shape[2])
    starts = qblock * jnp.arange(length // qblock, dtype=jnp.int32)
    outputs = lax.map(lambda loop_item: checked(loop_item[0], loop_item[1]), (blocks, starts))
    return outputs.reshape(length, -1)

def reference(tokens, cotangent, expert_ids, attention_gain, ffn_gain, query_gain, key_gain, w_query, key_weight, value_weight, w_output, w_router, w_gate, w_up, w_down):
    rows_total_count = tokens.shape[0]
    block_len = TOK_DEV // (2 * LOCAL_SEQUENCES)
    row_ids = jnp.arange(rows_total_count, dtype=jnp.int32)
    device = row_ids // TOK_DEV
    ctx_index = device // N_FSDP
    fsdp_index = device % N_FSDP
    local_row = row_ids % TOK_DEV
    seq_index = fsdp_index * LOCAL_SEQUENCES + local_row // (2 * block_len)
    within = local_row % block_len
    positions = jnp.where(local_row // block_len % 2 == 0, ctx_index * block_len + within, (2 * N_CTX - 1 - ctx_index) * block_len + within)
    seq_place = seq_index * SEQUENCE_LENGTH + positions
    sequence_order = jnp.zeros((rows_total_count,), jnp.int32).at[seq_place].set(row_ids)
    cosine, sine_tab = rotary(positions, HEAD_SIZE)
    qblock = math.gcd(SEQUENCE_LENGTH, 512)
    dev_count = N_CTX * N_FSDP
    routes = rows_total_count * TOP
    flat_ids = expert_ids.reshape(-1).astype(jnp.int32)
    route_dev = jnp.arange(routes, dtype=jnp.int32) // (TOK_DEV * TOP)
    chosen = (flat_ids.reshape(dev_count, TOK_DEV * TOP, 1) == jnp.arange(EXPERTS, dtype=jnp.int32)).astype(jnp.int32)
    route_ranks = lax.optimization_barrier(jnp.sum((jnp.cumsum(chosen, 1) - 1) * chosen, -1)).reshape(-1)
    slot_of_route = flat_ids * (dev_count * CAP) + route_dev * CAP + route_ranks
    route_of_slot = jnp.full((EXPERTS * dev_count * CAP,), routes, jnp.int32).at[slot_of_route].set(jnp.arange(routes, dtype=jnp.int32))
    token_of_slot = route_of_slot // TOP
    filled = (route_of_slot < routes).astype(jnp.float32)

    def forward(inputs, gain_attn, gain_ffn, gain_query, gain_key, proj_query, key_project, value_project, proj_output, proj_router, expert_gate, expert_up, expert_down):
        normalized_input = low(rms_apply(inputs, gain_attn))
        q_proj = lower_backward(matrix_product(normalized_input, proj_query)).reshape(rows_total_count, QUERY_HEADS, HEAD_SIZE)
        key_projected = lower_backward(matrix_product(normalized_input, key_project)).reshape(rows_total_count, KEY_VALUE_HEADS, HEAD_SIZE)
        value_projected = lower_backward(matrix_product(normalized_input, value_project)).reshape(rows_total_count, KEY_VALUE_HEADS, HEAD_SIZE)
        queries = low(rope_apply(rms_apply(q_proj, gain_query), cosine, sine_tab))
        key_row_matrix = low(rope_apply(rms_apply(key_projected, gain_key), cosine, sine_tab))
        value_rows_list = low(value_projected)
        q_seq = queries[sequence_order].reshape(TOTAL_SEQUENCES, SEQUENCE_LENGTH, QUERY_HEADS, HEAD_SIZE)
        key_sequence = key_row_matrix[sequence_order].reshape(TOTAL_SEQUENCES, SEQUENCE_LENGTH, KEY_VALUE_HEADS, HEAD_SIZE)
        value_sequence = value_rows_list[sequence_order].reshape(TOTAL_SEQUENCES, SEQUENCE_LENGTH, KEY_VALUE_HEADS, HEAD_SIZE)

        def per_seq(state_now, loop_item):
            return (state_now, attend_sequence(loop_item[0], loop_item[1], loop_item[2], qblock))
        unused, attended = lax.scan(per_seq, jnp.zeros((), jnp.float32), (q_seq, key_sequence, value_sequence))
        attended = attended.reshape(rows_total_count, QUERY_HEADS * HEAD_SIZE)[seq_place]
        attended = low(lower_backward(attended))
        mixed_attn = inputs + lower_backward(matrix_product(attended, proj_output))
        normed_ffn = low(rms_apply(mixed_attn, gain_ffn))
        logits = lower_backward(matrix_product(normed_ffn, proj_router))
        picked = jnp.take_along_axis(logits, expert_ids, 1)
        gate_probs = jax.nn.softmax(picked, -1)
        padded = jnp.concatenate([normed_ffn, jnp.zeros((1, MODEL_WIDTH), jnp.float32)], 0)
        sent_rows = lower_backward(padded[token_of_slot]) * filled[:, None]
        sent_rows = sent_rows.reshape(EXPERTS, dev_count * CAP, MODEL_WIDTH)
        gate_part = lower_backward(jnp.einsum('esd,edf->esf', sent_rows, expert_gate, precision=HIGH, preferred_element_type=jnp.float32))
        up_part = lower_backward(jnp.einsum('esd,edf->esf', sent_rows, expert_up, precision=HIGH, preferred_element_type=jnp.float32))
        hidden = low(jax.nn.silu(gate_part) * up_part)
        results = low(lower_backward(jnp.einsum('esf,efd->esd', hidden, expert_down, precision=HIGH, preferred_element_type=jnp.float32)))
        per_route = results.reshape(-1, MODEL_WIDTH)[slot_of_route].reshape(rows_total_count, TOP, MODEL_WIDTH)
        return mixed_attn + lax.optimization_barrier(jnp.sum(gate_probs[..., None] * per_route, 1))
    primals = (tokens.astype(jnp.float32), attention_gain.astype(jnp.float32), ffn_gain.astype(jnp.float32), query_gain.astype(jnp.float32), key_gain.astype(jnp.float32), w_query.astype(jnp.float32), key_weight.astype(jnp.float32), value_weight.astype(jnp.float32), w_output.astype(jnp.float32), w_router.astype(jnp.float32), w_gate.astype(jnp.float32), w_up.astype(jnp.float32), w_down.astype(jnp.float32))
    output, pullback = jax.vjp(forward, *primals)
    gradients = pullback(cotangent.astype(jnp.float32))
    return (output.astype(jnp.bfloat16), gradients[0].astype(jnp.bfloat16), gradients[1], gradients[2], gradients[3], gradients[4], gradients[5], gradients[6], gradients[7], gradients[8], gradients[9], gradients[10], gradients[11], gradients[12])
```

```python
import math

import jax
import jax.numpy as jnp
from jax import lax
from jax.experimental import pallas as pl
from jax.experimental.pallas import tpu as pltpu
from jax.sharding import Mesh
from jax.sharding import PartitionSpec as P

QUERY_HEADS = 32
KEY_VALUE_HEADS = 4
HEAD_SIZE = 128
TOP = 8
LOCAL_SEQUENCES = 3


EPS = 1e-06
THETA = 1000000.0
NEGATIVE_LIMIT = -1e30


def shard_positions(device, context_count, block_len):
    within = jnp.arange(2 * block_len, dtype=jnp.int32)
    lower_pos = device * block_len + within
    upper_pos = (2 * context_count - 1 - device) * block_len + within - block_len
    return jnp.where(within < block_len, lower_pos, upper_pos)


def group_positions(first_dev, query_group_size, context_count, block_len):
    devices = first_dev + jnp.arange(query_group_size, dtype=jnp.int32)
    return jax.vmap(lambda device: shard_positions(device, context_count, block_len))(
        devices
    ).reshape(-1)


def rotary(positions, head_width):
    half_width = head_width // 2
    frequency = jnp.exp(
        -math.log(THETA) * (2.0 * jnp.arange(half_width, dtype=jnp.float32)) / head_width
    )
    angles = positions.astype(jnp.float32)[:, None] * frequency[None, :]
    angles = jnp.concatenate([angles, angles], -1)
    return (jnp.cos(angles)[:, None, :], jnp.sin(angles)[:, None, :])


def rope_apply(value_rows_list, cosine, sine_tab):
    half_width = value_rows_list.shape[-1] // 2
    turned = jnp.concatenate(
        [-value_rows_list[..., half_width:], value_rows_list[..., :half_width]], -1
    )
    return value_rows_list * cosine + turned * sine_tab


def rope_back(upstream, cosine, sine_tab):
    half_width = upstream.shape[-1] // 2
    moved_part = upstream * sine_tab
    return upstream * cosine + jnp.concatenate(
        [moved_part[..., half_width:], -moved_part[..., :half_width]], -1
    )


def rms_apply(value_rows_list, gain_vec):
    inverse = lax.rsqrt(jnp.mean(value_rows_list * value_rows_list, -1, keepdims=True) + EPS)
    return (value_rows_list * inverse * gain_vec, inverse)


def rms_back(value_rows_list, inverse, gain_vec, upstream):
    normalized_input = value_rows_list * inverse
    gain_part = jnp.sum((upstream * normalized_input).reshape(-1, value_rows_list.shape[-1]), 0)
    scaled = upstream * gain_vec
    back_part = inverse * (
        scaled - normalized_input * jnp.mean(scaled * normalized_input, -1, keepdims=True)
    )
    return (back_part, gain_part)


def arrange(blocks):
    query_group_size, seq_count, paired_rows, heads_kv, head_dim = blocks.shape
    return blocks.transpose(1, 0, 2, 3, 4).reshape(
        seq_count, query_group_size * paired_rows, heads_kv, head_dim
    )


def unarrange(rows_all, query_group_size):
    seq_count, width_all, heads_kv, head_dim = rows_all.shape
    return rows_all.reshape(
        seq_count, query_group_size, width_all // query_group_size, heads_kv, head_dim
    ).transpose(1, 0, 2, 3, 4)


def attend_group(state_now, queries, key_row_matrix, value_rows, query_pos, key_pos, score_scale):
    run_max, run_sum, run_acc = state_now
    scores = (
        jnp.einsum("skgqd,swkd->skgqw", queries, key_row_matrix, preferred_element_type=jnp.float32)
        * score_scale
    )
    allowed = key_pos[None, :] <= query_pos[:, None]
    new_max = jnp.maximum(run_max, jnp.max(jnp.where(allowed, scores, NEGATIVE_LIMIT), -1))
    weights_now = jnp.where(allowed, jnp.exp(scores - new_max[..., None]), 0.0)
    factor = jnp.exp(run_max - new_max)
    new_sum = run_sum * factor + jnp.sum(weights_now, -1)
    update = jnp.einsum(
        "skgqw,swkd->skgqd",
        weights_now.astype(jnp.bfloat16),
        value_rows,
        preferred_element_type=jnp.float32,
    )
    return (new_max, new_sum, run_acc * factor[..., None] + update)


def routed_layer(
    tokens,
    cotangent,
    expert_ids,
    attention_gain,
    ffn_gain,
    query_gain,
    key_gain,
    w_query,
    key_weight,
    value_weight,
    w_output,
    w_router,
    w_gate,
    w_up,
    w_down,
):
    context_count = lax.axis_size("ctx")
    ctx_here = lax.axis_index("ctx")
    token_per_device = tokens.shape[0]
    block_len = token_per_device // (2 * LOCAL_SEQUENCES)
    paired_rows = 2 * block_len
    query_groups = QUERY_HEADS // KEY_VALUE_HEADS
    score_scale = 1.0 / math.sqrt(HEAD_SIZE)
    experts_all = w_router.shape[1]
    exp_dev = w_gate.shape[0]
    cap_rows = token_per_device * TOP * 5 // (4 * experts_all)
    routes = token_per_device * TOP
    inputs = tokens.astype(jnp.float32)
    normed_attn, inverse_attn = rms_apply(inputs, attention_gain)
    normed_low = normed_attn.astype(jnp.bfloat16)
    query_all, key_all, value_all, output_all, router_all = (
        lax.all_gather(w_query, ("ctx", "fsdp"), axis=0, tiled=True),
        lax.all_gather(key_weight, ("ctx", "fsdp"), axis=0, tiled=True),
        lax.all_gather(value_weight, ("ctx", "fsdp"), axis=0, tiled=True),
        lax.all_gather(w_output, ("ctx", "fsdp"), axis=0, tiled=True),
        lax.all_gather(w_router, ("ctx", "fsdp"), axis=0, tiled=True),
    )
    local_pos = shard_positions(ctx_here, context_count, block_len)
    row_pos = jnp.tile(local_pos, LOCAL_SEQUENCES)
    cosine, sine_tab = rotary(row_pos, HEAD_SIZE)
    query_proj = jnp.dot(normed_low, query_all, preferred_element_type=jnp.float32).reshape(
        token_per_device, QUERY_HEADS, HEAD_SIZE
    )
    key_proj = jnp.dot(normed_low, key_all, preferred_element_type=jnp.float32).reshape(
        token_per_device, KEY_VALUE_HEADS, HEAD_SIZE
    )
    value_proj = jnp.dot(normed_low, value_all, preferred_element_type=jnp.float32).reshape(
        token_per_device, KEY_VALUE_HEADS, HEAD_SIZE
    )
    query_normed, query_inverse = rms_apply(query_proj, query_gain)
    key_normed, key_inverse = rms_apply(key_proj, key_gain)
    query_lower = rope_apply(query_normed, cosine, sine_tab).astype(jnp.bfloat16)
    key_low = rope_apply(key_normed, cosine, sine_tab).astype(jnp.bfloat16)
    value_low = value_proj.astype(jnp.bfloat16)
    query_head_rows = query_lower.reshape(
        LOCAL_SEQUENCES, paired_rows, KEY_VALUE_HEADS, query_groups, HEAD_SIZE
    ).transpose(0, 2, 3, 1, 4)
    initial = (
        jnp.full(
            (LOCAL_SEQUENCES, KEY_VALUE_HEADS, query_groups, paired_rows),
            NEGATIVE_LIMIT,
            jnp.float32,
        ),
        jnp.zeros((LOCAL_SEQUENCES, KEY_VALUE_HEADS, query_groups, paired_rows), jnp.float32),
        jnp.zeros(
            (LOCAL_SEQUENCES, KEY_VALUE_HEADS, query_groups, paired_rows, HEAD_SIZE), jnp.float32
        ),
    )
    key_every, value_every = (
        lax.all_gather(key_low, "ctx", axis=0, tiled=True),
        lax.all_gather(value_low, "ctx", axis=0, tiled=True),
    )
    shard_total_count = key_every.shape[0] // token_per_device
    fold_query_group_size = 4
    key_block_list = key_every.reshape(
        shard_total_count // fold_query_group_size,
        fold_query_group_size,
        LOCAL_SEQUENCES,
        paired_rows,
        KEY_VALUE_HEADS,
        HEAD_SIZE,
    )
    value_block_list = value_every.reshape(
        shard_total_count // fold_query_group_size,
        fold_query_group_size,
        LOCAL_SEQUENCES,
        paired_rows,
        KEY_VALUE_HEADS,
        HEAD_SIZE,
    )
    first_devs = 0 // token_per_device + fold_query_group_size * jnp.arange(
        shard_total_count // fold_query_group_size, dtype=jnp.int32
    )

    def one_group(state_in, loop_item):
        key_group, value_group, first_dev = loop_item
        key_pos = group_positions(first_dev, fold_query_group_size, context_count, block_len)
        return (
            attend_group(
                state_in,
                query_head_rows,
                arrange(key_group),
                arrange(value_group),
                local_pos,
                key_pos,
                score_scale,
            ),
            None,
        )

    state_out, unused = lax.scan(one_group, initial, (key_block_list, value_block_list, first_devs))
    run_max, run_sum, run_acc = state_out
    log_sum = run_max + jnp.log(run_sum)
    attended = run_acc / run_sum[..., None]
    attended_low = (
        attended.transpose(0, 3, 1, 2, 4)
        .reshape(token_per_device, QUERY_HEADS * HEAD_SIZE)
        .astype(jnp.bfloat16)
    )
    mixed_attn = inputs + jnp.dot(attended_low, output_all, preferred_element_type=jnp.float32)
    normed_ffn, inverse_ffn = rms_apply(mixed_attn, ffn_gain)
    ffn_low = normed_ffn.astype(jnp.bfloat16)
    logits = jnp.dot(ffn_low, router_all, preferred_element_type=jnp.float32)
    chosen = (expert_ids[..., None] == jnp.arange(experts_all, dtype=jnp.int32)).astype(jnp.float32)
    picked = jnp.einsum("tje,te->tj", chosen, logits, precision=lax.Precision.HIGHEST)
    gate_probs = jax.nn.softmax(picked, -1)
    flat_ids = expert_ids.reshape(-1)
    route_marks = (flat_ids[:, None] == jnp.arange(experts_all, dtype=jnp.int32)).astype(jnp.int32)
    route_ranks = jnp.sum((jnp.cumsum(route_marks, 0) - 1) * route_marks, -1)
    slot_of_route = flat_ids * cap_rows + route_ranks
    route_of_slot = (
        jnp.full((experts_all * cap_rows,), routes, jnp.int32)
        .at[slot_of_route]
        .set(jnp.arange(routes, dtype=jnp.int32))
    )
    padded = jnp.concatenate([ffn_low, jnp.zeros((1, ffn_low.shape[1]), jnp.bfloat16)], 0)
    outgoing = padded[route_of_slot // TOP].reshape(experts_all, cap_rows, -1)
    arrived = lax.all_to_all(outgoing, "ctx", split_axis=0, concat_axis=0, tiled=True)

    def to_experts(buffer):
        return (
            buffer.reshape(context_count, exp_dev, cap_rows, -1)
            .transpose(1, 0, 2, 3)
            .reshape(exp_dev, context_count * cap_rows, -1)
        )

    def from_experts(buffer):
        return (
            buffer.reshape(exp_dev, context_count, cap_rows, -1)
            .transpose(1, 0, 2, 3)
            .reshape(context_count * exp_dev, cap_rows, -1)
        )

    expert_rows = to_experts(arrived)
    gate_all, up_all, down_all = (
        lax.all_gather(w_gate, "fsdp", axis=1, tiled=True),
        lax.all_gather(w_up, "fsdp", axis=1, tiled=True),
        lax.all_gather(w_down, "fsdp", axis=1, tiled=True),
    )
    gate_part = jnp.einsum(
        "esd,edf->esf", expert_rows, gate_all, preferred_element_type=jnp.float32
    )
    up_part = jnp.einsum("esd,edf->esf", expert_rows, up_all, preferred_element_type=jnp.float32)
    sigmoid_gate = jax.nn.sigmoid(gate_part)
    silu_gate = gate_part * sigmoid_gate
    hidden_low = (silu_gate * up_part).astype(jnp.bfloat16)
    results = jnp.einsum(
        "esf,efd->esd", hidden_low, down_all, preferred_element_type=jnp.float32
    ).astype(jnp.bfloat16)
    returned = lax.all_to_all(from_experts(results), "ctx", split_axis=0, concat_axis=0, tiled=True)
    route_out = returned.reshape(experts_all * cap_rows, -1)[slot_of_route].reshape(
        token_per_device, TOP, -1
    )
    mixed = (mixed_attn + jnp.sum(gate_probs[..., None] * route_out, 1)).astype(jnp.bfloat16)
    query_back, key_back, value_back, output_back, router_back = (
        lax.all_gather(w_query, ("ctx", "fsdp"), axis=0, tiled=True),
        lax.all_gather(key_weight, ("ctx", "fsdp"), axis=0, tiled=True),
        lax.all_gather(value_weight, ("ctx", "fsdp"), axis=0, tiled=True),
        lax.all_gather(w_output, ("ctx", "fsdp"), axis=0, tiled=True),
        lax.all_gather(w_router, ("ctx", "fsdp"), axis=0, tiled=True),
    )
    upstream = cotangent.astype(jnp.float32)
    dgates = jnp.sum(upstream[:, None, :] * route_out, -1)
    dpicked = gate_probs * (dgates - jnp.sum(gate_probs * dgates, -1, keepdims=True))
    dlogits_low = jnp.einsum("tj,tje->te", dpicked, chosen, precision=lax.Precision.HIGHEST).astype(
        jnp.bfloat16
    )
    router_grad = jnp.einsum("td,te->de", ffn_low, dlogits_low, preferred_element_type=jnp.float32)
    dresults = (
        (gate_probs[..., None] * upstream[:, None, :]).astype(jnp.bfloat16).reshape(routes, -1)
    )
    dresults = jnp.concatenate([dresults, jnp.zeros((1, dresults.shape[1]), jnp.bfloat16)], 0)
    dreturned = lax.all_to_all(
        dresults[route_of_slot].reshape(experts_all, cap_rows, -1),
        "ctx",
        split_axis=0,
        concat_axis=0,
        tiled=True,
    )
    dresult_rows = to_experts(dreturned)
    dhidden = jnp.einsum("esd,efd->esf", dresult_rows, down_all, preferred_element_type=jnp.float32)
    down_grad = jnp.einsum(
        "esf,esd->efd", hidden_low, dresult_rows, preferred_element_type=jnp.float32
    )
    dsilu_gate = sigmoid_gate * (1.0 + gate_part * (1.0 - sigmoid_gate))
    dgate_low = (dhidden * up_part * dsilu_gate).astype(jnp.bfloat16)
    dup_low = (dhidden * silu_gate).astype(jnp.bfloat16)
    gate_grad = jnp.einsum(
        "esd,esf->edf", expert_rows, dgate_low, preferred_element_type=jnp.float32
    )
    up_grad = jnp.einsum("esd,esf->edf", expert_rows, dup_low, preferred_element_type=jnp.float32)
    dexpert_rows = (
        jnp.einsum("esf,edf->esd", dgate_low, gate_all, preferred_element_type=jnp.float32)
        + jnp.einsum("esf,edf->esd", dup_low, up_all, preferred_element_type=jnp.float32)
    ).astype(jnp.bfloat16)
    dsent_rows = lax.all_to_all(
        from_experts(dexpert_rows), "ctx", split_axis=0, concat_axis=0, tiled=True
    )
    droutes = dsent_rows.reshape(experts_all * cap_rows, -1)[slot_of_route].reshape(
        token_per_device, TOP, -1
    )
    dffn_rows = jnp.sum(droutes.astype(jnp.float32), 1) + jnp.einsum(
        "te,de->td", dlogits_low, router_back, preferred_element_type=jnp.float32
    )
    expert_sums = (
        lax.psum_scatter(
            gate_grad.astype(jnp.bfloat16), "fsdp", scatter_dimension=1, tiled=True
        ).astype(jnp.float32),
        lax.psum_scatter(
            up_grad.astype(jnp.bfloat16), "fsdp", scatter_dimension=1, tiled=True
        ).astype(jnp.float32),
        lax.psum_scatter(
            down_grad.astype(jnp.bfloat16), "fsdp", scatter_dimension=1, tiled=True
        ).astype(jnp.float32),
    )
    dmixed_norm, ffn_gain_part = rms_back(mixed_attn, inverse_ffn, ffn_gain, dffn_rows)
    dmixed_attn = upstream + dmixed_norm
    dattn_low = dmixed_attn.astype(jnp.bfloat16)
    output_grad = jnp.einsum(
        "tc,td->cd", attended_low, dattn_low, preferred_element_type=jnp.float32
    )
    attended_lower_grad = jnp.einsum(
        "td,cd->tc", dattn_low, output_back, preferred_element_type=jnp.float32
    ).astype(jnp.bfloat16)
    output_heads_grad = attended_lower_grad.reshape(
        LOCAL_SEQUENCES, paired_rows, KEY_VALUE_HEADS, query_groups, HEAD_SIZE
    ).transpose(0, 2, 3, 1, 4)
    delta_row = jnp.sum(output_heads_grad.astype(jnp.float32) * attended, -1)
    key_recomputed, value_recomputed = (key_every, value_every)

    def score_grads(key_group, value_group, first_dev, query_group_size):
        key_row_matrix = arrange(key_group)
        value_rows = arrange(value_group)
        key_pos = group_positions(first_dev, query_group_size, context_count, block_len)
        scores = (
            jnp.einsum(
                "skgqd,swkd->skgqw",
                query_head_rows,
                key_row_matrix,
                preferred_element_type=jnp.float32,
            )
            * score_scale
        )
        allowed = key_pos[None, :] <= local_pos[:, None]
        weights_now = jnp.where(allowed, jnp.exp(scores - log_sum[..., None]), 0.0)
        dweights = jnp.einsum(
            "skgqd,swkd->skgqw", output_heads_grad, value_rows, preferred_element_type=jnp.float32
        )
        dscores = (weights_now * (dweights - delta_row[..., None])).astype(jnp.bfloat16)
        return (key_row_matrix, weights_now, dscores)

    def key_terms(weights_now, dscores, query_group_size):
        dkey_rows = jnp.einsum(
            "skgqw,skgqd->swkd", dscores, query_head_rows, preferred_element_type=jnp.float32
        )
        dvalue_rows = jnp.einsum(
            "skgqw,skgqd->swkd",
            weights_now.astype(jnp.bfloat16),
            output_heads_grad,
            preferred_element_type=jnp.float32,
        )
        return (unarrange(dkey_rows, query_group_size), unarrange(dvalue_rows, query_group_size))

    query_group_size = 4
    loop_step_count = context_count // query_group_size
    key_block_list = key_recomputed.reshape(
        loop_step_count, query_group_size, LOCAL_SEQUENCES, paired_rows, KEY_VALUE_HEADS, HEAD_SIZE
    )
    value_block_list = value_recomputed.reshape(
        loop_step_count, query_group_size, LOCAL_SEQUENCES, paired_rows, KEY_VALUE_HEADS, HEAD_SIZE
    )
    first_devs = query_group_size * jnp.arange(loop_step_count, dtype=jnp.int32)

    def back_group(dquery_acc, loop_item):
        key_group, value_group, first_dev = loop_item
        key_row_matrix, weights_now, dscores = score_grads(
            key_group, value_group, first_dev, query_group_size
        )
        dquery_acc = dquery_acc + jnp.einsum(
            "skgqw,swkd->skgqd", dscores, key_row_matrix, preferred_element_type=jnp.float32
        )
        return (dquery_acc, key_terms(weights_now, dscores, query_group_size))

    dquery_heads, key_value_pieces = lax.scan(
        back_group,
        jnp.zeros(query_head_rows.shape, jnp.float32),
        (key_block_list, value_block_list, first_devs),
    )
    key_grad_every = key_value_pieces[0].reshape(
        context_count * token_per_device, KEY_VALUE_HEADS, HEAD_SIZE
    )
    value_grad_every = key_value_pieces[1].reshape(
        context_count * token_per_device, KEY_VALUE_HEADS, HEAD_SIZE
    )
    dkey_own, value_local_grad = (
        lax.psum_scatter(key_grad_every, "ctx", scatter_dimension=0, tiled=True),
        lax.psum_scatter(value_grad_every, "ctx", scatter_dimension=0, tiled=True),
    )
    dquery = (
        (dquery_heads * score_scale)
        .transpose(0, 3, 1, 2, 4)
        .reshape(token_per_device, QUERY_HEADS, HEAD_SIZE)
    )
    dquery_proj, query_gain_part = rms_back(
        query_proj, query_inverse, query_gain, rope_back(dquery, cosine, sine_tab)
    )
    key_projection_grad, key_gain_part = rms_back(
        key_proj, key_inverse, key_gain, rope_back(dkey_own * score_scale, cosine, sine_tab)
    )
    dquery_low = dquery_proj.reshape(token_per_device, QUERY_HEADS * HEAD_SIZE).astype(jnp.bfloat16)
    key_lower_grad = key_projection_grad.reshape(
        token_per_device, KEY_VALUE_HEADS * HEAD_SIZE
    ).astype(jnp.bfloat16)
    value_lower_grad = value_local_grad.reshape(
        token_per_device, KEY_VALUE_HEADS * HEAD_SIZE
    ).astype(jnp.bfloat16)
    query_grad = jnp.einsum("td,tc->dc", normed_low, dquery_low, preferred_element_type=jnp.float32)
    key_grad = jnp.einsum(
        "td,tc->dc", normed_low, key_lower_grad, preferred_element_type=jnp.float32
    )
    value_grad = jnp.einsum(
        "td,tc->dc", normed_low, value_lower_grad, preferred_element_type=jnp.float32
    )
    dnormed = jnp.einsum("tc,dc->td", dquery_low, query_back, preferred_element_type=jnp.float32)
    dnormed = dnormed + jnp.einsum(
        "tc,dc->td", key_lower_grad, key_back, preferred_element_type=jnp.float32
    )
    dnormed = dnormed + jnp.einsum(
        "tc,dc->td", value_lower_grad, value_back, preferred_element_type=jnp.float32
    )
    dinput_norm, attention_gain_part = rms_back(inputs, inverse_attn, attention_gain, dnormed)
    d_tokens = (dmixed_attn + dinput_norm).astype(jnp.bfloat16)
    gain_sums = lax.psum(
        (attention_gain_part, ffn_gain_part, query_gain_part, key_gain_part), ("ctx", "fsdp")
    )
    layer_sums = (
        lax.psum_scatter(query_grad, ("ctx", "fsdp"), scatter_dimension=0, tiled=True),
        lax.psum_scatter(key_grad, ("ctx", "fsdp"), scatter_dimension=0, tiled=True),
        lax.psum_scatter(value_grad, ("ctx", "fsdp"), scatter_dimension=0, tiled=True),
        lax.psum_scatter(output_grad, ("ctx", "fsdp"), scatter_dimension=0, tiled=True),
        lax.psum_scatter(router_grad, ("ctx", "fsdp"), scatter_dimension=0, tiled=True),
    )
    return (
        mixed,
        d_tokens,
        gain_sums[0],
        gain_sums[1],
        gain_sums[2],
        gain_sums[3],
        layer_sums[0],
        layer_sums[1],
        layer_sums[2],
        layer_sums[3],
        layer_sums[4],
        expert_sums[0],
        expert_sums[1],
        expert_sums[2],
    )


MEMBERS = 4


def shift(block, axis, step):
    count = lax.axis_size(axis)
    return lax.ppermute(block, axis, [(i, (i + step) % count) for i in range(count)])


def swap(block, axis):
    return lax.ppermute(block, axis, [(0, 1), (1, 0)])


def after(block, *earlier):
    return lax.optimization_barrier((block,) + earlier)[0]


def gather_members(block):
    other = swap(block, "y")
    near = swap(jnp.stack([block, other]), "c")
    return jnp.stack([block, near[0], other, near[1]])


def scatter_members(parts):
    low = jnp.bfloat16
    near = swap(jnp.stack([parts[1].astype(low), parts[3].astype(low)]), "c")
    own = parts[0].astype(jnp.float32) + near[0].astype(jnp.float32)
    other = (parts[2].astype(jnp.float32) + near[1].astype(jnp.float32)).astype(low)
    return own + swap(other, "y").astype(jnp.float32)


def exchange_members(blocks):
    far = swap(jnp.stack([blocks[2], blocks[3]]), "y")
    near = swap(jnp.stack([blocks[1], far[1]]), "c")
    return [blocks[0], near[0], far[0], near[1]]


def pick(stack, index):
    return lax.dynamic_index_in_dim(stack, index, 0, keepdims=False)


def roped(raw, gain, cosine, sine):
    inverse = lax.rsqrt(jnp.mean(raw * raw, -1, keepdims=True) + EPS)
    scaled = raw * inverse * gain
    return scaled * cosine + pltpu.roll(scaled, HEAD_SIZE // 2, 1) * sine


def attend_kernel(heads_ref, q_ref, k_ref, v_ref, cos_ref, sin_ref, gain_ref, mask_ref, out_ref):
    queries = q_ref.shape[0] * q_ref.shape[2]
    keys = k_ref.shape[0] * k_ref.shape[1] * k_ref.shape[3]
    exponent = math.log2(math.e) / math.sqrt(HEAD_SIZE)
    q = roped(
        q_ref[...].reshape(queries, HEAD_SIZE), gain_ref[...], cos_ref[...], sin_ref[...]
    ).astype(jnp.bfloat16)
    k = k_ref[...].reshape(keys, HEAD_SIZE)
    v = v_ref[...].reshape(keys, HEAD_SIZE)
    scores = lax.dot_general(k, q, (((1,), (1,)), ((), ())), preferred_element_type=jnp.float32)
    weights = jnp.exp2(scores * exponent) * mask_ref[...]
    total = jnp.sum(weights, 0, keepdims=True)
    mixed = lax.dot_general(
        v,
        weights.astype(jnp.bfloat16),
        (((0,), (0,)), ((), ())),
        preferred_element_type=jnp.float32,
    )
    mixed = (mixed / total).T
    out_ref[...] = mixed.astype(jnp.bfloat16).reshape(out_ref.shape)


def attend_back_kernel(
    heads_ref,
    q_ref,
    up_ref,
    k_ref,
    v_ref,
    cos_ref,
    sin_ref,
    gain_ref,
    mask_ref,
    dq_ref,
    dkv_ref,
    dgain_ref,
):
    queries = q_ref.shape[0] * q_ref.shape[2]
    keys = k_ref.shape[0] * k_ref.shape[1] * k_ref.shape[3]
    score_scale = 1.0 / math.sqrt(HEAD_SIZE)
    exponent = math.log2(math.e) * score_scale
    cosine, sine, gain = cos_ref[...], sin_ref[...], gain_ref[...]
    raw = q_ref[...].reshape(queries, HEAD_SIZE)
    inverse = lax.rsqrt(jnp.mean(raw * raw, -1, keepdims=True) + EPS)
    unit = raw * inverse
    scaled = unit * gain
    q = (scaled * cosine + pltpu.roll(scaled, HEAD_SIZE // 2, 1) * sine).astype(jnp.bfloat16)
    up = up_ref[...].reshape(queries, HEAD_SIZE)
    k = k_ref[...].reshape(keys, HEAD_SIZE)
    v = v_ref[...].reshape(keys, HEAD_SIZE)
    across = (((1,), (1,)), ((), ()))
    down = (((0,), (0,)), ((), ()))
    scores = lax.dot_general(k, q, across, preferred_element_type=jnp.float32)
    weights = jnp.exp2(scores * exponent) * mask_ref[...]
    probs = weights * (1.0 / jnp.sum(weights, 0, keepdims=True))
    dprobs = lax.dot_general(v, up, across, preferred_element_type=jnp.float32)
    delta = jnp.sum(probs * dprobs, 0, keepdims=True)
    dscores = (probs * (dprobs - delta)).astype(jnp.bfloat16)
    dv = jnp.dot(probs.astype(jnp.bfloat16), up, preferred_element_type=jnp.float32)
    dk = jnp.dot(dscores, q, preferred_element_type=jnp.float32) * score_scale
    dq = lax.dot_general(k, dscores, down, preferred_element_type=jnp.float32).T * score_scale
    dkv = jnp.concatenate([dk, dv], 1).reshape(dkv_ref.shape)

    @pl.when(pl.program_id(1) == 0)
    def _():
        dkv_ref[...] = dkv

    @pl.when(pl.program_id(1) != 0)
    def _():
        dkv_ref[...] += dkv

    turned = dq * cosine - pltpu.roll(dq, HEAD_SIZE // 2, 1) * sine
    part = jnp.sum(turned * unit, 0, keepdims=True)
    part = jnp.concatenate([part, jnp.zeros((7, HEAD_SIZE), jnp.float32)], 0)
    first = (pl.program_id(0) == 0) & (pl.program_id(1) == 0)

    @pl.when(first)
    def _():
        dgain_ref[...] = part

    @pl.when(jnp.logical_not(first))
    def _():
        dgain_ref[...] += part

    turned = turned * gain
    back = inverse * (turned - unit * jnp.mean(turned * unit, -1, keepdims=True))
    dq_ref[...] = back.astype(jnp.bfloat16).reshape(dq_ref.shape)


def attention_specs(q, kv):
    nz, members, sequences, paired, _ = kv.shape
    q_block = (members, 1, paired, HEAD_SIZE)
    kv_block = (nz, members, 1, paired, HEAD_SIZE)
    keys, queries = nz * members * paired, members * paired
    own = pl.BlockSpec(q_block, lambda s, r, heads: (0, s, 0, heads[r]))
    relative = pl.BlockSpec(q_block, lambda s, r, heads: (0, s, 0, r))
    key = pl.BlockSpec(kv_block, lambda s, r, heads: (0, 0, s, 0, 0))
    value = pl.BlockSpec(kv_block, lambda s, r, heads: (0, 0, s, 0, 1))
    both = pl.BlockSpec(
        (nz, members, 1, paired, 2 * HEAD_SIZE), lambda s, r, heads: (0, 0, s, 0, 0)
    )
    fixed = lambda shape: pl.BlockSpec(shape, lambda s, r, heads: (0, 0))
    tables = [
        fixed((queries, HEAD_SIZE)),
        fixed((queries, HEAD_SIZE)),
        fixed((1, HEAD_SIZE)),
        fixed((keys, queries)),
    ]
    return own, relative, key, value, both, fixed, tables


def attend(heads, q, kv, cosine, sine, gain, mask):
    members, sequences, paired, width = q.shape
    own, relative, key, value, both, fixed, tables = attention_specs(q, kv)
    count = heads.shape[0]
    elements = sequences * count * mask.size
    return pl.pallas_call(
        attend_kernel,
        grid_spec=pltpu.PrefetchScalarGridSpec(
            num_scalar_prefetch=1,
            grid=(sequences, count),
            in_specs=[own, key, value] + tables,
            out_specs=relative,
        ),
        out_shape=jax.ShapeDtypeStruct(
            (members, sequences, paired, count * HEAD_SIZE), jnp.bfloat16
        ),
        compiler_params=pltpu.CompilerParams(vmem_limit_bytes=40 * 2**20),
        cost_estimate=pl.CostEstimate(
            flops=4 * elements * HEAD_SIZE, bytes_accessed=8 * 2**20, transcendentals=elements
        ),
    )(heads, q, kv, kv, cosine, sine, gain, mask)


def attend_back(heads, q, up, kv, cosine, sine, gain, mask):
    members, sequences, paired, width = q.shape
    own, relative, key, value, both, fixed, tables = attention_specs(q, kv)
    count = heads.shape[0]
    elements = sequences * count * mask.size
    return pl.pallas_call(
        attend_back_kernel,
        grid_spec=pltpu.PrefetchScalarGridSpec(
            num_scalar_prefetch=1,
            grid=(sequences, count),
            in_specs=[own, relative, key, value] + tables,
            out_specs=(own, both, fixed((8, HEAD_SIZE))),
        ),
        out_shape=(
            jax.ShapeDtypeStruct((members, sequences, paired, count * HEAD_SIZE), jnp.bfloat16),
            jax.ShapeDtypeStruct(kv.shape, jnp.float32),
            jax.ShapeDtypeStruct((8, HEAD_SIZE), jnp.float32),
        ),
        compiler_params=pltpu.CompilerParams(vmem_limit_bytes=40 * 2**20),
        cost_estimate=pl.CostEstimate(
            flops=10 * elements * HEAD_SIZE, bytes_accessed=16 * 2**20, transcendentals=elements
        ),
    )(heads, q, up, kv, kv, cosine, sine, gain, mask)


def dot32(subscripts, left, right):
    return jnp.einsum(subscripts, left, right, preferred_element_type=jnp.float32)


def member_layer(
    tokens,
    cotangent,
    expert_ids,
    attention_gain,
    ffn_gain,
    query_gain,
    key_gain,
    w_query,
    key_weight,
    value_weight,
    w_output,
    w_router,
    w_gate,
    w_up,
    w_down,
):
    low, wide = jnp.bfloat16, jnp.float32
    nz = lax.axis_size("z")
    zi, yi, ci, xi = (lax.axis_index(axis) for axis in ("z", "y", "c", "x"))
    member = 2 * yi + ci
    context_count = nz * MEMBERS
    rows, model = tokens.shape
    paired = rows // LOCAL_SEQUENCES
    block_len = paired // 2
    groups = QUERY_HEADS // KEY_VALUE_HEADS
    experts_all = w_router.shape[1]
    relative = jnp.arange(MEMBERS, dtype=jnp.int32)
    from_z = (zi - jnp.arange(nz, dtype=jnp.int32)) % nz
    members = member ^ relative

    inputs = tokens.astype(wide)
    normed_attn, inverse_attn = rms_apply(inputs, attention_gain)
    normed_low = normed_attn.astype(low)
    normed_all = gather_members(normed_low).reshape(MEMBERS * rows, model)

    piece = w_query.shape[0]
    columns = jnp.concatenate(
        [w.reshape(piece, KEY_VALUE_HEADS, -1) for w in (w_query, key_weight, value_weight)], -1
    ).transpose(1, 0, 2)
    width = columns.shape[-1]
    parts = exchange_members([pick(columns, members[j]) for j in range(MEMBERS)])
    ordered = jnp.stack(parts)[members]
    qkv_weight = jnp.zeros((nz, MEMBERS, 2, piece, width), low)
    last = None
    for k in range(nz):
        held = ordered if k == 0 else shift(ordered, "z", k)
        crossed = swap(held, "x")
        qkv_weight = lax.dynamic_update_slice(
            qkv_weight, held[None, :, None], (from_z[k], 0, xi, 0, 0)
        )
        qkv_weight = lax.dynamic_update_slice(
            qkv_weight, crossed[None, :, None], (from_z[k], 0, 1 - xi, 0, 0)
        )
        last = held
    qkv_weight = qkv_weight.reshape(model, width)

    router = jnp.stack([w_router] + [shift(w_router, "z", k) for k in range(1, nz)])
    for axis in ("y", "c", "x"):
        router = jnp.stack([router, swap(router, axis)], 1)
    router = router.reshape(nz, 2, 2, 2, piece, experts_all)
    order_z = from_z_index = (zi - jnp.arange(nz, dtype=jnp.int32)) % nz
    router = router[order_z]
    two = jnp.arange(2, dtype=jnp.int32)
    router = router[:, two ^ xi][:, :, two ^ ci][:, :, :, two ^ yi]
    router_all = router.transpose(0, 3, 2, 1, 4, 5).reshape(model, experts_all)
    ids = expert_ids.T
    ids_all = jnp.stack([ids] + [shift(ids, "z", k) for k in range(1, nz)])
    ids_all = jnp.stack([ids_all, swap(ids_all, "y")], 1)
    near = swap(ids_all, "c")
    ids_all = jnp.stack([ids_all, near], 2).reshape(nz, MEMBERS, TOP, rows)
    own_expert = zi * MEMBERS + member
    named = jnp.any(ids_all == own_expert, 2)
    before = (
        jnp.arange(rows, dtype=jnp.int32)[:, None] <= jnp.arange(rows, dtype=jnp.int32)[None, :]
    )
    ranks = dot32("kjs,st->kjt", named.astype(low), before.astype(low)).astype(jnp.int32) - 1
    cap_rows = rows * TOP * 5 // (4 * experts_all)
    slots = -(-cap_rows // 16) * 16
    places = (
        (ranks[:, :, None, :] == jnp.arange(slots, dtype=jnp.int32)[:, None])
        & named[:, :, None, :]
    ).astype(low)

    qkv = jnp.dot(normed_all, qkv_weight, preferred_element_type=wide)
    qkv = qkv.reshape(MEMBERS, LOCAL_SEQUENCES, paired, width)
    all_pos = jax.vmap(lambda device: shard_positions(device, context_count, block_len))(
        (from_z[:, None] * MEMBERS + members[None, :]).reshape(-1)
    )
    own_pos = all_pos[:MEMBERS].reshape(-1)
    mask = (all_pos.reshape(-1)[:, None] <= own_pos[None, :]).astype(wide)
    cosine, sine_tab = rotary(own_pos, HEAD_SIZE)
    cosine, sine_tab = cosine[:, 0], sine_tab[:, 0]
    half = HEAD_SIZE // 2
    sine = jnp.concatenate([-sine_tab[:, :half], sine_tab[:, half:]], -1)
    row_cosine = cosine.reshape(MEMBERS, 1, paired, HEAD_SIZE)
    row_sine = sine_tab.reshape(MEMBERS, 1, paired, HEAD_SIZE)
    query_width = groups * HEAD_SIZE
    key_proj = qkv[..., query_width : query_width + HEAD_SIZE]
    key_normed, key_inverse = rms_apply(key_proj, key_gain)
    key_low = rope_apply(key_normed, row_cosine, row_sine).astype(low)
    key_value = jnp.concatenate([key_low, qkv[..., query_width + HEAD_SIZE :].astype(low)], -1)
    key_value = jnp.stack([key_value] + [shift(key_value, "z", k) for k in range(1, nz)])

    relative_heads = jnp.arange(groups, dtype=jnp.int32)
    heads = ((relative_heads & 3) ^ member) * 2 + ((relative_heads >> 2) ^ xi)
    gain_row = query_gain[None]
    attended = attend(heads, qkv, key_value, cosine, sine, gain_row, mask)
    attended = attended.reshape(MEMBERS * rows, query_width)

    head_rows = w_output.shape[0]
    behind = after(w_output, last)
    planes = jnp.stack([behind] + [shift(behind, "z", k) for k in range(1, nz)])
    wanted = exchange_members([pick(planes, (zi - members[j]) % nz) for j in range(MEMBERS)])
    wanted = jnp.stack(wanted)
    output_weight = jnp.stack([wanted, swap(wanted, "x")]).reshape(query_width, model)
    mixed_part = jnp.dot(attended, output_weight, preferred_element_type=wide)
    mixed_attn = inputs + scatter_members(mixed_part.reshape(MEMBERS, rows, model))
    normed_ffn, inverse_ffn = rms_apply(mixed_attn, ffn_gain)
    ffn_low = normed_ffn.astype(low)

    logits = dot32("de,td->et", router_all, ffn_low)
    chosen = jnp.any(
        ids[:, None, :] == jnp.arange(experts_all, dtype=jnp.int32)[None, :, None], 0
    )
    highest = jnp.max(jnp.where(chosen, logits, NEGATIVE_LIMIT), 0, keepdims=True)
    raised = jnp.where(chosen, jnp.exp(jnp.where(chosen, logits, highest) - highest), 0.0)
    gates = raised / jnp.sum(raised, 0, keepdims=True)
    gates_all = jnp.stack([gates] + [shift(gates, "z", k) for k in range(1, nz)])
    gates_all = jnp.stack([gates_all, swap(gates_all, "y")], 1)
    near = swap(gates_all, "c")
    gates_all = jnp.stack([gates_all, near], 2).reshape(nz, MEMBERS, experts_all, rows)
    own_gates = lax.dynamic_index_in_dim(gates_all, own_expert, 2, keepdims=False)

    def whole(part, earlier):
        part = after(part, earlier)
        other = swap(part, "x")
        full = jnp.zeros((2,) + part.shape[1:], low)
        full = lax.dynamic_update_slice(full, part, (xi, 0, 0))
        full = lax.dynamic_update_slice(full, other, (1 - xi, 0, 0))
        return full.reshape(2 * part.shape[1], part.shape[2])

    gate_all, up_all, down_all = (
        whole(w_gate, last),
        whole(w_up, last),
        whole(w_down, last),
    )

    def spread(block):
        return [gather_members(block if k == 0 else shift(block, "z", k)) for k in range(nz)]

    cotangents = spread(after(cotangent, last))
    arrived = spread(ffn_low)
    sent, dsent, dgates, kept = [], [], [], []
    for k in range(nz):
        place, gate_col = places[k], own_gates[k][..., None]
        upstream = cotangents[k]
        expert_rows = dot32("jst,jtd->jsd", place, arrived[k]).astype(low)
        expert_rows = expert_rows.reshape(MEMBERS * slots, model)
        gate_part = jnp.dot(expert_rows, gate_all, preferred_element_type=wide)
        up_part = jnp.dot(expert_rows, up_all, preferred_element_type=wide)
        sigmoid_gate = jax.nn.sigmoid(gate_part)
        silu_gate = gate_part * sigmoid_gate
        hidden_low = (silu_gate * up_part).astype(low)
        results = jnp.dot(hidden_low, down_all, preferred_element_type=wide).astype(low)
        token_results = dot32(
            "jst,jsd->jtd", place, results.reshape(MEMBERS, slots, model)
        ).astype(low)
        sent.append((gate_col * token_results).astype(low))
        dgates.append(jnp.sum(upstream.astype(wide) * token_results.astype(wide), -1))
        dresults = dot32("jst,jtd->jsd", place, (gate_col * upstream).astype(low)).astype(low)
        dresults = dresults.reshape(MEMBERS * slots, model)
        dhidden = dot32("sd,fd->sf", dresults, down_all)
        dsilu_gate = sigmoid_gate * (1.0 + gate_part * (1.0 - sigmoid_gate))
        dgate_low = (dhidden * up_part * dsilu_gate).astype(low)
        dup_low = (dhidden * silu_gate).astype(low)
        dexpert_rows = (
            dot32("sf,df->sd", dgate_low, gate_all) + dot32("sf,df->sd", dup_low, up_all)
        ).astype(low)
        dsent.append(
            dot32("jst,jsd->jtd", place, dexpert_rows.reshape(MEMBERS, slots, model)).astype(low)
        )
        kept.append((expert_rows, hidden_low, dresults, dgate_low, dup_low))

    def collect(parts):
        total = None
        for k in range(nz):
            mine = scatter_members(parts[k])
            if k == 0:
                total = mine
            else:
                total = total + shift(mine.astype(low), "z", -k).astype(wide)
        return total

    dffn_routed = collect(dsent)
    mixed = (mixed_attn + collect(sent)).astype(low)
    returned = jnp.stack(dgates)
    near = swap(returned[:, 1::2], "c")
    returned = jnp.stack([returned[:, 0::2], near], 2)
    far = swap(returned[:, 1], "y")
    returned = jnp.stack([returned[:, 0], far], 1)
    returned = jnp.stack([returned[0]] + [shift(returned[k], "z", -k) for k in range(1, nz)])
    returned = returned.reshape(context_count, rows)
    expert_index = jnp.arange(context_count, dtype=jnp.int32)
    dgates_own = returned[
        ((expert_index // MEMBERS - zi) % nz) * MEMBERS + ((expert_index % MEMBERS) ^ member)
    ]
    dlogits = gates * (dgates_own - jnp.sum(gates * dgates_own, 0, keepdims=True))
    dlogits_low = dlogits.astype(low)
    router_grad = dot32("et,td->ed", dlogits_low, ffn_low)

    expert_rows, hidden_low, dresults, dgate_low, dup_low = (
        jnp.concatenate(column, 0) for column in zip(*kept)
    )

    def halves(grad):
        rows_half = grad.shape[0] // 2
        own = lax.dynamic_slice_in_dim(grad, xi * rows_half, rows_half, 0)
        other = lax.dynamic_slice_in_dim(grad, (1 - xi) * rows_half, rows_half, 0)
        return (own + swap(other.astype(low), "x").astype(wide))[None]

    gate_grad = halves(dot32("sd,sf->df", expert_rows, dgate_low))
    up_grad = halves(dot32("sd,sf->df", expert_rows, dup_low))
    down_grad = halves(dot32("sf,sd->fd", hidden_low, dresults))

    upstream = cotangent.astype(wide)
    dffn_rows = dffn_routed + dot32("et,de->td", dlogits_low, router_all)
    dmixed_norm, ffn_gain_part = rms_back(mixed_attn, inverse_ffn, ffn_gain, dffn_rows)
    dmixed_attn = upstream + dmixed_norm
    dattn_all = gather_members(dmixed_attn.astype(low)).reshape(MEMBERS * rows, model)
    attended_grad = dot32("td,cd->tc", dattn_all, output_weight).astype(low)
    attended_grad = attended_grad.reshape(MEMBERS, LOCAL_SEQUENCES, paired, query_width)
    dquery_low, dkey_value, query_gain_part = attend_back(
        heads, qkv, attended_grad, key_value, cosine, sine, gain_row, mask
    )
    query_gain_part = query_gain_part[0]
    dquery_low = dquery_low.reshape(MEMBERS * rows, query_width)
    dkey_value_own = dkey_value[0]
    for k in range(1, nz):
        dkey_value_own = dkey_value_own + shift(dkey_value[k].astype(low), "z", -k).astype(wide)

    output_part = dot32("tc,td->cd", attended, dattn_all).astype(low)
    output_part = output_part.reshape(2, MEMBERS, head_rows, model)
    output_part = (
        output_part[0].astype(wide) + swap(output_part[1], "x").astype(wide)
    ).astype(low)
    output_part = exchange_members([output_part[j] for j in range(MEMBERS)])
    output_part = jnp.stack(output_part)[members]
    output_grad = pick(output_part, zi).astype(wide)
    for k in range(1, nz):
        sending = pick(output_part, (zi + k) % nz)
        output_grad = output_grad + shift(sending, "z", k).astype(wide)

    def weight_grad(grad_low):
        part = dot32("td,tc->dc", normed_all, grad_low)
        part = part.reshape(nz, MEMBERS, 2, piece, grad_low.shape[1])
        total = None
        for k in range(nz):
            plane = pick(part, (zi + k) % nz)
            own = lax.dynamic_index_in_dim(plane, xi, 1, keepdims=False)
            other = lax.dynamic_index_in_dim(plane, 1 - xi, 1, keepdims=False)
            summed = own + swap(other.astype(low), "x").astype(wide)
            if k == 0:
                total = summed
            else:
                total = total + shift(summed.astype(low), "z", k).astype(wide)
        total = total.astype(low)
        pieces = exchange_members([pick(total, members[j]) for j in range(MEMBERS)])
        return jnp.stack(pieces)[members].astype(wide)

    query_grad = weight_grad(dquery_low).transpose(1, 0, 2).reshape(piece, -1)
    dkey, dvalue = dkey_value_own[..., :HEAD_SIZE], dkey_value_own[..., HEAD_SIZE:]
    dkey_proj, key_gain_part = rms_back(
        key_proj, key_inverse, key_gain, rope_back(dkey, row_cosine, row_sine)
    )
    dkey_value_low = jnp.concatenate([dkey_proj, dvalue], -1).astype(low)
    dkey_value_low = dkey_value_low.reshape(MEMBERS * rows, 2 * HEAD_SIZE)
    key_value_grad = weight_grad(dkey_value_low)
    key_grad = key_value_grad[..., :HEAD_SIZE].transpose(1, 0, 2).reshape(piece, -1)
    value_grad = key_value_grad[..., HEAD_SIZE:].transpose(1, 0, 2).reshape(piece, -1)
    dnormed = dot32("tc,dc->td", dquery_low, qkv_weight[:, :query_width])
    dnormed = dnormed + dot32("tc,dc->td", dkey_value_low, qkv_weight[:, query_width:])
    dnormed = scatter_members(dnormed.reshape(MEMBERS, rows, model))
    dinput_norm, attention_gain_part = rms_back(inputs, inverse_attn, attention_gain, dnormed)
    d_tokens = (dmixed_attn + dinput_norm).astype(low)

    def everywhere(part):
        for axis in ("x", "y", "c"):
            part = part + swap(part, axis)
        return part + sum(shift(part, "z", k) for k in range(1, nz))

    early = everywhere(jnp.concatenate([router_grad, ffn_gain_part[None]], 0))
    device = (zi * MEMBERS + member) * 2 + xi
    router_own = lax.dynamic_slice_in_dim(early[:experts_all], device * piece, piece, 1).T
    gains = everywhere(
        jnp.concatenate([attention_gain_part, query_gain_part, key_gain_part]).reshape(-1, 128)
    ).reshape(-1)
    return (
        mixed,
        d_tokens,
        gains[:model],
        early[experts_all],
        gains[model : model + HEAD_SIZE],
        gains[model + HEAD_SIZE :],
        query_grad,
        key_grad,
        value_grad,
        output_grad,
        router_own,
        gate_grad,
        up_grad,
        down_grad,
    )


def solution(mesh):
    contexts, pairs = mesh.shape["ctx"], mesh.shape["fsdp"]
    planes = contexts // MEMBERS
    if planes == KEY_VALUE_HEADS and pairs * MEMBERS * KEY_VALUE_HEADS == QUERY_HEADS:
        layer, every, split = member_layer, ("z", "y", "c", "x"), ("z", "y", "c")
        pair = "x"
        mesh = Mesh(mesh.devices.reshape(planes, 2, 2, pairs), every)
    else:
        layer, every, split, pair = routed_layer, ("ctx", "fsdp"), "ctx", "fsdp"
    by_row = P(every, None)
    by_expert = P(split, pair, None)
    return jax.shard_map(
        layer,
        mesh=mesh,
        in_specs=(by_row,) * 3 + (P(),) * 4 + (by_row,) * 5 + (by_expert,) * 3,
        out_specs=(by_row,) * 2 + (P(),) * 4 + (by_row,) * 5 + (by_expert,) * 3,
        check_vma=False,
    )
```

```python
import functools
import math

import jax
import jax.numpy as jnp
from jax import lax
from jax.experimental import pallas as pl
from jax.experimental.pallas import tpu as pltpu
from jax.sharding import Mesh
from jax.sharding import PartitionSpec as P

QUERY_HEADS = 32
KEY_VALUE_HEADS = 4
HEAD_SIZE = 128
TOP = 8
LOCAL_SEQUENCES = 3


EPS = 1e-06
THETA = 1000000.0
NEGATIVE_LIMIT = -1e30


def shard_positions(device, context_count, block_len):
    within = jnp.arange(2 * block_len, dtype=jnp.int32)
    lower_pos = device * block_len + within
    upper_pos = (2 * context_count - 1 - device) * block_len + within - block_len
    return jnp.where(within < block_len, lower_pos, upper_pos)


def group_positions(first_dev, query_group_size, context_count, block_len):
    devices = first_dev + jnp.arange(query_group_size, dtype=jnp.int32)
    return jax.vmap(lambda device: shard_positions(device, context_count, block_len))(
        devices
    ).reshape(-1)


def rotary(positions, head_width):
    half_width = head_width // 2
    frequency = jnp.exp(
        -math.log(THETA) * (2.0 * jnp.arange(half_width, dtype=jnp.float32)) / head_width
    )
    angles = positions.astype(jnp.float32)[:, None] * frequency[None, :]
    angles = jnp.concatenate([angles, angles], -1)
    return (jnp.cos(angles)[:, None, :], jnp.sin(angles)[:, None, :])


def rope_apply(value_rows_list, cosine, sine_tab):
    half_width = value_rows_list.shape[-1] // 2
    turned = jnp.concatenate(
        [-value_rows_list[..., half_width:], value_rows_list[..., :half_width]], -1
    )
    return value_rows_list * cosine + turned * sine_tab


def rope_back(upstream, cosine, sine_tab):
    half_width = upstream.shape[-1] // 2
    moved_part = upstream * sine_tab
    return upstream * cosine + jnp.concatenate(
        [moved_part[..., half_width:], -moved_part[..., :half_width]], -1
    )


def rms_apply(value_rows_list, gain_vec):
    inverse = lax.rsqrt(jnp.mean(value_rows_list * value_rows_list, -1, keepdims=True) + EPS)
    return (value_rows_list * inverse * gain_vec, inverse)


def rms_back(value_rows_list, inverse, gain_vec, upstream):
    normalized_input = value_rows_list * inverse
    gain_part = jnp.sum((upstream * normalized_input).reshape(-1, value_rows_list.shape[-1]), 0)
    scaled = upstream * gain_vec
    back_part = inverse * (
        scaled - normalized_input * jnp.mean(scaled * normalized_input, -1, keepdims=True)
    )
    return (back_part, gain_part)


def arrange(blocks):
    query_group_size, seq_count, paired_rows, heads_kv, head_dim = blocks.shape
    return blocks.transpose(1, 0, 2, 3, 4).reshape(
        seq_count, query_group_size * paired_rows, heads_kv, head_dim
    )


def unarrange(rows_all, query_group_size):
    seq_count, width_all, heads_kv, head_dim = rows_all.shape
    return rows_all.reshape(
        seq_count, query_group_size, width_all // query_group_size, heads_kv, head_dim
    ).transpose(1, 0, 2, 3, 4)


def attend_group(state_now, queries, key_row_matrix, value_rows, query_pos, key_pos, score_scale):
    run_max, run_sum, run_acc = state_now
    scores = (
        jnp.einsum("skgqd,swkd->skgqw", queries, key_row_matrix, preferred_element_type=jnp.float32)
        * score_scale
    )
    allowed = key_pos[None, :] <= query_pos[:, None]
    new_max = jnp.maximum(run_max, jnp.max(jnp.where(allowed, scores, NEGATIVE_LIMIT), -1))
    weights_now = jnp.where(allowed, jnp.exp(scores - new_max[..., None]), 0.0)
    factor = jnp.exp(run_max - new_max)
    new_sum = run_sum * factor + jnp.sum(weights_now, -1)
    update = jnp.einsum(
        "skgqw,swkd->skgqd",
        weights_now.astype(jnp.bfloat16),
        value_rows,
        preferred_element_type=jnp.float32,
    )
    return (new_max, new_sum, run_acc * factor[..., None] + update)


def routed_layer(
    tokens,
    cotangent,
    expert_ids,
    attention_gain,
    ffn_gain,
    query_gain,
    key_gain,
    w_query,
    key_weight,
    value_weight,
    w_output,
    w_router,
    w_gate,
    w_up,
    w_down,
):
    context_count = lax.axis_size("ctx")
    ctx_here = lax.axis_index("ctx")
    token_per_device = tokens.shape[0]
    block_len = token_per_device // (2 * LOCAL_SEQUENCES)
    paired_rows = 2 * block_len
    query_groups = QUERY_HEADS // KEY_VALUE_HEADS
    score_scale = 1.0 / math.sqrt(HEAD_SIZE)
    experts_all = w_router.shape[1]
    exp_dev = w_gate.shape[0]
    cap_rows = token_per_device * TOP * 5 // (4 * experts_all)
    routes = token_per_device * TOP
    inputs = tokens.astype(jnp.float32)
    normed_attn, inverse_attn = rms_apply(inputs, attention_gain)
    normed_low = normed_attn.astype(jnp.bfloat16)
    query_all, key_all, value_all, output_all, router_all = (
        lax.all_gather(w_query, ("ctx", "fsdp"), axis=0, tiled=True),
        lax.all_gather(key_weight, ("ctx", "fsdp"), axis=0, tiled=True),
        lax.all_gather(value_weight, ("ctx", "fsdp"), axis=0, tiled=True),
        lax.all_gather(w_output, ("ctx", "fsdp"), axis=0, tiled=True),
        lax.all_gather(w_router, ("ctx", "fsdp"), axis=0, tiled=True),
    )
    local_pos = shard_positions(ctx_here, context_count, block_len)
    row_pos = jnp.tile(local_pos, LOCAL_SEQUENCES)
    cosine, sine_tab = rotary(row_pos, HEAD_SIZE)
    query_proj = jnp.dot(normed_low, query_all, preferred_element_type=jnp.float32).reshape(
        token_per_device, QUERY_HEADS, HEAD_SIZE
    )
    key_proj = jnp.dot(normed_low, key_all, preferred_element_type=jnp.float32).reshape(
        token_per_device, KEY_VALUE_HEADS, HEAD_SIZE
    )
    value_proj = jnp.dot(normed_low, value_all, preferred_element_type=jnp.float32).reshape(
        token_per_device, KEY_VALUE_HEADS, HEAD_SIZE
    )
    query_normed, query_inverse = rms_apply(query_proj, query_gain)
    key_normed, key_inverse = rms_apply(key_proj, key_gain)
    query_lower = rope_apply(query_normed, cosine, sine_tab).astype(jnp.bfloat16)
    key_low = rope_apply(key_normed, cosine, sine_tab).astype(jnp.bfloat16)
    value_low = value_proj.astype(jnp.bfloat16)
    query_head_rows = query_lower.reshape(
        LOCAL_SEQUENCES, paired_rows, KEY_VALUE_HEADS, query_groups, HEAD_SIZE
    ).transpose(0, 2, 3, 1, 4)
    initial = (
        jnp.full(
            (LOCAL_SEQUENCES, KEY_VALUE_HEADS, query_groups, paired_rows),
            NEGATIVE_LIMIT,
            jnp.float32,
        ),
        jnp.zeros((LOCAL_SEQUENCES, KEY_VALUE_HEADS, query_groups, paired_rows), jnp.float32),
        jnp.zeros(
            (LOCAL_SEQUENCES, KEY_VALUE_HEADS, query_groups, paired_rows, HEAD_SIZE), jnp.float32
        ),
    )
    key_every, value_every = (
        lax.all_gather(key_low, "ctx", axis=0, tiled=True),
        lax.all_gather(value_low, "ctx", axis=0, tiled=True),
    )
    shard_total_count = key_every.shape[0] // token_per_device
    fold_query_group_size = 4
    key_block_list = key_every.reshape(
        shard_total_count // fold_query_group_size,
        fold_query_group_size,
        LOCAL_SEQUENCES,
        paired_rows,
        KEY_VALUE_HEADS,
        HEAD_SIZE,
    )
    value_block_list = value_every.reshape(
        shard_total_count // fold_query_group_size,
        fold_query_group_size,
        LOCAL_SEQUENCES,
        paired_rows,
        KEY_VALUE_HEADS,
        HEAD_SIZE,
    )
    first_devs = 0 // token_per_device + fold_query_group_size * jnp.arange(
        shard_total_count // fold_query_group_size, dtype=jnp.int32
    )

    def one_group(state_in, loop_item):
        key_group, value_group, first_dev = loop_item
        key_pos = group_positions(first_dev, fold_query_group_size, context_count, block_len)
        return (
            attend_group(
                state_in,
                query_head_rows,
                arrange(key_group),
                arrange(value_group),
                local_pos,
                key_pos,
                score_scale,
            ),
            None,
        )

    state_out, unused = lax.scan(one_group, initial, (key_block_list, value_block_list, first_devs))
    run_max, run_sum, run_acc = state_out
    log_sum = run_max + jnp.log(run_sum)
    attended = run_acc / run_sum[..., None]
    attended_low = (
        attended.transpose(0, 3, 1, 2, 4)
        .reshape(token_per_device, QUERY_HEADS * HEAD_SIZE)
        .astype(jnp.bfloat16)
    )
    mixed_attn = inputs + jnp.dot(attended_low, output_all, preferred_element_type=jnp.float32)
    normed_ffn, inverse_ffn = rms_apply(mixed_attn, ffn_gain)
    ffn_low = normed_ffn.astype(jnp.bfloat16)
    logits = jnp.dot(ffn_low, router_all, preferred_element_type=jnp.float32)
    chosen = (expert_ids[..., None] == jnp.arange(experts_all, dtype=jnp.int32)).astype(jnp.float32)
    picked = jnp.einsum("tje,te->tj", chosen, logits, precision=lax.Precision.HIGHEST)
    gate_probs = jax.nn.softmax(picked, -1)
    flat_ids = expert_ids.reshape(-1)
    route_marks = (flat_ids[:, None] == jnp.arange(experts_all, dtype=jnp.int32)).astype(jnp.int32)
    route_ranks = jnp.sum((jnp.cumsum(route_marks, 0) - 1) * route_marks, -1)
    slot_of_route = flat_ids * cap_rows + route_ranks
    route_of_slot = (
        jnp.full((experts_all * cap_rows,), routes, jnp.int32)
        .at[slot_of_route]
        .set(jnp.arange(routes, dtype=jnp.int32))
    )
    padded = jnp.concatenate([ffn_low, jnp.zeros((1, ffn_low.shape[1]), jnp.bfloat16)], 0)
    outgoing = padded[route_of_slot // TOP].reshape(experts_all, cap_rows, -1)
    arrived = lax.all_to_all(outgoing, "ctx", split_axis=0, concat_axis=0, tiled=True)

    def to_experts(buffer):
        return (
            buffer.reshape(context_count, exp_dev, cap_rows, -1)
            .transpose(1, 0, 2, 3)
            .reshape(exp_dev, context_count * cap_rows, -1)
        )

    def from_experts(buffer):
        return (
            buffer.reshape(exp_dev, context_count, cap_rows, -1)
            .transpose(1, 0, 2, 3)
            .reshape(context_count * exp_dev, cap_rows, -1)
        )

    expert_rows = to_experts(arrived)
    gate_all, up_all, down_all = (
        lax.all_gather(w_gate, "fsdp", axis=1, tiled=True),
        lax.all_gather(w_up, "fsdp", axis=1, tiled=True),
        lax.all_gather(w_down, "fsdp", axis=1, tiled=True),
    )
    gate_part = jnp.einsum(
        "esd,edf->esf", expert_rows, gate_all, preferred_element_type=jnp.float32
    )
    up_part = jnp.einsum("esd,edf->esf", expert_rows, up_all, preferred_element_type=jnp.float32)
    sigmoid_gate = jax.nn.sigmoid(gate_part)
    silu_gate = gate_part * sigmoid_gate
    hidden_low = (silu_gate * up_part).astype(jnp.bfloat16)
    results = jnp.einsum(
        "esf,efd->esd", hidden_low, down_all, preferred_element_type=jnp.float32
    ).astype(jnp.bfloat16)
    returned = lax.all_to_all(from_experts(results), "ctx", split_axis=0, concat_axis=0, tiled=True)
    route_out = returned.reshape(experts_all * cap_rows, -1)[slot_of_route].reshape(
        token_per_device, TOP, -1
    )
    mixed = (mixed_attn + jnp.sum(gate_probs[..., None] * route_out, 1)).astype(jnp.bfloat16)
    query_back, key_back, value_back, output_back, router_back = (
        lax.all_gather(w_query, ("ctx", "fsdp"), axis=0, tiled=True),
        lax.all_gather(key_weight, ("ctx", "fsdp"), axis=0, tiled=True),
        lax.all_gather(value_weight, ("ctx", "fsdp"), axis=0, tiled=True),
        lax.all_gather(w_output, ("ctx", "fsdp"), axis=0, tiled=True),
        lax.all_gather(w_router, ("ctx", "fsdp"), axis=0, tiled=True),
    )
    upstream = cotangent.astype(jnp.float32)
    dgates = jnp.sum(upstream[:, None, :] * route_out, -1)
    dpicked = gate_probs * (dgates - jnp.sum(gate_probs * dgates, -1, keepdims=True))
    dlogits_low = jnp.einsum("tj,tje->te", dpicked, chosen, precision=lax.Precision.HIGHEST).astype(
        jnp.bfloat16
    )
    router_grad = jnp.einsum("td,te->de", ffn_low, dlogits_low, preferred_element_type=jnp.float32)
    dresults = (
        (gate_probs[..., None] * upstream[:, None, :]).astype(jnp.bfloat16).reshape(routes, -1)
    )
    dresults = jnp.concatenate([dresults, jnp.zeros((1, dresults.shape[1]), jnp.bfloat16)], 0)
    dreturned = lax.all_to_all(
        dresults[route_of_slot].reshape(experts_all, cap_rows, -1),
        "ctx",
        split_axis=0,
        concat_axis=0,
        tiled=True,
    )
    dresult_rows = to_experts(dreturned)
    dhidden = jnp.einsum("esd,efd->esf", dresult_rows, down_all, preferred_element_type=jnp.float32)
    down_grad = jnp.einsum(
        "esf,esd->efd", hidden_low, dresult_rows, preferred_element_type=jnp.float32
    )
    dsilu_gate = sigmoid_gate * (1.0 + gate_part * (1.0 - sigmoid_gate))
    dgate_low = (dhidden * up_part * dsilu_gate).astype(jnp.bfloat16)
    dup_low = (dhidden * silu_gate).astype(jnp.bfloat16)
    gate_grad = jnp.einsum(
        "esd,esf->edf", expert_rows, dgate_low, preferred_element_type=jnp.float32
    )
    up_grad = jnp.einsum("esd,esf->edf", expert_rows, dup_low, preferred_element_type=jnp.float32)
    dexpert_rows = (
        jnp.einsum("esf,edf->esd", dgate_low, gate_all, preferred_element_type=jnp.float32)
        + jnp.einsum("esf,edf->esd", dup_low, up_all, preferred_element_type=jnp.float32)
    ).astype(jnp.bfloat16)
    dsent_rows = lax.all_to_all(
        from_experts(dexpert_rows), "ctx", split_axis=0, concat_axis=0, tiled=True
    )
    droutes = dsent_rows.reshape(experts_all * cap_rows, -1)[slot_of_route].reshape(
        token_per_device, TOP, -1
    )
    dffn_rows = jnp.sum(droutes.astype(jnp.float32), 1) + jnp.einsum(
        "te,de->td", dlogits_low, router_back, preferred_element_type=jnp.float32
    )
    expert_sums = (
        lax.psum_scatter(
            gate_grad.astype(jnp.bfloat16), "fsdp", scatter_dimension=1, tiled=True
        ).astype(jnp.float32),
        lax.psum_scatter(
            up_grad.astype(jnp.bfloat16), "fsdp", scatter_dimension=1, tiled=True
        ).astype(jnp.float32),
        lax.psum_scatter(
            down_grad.astype(jnp.bfloat16), "fsdp", scatter_dimension=1, tiled=True
        ).astype(jnp.float32),
    )
    dmixed_norm, ffn_gain_part = rms_back(mixed_attn, inverse_ffn, ffn_gain, dffn_rows)
    dmixed_attn = upstream + dmixed_norm
    dattn_low = dmixed_attn.astype(jnp.bfloat16)
    output_grad = jnp.einsum(
        "tc,td->cd", attended_low, dattn_low, preferred_element_type=jnp.float32
    )
    attended_lower_grad = jnp.einsum(
        "td,cd->tc", dattn_low, output_back, preferred_element_type=jnp.float32
    ).astype(jnp.bfloat16)
    output_heads_grad = attended_lower_grad.reshape(
        LOCAL_SEQUENCES, paired_rows, KEY_VALUE_HEADS, query_groups, HEAD_SIZE
    ).transpose(0, 2, 3, 1, 4)
    delta_row = jnp.sum(output_heads_grad.astype(jnp.float32) * attended, -1)
    key_recomputed, value_recomputed = (key_every, value_every)

    def score_grads(key_group, value_group, first_dev, query_group_size):
        key_row_matrix = arrange(key_group)
        value_rows = arrange(value_group)
        key_pos = group_positions(first_dev, query_group_size, context_count, block_len)
        scores = (
            jnp.einsum(
                "skgqd,swkd->skgqw",
                query_head_rows,
                key_row_matrix,
                preferred_element_type=jnp.float32,
            )
            * score_scale
        )
        allowed = key_pos[None, :] <= local_pos[:, None]
        weights_now = jnp.where(allowed, jnp.exp(scores - log_sum[..., None]), 0.0)
        dweights = jnp.einsum(
            "skgqd,swkd->skgqw", output_heads_grad, value_rows, preferred_element_type=jnp.float32
        )
        dscores = (weights_now * (dweights - delta_row[..., None])).astype(jnp.bfloat16)
        return (key_row_matrix, weights_now, dscores)

    def key_terms(weights_now, dscores, query_group_size):
        dkey_rows = jnp.einsum(
            "skgqw,skgqd->swkd", dscores, query_head_rows, preferred_element_type=jnp.float32
        )
        dvalue_rows = jnp.einsum(
            "skgqw,skgqd->swkd",
            weights_now.astype(jnp.bfloat16),
            output_heads_grad,
            preferred_element_type=jnp.float32,
        )
        return (unarrange(dkey_rows, query_group_size), unarrange(dvalue_rows, query_group_size))

    query_group_size = 4
    loop_step_count = context_count // query_group_size
    key_block_list = key_recomputed.reshape(
        loop_step_count, query_group_size, LOCAL_SEQUENCES, paired_rows, KEY_VALUE_HEADS, HEAD_SIZE
    )
    value_block_list = value_recomputed.reshape(
        loop_step_count, query_group_size, LOCAL_SEQUENCES, paired_rows, KEY_VALUE_HEADS, HEAD_SIZE
    )
    first_devs = query_group_size * jnp.arange(loop_step_count, dtype=jnp.int32)

    def back_group(dquery_acc, loop_item):
        key_group, value_group, first_dev = loop_item
        key_row_matrix, weights_now, dscores = score_grads(
            key_group, value_group, first_dev, query_group_size
        )
        dquery_acc = dquery_acc + jnp.einsum(
            "skgqw,swkd->skgqd", dscores, key_row_matrix, preferred_element_type=jnp.float32
        )
        return (dquery_acc, key_terms(weights_now, dscores, query_group_size))

    dquery_heads, key_value_pieces = lax.scan(
        back_group,
        jnp.zeros(query_head_rows.shape, jnp.float32),
        (key_block_list, value_block_list, first_devs),
    )
    key_grad_every = key_value_pieces[0].reshape(
        context_count * token_per_device, KEY_VALUE_HEADS, HEAD_SIZE
    )
    value_grad_every = key_value_pieces[1].reshape(
        context_count * token_per_device, KEY_VALUE_HEADS, HEAD_SIZE
    )
    dkey_own, value_local_grad = (
        lax.psum_scatter(key_grad_every, "ctx", scatter_dimension=0, tiled=True),
        lax.psum_scatter(value_grad_every, "ctx", scatter_dimension=0, tiled=True),
    )
    dquery = (
        (dquery_heads * score_scale)
        .transpose(0, 3, 1, 2, 4)
        .reshape(token_per_device, QUERY_HEADS, HEAD_SIZE)
    )
    dquery_proj, query_gain_part = rms_back(
        query_proj, query_inverse, query_gain, rope_back(dquery, cosine, sine_tab)
    )
    key_projection_grad, key_gain_part = rms_back(
        key_proj, key_inverse, key_gain, rope_back(dkey_own * score_scale, cosine, sine_tab)
    )
    dquery_low = dquery_proj.reshape(token_per_device, QUERY_HEADS * HEAD_SIZE).astype(jnp.bfloat16)
    key_lower_grad = key_projection_grad.reshape(
        token_per_device, KEY_VALUE_HEADS * HEAD_SIZE
    ).astype(jnp.bfloat16)
    value_lower_grad = value_local_grad.reshape(
        token_per_device, KEY_VALUE_HEADS * HEAD_SIZE
    ).astype(jnp.bfloat16)
    query_grad = jnp.einsum("td,tc->dc", normed_low, dquery_low, preferred_element_type=jnp.float32)
    key_grad = jnp.einsum(
        "td,tc->dc", normed_low, key_lower_grad, preferred_element_type=jnp.float32
    )
    value_grad = jnp.einsum(
        "td,tc->dc", normed_low, value_lower_grad, preferred_element_type=jnp.float32
    )
    dnormed = jnp.einsum("tc,dc->td", dquery_low, query_back, preferred_element_type=jnp.float32)
    dnormed = dnormed + jnp.einsum(
        "tc,dc->td", key_lower_grad, key_back, preferred_element_type=jnp.float32
    )
    dnormed = dnormed + jnp.einsum(
        "tc,dc->td", value_lower_grad, value_back, preferred_element_type=jnp.float32
    )
    dinput_norm, attention_gain_part = rms_back(inputs, inverse_attn, attention_gain, dnormed)
    d_tokens = (dmixed_attn + dinput_norm).astype(jnp.bfloat16)
    gain_sums = lax.psum(
        (attention_gain_part, ffn_gain_part, query_gain_part, key_gain_part), ("ctx", "fsdp")
    )
    layer_sums = (
        lax.psum_scatter(query_grad, ("ctx", "fsdp"), scatter_dimension=0, tiled=True),
        lax.psum_scatter(key_grad, ("ctx", "fsdp"), scatter_dimension=0, tiled=True),
        lax.psum_scatter(value_grad, ("ctx", "fsdp"), scatter_dimension=0, tiled=True),
        lax.psum_scatter(output_grad, ("ctx", "fsdp"), scatter_dimension=0, tiled=True),
        lax.psum_scatter(router_grad, ("ctx", "fsdp"), scatter_dimension=0, tiled=True),
    )
    return (
        mixed,
        d_tokens,
        gain_sums[0],
        gain_sums[1],
        gain_sums[2],
        gain_sums[3],
        layer_sums[0],
        layer_sums[1],
        layer_sums[2],
        layer_sums[3],
        layer_sums[4],
        expert_sums[0],
        expert_sums[1],
        expert_sums[2],
    )


MEMBERS = 4


def shift(block, axis, step):
    count = lax.axis_size(axis)
    return lax.ppermute(block, axis, [(i, (i + step) % count) for i in range(count)])


def swap(block, axis):
    return lax.ppermute(block, axis, [(0, 1), (1, 0)])


def after(block, *earlier):
    return lax.optimization_barrier((block,) + earlier)[0]


class Steps:
    def __init__(self):
        self.mark = None

    def __call__(self, sends, work=None, given=(), join=()):
        blocks = tuple(send[0] for send in sends)
        mark = () if self.mark is None else (self.mark,)
        blocks, given, mark = lax.optimization_barrier((blocks, tuple(given), mark))
        moved = tuple(
            swap(block, send[1]) if len(send) == 2 else shift(block, send[1], send[2])
            for block, send in zip(blocks, sends)
        )
        done = () if work is None else work(*given)
        moved, done, join, mark = lax.optimization_barrier((moved, done, tuple(join), mark))
        self.mark = jax.tree.leaves((moved, done, join))[0]
        return moved, done, join

    def start(self, block, axis):
        return swap(after(block, self.mark), axis)


def scatter_members(parts):
    low, wide = jnp.bfloat16, jnp.float32
    near = swap(parts[1].astype(low), "c")
    far = swap((parts[0, 1] + near[1].astype(wide)).astype(low), "y")
    return parts[0, 0] + near[0].astype(wide) + far.astype(wide)


def pick(stack, index):
    return lax.dynamic_index_in_dim(stack, index, 0, keepdims=False)


def roped(raw, gain, cosine, sine):
    inverse = lax.rsqrt(jnp.mean(raw * raw, -1, keepdims=True) + EPS)
    scaled = raw * inverse * gain
    return scaled * cosine + pltpu.roll(scaled, HEAD_SIZE // 2, 1) * sine


def split_heads(ref, start, heads):
    size = ref.shape[2] // 2
    rows = ref[:, 0, start * size : (start + 1) * size, :]
    rows = rows.reshape(ref.shape[0] * size, ref.shape[3])
    return jnp.concatenate(
        [rows[:, i * HEAD_SIZE : (i + 1) * HEAD_SIZE] for i in range(heads)], 0
    )


def key_half(ref, k, start):
    size = ref.shape[3] // 2
    rows = ref[k, :, 0, start * size : (start + 1) * size, :]
    return rows.reshape(ref.shape[1] * size, HEAD_SIZE)


def twice(rows):
    return jnp.concatenate([rows, rows], 0)


ACROSS = (((1,), (1,)), ((), ()))
DOWN = (((0,), (0,)), ((), ()))


def score_blocks(z_here, queries, k_ref):
    nz = k_ref.shape[0]
    low_q, high_q = queries
    low_keys = jnp.concatenate([key_half(k_ref, k, 0) for k in range(nz)], 0)
    blocks = [(low_keys, high_q, None)]
    for k in range(1, nz):
        before = z_here >= k
        keys = jnp.where(before, key_half(k_ref, k, 0), key_half(k_ref, k, 1))
        blocks.append((keys, jnp.where(before, low_q, high_q), before))
    blocks.append((key_half(k_ref, 0, 0), low_q, None))
    blocks.append((key_half(k_ref, 0, 1), high_q, None))
    return blocks


def value_blocks(z_here, ref):
    nz = ref.shape[0]
    blocks = [jnp.concatenate([key_half(ref, k, 0) for k in range(nz)], 0)]
    for k in range(1, nz):
        blocks.append(jnp.where(z_here >= k, key_half(ref, k, 0), key_half(ref, k, 1)))
    return blocks + [key_half(ref, 0, 0), key_half(ref, 0, 1)]


def to_halves(parts, blocks):
    low_sum, high_sum = parts[-2], parts[0] + parts[-1]
    for part, (_, _, before) in zip(parts[1:-2], blocks[1:-2]):
        low_sum = low_sum + jnp.where(before, part, 0.0)
        high_sum = high_sum + jnp.where(before, 0.0, part)
    return low_sum, high_sum


def of_halves(low_row, high_row, blocks):
    rows = [high_row]
    rows += [jnp.where(before, low_row, high_row) for _, _, before in blocks[1:-2]]
    return rows + [low_row, high_row]


def weigh(blocks, mask_ref):
    exponent = math.log2(math.e) / math.sqrt(HEAD_SIZE)
    weights = []
    for keys, queries, _ in blocks:
        scores = lax.dot_general(keys, queries, ACROSS, preferred_element_type=jnp.float32)
        weights.append(jnp.exp2(scores * exponent))
    weights[-2] = weights[-2] * mask_ref[0]
    weights[-1] = weights[-1] * mask_ref[1]
    return weights


def attend_kernel(places_ref, q_ref, k_ref, v_ref, cos_ref, sin_ref, gain_ref, mask_ref, out_ref):
    count = q_ref.shape[3] // HEAD_SIZE
    size = q_ref.shape[2] // 2
    queries = []
    for half in range(2):
        raw = split_heads(q_ref, half, count)
        queries.append(
            roped(raw, gain_ref[...], twice(cos_ref[half]), twice(sin_ref[half])).astype(
                jnp.bfloat16
            )
        )
    z_here = places_ref[1]
    blocks = score_blocks(z_here, queries, k_ref)
    weights = weigh(blocks, mask_ref)
    totals = to_halves([jnp.sum(weight, 0, keepdims=True) for weight in weights], blocks)
    mixed = [
        lax.dot_general(
            values, weight.astype(jnp.bfloat16), DOWN, preferred_element_type=jnp.float32
        )
        for values, weight in zip(value_blocks(z_here, v_ref), weights)
    ]
    mixed = to_halves(mixed, blocks)
    for half in range(2):
        out = (mixed[half] / totals[half]).T.astype(jnp.bfloat16)
        rows = out.shape[0] // count
        for i in range(count):
            out_ref[:, 0, half * size : (half + 1) * size, i * HEAD_SIZE : (i + 1) * HEAD_SIZE] = (
                out[i * rows : (i + 1) * rows].reshape(-1, size, HEAD_SIZE)
            )


def attend_back_kernel(
    places_ref,
    q_ref,
    up_ref,
    k_ref,
    v_ref,
    cos_ref,
    sin_ref,
    gain_ref,
    mask_ref,
    dq_ref,
    dkv_ref,
    dgain_ref,
):
    nz = k_ref.shape[0]
    count = q_ref.shape[3] // HEAD_SIZE
    size = q_ref.shape[2] // 2
    low = jnp.bfloat16
    score_scale = 1.0 / math.sqrt(HEAD_SIZE)
    gain = gain_ref[...]
    z_here = places_ref[1]
    raws, queries, ups = [], [], []
    for half in range(2):
        raw = split_heads(q_ref, half, count)
        raws.append(raw)
        queries.append(roped(raw, gain, twice(cos_ref[half]), twice(sin_ref[half])).astype(low))
        ups.append(split_heads(up_ref, half, count))
    blocks = score_blocks(z_here, queries, k_ref)
    weights = weigh(blocks, mask_ref)
    totals = to_halves([jnp.sum(weight, 0, keepdims=True) for weight in weights], blocks)
    inverses = [1.0 / total for total in totals]
    block_ups = [ups[1]]
    block_ups += [jnp.where(before, ups[0], ups[1]) for _, _, before in blocks[1:-2]]
    block_ups += ups
    dprobs = [
        lax.dot_general(values, up, ACROSS, preferred_element_type=jnp.float32)
        for values, up in zip(value_blocks(z_here, v_ref), block_ups)
    ]
    probs = [
        weight * inverse
        for weight, inverse in zip(weights, of_halves(inverses[0], inverses[1], blocks))
    ]
    deltas = to_halves(
        [jnp.sum(p * d, 0, keepdims=True) for p, d in zip(probs, dprobs)], blocks
    )
    dscores = [
        (p * (d - delta)).astype(low)
        for p, d, delta in zip(probs, dprobs, of_halves(deltas[0], deltas[1], blocks))
    ]
    dvs = [
        jnp.dot(p.astype(low), up, preferred_element_type=jnp.float32)
        for p, up in zip(probs, block_ups)
    ]
    dks = [
        jnp.dot(d, block[1], preferred_element_type=jnp.float32) * score_scale
        for d, block in zip(dscores, blocks)
    ]
    dqs = [
        lax.dot_general(block[0], d, DOWN, preferred_element_type=jnp.float32)
        for d, block in zip(dscores, blocks)
    ]
    dqs = to_halves(dqs, blocks)
    each = dks[-1].shape[0]
    fresh = pl.program_id(1) == 0
    for k in range(nz):
        both = [
            jnp.concatenate([dk, dv], 1)
            for dk, dv in (
                (dks[0][k * each : (k + 1) * each], dvs[0][k * each : (k + 1) * each]),
                (dks[k], dvs[k]) if k > 0 else (dks[-2], dvs[-2]),
            )
        ]
        if k == 0:
            halves = (both[0] + both[1], jnp.concatenate([dks[-1], dvs[-1]], 1))
        else:
            before = z_here >= k
            halves = (
                both[0] + jnp.where(before, both[1], 0.0),
                jnp.where(before, 0.0, both[1]),
            )
        for half in range(2):
            part = slice(half * size, (half + 1) * size)
            earlier = jnp.where(fresh, 0.0, dkv_ref[k, :, 0, part, :])
            dkv_ref[k, :, 0, part, :] = earlier + halves[half].reshape(-1, size, 2 * HEAD_SIZE)

    gain_part = jnp.zeros((1, HEAD_SIZE), jnp.float32)
    for half in range(2):
        cosine, sine = twice(cos_ref[half]), twice(sin_ref[half])
        raw = raws[half]
        inverse = lax.rsqrt(jnp.mean(raw * raw, -1, keepdims=True) + EPS)
        unit = raw * inverse
        dq = dqs[half].T * score_scale
        turned = dq * cosine - pltpu.roll(dq, HEAD_SIZE // 2, 1) * sine
        gain_part = gain_part + jnp.sum(turned * unit, 0, keepdims=True)
        turned = turned * gain
        back = inverse * (turned - unit * jnp.mean(turned * unit, -1, keepdims=True))
        back = back.astype(low)
        rows = back.shape[0] // count
        for i in range(count):
            dq_ref[:, 0, half * size : (half + 1) * size, i * HEAD_SIZE : (i + 1) * HEAD_SIZE] = (
                back[i * rows : (i + 1) * rows].reshape(-1, size, HEAD_SIZE)
            )
    gain_part = jnp.concatenate([gain_part, jnp.zeros((7, HEAD_SIZE), jnp.float32)], 0)
    first = fresh & (pl.program_id(0) == 0)
    dgain_ref[...] = jnp.where(first, 0.0, dgain_ref[...]) + gain_part


def attention_specs(q, kv, mask):
    nz, members, sequences, paired, _ = kv.shape
    pair = q.shape[-1] // MEMBERS
    q_block = (members, 1, paired, pair)
    kv_block = (nz, members, 1, paired, HEAD_SIZE)
    own = pl.BlockSpec(q_block, lambda s, r, places: (0, s, 0, r ^ places[0]))
    relative = pl.BlockSpec(q_block, lambda s, r, places: (0, s, 0, r))
    key = pl.BlockSpec(kv_block, lambda s, r, places: (0, 0, s, 0, 0))
    value = pl.BlockSpec(kv_block, lambda s, r, places: (0, 0, s, 0, 1))
    both = pl.BlockSpec(
        (nz, members, 1, paired, 2 * HEAD_SIZE), lambda s, r, places: (0, 0, s, 0, 0)
    )
    fixed = lambda shape: pl.BlockSpec(shape, lambda s, r, places: (0,) * len(shape))
    table = fixed((2, members * paired // 2, HEAD_SIZE))
    tables = [table, table, fixed((1, HEAD_SIZE)), fixed(mask.shape)]
    return own, relative, key, value, both, fixed, tables


def attend(places, q, kv, cosine, sine, gain, mask):
    members, sequences, paired, width = q.shape
    own, relative, key, value, both, fixed, tables = attention_specs(q, kv, mask)
    elements = sequences * width // HEAD_SIZE * members * paired * kv.shape[0] * members * paired
    return pl.pallas_call(
        attend_kernel,
        grid_spec=pltpu.PrefetchScalarGridSpec(
            num_scalar_prefetch=1,
            grid=(sequences, MEMBERS),
            in_specs=[own, key, value] + tables,
            out_specs=relative,
        ),
        out_shape=jax.ShapeDtypeStruct(q.shape, jnp.bfloat16),
        compiler_params=pltpu.CompilerParams(vmem_limit_bytes=40 * 2**20),
        cost_estimate=pl.CostEstimate(
            flops=4 * elements * HEAD_SIZE, bytes_accessed=8 * 2**20, transcendentals=elements
        ),
    )(places, q, kv, kv, cosine, sine, gain, mask)


def attend_back(places, q, up, kv, cosine, sine, gain, mask):
    members, sequences, paired, width = q.shape
    own, relative, key, value, both, fixed, tables = attention_specs(q, kv, mask)
    elements = sequences * width // HEAD_SIZE * members * paired * kv.shape[0] * members * paired
    return pl.pallas_call(
        attend_back_kernel,
        grid_spec=pltpu.PrefetchScalarGridSpec(
            num_scalar_prefetch=1,
            grid=(sequences, MEMBERS),
            in_specs=[own, relative, key, value] + tables,
            out_specs=(own, both, fixed((8, HEAD_SIZE))),
        ),
        out_shape=(
            jax.ShapeDtypeStruct(q.shape, jnp.bfloat16),
            jax.ShapeDtypeStruct(kv.shape, jnp.float32),
            jax.ShapeDtypeStruct((8, HEAD_SIZE), jnp.float32),
        ),
        compiler_params=pltpu.CompilerParams(vmem_limit_bytes=40 * 2**20),
        cost_estimate=pl.CostEstimate(
            flops=10 * elements * HEAD_SIZE, bytes_accessed=16 * 2**20, transcendentals=elements
        ),
    )(places, q, up, kv, kv, cosine, sine, gain, mask)


def dot32(subscripts, left, right):
    return jnp.einsum(subscripts, left, right, preferred_element_type=jnp.float32)


def expert_kernel(*refs):
    scalars_ref, x_refs = refs[0], refs[1:5]
    c_ref, rank_ref, chosen_ref, router_ref, gate_ref, up_ref, down_ref = refs[5:12]
    rows_ref, hidden_ref, dresults_ref, dgate_ref, dup_ref = refs[-9:-4]
    sent_refs, back_refs = refs[-4:-2], refs[-2:]
    low, wide = jnp.bfloat16, jnp.float32
    blocks = 2
    tokens, model = x_refs[0].shape
    opening = pl.program_id(0) == 0
    slots = rows_ref.shape[2]
    experts_all = router_ref.shape[0]
    across = (((1,), (1,)), ((), ()))
    down = (((0,), (0,)), ((), ()))
    own_expert = scalars_ref[3]
    places, picked, upstream, gates = [], [], [], []
    for block in range(blocks):
        rows = jnp.where(opening, x_refs[block][...], x_refs[2 + block][...])
        slot = lax.broadcasted_iota(jnp.int32, (slots, tokens), 0)
        place = jnp.where(slot == rank_ref[0, block], 1.0, 0.0)
        chosen = chosen_ref[0, block] > 0.5
        logits = lax.dot_general(router_ref[...], rows, across, preferred_element_type=wide)
        highest = jnp.max(jnp.where(chosen, logits, NEGATIVE_LIMIT), 0, keepdims=True)
        raised = jnp.where(chosen, jnp.exp(jnp.minimum(logits - highest, 0.0)), 0.0)
        expert = lax.broadcasted_iota(jnp.int32, (experts_all, tokens), 0)
        mine = jnp.sum(jnp.where(expert == own_expert, raised, 0.0), 0, keepdims=True)
        gate_row = mine / jnp.sum(raised, 0, keepdims=True)
        gates.append(jnp.sum(place * gate_row, 1, keepdims=True))
        place = place.astype(low)
        places.append(place)
        picked.append(jnp.dot(place, rows, preferred_element_type=wide).astype(low))
        cotangent = c_ref[0, block ^ scalars_ref[2]]
        upstream.append(jnp.dot(place, cotangent, preferred_element_type=wide))
    rows = jnp.concatenate(picked, 0)
    upstream = jnp.concatenate(upstream, 0)
    gates = jnp.concatenate(gates, 0)
    gate_part = jnp.dot(rows, gate_ref[...], preferred_element_type=wide)
    up_part = jnp.dot(rows, up_ref[...], preferred_element_type=wide)
    sigmoid_gate = 1.0 / (1.0 + jnp.exp(-gate_part))
    silu_gate = gate_part * sigmoid_gate
    hidden = (silu_gate * up_part).astype(low)
    results = jnp.dot(hidden, down_ref[...], preferred_element_type=wide).astype(low).astype(wide)
    dgates = jnp.sum(upstream * results, 1, keepdims=True)
    scaled = (gates * results).astype(low)
    dresults = (gates * upstream).astype(low)
    dhidden = lax.dot_general(dresults, down_ref[...], across, preferred_element_type=wide)
    dsilu_gate = sigmoid_gate * (1.0 + gate_part * (1.0 - sigmoid_gate))
    dgate_low = (dhidden * up_part * dsilu_gate).astype(low)
    dup_low = (dhidden * silu_gate).astype(low)
    drows = lax.dot_general(dgate_low, gate_ref[...], across, preferred_element_type=wide)
    drows = drows + lax.dot_general(dup_low, up_ref[...], across, preferred_element_type=wide)
    drows = drows.astype(low)
    lane = lax.broadcasted_iota(jnp.int32, (blocks * slots, 128), 1)
    coarse = dgates.astype(low).astype(wide)
    extra = jnp.where(lane == own_expert, coarse, 0.0)
    extra = extra + jnp.where(lane == own_expert + experts_all, dgates - coarse, 0.0)
    extra = extra.astype(low)
    for block in range(blocks):
        part = slice(block * slots, (block + 1) * slots)
        sent_refs[block][0] = lax.dot_general(
            places[block], scaled[part], down, preferred_element_type=wide
        ).astype(low)
        back_refs[block][0, :, :model] = lax.dot_general(
            places[block], drows[part], down, preferred_element_type=wide
        ).astype(low)
        back_refs[block][0, :, model:] = lax.dot_general(
            places[block], extra[part], down, preferred_element_type=wide
        ).astype(low)
        rows_ref[0, block] = rows[part]
        hidden_ref[0, block] = hidden[part]
        dresults_ref[0, block] = dresults[part]
        dgate_ref[0, block] = dgate_low[part]
        dup_ref[0, block] = dup_low[part]


def experts(scalars, x_blocks, cotangents, ranks, chosen, router, gate, up, down, slots, earlier):
    tokens, model = x_blocks[0].shape
    nz, members = cotangents.shape[:2]
    hidden = gate.shape[1]
    low = jnp.bfloat16
    pair = members // 2
    experts_all = router.shape[0]
    whole = lambda array: pl.BlockSpec(
        array.shape, lambda a, s: (0, 0), pipeline_mode=pl.Buffered(1)
    )
    by_plane = pl.BlockSpec(
        (1, pair, tokens, model), lambda a, s: (s[0], a ^ s[1], 0, 0)
    )
    turn = lambda *tail: pl.BlockSpec((1, pair) + tail, lambda a, s: (s[4], a, 0, 0))
    in_specs = [
        *[whole(block) for block in x_blocks],
        by_plane,
        turn(1, tokens),
        turn(experts_all, tokens),
        whole(router),
        whole(gate),
        whole(up),
        whole(down),
    ]
    shapes = [(slots, model), (slots, hidden), (slots, model)]
    shapes += [(slots, hidden), (slots, hidden)]
    out_shape = [jax.ShapeDtypeStruct((nz, members) + shape, low) for shape in shapes]
    out_specs = [turn(*shape) for shape in shapes]
    wide_model = model + 128
    for columns in (model, wide_model):
        out_shape += [jax.ShapeDtypeStruct((2, tokens, columns), low)] * 2
        out_specs += [pl.BlockSpec((1, tokens, columns), lambda a, s: (a, 0, 0))] * 2
    aliases = {}
    if earlier:
        in_specs = in_specs + [pl.BlockSpec(memory_space=pl.ANY)] * len(earlier)
        aliases = {12 + i: i for i in range(len(earlier))}
    return pl.pallas_call(
        expert_kernel,
        grid_spec=pltpu.PrefetchScalarGridSpec(
            num_scalar_prefetch=1, grid=(2,), in_specs=in_specs, out_specs=out_specs
        ),
        out_shape=out_shape,
        input_output_aliases=aliases,
        compiler_params=pltpu.CompilerParams(vmem_limit_bytes=58 * 2**20),
        cost_estimate=pl.CostEstimate(
            flops=12 * members * slots * model * hidden,
            bytes_accessed=40 * 2**20,
            transcendentals=2 * members * slots * hidden,
        ),
    )(scalars, *x_blocks, cotangents, ranks, chosen, router, gate, up, down, *earlier)


def dot32(subscripts, left, right):
    return jnp.einsum(subscripts, left, right, preferred_element_type=jnp.float32)


def member_layer(
    tokens,
    cotangent,
    expert_ids,
    attention_gain,
    ffn_gain,
    query_gain,
    key_gain,
    w_query,
    key_weight,
    value_weight,
    w_output,
    w_router,
    w_gate,
    w_up,
    w_down,
):
    low, wide = jnp.bfloat16, jnp.float32
    nz = lax.axis_size("z")
    zi, yi, ci, xi = (lax.axis_index(axis) for axis in ("z", "y", "c", "x"))
    member = 2 * yi + ci
    context_count = nz * MEMBERS
    rows, model = tokens.shape
    paired = rows // LOCAL_SEQUENCES
    block_len = paired // 2
    groups = QUERY_HEADS // KEY_VALUE_HEADS
    experts_all = w_router.shape[1]
    around = lambda k: lax.rem(zi + (k % nz), jnp.int32(nz))
    from_z = [around(-k) for k in range(nz)]
    crossed = [member ^ r for r in range(MEMBERS)]
    token_members = member ^ jnp.array([0, 2, 1, 3], jnp.int32)

    def uncrossed(blocks):
        for bit, odd in ((1, ci), (2, yi)):
            blocks = [jnp.where(odd == 0, blocks[r], blocks[r ^ bit]) for r in range(MEMBERS)]
        return jnp.stack(blocks)

    own_expert = zi * MEMBERS + member
    step = Steps()

    piece = w_query.shape[0]
    head_rows = w_output.shape[0]
    query_width = groups * HEAD_SIZE
    third = w_down.shape[1] // 3

    def prepare(w_query, key_weight, value_weight, w_router, expert_ids):
        columns = jnp.concatenate(
            [w.reshape(piece, KEY_VALUE_HEADS, -1) for w in (w_query, key_weight, value_weight)],
            -1,
        ).transpose(1, 0, 2)
        packed = jnp.concatenate([w_router.T.reshape(-1), expert_ids.T.astype(low).reshape(-1)])
        parts = [pick(columns, crossed[r]) for r in range(MEMBERS)]
        return parts[0], parts[1], jnp.stack(parts[2:]), packed.reshape(-1, 128)

    (plane1,), (part0, part1, parts_far, packed), _ = step(
        [(w_output, "z", 1)],
        prepare,
        (w_query, key_weight, value_weight, w_router, expert_ids),
    )
    width = part0.shape[-1]
    inputs = tokens.astype(wide)
    (far, plane3, down0, *small), (normed_attn, inverse_attn), _ = step(
        [(parts_far, "y"), (w_output, "z", 3), (w_down[0, :third], "x")]
        + [(packed, "z", k) for k in range(1, nz)],
        lambda tokens: rms_apply(tokens.astype(wide), attention_gain),
        (tokens,),
    )
    packed = jnp.stack([packed] + small)
    normed_low = normed_attn.astype(low)
    (near, other), _, _ = step([(jnp.stack([part1, far[1]]), "c"), (packed, "y")])
    packed = jnp.stack([packed, other], 1)
    ordered = uncrossed([part0, near[0], far[0], near[1]])
    held = [ordered]
    over_x = []
    (moved, cross, other, near, packed_near), _, _ = step(
        [
            (ordered, "z", 1),
            (ordered, "x"),
            (normed_low, "y"),
            (normed_low, "c"),
            (packed, "c"),
        ]
    )
    held.append(moved)
    over_x.append(cross)
    packed = jnp.stack([packed, packed_near], 1)
    (moved, cross, other_near, packed_cross, down1), _, _ = step(
        [
            (ordered, "z", 2),
            (held[1], "x"),
            (other, "c"),
            (packed, "x"),
            (w_down[0, third : 2 * third], "x"),
        ]
    )
    held.append(moved)
    over_x.append(cross)
    normed_all = jnp.concatenate([normed_low, other, near, other_near])
    packed = jnp.stack([packed, packed_cross], 1)
    (moved, cross), _, _ = step([(ordered, "z", 3), (held[2], "x")])
    held.append(moved)
    over_x.append(cross)
    middle = head_rows // 2
    (cross, plane2_low), _, _ = step([(held[3], "x"), (w_output[:middle], "z", 2)])
    over_x.append(cross)

    def assemble(start, stop):
        full = jnp.zeros((nz, MEMBERS, 2, piece, stop - start), low)
        for k in range(nz):
            full = lax.dynamic_update_slice(
                full, held[k][None, :, None, :, start:stop], (from_z[k], 0, xi, 0, 0)
            )
            full = lax.dynamic_update_slice(
                full, over_x[k][None, :, None, :, start:stop], (from_z[k], 0, 1 - xi, 0, 0)
            )
        return full.reshape(model, stop - start)

    query_weight = assemble(0, query_width)
    key_value_weight = assemble(query_width, width)

    own_pos = jax.vmap(lambda device: shard_positions(device, context_count, block_len))(
        zi * MEMBERS + token_members
    )
    cosine, sine_tab = rotary(own_pos.reshape(-1), HEAD_SIZE)
    row_cosine = cosine.reshape(MEMBERS, 1, paired, HEAD_SIZE)
    row_sine = sine_tab.reshape(MEMBERS, 1, paired, HEAD_SIZE)

    def halves(table):
        table = table.reshape(MEMBERS, 2, block_len, HEAD_SIZE).transpose(1, 0, 2, 3)
        return table.reshape(2, MEMBERS * block_len, HEAD_SIZE)

    half = HEAD_SIZE // 2
    signs = jnp.where(jnp.arange(HEAD_SIZE) < half, -1.0, 1.0)
    kernel_cosine, kernel_sine = halves(row_cosine), halves(row_sine * signs)
    half_pos = own_pos.reshape(MEMBERS, 2, block_len).transpose(1, 0, 2).reshape(2, -1)
    mask = (half_pos[:, :, None] <= half_pos[:, None, :]).astype(wide)
    mask = jnp.concatenate([mask, mask], 2)

    width_small = piece * experts_all
    flat = packed.reshape(nz * 8, -1)
    device = jnp.arange(nz * 8, dtype=jnp.int32)
    source = ((zi - device // 8) % nz) * 8 + ((device & 1) ^ xi) * 4
    source = source + (((device >> 1) & 1) ^ ci) * 2 + (((device >> 2) & 1) ^ yi)
    router = flat[:, :width_small][source].reshape(nz * 8, experts_all, piece)
    router = router.transpose(1, 0, 2).reshape(experts_all, model)
    ids_all = packed.reshape(nz, 2, 2, 2, -1)[:, 0, :, :, width_small:].transpose(0, 2, 1, 3)
    ids_all = ids_all.reshape(nz, MEMBERS, TOP, rows).astype(jnp.int32)
    named = jnp.any(ids_all == own_expert, 2)
    before = (
        jnp.arange(rows, dtype=jnp.int32)[:, None] <= jnp.arange(rows, dtype=jnp.int32)[None, :]
    )
    ranks = dot32("kjs,st->kjt", named.astype(low), before.astype(low)).astype(jnp.int32) - 1
    ranks = jnp.where(named, ranks, -1)[:, :, None, :]
    expert_column = jnp.arange(experts_all, dtype=jnp.int32)[:, None]
    chosen_all = jnp.any(ids_all[:, :, :, None, :] == expert_column, 2).astype(wide)
    cap_rows = rows * TOP * 5 // (4 * experts_all)
    slots = -(-cap_rows // 16) * 16

    def project_keys(normed_all, key_value_weight):
        raw = jnp.dot(normed_all, key_value_weight, preferred_element_type=wide)
        raw = raw.reshape(MEMBERS, LOCAL_SEQUENCES, paired, 2 * HEAD_SIZE)
        key_proj = raw[..., :HEAD_SIZE]
        key_normed, key_inverse = rms_apply(key_proj, key_gain)
        key_low = rope_apply(key_normed, row_cosine, row_sine).astype(low)
        value_low = raw[..., HEAD_SIZE:].astype(low)
        return key_proj, key_inverse, jnp.concatenate([key_low, value_low], -1)

    gate_cut = w_gate.shape[1] * 5 // 8
    (plane2_high, down2), (key_proj, key_inverse, key_value), _ = step(
        [(w_output[middle:], "z", 2), (w_down[0, 2 * third :], "x")],
        project_keys,
        (normed_all, key_value_weight),
    )
    planes = jnp.stack([w_output, plane1, jnp.concatenate([plane2_low, plane2_high]), plane3])
    wanted = [pick(planes, lax.rem(zi + nz - crossed[r], jnp.int32(nz))) for r in range(MEMBERS)]
    (key_value1, key_value3, far, gate0), queries, _ = step(
        [
            (key_value, "z", 1),
            (key_value, "z", 3),
            (jnp.stack(wanted[2:]), "y"),
            (w_gate[0, :gate_cut], "x"),
        ],
        lambda normed_all, query_weight: jnp.dot(
            normed_all, query_weight, preferred_element_type=wide
        ),
        (normed_all, query_weight),
    )
    queries = queries.reshape(MEMBERS, LOCAL_SEQUENCES, paired, query_width)
    cotangents = lax.all_gather(
        after(cotangent, step.mark), ("z", "y", "c"), axis=0, tiled=True
    ).reshape(nz, MEMBERS, rows, model)
    mine = jnp.stack([wanted[0], far[0]])
    (key_value2, near, cross_mine), _, _ = step(
        [(key_value, "z", 2), (jnp.stack([wanted[1], far[1]]), "c"), (mine, "x")]
    )
    key_value = jnp.stack([key_value, key_value1, key_value2, key_value3])

    places = jnp.stack([member, zi]).astype(jnp.int32)
    gain_row = query_gain[None]
    (cross_near,), attended, _ = step(
        [(near, "x")],
        attend,
        (places, queries, key_value, kernel_cosine, kernel_sine, gain_row, mask),
    )
    attended = attended.reshape(MEMBERS * rows, query_width)
    own_heads = jnp.stack([mine[0], near[0], mine[1], near[1]])
    other_heads = jnp.stack([cross_mine[0], cross_near[0], cross_mine[1], cross_near[1]])
    output_weight = jnp.where(
        xi == 0, jnp.stack([own_heads, other_heads], 1), jnp.stack([other_heads, own_heads], 1)
    ).reshape(query_width, model)

    mixed_part = jnp.dot(attended, output_weight, preferred_element_type=wide)
    mixed_part = mixed_part.reshape(2, 2, rows, model)
    (near,), _, _ = step([(mixed_part[1].astype(low), "c")])
    summed_far = (mixed_part[0, 1] + near[1].astype(wide)).astype(low)
    (other, gate1), _, _ = step([(summed_far, "y"), (w_gate[0, gate_cut:], "x")])
    mixed_attn = inputs + (mixed_part[0, 0] + near[0].astype(wide) + other.astype(wide))
    normed_ffn, inverse_ffn = rms_apply(mixed_attn, ffn_gain)
    ffn_low = normed_ffn.astype(low)

    logits = dot32("td,ed->te", ffn_low, router)
    chosen = jnp.any(
        expert_ids[:, :, None] == jnp.arange(experts_all, dtype=jnp.int32)[None, None, :], 1
    )
    highest = jnp.max(jnp.where(chosen, logits, NEGATIVE_LIMIT), 1, keepdims=True)
    raised = jnp.where(chosen, jnp.exp(jnp.minimum(logits - highest, 0.0)), 0.0)
    gates = raised / jnp.sum(raised, 1, keepdims=True)

    def whole(own, others):
        full = jnp.zeros((2,) + own.shape, low)
        full = lax.dynamic_update_slice(full, own[None], (xi, 0, 0))
        start = 0
        for other in others:
            full = lax.dynamic_update_slice(full, other[None], (1 - xi, start, 0))
            start += other.shape[0]
        return full.reshape(2 * own.shape[0], own.shape[1])

    def run_experts(k, x_blocks, kept, weights):
        scalars = jnp.stack([from_z[k], yi, ci, own_expert, jnp.int32(k)]).astype(jnp.int32)
        out = experts(
            scalars, x_blocks, cotangents, ranks, chosen_all, router, *weights, slots, kept
        )
        return tuple(out[:-4]), out[-4:-2], out[-2:]

    def added(pair, back, a):
        return pair[0][a].astype(wide) + back[a].astype(wide)

    def assemble_experts(*pieces):
        gates_part, ups_part, downs_part = pieces
        return (
            whole(w_gate[0], gates_part),
            whole(w_up[0], ups_part),
            whole(w_down[0], downs_part),
        )

    (x2, y0, n0, up_other), _, _ = step(
        [(ffn_low, "z", 2), (ffn_low, "y"), (ffn_low, "c"), (w_up[0], "x")]
    )
    (x1, y2, ny0, n2), weights, _ = step(
        [(ffn_low, "z", 1), (x2, "y"), (y0, "c"), (x2, "c")],
        assemble_experts,
        ([gate0, gate1], [up_other], [down0, down1, down2]),
    )
    (x3, y1, ny2, n1), (kept, mixed0, rows0), _ = step(
        [(ffn_low, "z", 3), (x1, "y"), (y2, "c"), (x1, "c")],
        functools.partial(run_experts, 0),
        ([ffn_low, n0, y0, ny0], (), weights),
    )
    (y3, ny1, n3, back0, mixed_back0), (kept, mixed2, rows2), _ = step(
        [(x3, "y"), (y1, "c"), (x3, "c"), (rows0[1], "c"), (mixed0[1], "c")],
        functools.partial(run_experts, 2),
        ([x2, n2, y2, ny2], kept, weights),
    )
    (ny3, back2, mixed_back2, far0), (kept, mixed1, rows1), _ = step(
        [
            (y3, "c"),
            (rows2[1], "c"),
            (mixed2[1], "c"),
            (added(rows0, back0, 1).astype(low), "y"),
        ],
        functools.partial(run_experts, 1),
        ([x1, n1, y1, ny1], kept, weights),
    )
    (back1, mixed_back1, far2), (kept, mixed3, rows3), _ = step(
        [(rows1[1], "c"), (mixed1[1], "c"), (added(rows2, back2, 1).astype(low), "y")],
        functools.partial(run_experts, 3),
        ([x3, n3, y3, ny3], kept, weights),
    )
    expert_rows, hidden_low, dresults, dgate_low, dup_low = (
        block.reshape(context_count * slots, -1) for block in kept
    )

    def halved(grad, cuts):
        size = grad.shape[0] // 2
        own = lax.dynamic_slice_in_dim(grad, xi * size, size, 0)
        other = lax.dynamic_slice_in_dim(grad, (1 - xi) * size, size, 0).astype(low)
        cut = size // cuts
        return own, [other[i * cut : (i + 1) * cut] for i in range(cuts)]

    def joined(own, moved):
        return (own + jnp.concatenate(moved, 0).astype(wide))[None]

    total2 = (added(rows2, back2, 0) + far2.astype(wide)).astype(low)
    cut = rows // 2
    (z2_low, far1, back3, mixed_back3), down_grad, _ = step(
        [
            (total2[:cut], "z", -2),
            (added(rows1, back1, 1).astype(low), "y"),
            (rows3[1], "c"),
            (mixed3[1], "c"),
        ],
        functools.partial(dot32, "sf,sd->fd"),
        (hidden_low, dresults),
    )
    down_grad, down_sends = halved(down_grad, 2)
    (z2_high, far3, down0), gate_grad, _ = step(
        [
            (total2[cut:], "z", -2),
            (added(rows3, back3, 1).astype(low), "y"),
            (down_sends[0], "x"),
        ],
        functools.partial(dot32, "sd,sf->df"),
        (expert_rows, dgate_low),
    )
    total1 = (added(rows1, back1, 0) + far1.astype(wide)).astype(low)
    total3 = (added(rows3, back3, 0) + far3.astype(wide)).astype(low)
    (z1, down1, mixed_far2), up_grad, _ = step(
        [
            (total1, "z", -1),
            (down_sends[1], "x"),
            (added(mixed2, mixed_back2, 1).astype(low), "y"),
        ],
        functools.partial(dot32, "sd,sf->df"),
        (expert_rows, dup_low),
    )
    gate_grad, gate_sends = halved(gate_grad, 2)
    (z3, gate0, mixed_far1), (down_grad, mixed_send2), _ = step(
        [
            (total3, "z", -3),
            (gate_sends[0], "x"),
            (added(mixed1, mixed_back1, 1).astype(low), "y"),
        ],
        lambda own, moved, pair, back, far: (
            joined(own, moved),
            (added(pair, back, 0) + far.astype(wide)).astype(low),
        ),
        (down_grad, [down0, down1], mixed2, mixed_back2, mixed_far2),
    )
    returned = added(rows0, back0, 0) + far0.astype(wide) + z1.astype(wide) + z3.astype(wide)
    returned = returned + jnp.concatenate([z2_low, z2_high], 0).astype(wide)
    dffn_routed = returned[:, :model]
    dgates = returned[:, model : model + experts_all]
    dgates = dgates + returned[:, model + experts_all : model + 2 * experts_all]
    dlogits = gates * (dgates - jnp.sum(gates * dgates, 1, keepdims=True))
    dlogits_low = dlogits.astype(low)
    router_grad = dot32("te,td->ed", dlogits_low, ffn_low)

    upstream = cotangent.astype(wide)
    dffn_rows = dffn_routed + dot32("te,ed->td", dlogits_low, router)
    dmixed_norm, ffn_gain_part = rms_back(mixed_attn, inverse_ffn, ffn_gain, dffn_rows)
    dmixed_attn = upstream + dmixed_norm
    dattn_low = dmixed_attn.astype(low)
    (other, near, gate1, mixed_z2_low), (mixed_send1, up_grad, up_sends), _ = step(
        [
            (dattn_low, "y"),
            (dattn_low, "c"),
            (gate_sends[1], "x"),
            (mixed_send2[:cut], "z", -2),
        ],
        lambda pair, back, far, grad: (
            (added(pair, back, 0) + far.astype(wide)).astype(low),
            *halved(grad, 2),
        ),
        (mixed1, mixed_back1, mixed_far1, up_grad),
    )
    (other_near,), _, _ = step([(other, "c")])
    dattn_all = jnp.concatenate([dattn_low, other, near, other_near])

    def through_output(dattn_all, output_weight, attended):
        attended_grad = dot32("td,cd->tc", dattn_all, output_weight).astype(low)
        output_part = dot32("tc,td->cd", attended, dattn_all).astype(low)
        output_part = output_part.reshape(MEMBERS, 2, head_rows, model)
        own = lax.dynamic_index_in_dim(output_part, xi, 1, keepdims=False)
        other = lax.dynamic_index_in_dim(output_part, 1 - xi, 1, keepdims=False)
        return attended_grad, own[:2], own[2:], other[:1], other[1:]

    (mixed_far3, up0), (attended_grad, own_near, own_far, cross_first, cross_rest), _ = step(
        [(added(mixed3, mixed_back3, 1).astype(low), "y"), (up_sends[0], "x")],
        through_output,
        (dattn_all, output_weight, attended),
    )
    attended_grad = attended_grad.reshape(MEMBERS, LOCAL_SEQUENCES, paired, query_width)
    early = jnp.concatenate([router_grad, ffn_gain_part[None]], 0)
    moved, (dquery_low, dkey_value, query_gain_part), _ = step(
        [
            (cross_rest, "x"),
            (early, "x"),
            (mixed_send1, "z", -1),
            (mixed_send2[cut:], "z", -2),
        ],
        attend_back,
        (
            places,
            queries,
            attended_grad,
            key_value,
            kernel_cosine,
            kernel_sine,
            gain_row,
            mask,
        ),
    )
    cross, early_x, mixed_z1, mixed_z2_high = moved
    early = early + early_x
    output_far = (own_far.astype(wide) + cross[1:].astype(wide)).astype(low)
    query_gain_part = query_gain_part[0]
    dquery_low = dquery_low.reshape(MEMBERS * rows, query_width)

    def planes_of(part):
        own = lax.dynamic_index_in_dim(part, xi, 2, keepdims=False)
        other = lax.dynamic_index_in_dim(part, 1 - xi, 2, keepdims=False)
        return [(pick(own, around(k)), pick(other, around(k))) for k in range(nz)]

    query_part = dot32("td,tc->dc", normed_all, dquery_low).astype(low)
    query_planes = planes_of(query_part.reshape(nz, MEMBERS, 2, piece, query_width))
    near_rest = cross[:1]
    moved, (dnormed, mixed_send3, gate_grad), _ = step(
        [(dkey_value[k].astype(low), "z", -k) for k in range(1, nz)]
        + [(query_planes[2][1], "x"), (cross_first, "x"), (output_far, "y")],
        lambda grad, weight, pair, back, far, own, moved: (
            dot32("tc,dc->td", grad, weight),
            (added(pair, back, 0) + far.astype(wide)).astype(low),
            joined(own, moved),
        ),
        (
            dquery_low,
            query_weight,
            mixed3,
            mixed_back3,
            mixed_far3,
            gate_grad,
            [gate0, gate1],
        ),
    )
    cross, near_first, output_far = moved[nz - 1 :]
    output_cross = jnp.concatenate([near_first, near_rest])
    query_sum2 = (query_planes[2][0].astype(wide) + cross.astype(wide)).astype(low)
    output_near = (own_near.astype(wide) + output_cross.astype(wide)).astype(low)

    def project_keys_back(dnormed, dkey_value_own, moved, key_value_weight):
        dkey_value_own = dkey_value_own + sum(block.astype(wide) for block in moved)
        dkey, dvalue = dkey_value_own[..., :HEAD_SIZE], dkey_value_own[..., HEAD_SIZE:]
        dkey_proj, key_gain_part = rms_back(
            key_proj, key_inverse, key_gain, rope_back(dkey, row_cosine, row_sine)
        )
        dkey_value_low = jnp.concatenate([dkey_proj, dvalue], -1).astype(low)
        dkey_value_low = dkey_value_low.reshape(MEMBERS * rows, 2 * HEAD_SIZE)
        dnormed = dnormed + dot32("tc,dc->td", dkey_value_low, key_value_weight)
        dnormed = scatter_members(dnormed.reshape(2, 2, rows, model))
        key_part = dot32("td,tc->dc", normed_all, dkey_value_low).astype(low)
        key_part = key_part.reshape(nz, MEMBERS, 2, piece, 2 * HEAD_SIZE)
        key_own = lax.dynamic_index_in_dim(key_part, xi, 2, keepdims=False)
        key_other = lax.dynamic_index_in_dim(key_part, 1 - xi, 2, keepdims=False)
        return dnormed, key_own, key_other, key_gain_part

    moved_z, (dnormed, key_own, key_other, key_gain_part), _ = step(
        [
            (query_sum2, "z", 2),
            (mixed_send3[:cut], "z", -3),
            (jnp.stack([query_planes[1][1], query_planes[3][1]]), "x"),
            (jnp.stack([output_near[1], output_far[1]]), "c"),
        ],
        project_keys_back,
        (dnormed, dkey_value[0], moved[: nz - 1], key_value_weight),
    )
    query_z2, mixed_z3_low, cross, output_back = moved_z
    query_sum1 = (query_planes[1][0].astype(wide) + cross[0].astype(wide)).astype(low)
    query_sum3 = (query_planes[3][0].astype(wide) + cross[1].astype(wide)).astype(low)
    dinput_norm, attention_gain_part = rms_back(inputs, inverse_attn, attention_gain, dnormed)
    late = jnp.concatenate([attention_gain_part, query_gain_part, key_gain_part])
    small = jnp.concatenate([early.reshape(-1, 128), late.reshape(-1, 128)], 0)
    output_blocks = [output_near[0], output_back[0], output_far[0], output_back[1]]

    def order_output(blocks, dmixed_attn, dinput_norm):
        blocks = uncrossed(blocks)
        sends = [pick(blocks, around(k)) for k in range(nz)]
        return sends, (dmixed_attn + dinput_norm).astype(low)

    (query_z1, query_z3, cross, key_cross, late_x), (output_sends, d_tokens), _ = step(
        [
            (query_sum1, "z", 1),
            (query_sum3, "z", 3),
            (query_planes[0][1], "x"),
            (key_other, "x"),
            (late.reshape(-1, 128), "x"),
        ],
        order_output,
        (output_blocks, dmixed_attn, dinput_norm),
    )
    early_rows = early.size // 128
    small = jnp.concatenate([small[:early_rows], small[early_rows:] + late_x], 0)
    key_sum = (key_own.astype(wide) + key_cross.astype(wide)).astype(low)

    def total_queries(own, cross, *moved):
        total = own.astype(wide) + cross.astype(wide) + sum(m.astype(wide) for m in moved)
        total = total.astype(low)
        parts = [pick(total, crossed[r]) for r in range(MEMBERS)]
        return parts[0], parts[1], jnp.stack(parts[2:])

    query_parts = total_queries(query_planes[0][0], cross, query_z1, query_z2, query_z3)
    (output_z1, query_far, small_y, mixed_far0, mixed_z3_high, *key_moves), _, _ = step(
        [
            (output_sends[1], "z", 1),
            (query_parts[2], "y"),
            (small, "y"),
            (added(mixed0, mixed_back0, 1).astype(low), "y"),
            (mixed_send3[cut:], "z", -3),
        ]
        + [(pick(key_sum, around(k)), "z", k) for k in range(1, nz)],
    )
    small = small + small_y
    key_total = pick(key_sum, zi).astype(wide)
    key_total = (key_total + sum(m.astype(wide) for m in key_moves)).astype(low)
    key_parts = [pick(key_total, crossed[r]) for r in range(MEMBERS)]

    def member_columns(part0, near, far):
        grads = uncrossed([part0, near[0], far[0], near[1]])
        return grads.astype(wide).transpose(1, 0, 2)

    (output_z2, up1, key_far, query_near, small_c), (mixed,), _ = step(
        [
            (output_sends[2], "z", 2),
            (up_sends[1], "x"),
            (jnp.stack(key_parts[2:]), "y"),
            (jnp.stack([query_parts[1], query_far[1]]), "c"),
            (small, "c"),
        ],
        lambda base, pair, back, far, z1, *halves: (
            (
                base
                + added(pair, back, 0)
                + far.astype(wide)
                + z1.astype(wide)
                + jnp.concatenate(halves[:2], 0).astype(wide)
                + jnp.concatenate(halves[2:], 0).astype(wide)
            ).astype(low),
        ),
        (
            mixed_attn,
            mixed0,
            mixed_back0,
            mixed_far0,
            mixed_z1,
            mixed_z2_low,
            mixed_z2_high,
            mixed_z3_low,
            mixed_z3_high,
        ),
    )
    small = small + small_c

    def finish(own, moved, output_own, z1, z2, parts, near, far):
        output = output_own.astype(wide) + z1.astype(wide) + z2.astype(wide)
        return joined(own, moved), output, member_columns(parts, near, far)

    (output_z3, key_near, *small_z), (up_grad, output_grad, query_grad), _ = step(
        [
            (output_sends[3], "z", 3),
            (jnp.stack([key_parts[1], key_far[1]]), "c"),
        ]
        + [(small, "z", k) for k in range(1, nz)],
        finish,
        (
            up_grad,
            [up0, up1],
            output_sends[0],
            output_z1,
            output_z2,
            query_parts[0],
            query_near,
            query_far,
        ),
    )
    query_grad = query_grad.reshape(piece, -1)
    output_grad = output_grad + output_z3.astype(wide)
    small = small + sum(small_z)
    early = small[:early_rows].reshape(early.shape)
    gains = small[early_rows:].reshape(-1)
    key_grads = member_columns(key_parts[0], key_near, key_far)
    key_grad = key_grads[..., :HEAD_SIZE].reshape(piece, -1)
    value_grad = key_grads[..., HEAD_SIZE:].reshape(piece, -1)
    device = own_expert * 2 + xi
    router_own = lax.dynamic_slice_in_dim(early[:experts_all], device * piece, piece, 1).T
    return (
        mixed,
        d_tokens,
        gains[:model],
        early[experts_all],
        gains[model : model + HEAD_SIZE],
        gains[model + HEAD_SIZE :],
        query_grad,
        key_grad,
        value_grad,
        output_grad,
        router_own,
        gate_grad,
        up_grad,
        down_grad,
    )


def solution(mesh):
    contexts, pairs = mesh.shape["ctx"], mesh.shape["fsdp"]
    planes = contexts // MEMBERS
    if planes == KEY_VALUE_HEADS and pairs * MEMBERS * KEY_VALUE_HEADS == QUERY_HEADS:
        layer, every, split = member_layer, ("z", "y", "c", "x"), ("z", "y", "c")
        pair = "x"
        mesh = Mesh(mesh.devices.reshape(planes, 2, 2, pairs), every)
    else:
        layer, every, split, pair = routed_layer, ("ctx", "fsdp"), "ctx", "fsdp"
    by_row = P(every, None)
    by_expert = P(split, pair, None)
    return jax.shard_map(
        layer,
        mesh=mesh,
        in_specs=(by_row,) * 3 + (P(),) * 4 + (by_row,) * 5 + (by_expert,) * 3,
        out_specs=(by_row,) * 2 + (P(),) * 4 + (by_row,) * 5 + (by_expert,) * 3,
        check_vma=False,
    )
```

```python
import functools
import math

import jax
import jax.numpy as jnp
from jax import lax
from jax.experimental import pallas as pl
from jax.experimental.pallas import tpu as pltpu
from jax.sharding import Mesh
from jax.sharding import PartitionSpec as P

QUERY_HEADS = 32
KEY_VALUE_HEADS = 4
HEAD_SIZE = 128
TOP = 8
LOCAL_SEQUENCES = 3


EPS = 1e-06
THETA = 1000000.0
NEGATIVE_LIMIT = -1e30


def shard_positions(device, context_count, block_len):
    within = jnp.arange(2 * block_len, dtype=jnp.int32)
    lower_pos = device * block_len + within
    upper_pos = (2 * context_count - 1 - device) * block_len + within - block_len
    return jnp.where(within < block_len, lower_pos, upper_pos)


def group_positions(first_dev, query_group_size, context_count, block_len):
    devices = first_dev + jnp.arange(query_group_size, dtype=jnp.int32)
    return jax.vmap(lambda device: shard_positions(device, context_count, block_len))(
        devices
    ).reshape(-1)


def rotary(positions, head_width):
    half_width = head_width // 2
    frequency = jnp.exp(
        -math.log(THETA) * (2.0 * jnp.arange(half_width, dtype=jnp.float32)) / head_width
    )
    angles = positions.astype(jnp.float32)[:, None] * frequency[None, :]
    angles = jnp.concatenate([angles, angles], -1)
    return (jnp.cos(angles)[:, None, :], jnp.sin(angles)[:, None, :])


def rope_apply(value_rows_list, cosine, sine_tab):
    half_width = value_rows_list.shape[-1] // 2
    turned = jnp.concatenate(
        [-value_rows_list[..., half_width:], value_rows_list[..., :half_width]], -1
    )
    return value_rows_list * cosine + turned * sine_tab


def rope_back(upstream, cosine, sine_tab):
    half_width = upstream.shape[-1] // 2
    moved_part = upstream * sine_tab
    return upstream * cosine + jnp.concatenate(
        [moved_part[..., half_width:], -moved_part[..., :half_width]], -1
    )


def rms_apply(value_rows_list, gain_vec):
    inverse = lax.rsqrt(jnp.mean(value_rows_list * value_rows_list, -1, keepdims=True) + EPS)
    return (value_rows_list * inverse * gain_vec, inverse)


def rms_back(value_rows_list, inverse, gain_vec, upstream):
    normalized_input = value_rows_list * inverse
    gain_part = jnp.sum((upstream * normalized_input).reshape(-1, value_rows_list.shape[-1]), 0)
    scaled = upstream * gain_vec
    back_part = inverse * (
        scaled - normalized_input * jnp.mean(scaled * normalized_input, -1, keepdims=True)
    )
    return (back_part, gain_part)


def arrange(blocks):
    query_group_size, seq_count, paired_rows, heads_kv, head_dim = blocks.shape
    return blocks.transpose(1, 0, 2, 3, 4).reshape(
        seq_count, query_group_size * paired_rows, heads_kv, head_dim
    )


def unarrange(rows_all, query_group_size):
    seq_count, width_all, heads_kv, head_dim = rows_all.shape
    return rows_all.reshape(
        seq_count, query_group_size, width_all // query_group_size, heads_kv, head_dim
    ).transpose(1, 0, 2, 3, 4)


def attend_group(state_now, queries, key_row_matrix, value_rows, query_pos, key_pos, score_scale):
    run_max, run_sum, run_acc = state_now
    scores = (
        jnp.einsum("skgqd,swkd->skgqw", queries, key_row_matrix, preferred_element_type=jnp.float32)
        * score_scale
    )
    allowed = key_pos[None, :] <= query_pos[:, None]
    new_max = jnp.maximum(run_max, jnp.max(jnp.where(allowed, scores, NEGATIVE_LIMIT), -1))
    weights_now = jnp.where(allowed, jnp.exp(scores - new_max[..., None]), 0.0)
    factor = jnp.exp(run_max - new_max)
    new_sum = run_sum * factor + jnp.sum(weights_now, -1)
    update = jnp.einsum(
        "skgqw,swkd->skgqd",
        weights_now.astype(jnp.bfloat16),
        value_rows,
        preferred_element_type=jnp.float32,
    )
    return (new_max, new_sum, run_acc * factor[..., None] + update)


def routed_layer(
    tokens,
    cotangent,
    expert_ids,
    attention_gain,
    ffn_gain,
    query_gain,
    key_gain,
    w_query,
    key_weight,
    value_weight,
    w_output,
    w_router,
    w_gate,
    w_up,
    w_down,
):
    context_count = lax.axis_size("ctx")
    ctx_here = lax.axis_index("ctx")
    token_per_device = tokens.shape[0]
    block_len = token_per_device // (2 * LOCAL_SEQUENCES)
    paired_rows = 2 * block_len
    query_groups = QUERY_HEADS // KEY_VALUE_HEADS
    score_scale = 1.0 / math.sqrt(HEAD_SIZE)
    experts_all = w_router.shape[1]
    exp_dev = w_gate.shape[0]
    cap_rows = token_per_device * TOP * 5 // (4 * experts_all)
    routes = token_per_device * TOP
    inputs = tokens.astype(jnp.float32)
    normed_attn, inverse_attn = rms_apply(inputs, attention_gain)
    normed_low = normed_attn.astype(jnp.bfloat16)
    query_all, key_all, value_all, output_all, router_all = (
        lax.all_gather(w_query, ("ctx", "fsdp"), axis=0, tiled=True),
        lax.all_gather(key_weight, ("ctx", "fsdp"), axis=0, tiled=True),
        lax.all_gather(value_weight, ("ctx", "fsdp"), axis=0, tiled=True),
        lax.all_gather(w_output, ("ctx", "fsdp"), axis=0, tiled=True),
        lax.all_gather(w_router, ("ctx", "fsdp"), axis=0, tiled=True),
    )
    local_pos = shard_positions(ctx_here, context_count, block_len)
    row_pos = jnp.tile(local_pos, LOCAL_SEQUENCES)
    cosine, sine_tab = rotary(row_pos, HEAD_SIZE)
    query_proj = jnp.dot(normed_low, query_all, preferred_element_type=jnp.float32).reshape(
        token_per_device, QUERY_HEADS, HEAD_SIZE
    )
    key_proj = jnp.dot(normed_low, key_all, preferred_element_type=jnp.float32).reshape(
        token_per_device, KEY_VALUE_HEADS, HEAD_SIZE
    )
    value_proj = jnp.dot(normed_low, value_all, preferred_element_type=jnp.float32).reshape(
        token_per_device, KEY_VALUE_HEADS, HEAD_SIZE
    )
    query_normed, query_inverse = rms_apply(query_proj, query_gain)
    key_normed, key_inverse = rms_apply(key_proj, key_gain)
    query_lower = rope_apply(query_normed, cosine, sine_tab).astype(jnp.bfloat16)
    key_low = rope_apply(key_normed, cosine, sine_tab).astype(jnp.bfloat16)
    value_low = value_proj.astype(jnp.bfloat16)
    query_head_rows = query_lower.reshape(
        LOCAL_SEQUENCES, paired_rows, KEY_VALUE_HEADS, query_groups, HEAD_SIZE
    ).transpose(0, 2, 3, 1, 4)
    initial = (
        jnp.full(
            (LOCAL_SEQUENCES, KEY_VALUE_HEADS, query_groups, paired_rows),
            NEGATIVE_LIMIT,
            jnp.float32,
        ),
        jnp.zeros((LOCAL_SEQUENCES, KEY_VALUE_HEADS, query_groups, paired_rows), jnp.float32),
        jnp.zeros(
            (LOCAL_SEQUENCES, KEY_VALUE_HEADS, query_groups, paired_rows, HEAD_SIZE), jnp.float32
        ),
    )
    key_every, value_every = (
        lax.all_gather(key_low, "ctx", axis=0, tiled=True),
        lax.all_gather(value_low, "ctx", axis=0, tiled=True),
    )
    shard_total_count = key_every.shape[0] // token_per_device
    fold_query_group_size = 4
    key_block_list = key_every.reshape(
        shard_total_count // fold_query_group_size,
        fold_query_group_size,
        LOCAL_SEQUENCES,
        paired_rows,
        KEY_VALUE_HEADS,
        HEAD_SIZE,
    )
    value_block_list = value_every.reshape(
        shard_total_count // fold_query_group_size,
        fold_query_group_size,
        LOCAL_SEQUENCES,
        paired_rows,
        KEY_VALUE_HEADS,
        HEAD_SIZE,
    )
    first_devs = 0 // token_per_device + fold_query_group_size * jnp.arange(
        shard_total_count // fold_query_group_size, dtype=jnp.int32
    )

    def one_group(state_in, loop_item):
        key_group, value_group, first_dev = loop_item
        key_pos = group_positions(first_dev, fold_query_group_size, context_count, block_len)
        return (
            attend_group(
                state_in,
                query_head_rows,
                arrange(key_group),
                arrange(value_group),
                local_pos,
                key_pos,
                score_scale,
            ),
            None,
        )

    state_out, unused = lax.scan(one_group, initial, (key_block_list, value_block_list, first_devs))
    run_max, run_sum, run_acc = state_out
    log_sum = run_max + jnp.log(run_sum)
    attended = run_acc / run_sum[..., None]
    attended_low = (
        attended.transpose(0, 3, 1, 2, 4)
        .reshape(token_per_device, QUERY_HEADS * HEAD_SIZE)
        .astype(jnp.bfloat16)
    )
    mixed_attn = inputs + jnp.dot(attended_low, output_all, preferred_element_type=jnp.float32)
    normed_ffn, inverse_ffn = rms_apply(mixed_attn, ffn_gain)
    ffn_low = normed_ffn.astype(jnp.bfloat16)
    logits = jnp.dot(ffn_low, router_all, preferred_element_type=jnp.float32)
    chosen = (expert_ids[..., None] == jnp.arange(experts_all, dtype=jnp.int32)).astype(jnp.float32)
    picked = jnp.einsum("tje,te->tj", chosen, logits, precision=lax.Precision.HIGHEST)
    gate_probs = jax.nn.softmax(picked, -1)
    flat_ids = expert_ids.reshape(-1)
    route_marks = (flat_ids[:, None] == jnp.arange(experts_all, dtype=jnp.int32)).astype(jnp.int32)
    route_ranks = jnp.sum((jnp.cumsum(route_marks, 0) - 1) * route_marks, -1)
    slot_of_route = flat_ids * cap_rows + route_ranks
    route_of_slot = (
        jnp.full((experts_all * cap_rows,), routes, jnp.int32)
        .at[slot_of_route]
        .set(jnp.arange(routes, dtype=jnp.int32))
    )
    padded = jnp.concatenate([ffn_low, jnp.zeros((1, ffn_low.shape[1]), jnp.bfloat16)], 0)
    outgoing = padded[route_of_slot // TOP].reshape(experts_all, cap_rows, -1)
    arrived = lax.all_to_all(outgoing, "ctx", split_axis=0, concat_axis=0, tiled=True)

    def to_experts(buffer):
        return (
            buffer.reshape(context_count, exp_dev, cap_rows, -1)
            .transpose(1, 0, 2, 3)
            .reshape(exp_dev, context_count * cap_rows, -1)
        )

    def from_experts(buffer):
        return (
            buffer.reshape(exp_dev, context_count, cap_rows, -1)
            .transpose(1, 0, 2, 3)
            .reshape(context_count * exp_dev, cap_rows, -1)
        )

    expert_rows = to_experts(arrived)
    gate_all, up_all, down_all = (
        lax.all_gather(w_gate, "fsdp", axis=1, tiled=True),
        lax.all_gather(w_up, "fsdp", axis=1, tiled=True),
        lax.all_gather(w_down, "fsdp", axis=1, tiled=True),
    )
    gate_part = jnp.einsum(
        "esd,edf->esf", expert_rows, gate_all, preferred_element_type=jnp.float32
    )
    up_part = jnp.einsum("esd,edf->esf", expert_rows, up_all, preferred_element_type=jnp.float32)
    sigmoid_gate = jax.nn.sigmoid(gate_part)
    silu_gate = gate_part * sigmoid_gate
    hidden_low = (silu_gate * up_part).astype(jnp.bfloat16)
    results = jnp.einsum(
        "esf,efd->esd", hidden_low, down_all, preferred_element_type=jnp.float32
    ).astype(jnp.bfloat16)
    returned = lax.all_to_all(from_experts(results), "ctx", split_axis=0, concat_axis=0, tiled=True)
    route_out = returned.reshape(experts_all * cap_rows, -1)[slot_of_route].reshape(
        token_per_device, TOP, -1
    )
    mixed = (mixed_attn + jnp.sum(gate_probs[..., None] * route_out, 1)).astype(jnp.bfloat16)
    query_back, key_back, value_back, output_back, router_back = (
        lax.all_gather(w_query, ("ctx", "fsdp"), axis=0, tiled=True),
        lax.all_gather(key_weight, ("ctx", "fsdp"), axis=0, tiled=True),
        lax.all_gather(value_weight, ("ctx", "fsdp"), axis=0, tiled=True),
        lax.all_gather(w_output, ("ctx", "fsdp"), axis=0, tiled=True),
        lax.all_gather(w_router, ("ctx", "fsdp"), axis=0, tiled=True),
    )
    upstream = cotangent.astype(jnp.float32)
    dgates = jnp.sum(upstream[:, None, :] * route_out, -1)
    dpicked = gate_probs * (dgates - jnp.sum(gate_probs * dgates, -1, keepdims=True))
    dlogits_low = jnp.einsum("tj,tje->te", dpicked, chosen, precision=lax.Precision.HIGHEST).astype(
        jnp.bfloat16
    )
    router_grad = jnp.einsum("td,te->de", ffn_low, dlogits_low, preferred_element_type=jnp.float32)
    dresults = (
        (gate_probs[..., None] * upstream[:, None, :]).astype(jnp.bfloat16).reshape(routes, -1)
    )
    dresults = jnp.concatenate([dresults, jnp.zeros((1, dresults.shape[1]), jnp.bfloat16)], 0)
    dreturned = lax.all_to_all(
        dresults[route_of_slot].reshape(experts_all, cap_rows, -1),
        "ctx",
        split_axis=0,
        concat_axis=0,
        tiled=True,
    )
    dresult_rows = to_experts(dreturned)
    dhidden = jnp.einsum("esd,efd->esf", dresult_rows, down_all, preferred_element_type=jnp.float32)
    down_grad = jnp.einsum(
        "esf,esd->efd", hidden_low, dresult_rows, preferred_element_type=jnp.float32
    )
    dsilu_gate = sigmoid_gate * (1.0 + gate_part * (1.0 - sigmoid_gate))
    dgate_low = (dhidden * up_part * dsilu_gate).astype(jnp.bfloat16)
    dup_low = (dhidden * silu_gate).astype(jnp.bfloat16)
    gate_grad = jnp.einsum(
        "esd,esf->edf", expert_rows, dgate_low, preferred_element_type=jnp.float32
    )
    up_grad = jnp.einsum("esd,esf->edf", expert_rows, dup_low, preferred_element_type=jnp.float32)
    dexpert_rows = (
        jnp.einsum("esf,edf->esd", dgate_low, gate_all, preferred_element_type=jnp.float32)
        + jnp.einsum("esf,edf->esd", dup_low, up_all, preferred_element_type=jnp.float32)
    ).astype(jnp.bfloat16)
    dsent_rows = lax.all_to_all(
        from_experts(dexpert_rows), "ctx", split_axis=0, concat_axis=0, tiled=True
    )
    droutes = dsent_rows.reshape(experts_all * cap_rows, -1)[slot_of_route].reshape(
        token_per_device, TOP, -1
    )
    dffn_rows = jnp.sum(droutes.astype(jnp.float32), 1) + jnp.einsum(
        "te,de->td", dlogits_low, router_back, preferred_element_type=jnp.float32
    )
    expert_sums = (
        lax.psum_scatter(
            gate_grad.astype(jnp.bfloat16), "fsdp", scatter_dimension=1, tiled=True
        ).astype(jnp.float32),
        lax.psum_scatter(
            up_grad.astype(jnp.bfloat16), "fsdp", scatter_dimension=1, tiled=True
        ).astype(jnp.float32),
        lax.psum_scatter(
            down_grad.astype(jnp.bfloat16), "fsdp", scatter_dimension=1, tiled=True
        ).astype(jnp.float32),
    )
    dmixed_norm, ffn_gain_part = rms_back(mixed_attn, inverse_ffn, ffn_gain, dffn_rows)
    dmixed_attn = upstream + dmixed_norm
    dattn_low = dmixed_attn.astype(jnp.bfloat16)
    output_grad = jnp.einsum(
        "tc,td->cd", attended_low, dattn_low, preferred_element_type=jnp.float32
    )
    attended_lower_grad = jnp.einsum(
        "td,cd->tc", dattn_low, output_back, preferred_element_type=jnp.float32
    ).astype(jnp.bfloat16)
    output_heads_grad = attended_lower_grad.reshape(
        LOCAL_SEQUENCES, paired_rows, KEY_VALUE_HEADS, query_groups, HEAD_SIZE
    ).transpose(0, 2, 3, 1, 4)
    delta_row = jnp.sum(output_heads_grad.astype(jnp.float32) * attended, -1)
    key_recomputed, value_recomputed = (key_every, value_every)

    def score_grads(key_group, value_group, first_dev, query_group_size):
        key_row_matrix = arrange(key_group)
        value_rows = arrange(value_group)
        key_pos = group_positions(first_dev, query_group_size, context_count, block_len)
        scores = (
            jnp.einsum(
                "skgqd,swkd->skgqw",
                query_head_rows,
                key_row_matrix,
                preferred_element_type=jnp.float32,
            )
            * score_scale
        )
        allowed = key_pos[None, :] <= local_pos[:, None]
        weights_now = jnp.where(allowed, jnp.exp(scores - log_sum[..., None]), 0.0)
        dweights = jnp.einsum(
            "skgqd,swkd->skgqw", output_heads_grad, value_rows, preferred_element_type=jnp.float32
        )
        dscores = (weights_now * (dweights - delta_row[..., None])).astype(jnp.bfloat16)
        return (key_row_matrix, weights_now, dscores)

    def key_terms(weights_now, dscores, query_group_size):
        dkey_rows = jnp.einsum(
            "skgqw,skgqd->swkd", dscores, query_head_rows, preferred_element_type=jnp.float32
        )
        dvalue_rows = jnp.einsum(
            "skgqw,skgqd->swkd",
            weights_now.astype(jnp.bfloat16),
            output_heads_grad,
            preferred_element_type=jnp.float32,
        )
        return (unarrange(dkey_rows, query_group_size), unarrange(dvalue_rows, query_group_size))

    query_group_size = 4
    loop_step_count = context_count // query_group_size
    key_block_list = key_recomputed.reshape(
        loop_step_count, query_group_size, LOCAL_SEQUENCES, paired_rows, KEY_VALUE_HEADS, HEAD_SIZE
    )
    value_block_list = value_recomputed.reshape(
        loop_step_count, query_group_size, LOCAL_SEQUENCES, paired_rows, KEY_VALUE_HEADS, HEAD_SIZE
    )
    first_devs = query_group_size * jnp.arange(loop_step_count, dtype=jnp.int32)

    def back_group(dquery_acc, loop_item):
        key_group, value_group, first_dev = loop_item
        key_row_matrix, weights_now, dscores = score_grads(
            key_group, value_group, first_dev, query_group_size
        )
        dquery_acc = dquery_acc + jnp.einsum(
            "skgqw,swkd->skgqd", dscores, key_row_matrix, preferred_element_type=jnp.float32
        )
        return (dquery_acc, key_terms(weights_now, dscores, query_group_size))

    dquery_heads, key_value_pieces = lax.scan(
        back_group,
        jnp.zeros(query_head_rows.shape, jnp.float32),
        (key_block_list, value_block_list, first_devs),
    )
    key_grad_every = key_value_pieces[0].reshape(
        context_count * token_per_device, KEY_VALUE_HEADS, HEAD_SIZE
    )
    value_grad_every = key_value_pieces[1].reshape(
        context_count * token_per_device, KEY_VALUE_HEADS, HEAD_SIZE
    )
    dkey_own, value_local_grad = (
        lax.psum_scatter(key_grad_every, "ctx", scatter_dimension=0, tiled=True),
        lax.psum_scatter(value_grad_every, "ctx", scatter_dimension=0, tiled=True),
    )
    dquery = (
        (dquery_heads * score_scale)
        .transpose(0, 3, 1, 2, 4)
        .reshape(token_per_device, QUERY_HEADS, HEAD_SIZE)
    )
    dquery_proj, query_gain_part = rms_back(
        query_proj, query_inverse, query_gain, rope_back(dquery, cosine, sine_tab)
    )
    key_projection_grad, key_gain_part = rms_back(
        key_proj, key_inverse, key_gain, rope_back(dkey_own * score_scale, cosine, sine_tab)
    )
    dquery_low = dquery_proj.reshape(token_per_device, QUERY_HEADS * HEAD_SIZE).astype(jnp.bfloat16)
    key_lower_grad = key_projection_grad.reshape(
        token_per_device, KEY_VALUE_HEADS * HEAD_SIZE
    ).astype(jnp.bfloat16)
    value_lower_grad = value_local_grad.reshape(
        token_per_device, KEY_VALUE_HEADS * HEAD_SIZE
    ).astype(jnp.bfloat16)
    query_grad = jnp.einsum("td,tc->dc", normed_low, dquery_low, preferred_element_type=jnp.float32)
    key_grad = jnp.einsum(
        "td,tc->dc", normed_low, key_lower_grad, preferred_element_type=jnp.float32
    )
    value_grad = jnp.einsum(
        "td,tc->dc", normed_low, value_lower_grad, preferred_element_type=jnp.float32
    )
    dnormed = jnp.einsum("tc,dc->td", dquery_low, query_back, preferred_element_type=jnp.float32)
    dnormed = dnormed + jnp.einsum(
        "tc,dc->td", key_lower_grad, key_back, preferred_element_type=jnp.float32
    )
    dnormed = dnormed + jnp.einsum(
        "tc,dc->td", value_lower_grad, value_back, preferred_element_type=jnp.float32
    )
    dinput_norm, attention_gain_part = rms_back(inputs, inverse_attn, attention_gain, dnormed)
    d_tokens = (dmixed_attn + dinput_norm).astype(jnp.bfloat16)
    gain_sums = lax.psum(
        (attention_gain_part, ffn_gain_part, query_gain_part, key_gain_part), ("ctx", "fsdp")
    )
    layer_sums = (
        lax.psum_scatter(query_grad, ("ctx", "fsdp"), scatter_dimension=0, tiled=True),
        lax.psum_scatter(key_grad, ("ctx", "fsdp"), scatter_dimension=0, tiled=True),
        lax.psum_scatter(value_grad, ("ctx", "fsdp"), scatter_dimension=0, tiled=True),
        lax.psum_scatter(output_grad, ("ctx", "fsdp"), scatter_dimension=0, tiled=True),
        lax.psum_scatter(router_grad, ("ctx", "fsdp"), scatter_dimension=0, tiled=True),
    )
    return (
        mixed,
        d_tokens,
        gain_sums[0],
        gain_sums[1],
        gain_sums[2],
        gain_sums[3],
        layer_sums[0],
        layer_sums[1],
        layer_sums[2],
        layer_sums[3],
        layer_sums[4],
        expert_sums[0],
        expert_sums[1],
        expert_sums[2],
    )


MEMBERS = 4


def shift(block, axis, step):
    count = lax.axis_size(axis)
    return lax.ppermute(block, axis, [(i, (i + step) % count) for i in range(count)])


def swap(block, axis):
    return lax.ppermute(block, axis, [(0, 1), (1, 0)])


def after(block, *earlier):
    return lax.optimization_barrier((block,) + earlier)[0]


class Steps:
    def __init__(self):
        self.mark = None

    def __call__(self, sends, work=None, given=(), join=()):
        blocks = tuple(send[0] for send in sends)
        mark = () if self.mark is None else (self.mark,)
        blocks, given, mark = lax.optimization_barrier((blocks, tuple(given), mark))
        moved = tuple(
            swap(block, send[1]) if len(send) == 2 else shift(block, send[1], send[2])
            for block, send in zip(blocks, sends)
        )
        done = () if work is None else work(*given)
        moved, done, join, mark = lax.optimization_barrier((moved, done, tuple(join), mark))
        self.mark = jax.tree.leaves((moved, done, join))[0]
        return moved, done, join


def pick(stack, index):
    return lax.dynamic_index_in_dim(stack, index, 0, keepdims=False)


def roped(raw, gain, cosine, sine):
    inverse = lax.rsqrt(jnp.mean(raw * raw, -1, keepdims=True) + EPS)
    scaled = raw * inverse * gain
    return scaled * cosine + pltpu.roll(scaled, HEAD_SIZE // 2, 1) * sine


def split_heads(ref, start, heads):
    size = ref.shape[2] // 2
    rows = ref[:, 0, start * size : (start + 1) * size, :]
    rows = rows.reshape(ref.shape[0] * size, ref.shape[3])
    return jnp.concatenate(
        [rows[:, i * HEAD_SIZE : (i + 1) * HEAD_SIZE] for i in range(heads)], 0
    )


def key_half(ref, k, start):
    size = ref.shape[3] // 2
    rows = ref[k, :, 0, start * size : (start + 1) * size, :]
    return rows.reshape(ref.shape[1] * size, HEAD_SIZE)


def twice(rows):
    return jnp.concatenate([rows, rows], 0)


ACROSS = (((1,), (1,)), ((), ()))
DOWN = (((0,), (0,)), ((), ()))


def score_blocks(z_here, queries, k_ref):
    nz = k_ref.shape[0]
    low_q, high_q = queries
    low_keys = jnp.concatenate([key_half(k_ref, k, 0) for k in range(nz)], 0)
    blocks = [(low_keys, high_q, None)]
    for k in range(1, nz):
        before = z_here >= k
        keys = jnp.where(before, key_half(k_ref, k, 0), key_half(k_ref, k, 1))
        blocks.append((keys, jnp.where(before, low_q, high_q), before))
    blocks.append((key_half(k_ref, 0, 0), low_q, None))
    blocks.append((key_half(k_ref, 0, 1), high_q, None))
    return blocks


def value_blocks(z_here, ref):
    nz = ref.shape[0]
    blocks = [jnp.concatenate([key_half(ref, k, 0) for k in range(nz)], 0)]
    for k in range(1, nz):
        blocks.append(jnp.where(z_here >= k, key_half(ref, k, 0), key_half(ref, k, 1)))
    return blocks + [key_half(ref, 0, 0), key_half(ref, 0, 1)]


def to_halves(parts, blocks):
    low_sum, high_sum = parts[-2], parts[0] + parts[-1]
    for part, (_, _, before) in zip(parts[1:-2], blocks[1:-2]):
        low_sum = low_sum + jnp.where(before, part, 0.0)
        high_sum = high_sum + jnp.where(before, 0.0, part)
    return low_sum, high_sum


def of_halves(low_row, high_row, blocks):
    rows = [high_row]
    rows += [jnp.where(before, low_row, high_row) for _, _, before in blocks[1:-2]]
    return rows + [low_row, high_row]


def weigh(blocks, mask_ref):
    exponent = math.log2(math.e) / math.sqrt(HEAD_SIZE)
    weights = []
    for keys, queries, _ in blocks:
        scores = lax.dot_general(keys, queries, ACROSS, preferred_element_type=jnp.float32)
        weights.append(jnp.exp2(scores * exponent))
    weights[-2] = weights[-2] * mask_ref[0]
    weights[-1] = weights[-1] * mask_ref[1]
    return weights


def attend_kernel(places_ref, q_ref, k_ref, v_ref, cos_ref, sin_ref, gain_ref, mask_ref, out_ref):
    count = q_ref.shape[3] // HEAD_SIZE
    size = q_ref.shape[2] // 2
    queries = []
    for half in range(2):
        raw = split_heads(q_ref, half, count)
        queries.append(
            roped(raw, gain_ref[...], twice(cos_ref[half]), twice(sin_ref[half])).astype(
                jnp.bfloat16
            )
        )
    z_here = places_ref[1]
    blocks = score_blocks(z_here, queries, k_ref)
    weights = weigh(blocks, mask_ref)
    totals = to_halves([jnp.sum(weight, 0, keepdims=True) for weight in weights], blocks)
    mixed = [
        lax.dot_general(
            values, weight.astype(jnp.bfloat16), DOWN, preferred_element_type=jnp.float32
        )
        for values, weight in zip(value_blocks(z_here, v_ref), weights)
    ]
    mixed = to_halves(mixed, blocks)
    for half in range(2):
        out = (mixed[half] / totals[half]).T.astype(jnp.bfloat16)
        rows = out.shape[0] // count
        for i in range(count):
            out_ref[:, 0, half * size : (half + 1) * size, i * HEAD_SIZE : (i + 1) * HEAD_SIZE] = (
                out[i * rows : (i + 1) * rows].reshape(-1, size, HEAD_SIZE)
            )


def attend_back_kernel(
    places_ref,
    q_ref,
    up_ref,
    k_ref,
    v_ref,
    cos_ref,
    sin_ref,
    gain_ref,
    mask_ref,
    dq_ref,
    dkv_ref,
    dgain_ref,
):
    nz = k_ref.shape[0]
    count = q_ref.shape[3] // HEAD_SIZE
    size = q_ref.shape[2] // 2
    low = jnp.bfloat16
    score_scale = 1.0 / math.sqrt(HEAD_SIZE)
    gain = gain_ref[...]
    z_here = places_ref[1]
    raws, queries, ups = [], [], []
    for half in range(2):
        raw = split_heads(q_ref, half, count)
        raws.append(raw)
        queries.append(roped(raw, gain, twice(cos_ref[half]), twice(sin_ref[half])).astype(low))
        ups.append(split_heads(up_ref, half, count))
    blocks = score_blocks(z_here, queries, k_ref)
    weights = weigh(blocks, mask_ref)
    totals = to_halves([jnp.sum(weight, 0, keepdims=True) for weight in weights], blocks)
    inverses = [1.0 / total for total in totals]
    block_ups = [ups[1]]
    block_ups += [jnp.where(before, ups[0], ups[1]) for _, _, before in blocks[1:-2]]
    block_ups += ups
    dprobs = [
        lax.dot_general(values, up, ACROSS, preferred_element_type=jnp.float32)
        for values, up in zip(value_blocks(z_here, v_ref), block_ups)
    ]
    probs = [
        weight * inverse
        for weight, inverse in zip(weights, of_halves(inverses[0], inverses[1], blocks))
    ]
    deltas = to_halves(
        [jnp.sum(p * d, 0, keepdims=True) for p, d in zip(probs, dprobs)], blocks
    )
    dscores = [
        (p * (d - delta)).astype(low)
        for p, d, delta in zip(probs, dprobs, of_halves(deltas[0], deltas[1], blocks))
    ]
    dvs = [
        jnp.dot(p.astype(low), up, preferred_element_type=jnp.float32)
        for p, up in zip(probs, block_ups)
    ]
    dks = [
        jnp.dot(d, block[1], preferred_element_type=jnp.float32) * score_scale
        for d, block in zip(dscores, blocks)
    ]
    dqs = [
        lax.dot_general(block[0], d, DOWN, preferred_element_type=jnp.float32)
        for d, block in zip(dscores, blocks)
    ]
    dqs = to_halves(dqs, blocks)
    each = dks[-1].shape[0]
    fresh = pl.program_id(1) == 0
    for k in range(nz):
        both = [
            jnp.concatenate([dk, dv], 1)
            for dk, dv in (
                (dks[0][k * each : (k + 1) * each], dvs[0][k * each : (k + 1) * each]),
                (dks[k], dvs[k]) if k > 0 else (dks[-2], dvs[-2]),
            )
        ]
        if k == 0:
            halves = (both[0] + both[1], jnp.concatenate([dks[-1], dvs[-1]], 1))
        else:
            before = z_here >= k
            halves = (
                both[0] + jnp.where(before, both[1], 0.0),
                jnp.where(before, 0.0, both[1]),
            )
        for half in range(2):
            part = slice(half * size, (half + 1) * size)
            earlier = jnp.where(fresh, 0.0, dkv_ref[k, :, 0, part, :])
            dkv_ref[k, :, 0, part, :] = earlier + halves[half].reshape(-1, size, 2 * HEAD_SIZE)

    gain_part = jnp.zeros((1, HEAD_SIZE), jnp.float32)
    for half in range(2):
        cosine, sine = twice(cos_ref[half]), twice(sin_ref[half])
        raw = raws[half]
        inverse = lax.rsqrt(jnp.mean(raw * raw, -1, keepdims=True) + EPS)
        unit = raw * inverse
        dq = dqs[half].T * score_scale
        turned = dq * cosine - pltpu.roll(dq, HEAD_SIZE // 2, 1) * sine
        gain_part = gain_part + jnp.sum(turned * unit, 0, keepdims=True)
        turned = turned * gain
        back = inverse * (turned - unit * jnp.mean(turned * unit, -1, keepdims=True))
        back = back.astype(low)
        rows = back.shape[0] // count
        for i in range(count):
            dq_ref[:, 0, half * size : (half + 1) * size, i * HEAD_SIZE : (i + 1) * HEAD_SIZE] = (
                back[i * rows : (i + 1) * rows].reshape(-1, size, HEAD_SIZE)
            )
    gain_part = jnp.concatenate([gain_part, jnp.zeros((7, HEAD_SIZE), jnp.float32)], 0)
    first = fresh & (pl.program_id(0) == 0)
    dgain_ref[...] = jnp.where(first, 0.0, dgain_ref[...]) + gain_part


def attention_specs(q, kv, mask):
    nz, members, sequences, paired, _ = kv.shape
    pair = q.shape[-1] // MEMBERS
    q_block = (members, 1, paired, pair)
    kv_block = (nz, members, 1, paired, HEAD_SIZE)
    own = pl.BlockSpec(q_block, lambda s, r, places: (0, s, 0, r ^ places[0]))
    relative = pl.BlockSpec(q_block, lambda s, r, places: (0, s, 0, r))
    key = pl.BlockSpec(kv_block, lambda s, r, places: (0, 0, s, 0, 0))
    value = pl.BlockSpec(kv_block, lambda s, r, places: (0, 0, s, 0, 1))
    both = pl.BlockSpec(
        (nz, members, 1, paired, 2 * HEAD_SIZE), lambda s, r, places: (0, 0, s, 0, 0)
    )
    fixed = lambda shape: pl.BlockSpec(shape, lambda s, r, places: (0,) * len(shape))
    table = fixed((2, members * paired // 2, HEAD_SIZE))
    tables = [table, table, fixed((1, HEAD_SIZE)), fixed(mask.shape)]
    return own, relative, key, value, both, fixed, tables


def attend(places, q, kv, cosine, sine, gain, mask):
    members, sequences, paired, width = q.shape
    own, relative, key, value, both, fixed, tables = attention_specs(q, kv, mask)
    elements = sequences * width // HEAD_SIZE * members * paired * kv.shape[0] * members * paired
    return pl.pallas_call(
        attend_kernel,
        grid_spec=pltpu.PrefetchScalarGridSpec(
            num_scalar_prefetch=1,
            grid=(sequences, MEMBERS),
            in_specs=[own, key, value] + tables,
            out_specs=relative,
        ),
        out_shape=jax.ShapeDtypeStruct(q.shape, jnp.bfloat16),
        compiler_params=pltpu.CompilerParams(vmem_limit_bytes=40 * 2**20),
        cost_estimate=pl.CostEstimate(
            flops=4 * elements * HEAD_SIZE, bytes_accessed=8 * 2**20, transcendentals=elements
        ),
    )(places, q, kv, kv, cosine, sine, gain, mask)


def attend_back(places, q, up, kv, cosine, sine, gain, mask):
    members, sequences, paired, width = q.shape
    own, relative, key, value, both, fixed, tables = attention_specs(q, kv, mask)
    elements = sequences * width // HEAD_SIZE * members * paired * kv.shape[0] * members * paired
    return pl.pallas_call(
        attend_back_kernel,
        grid_spec=pltpu.PrefetchScalarGridSpec(
            num_scalar_prefetch=1,
            grid=(sequences, MEMBERS),
            in_specs=[own, relative, key, value] + tables,
            out_specs=(own, both, fixed((8, HEAD_SIZE))),
        ),
        out_shape=(
            jax.ShapeDtypeStruct(q.shape, jnp.bfloat16),
            jax.ShapeDtypeStruct(kv.shape, jnp.float32),
            jax.ShapeDtypeStruct((8, HEAD_SIZE), jnp.float32),
        ),
        compiler_params=pltpu.CompilerParams(vmem_limit_bytes=40 * 2**20),
        cost_estimate=pl.CostEstimate(
            flops=10 * elements * HEAD_SIZE, bytes_accessed=16 * 2**20, transcendentals=elements
        ),
    )(places, q, up, kv, kv, cosine, sine, gain, mask)


def dot32(subscripts, left, right):
    return jnp.einsum(subscripts, left, right, preferred_element_type=jnp.float32)


def expert_kernel(*refs):
    scalars_ref, x_refs, c_refs = refs[0], refs[1:5], refs[5:9]
    rank_ref, chosen_ref, router_ref, gate_ref, up_ref, down_ref = refs[9:15]
    rows_ref, hidden_ref, dresults_ref, dgate_ref, dup_ref = refs[-9:-4]
    sent_refs, back_refs = refs[-4:-2], refs[-2:]
    low, wide = jnp.bfloat16, jnp.float32
    blocks = 2
    tokens, model = x_refs[0].shape
    opening = pl.program_id(0) == 0
    slots = rows_ref.shape[2]
    experts_all = router_ref.shape[0]
    across = (((1,), (1,)), ((), ()))
    down = (((0,), (0,)), ((), ()))
    own_expert = scalars_ref[0]
    places, picked, upstream, gates = [], [], [], []
    for block in range(blocks):
        rows = jnp.where(opening, x_refs[block][...], x_refs[2 + block][...])
        slot = lax.broadcasted_iota(jnp.int32, (slots, tokens), 0)
        place = jnp.where(slot == rank_ref[0, block], 1.0, 0.0)
        chosen = chosen_ref[0, block] > 0.5
        logits = lax.dot_general(router_ref[...], rows, across, preferred_element_type=wide)
        highest = jnp.max(jnp.where(chosen, logits, NEGATIVE_LIMIT), 0, keepdims=True)
        raised = jnp.where(chosen, jnp.exp(jnp.minimum(logits - highest, 0.0)), 0.0)
        expert = lax.broadcasted_iota(jnp.int32, (experts_all, tokens), 0)
        mine = jnp.sum(jnp.where(expert == own_expert, raised, 0.0), 0, keepdims=True)
        gate_row = mine / jnp.sum(raised, 0, keepdims=True)
        gates.append(jnp.sum(place * gate_row, 1, keepdims=True))
        place = place.astype(low)
        places.append(place)
        picked.append(jnp.dot(place, rows, preferred_element_type=wide).astype(low))
        cotangent = jnp.where(opening, c_refs[block][...], c_refs[2 + block][...])
        upstream.append(jnp.dot(place, cotangent, preferred_element_type=wide))
    rows = jnp.concatenate(picked, 0)
    upstream = jnp.concatenate(upstream, 0)
    gates = jnp.concatenate(gates, 0)
    gate_part = jnp.dot(rows, gate_ref[...], preferred_element_type=wide)
    up_part = jnp.dot(rows, up_ref[...], preferred_element_type=wide)
    sigmoid_gate = 1.0 / (1.0 + jnp.exp(-gate_part))
    silu_gate = gate_part * sigmoid_gate
    hidden = (silu_gate * up_part).astype(low)
    results = jnp.dot(hidden, down_ref[...], preferred_element_type=wide).astype(low).astype(wide)
    dgates = jnp.sum(upstream * results, 1, keepdims=True)
    scaled = (gates * results).astype(low)
    dresults = (gates * upstream).astype(low)
    dhidden = lax.dot_general(dresults, down_ref[...], across, preferred_element_type=wide)
    dsilu_gate = sigmoid_gate * (1.0 + gate_part * (1.0 - sigmoid_gate))
    dgate_low = (dhidden * up_part * dsilu_gate).astype(low)
    dup_low = (dhidden * silu_gate).astype(low)
    drows = lax.dot_general(dgate_low, gate_ref[...], across, preferred_element_type=wide)
    drows = drows + lax.dot_general(dup_low, up_ref[...], across, preferred_element_type=wide)
    drows = drows.astype(low)
    lane = lax.broadcasted_iota(jnp.int32, (blocks * slots, 128), 1)
    coarse = dgates.astype(low).astype(wide)
    extra = jnp.where(lane == own_expert, coarse, 0.0)
    extra = extra + jnp.where(lane == own_expert + experts_all, dgates - coarse, 0.0)
    extra = extra.astype(low)
    for block in range(blocks):
        part = slice(block * slots, (block + 1) * slots)
        sent_refs[block][0] = lax.dot_general(
            places[block], scaled[part], down, preferred_element_type=wide
        ).astype(low)
        back_refs[block][0, :, :model] = lax.dot_general(
            places[block], drows[part], down, preferred_element_type=wide
        ).astype(low)
        back_refs[block][0, :, model:] = lax.dot_general(
            places[block], extra[part], down, preferred_element_type=wide
        ).astype(low)
        rows_ref[0, block] = rows[part]
        hidden_ref[0, block] = hidden[part]
        dresults_ref[0, block] = dresults[part]
        dgate_ref[0, block] = dgate_low[part]
        dup_ref[0, block] = dup_low[part]


def experts(scalars, x_blocks, c_blocks, ranks, chosen, router, gate, up, down, slots, earlier):
    tokens, model = x_blocks[0].shape
    nz, members = ranks.shape[:2]
    hidden = gate.shape[1]
    low = jnp.bfloat16
    pair = members // 2
    experts_all = router.shape[0]
    whole = lambda array: pl.BlockSpec(
        array.shape, lambda a, s: (0, 0), pipeline_mode=pl.Buffered(1)
    )
    turn = lambda *tail: pl.BlockSpec((1, pair) + tail, lambda a, s: (s[1], a, 0, 0))
    in_specs = [
        *[whole(block) for block in x_blocks],
        *[whole(block) for block in c_blocks],
        turn(1, tokens),
        turn(experts_all, tokens),
        whole(router),
        whole(gate),
        whole(up),
        whole(down),
    ]
    shapes = [(slots, model), (slots, hidden), (slots, model)]
    shapes += [(slots, hidden), (slots, hidden)]
    out_shape = [jax.ShapeDtypeStruct((nz, members) + shape, low) for shape in shapes]
    out_specs = [turn(*shape) for shape in shapes]
    wide_model = model + 128
    for columns in (model, wide_model):
        out_shape += [jax.ShapeDtypeStruct((2, tokens, columns), low)] * 2
        out_specs += [pl.BlockSpec((1, tokens, columns), lambda a, s: (a, 0, 0))] * 2
    aliases = {}
    if earlier:
        in_specs = in_specs + [pl.BlockSpec(memory_space=pl.ANY)] * len(earlier)
        aliases = {15 + i: i for i in range(len(earlier))}
    return pl.pallas_call(
        expert_kernel,
        grid_spec=pltpu.PrefetchScalarGridSpec(
            num_scalar_prefetch=1, grid=(2,), in_specs=in_specs, out_specs=out_specs
        ),
        out_shape=out_shape,
        input_output_aliases=aliases,
        compiler_params=pltpu.CompilerParams(vmem_limit_bytes=58 * 2**20),
        cost_estimate=pl.CostEstimate(
            flops=12 * members * slots * model * hidden,
            bytes_accessed=40 * 2**20,
            transcendentals=2 * members * slots * hidden,
        ),
    )(scalars, *x_blocks, *c_blocks, ranks, chosen, router, gate, up, down, *earlier)


def dot32(subscripts, left, right):
    return jnp.einsum(subscripts, left, right, preferred_element_type=jnp.float32)


def member_layer(
    tokens,
    cotangent,
    expert_ids,
    attention_gain,
    ffn_gain,
    query_gain,
    key_gain,
    w_query,
    key_weight,
    value_weight,
    w_output,
    w_router,
    w_gate,
    w_up,
    w_down,
):
    low, wide = jnp.bfloat16, jnp.float32
    nz = lax.axis_size("z")
    zi, yi, ci, xi = (lax.axis_index(axis) for axis in ("z", "y", "c", "x"))
    member = 2 * yi + ci
    context_count = nz * MEMBERS
    rows, model = tokens.shape
    paired = rows // LOCAL_SEQUENCES
    block_len = paired // 2
    groups = QUERY_HEADS // KEY_VALUE_HEADS
    experts_all = w_router.shape[1]
    around = lambda k: lax.rem(zi + (k % nz), jnp.int32(nz))
    from_z = [around(-k) for k in range(nz)]
    crossed = [member ^ r for r in range(MEMBERS)]
    token_members = member ^ jnp.array([0, 2, 1, 3], jnp.int32)

    def uncrossed(blocks):
        for bit, odd in ((1, ci), (2, yi)):
            blocks = [jnp.where(odd == 0, blocks[r], blocks[r ^ bit]) for r in range(MEMBERS)]
        return jnp.stack(blocks)

    own_expert = zi * MEMBERS + member
    step = Steps()

    piece = w_query.shape[0]
    head_rows = w_output.shape[0]
    query_width = groups * HEAD_SIZE
    third = w_down.shape[1] // 3

    def make_tables(zi, token_members):
        own_pos = jax.vmap(lambda device: shard_positions(device, context_count, block_len))(
            zi * MEMBERS + token_members
        )
        cosine, sine_tab = rotary(own_pos.reshape(-1), HEAD_SIZE)
        row_cosine = cosine.reshape(MEMBERS, 1, paired, HEAD_SIZE)
        row_sine = sine_tab.reshape(MEMBERS, 1, paired, HEAD_SIZE)

        def halves(table):
            table = table.reshape(MEMBERS, 2, block_len, HEAD_SIZE).transpose(1, 0, 2, 3)
            return table.reshape(2, MEMBERS * block_len, HEAD_SIZE)

        half = HEAD_SIZE // 2
        signs = jnp.where(jnp.arange(HEAD_SIZE) < half, -1.0, 1.0)
        kernel_cosine, kernel_sine = halves(row_cosine), halves(row_sine * signs)
        half_pos = own_pos.reshape(MEMBERS, 2, block_len).transpose(1, 0, 2).reshape(2, -1)
        mask = (half_pos[:, :, None] <= half_pos[:, None, :]).astype(wide)
        mask = jnp.concatenate([mask, mask], 2)
        return row_cosine, row_sine, kernel_cosine, kernel_sine, mask

    def make_slots(packed):
        width_small = piece * experts_all
        flat = packed.reshape(nz * 8, -1)
        device = jnp.arange(nz * 8, dtype=jnp.int32)
        source = ((zi - device // 8) % nz) * 8 + ((device & 1) ^ xi) * 4
        source = source + (((device >> 1) & 1) ^ ci) * 2 + (((device >> 2) & 1) ^ yi)
        router = flat[:, :width_small][source].reshape(nz * 8, experts_all, piece)
        router = router.transpose(1, 0, 2).reshape(experts_all, model)
        ids_all = packed.reshape(nz, 2, 2, 2, -1)[:, 0, :, :, width_small:].transpose(0, 2, 1, 3)
        ids_all = ids_all.reshape(nz, MEMBERS, TOP, rows).astype(jnp.int32)
        named = jnp.any(ids_all == own_expert, 2)
        before = (
            jnp.arange(rows, dtype=jnp.int32)[:, None] <= jnp.arange(rows, dtype=jnp.int32)[None, :]
        )
        ranks = dot32("kjs,st->kjt", named.astype(low), before.astype(low)).astype(jnp.int32) - 1
        ranks = jnp.where(named, ranks, -1)[:, :, None, :]
        expert_column = jnp.arange(experts_all, dtype=jnp.int32)[:, None]
        chosen_all = jnp.any(ids_all[:, :, :, None, :] == expert_column, 2).astype(wide)
        return router, ranks, chosen_all

    cap_rows = rows * TOP * 5 // (4 * experts_all)
    slots = -(-cap_rows // 16) * 16

    def prepare(w_query, key_weight, value_weight, w_router, expert_ids):
        columns = jnp.concatenate(
            [w.reshape(piece, KEY_VALUE_HEADS, -1) for w in (w_query, key_weight, value_weight)],
            -1,
        ).transpose(1, 0, 2)
        packed = jnp.concatenate([w_router.T.reshape(-1), expert_ids.T.astype(low).reshape(-1)])
        parts = [pick(columns, crossed[r]) for r in range(MEMBERS)]
        return parts[0], parts[1], jnp.stack(parts[2:]), packed.reshape(-1, 128)

    (plane1,), (part0, part1, parts_far, packed), _ = step(
        [(w_output, "z", 1)],
        prepare,
        (w_query, key_weight, value_weight, w_router, expert_ids),
    )
    width = part0.shape[-1]
    inputs = tokens.astype(wide)
    (far, plane3, *small), (normed_attn, inverse_attn), _ = step(
        [(parts_far, "y"), (w_output, "z", 3)] + [(packed, "z", k) for k in range(1, nz)],
        lambda tokens: rms_apply(tokens.astype(wide), attention_gain),
        (tokens,),
    )
    packed = jnp.stack([packed] + small)
    normed_low = normed_attn.astype(low)
    (near, other), _, _ = step([(jnp.stack([part1, far[1]]), "c"), (packed, "y")])
    packed = jnp.stack([packed, other], 1)
    ordered = uncrossed([part0, near[0], far[0], near[1]])
    held = [ordered]
    over_x = []
    (moved, cross, other, near, packed_near), _, _ = step(
        [
            (ordered, "z", 1),
            (ordered, "x"),
            (normed_low, "y"),
            (normed_low, "c"),
            (packed, "c"),
        ]
    )
    held.append(moved)
    over_x.append(cross)
    packed = jnp.stack([packed, packed_near], 1)
    (moved, cross, other_near, packed_cross, down1), tables, _ = step(
        [
            (ordered, "z", 2),
            (held[1], "x"),
            (other, "c"),
            (packed, "x"),
            (w_down[0, third : 2 * third], "x"),
        ],
        make_tables,
        (zi, token_members),
    )
    row_cosine, row_sine, kernel_cosine, kernel_sine, mask = tables
    held.append(moved)
    over_x.append(cross)
    normed_all = jnp.concatenate([normed_low, other, near, other_near])
    packed = jnp.stack([packed, packed_cross], 1)
    (moved, cross, c_near0), (router, ranks, chosen_all), _ = step(
        [(ordered, "z", 3), (held[2], "x"), (cotangent, "c")], make_slots, (packed,)
    )
    held.append(moved)
    over_x.append(cross)
    (cross, plane2, c_far0, down0), (planes,), _ = step(
        [(held[3], "x"), (w_output, "z", 2), (cotangent, "y"), (w_down[0, :third], "x")],
        lambda own, one, three: (jnp.stack([own, one, one, three]),),
        (w_output, plane1, plane3),
    )
    over_x.append(cross)

    def assemble(start, stop):
        full = jnp.zeros((nz, MEMBERS, 2, piece, stop - start), low)
        for k in range(nz):
            full = lax.dynamic_update_slice(
                full, held[k][None, :, None, :, start:stop], (from_z[k], 0, xi, 0, 0)
            )
            full = lax.dynamic_update_slice(
                full, over_x[k][None, :, None, :, start:stop], (from_z[k], 0, 1 - xi, 0, 0)
            )
        return full.reshape(model, stop - start)

    query_weight = assemble(0, query_width)
    key_value_weight = assemble(query_width, width)

    def project_keys(normed_all, key_value_weight):
        raw = jnp.dot(normed_all, key_value_weight, preferred_element_type=wide)
        raw = raw.reshape(MEMBERS, LOCAL_SEQUENCES, paired, 2 * HEAD_SIZE)
        key_proj = raw[..., :HEAD_SIZE]
        key_normed, key_inverse = rms_apply(key_proj, key_gain)
        key_low = rope_apply(key_normed, row_cosine, row_sine).astype(low)
        value_low = raw[..., HEAD_SIZE:].astype(low)
        return key_proj, key_inverse, jnp.concatenate([key_low, value_low], -1)

    planes = lax.dynamic_update_index_in_dim(planes, plane2, 2, 0)
    wanted = [pick(planes, lax.rem(zi + nz - crossed[r], jnp.int32(nz))) for r in range(MEMBERS)]
    cut = rows // 2
    gate_cut = w_gate.shape[1] * 5 // 16
    gate_next = w_gate.shape[1] * 9 // 16
    moved, (key_proj, key_inverse, key_value), _ = step(
        [
            (jnp.stack(wanted[2:]), "y"),
            (cotangent, "z", 1),
            (w_down[0, 2 * third :], "x"),
            (w_gate[0, :gate_cut], "x"),
            (c_far0, "c"),
        ],
        project_keys,
        (normed_all, key_value_weight),
    )
    far, c1, down2, gate0, c_far_near0 = moved
    mine = jnp.stack([wanted[0], far[0]])

    def project_queries(normed_all, query_weight, pair):
        near = swap(pair, "c")
        return (
            near,
            swap(near[0], "x"),
            jnp.dot(normed_all, query_weight, preferred_element_type=wide),
        )

    moved, (near, cross_first, queries), _ = step(
        [(key_value, "z", k) for k in range(1, nz)] + [(mine, "x")],
        project_queries,
        (normed_all, query_weight, jnp.stack([wanted[1], far[1]])),
    )
    key_value = jnp.stack((key_value,) + moved[: nz - 1])
    cross_mine = moved[nz - 1]
    queries = queries.reshape(MEMBERS, LOCAL_SEQUENCES, paired, query_width)

    places = jnp.stack([member, zi]).astype(jnp.int32)
    gain_row = query_gain[None]
    (cross_last, c2_low, c_far1, gate1), attended, _ = step(
        [
            (near[1], "x"),
            (cotangent[:cut], "z", 2),
            (c1, "y"),
            (w_gate[0, gate_cut:gate_next], "x"),
        ],
        attend,
        (places, queries, key_value, kernel_cosine, kernel_sine, gain_row, mask),
    )
    attended = attended.reshape(MEMBERS * rows, query_width)
    own_heads = jnp.stack([mine[0], near[0], mine[1], near[1]])
    other_heads = jnp.stack([cross_mine[0], cross_first, cross_mine[1], cross_last])
    output_weight = jnp.where(
        xi == 0, jnp.stack([own_heads, other_heads], 1), jnp.stack([other_heads, own_heads], 1)
    ).reshape(query_width, model)

    mixed_part = jnp.dot(attended, output_weight, preferred_element_type=wide)
    mixed_part = mixed_part.reshape(2, 2, rows, model)
    (near, c_near1), _, _ = step([(mixed_part[1].astype(low), "c"), (c1, "c")])
    summed_far = (mixed_part[0, 1] + near[1].astype(wide)).astype(low)
    (other, gate2, c2_high, c_far_near1), _, _ = step(
        [
            (summed_far, "y"),
            (w_gate[0, gate_next:], "x"),
            (cotangent[cut:], "z", 2),
            (c_far1, "c"),
        ]
    )
    c2 = jnp.concatenate([c2_low, c2_high])
    mixed_attn = inputs + (mixed_part[0, 0] + near[0].astype(wide) + other.astype(wide))
    normed_ffn, inverse_ffn = rms_apply(mixed_attn, ffn_gain)
    ffn_low = normed_ffn.astype(low)

    logits = dot32("td,ed->te", ffn_low, router)
    chosen = jnp.any(
        expert_ids[:, :, None] == jnp.arange(experts_all, dtype=jnp.int32)[None, None, :], 1
    )
    highest = jnp.max(jnp.where(chosen, logits, NEGATIVE_LIMIT), 1, keepdims=True)
    raised = jnp.where(chosen, jnp.exp(jnp.minimum(logits - highest, 0.0)), 0.0)
    gates = raised / jnp.sum(raised, 1, keepdims=True)

    def whole(own, others):
        full = jnp.zeros((2,) + own.shape, low)
        full = lax.dynamic_update_slice(full, own[None], (xi, 0, 0))
        start = 0
        for other in others:
            full = lax.dynamic_update_slice(full, other[None], (1 - xi, start, 0))
            start += other.shape[0]
        return full.reshape(2 * own.shape[0], own.shape[1])

    def run_experts(k, x_blocks, c_blocks, kept, weights):
        scalars = jnp.stack([own_expert, jnp.int32(k)]).astype(jnp.int32)
        out = experts(
            scalars, x_blocks, c_blocks, ranks, chosen_all, router, *weights, slots, kept
        )
        return tuple(out[:-4]), out[-4:-2], out[-2:]

    def added(pair, back, a):
        return pair[0][a].astype(wide) + back[a].astype(wide)

    def both_rows(block):
        far = swap(block, "y")
        return far, swap(far, "c")

    (x2, up_other, c_far2, y0, c_near2), (gate_all, down_all), _ = step(
        [
            (ffn_low, "z", 2),
            (w_up[0], "x"),
            (c2, "y"),
            (ffn_low, "y"),
            (c2, "c"),
        ],
        lambda owns, others: [whole(own, other) for own, other in zip(owns, others)],
        ([w_gate[0], w_down[0]], [[gate0, gate1, gate2], [down0, down1, down2]]),
    )
    (x1, c3_low, y2, n2, c_far_near2), up_all, _ = step(
        [
            (ffn_low, "z", 1),
            (cotangent[:cut], "z", 3),
            (x2, "y"),
            (x2, "c"),
            (c_far2, "c"),
        ],
        lambda own, other: whole(own, [other]),
        (w_up[0], up_other),
    )
    weights = [gate_all, up_all, down_all]
    (ny2, n0, ny0), _, _ = step([(y2, "c"), (ffn_low, "c"), (y0, "c")])
    (x3, c3_high, y1, c_far3_low, n1), (kept, mixed2, rows2), _ = step(
        [
            (ffn_low, "z", 3),
            (cotangent[cut:], "z", 3),
            (x1, "y"),
            (c3_low, "y"),
            (x1, "c"),
        ],
        functools.partial(run_experts, 2),
        ([x2, n2, y2, ny2], [c2, c_near2, c_far2, c_far_near2], (), weights),
    )
    (ny1,), c3, _ = step(
        [(y1, "c")], lambda *halves: jnp.concatenate(halves), (c3_low, c3_high)
    )
    (y3, c_far3_high, n3, c_near3, back2), (kept, mixed1, rows1), _ = step(
        [(x3, "y"), (c3_high, "y"), (x3, "c"), (c3, "c"), (rows2[1], "c")],
        functools.partial(run_experts, 1),
        ([x1, n1, y1, ny1], [c1, c_near1, c_far1, c_far_near1], kept, weights),
    )
    c_far3 = jnp.concatenate([c_far3_low, c_far3_high])
    (ny3, c_far_near3, mixed_back2), row_send2, _ = step(
        [(y3, "c"), (c_far3, "c"), (mixed2[1], "c")],
        lambda pair, back: added(pair, back, 1).astype(low),
        (rows2, back2),
    )
    (far2, mixed_far2, back1, mixed_back1), (kept, mixed3, rows3), _ = step(
        [
            (row_send2, "y"),
            (added(mixed2, mixed_back2, 1).astype(low), "y"),
            (rows1[1], "c"),
            (mixed1[1], "c"),
        ],
        functools.partial(run_experts, 3),
        ([x3, n3, y3, ny3], [c3, c_near3, c_far3, c_far_near3], kept, weights),
    )
    total2 = (added(rows2, back2, 0) + far2.astype(wide)).astype(low)
    (z2, far1, mixed_far1, back3, mixed_back3), (kept, mixed0, rows0), _ = step(
        [
            (total2, "z", -2),
            (added(rows1, back1, 1).astype(low), "y"),
            (added(mixed1, mixed_back1, 1).astype(low), "y"),
            (rows3[1], "c"),
            (mixed3[1], "c"),
        ],
        functools.partial(run_experts, 0),
        (
            [ffn_low, n0, y0, ny0],
            [cotangent, c_near0, c_far0, c_far_near0],
            kept,
            weights,
        ),
    )
    expert_rows, hidden_low, dresults, dgate_low, dup_low = (
        block.reshape(context_count * slots, -1) for block in kept
    )

    def halved(grad):
        size = grad.shape[0] // 2
        own = lax.dynamic_slice_in_dim(grad, xi * size, size, 0)
        return own, lax.dynamic_slice_in_dim(grad, (1 - xi) * size, size, 0).astype(low)

    def joined(own, moved):
        return (own + jnp.concatenate(moved, 0).astype(wide))[None]

    total1 = (added(rows1, back1, 0) + far1.astype(wide)).astype(low)

    def total(pair, back, far):
        return (added(pair, back, 0) + far.astype(wide)).astype(low)

    (z1, far3, back0, mixed_back0), ((down_grad, down_send), mixed_send1), _ = step(
        [
            (total1, "z", -1),
            (added(rows3, back3, 1).astype(low), "y"),
            (rows0[1], "c"),
            (mixed0[1], "c"),
        ],
        lambda rows, grad, *given: (halved(dot32("sf,sd->fd", rows, grad)), total(*given)),
        (hidden_low, dresults, mixed1, mixed_back1, mixed_far1),
    )
    total3 = (added(rows3, back3, 0) + far3.astype(wide)).astype(low)
    down_cut = down_send.shape[0] * 5 // 8
    (z3, far0, down0), ((gate_grad, gate_send), mixed_send2), _ = step(
        [
            (total3, "z", -3),
            (added(rows0, back0, 1).astype(low), "y"),
            (down_send[:down_cut], "x"),
        ],
        lambda rows, grad, *given: (halved(dot32("sd,sf->df", rows, grad)), total(*given)),
        (expert_rows, dgate_low, mixed2, mixed_back2, mixed_far2),
    )
    returned = added(rows0, back0, 0) + far0.astype(wide) + z1.astype(wide)
    returned = returned + z2.astype(wide) + z3.astype(wide)
    dffn_routed = returned[:, :model]
    dgates = returned[:, model : model + experts_all]
    dgates = dgates + returned[:, model + experts_all : model + 2 * experts_all]
    dlogits = gates * (dgates - jnp.sum(gates * dgates, 1, keepdims=True))
    dlogits_low = dlogits.astype(low)
    router_rows = dot32("td,te->de", ffn_low, dlogits_low).astype(low)
    router_rows = router_rows.reshape(nz, MEMBERS, 2, -1, 2 * HEAD_SIZE)
    extra_rows = router_rows.shape[3]
    router_rows = jnp.pad(router_rows, ((0, 0),) * 3 + ((0, -extra_rows % 16), (0, 0)))

    upstream = cotangent.astype(wide)
    dffn_rows = dffn_routed + dot32("te,ed->td", dlogits_low, router)
    dmixed_norm, ffn_gain_part = rms_back(mixed_attn, inverse_ffn, ffn_gain, dffn_rows)
    dmixed_attn = upstream + dmixed_norm
    dattn_low = dmixed_attn.astype(low)
    gate_cut = gate_send.shape[0] * 5 // 8
    moved, (up_grad, up_send), _ = step(
        [
            (dattn_low, "y"),
            (dattn_low, "c"),
            (gate_send[:gate_cut], "x"),
            (mixed_send1, "z", -1),
        ],
        lambda rows, grad: halved(dot32("sd,sf->df", rows, grad)),
        (expert_rows, dup_low),
    )
    other, near, gate0, mixed_z1 = moved
    (other_near,), _, _ = step([(other, "c")])
    dattn_all = jnp.concatenate([dattn_low, other, near, other_near])

    output_part = dot32("tc,td->cd", attended, dattn_all).astype(low)
    output_part = output_part.reshape(MEMBERS, 2, head_rows, model)
    output_own = lax.dynamic_index_in_dim(output_part, xi, 1, keepdims=False)
    output_other = lax.dynamic_index_in_dim(output_part, 1 - xi, 1, keepdims=False)

    def planes_of(part):
        own = lax.dynamic_index_in_dim(part, xi, 2, keepdims=False)
        other = lax.dynamic_index_in_dim(part, 1 - xi, 2, keepdims=False)
        return [(pick(own, around(k)), pick(other, around(k))) for k in range(nz)]

    def attention_back(dattn_all, output_weight, *given):
        attended_grad = dot32("td,cd->tc", dattn_all, output_weight).astype(low)
        attended_grad = attended_grad.reshape(MEMBERS, LOCAL_SEQUENCES, paired, query_width)
        return attend_back(*given[:2], attended_grad, *given[2:])

    moved, attention_grads, _ = step(
        [
            (output_other[1:], "x"),
            (mixed_send2, "z", -2),
            (added(mixed3, mixed_back3, 1).astype(low), "y"),
            (added(mixed0, mixed_back0, 1).astype(low), "y"),
        ],
        attention_back,
        (
            dattn_all,
            output_weight,
            places,
            queries,
            key_value,
            kernel_cosine,
            kernel_sine,
            gain_row,
            mask,
        ),
    )
    cross_rest, mixed_z2, mixed_far3, mixed_far0 = moved
    dquery_low, dkey_value, query_gain_part = attention_grads
    query_gain_part = query_gain_part[0]
    dquery_low = dquery_low.reshape(MEMBERS * rows, query_width)
    query_part = dot32("td,tc->dc", normed_all, dquery_low).astype(low)
    query_planes = planes_of(query_part.reshape(nz, MEMBERS, 2, piece, query_width))
    output_far = (output_own[2:].astype(wide) + cross_rest[1:].astype(wide)).astype(low)

    def query_back(grad, weight, third):
        return dot32("tc,dc->td", grad, weight), total(*third)

    query_plane = query_planes[2][1].reshape(-1, query_width)
    first_head = [output_other[0][:, a : a + query_width] for a in range(0, model, query_width)]
    moved, (dnormed, mixed_send3), _ = step(
        [(dkey_value[k].astype(low), "z", -k) for k in range(1, nz)]
        + [(jnp.concatenate([query_plane] + first_head), "x"), (output_far, "y")],
        query_back,
        (dquery_low, query_weight, [mixed3, mixed_back3, mixed_far3]),
    )
    *key_moves, cross, output_far = moved
    plane_rows = query_plane.shape[0]
    cross_first = [
        cross[a : a + head_rows] for a in range(plane_rows, cross.shape[0], head_rows)
    ]
    cross_first = jnp.concatenate(cross_first, 1)
    cross = cross[:plane_rows].reshape(query_planes[2][0].shape)
    query_sum2 = (query_planes[2][0].astype(wide) + cross.astype(wide)).astype(low)
    near_first = (output_own[0].astype(wide) + cross_first.astype(wide)).astype(low)
    near_last = (output_own[1].astype(wide) + cross_rest[0].astype(wide)).astype(low)

    def project_keys_back(dnormed, dkey_value_own, moved, key_value_weight):
        dkey_value_own = dkey_value_own + sum(block.astype(wide) for block in moved)
        dkey, dvalue = dkey_value_own[..., :HEAD_SIZE], dkey_value_own[..., HEAD_SIZE:]
        dkey_proj, key_gain_part = rms_back(
            key_proj, key_inverse, key_gain, rope_back(dkey, row_cosine, row_sine)
        )
        dkey_value_low = jnp.concatenate([dkey_proj, dvalue], -1).astype(low)
        dkey_value_low = dkey_value_low.reshape(MEMBERS * rows, 2 * HEAD_SIZE)
        dnormed = dnormed + dot32("tc,dc->td", dkey_value_low, key_value_weight)
        dnormed = dnormed.reshape(2, 2, rows, model)
        key_part = dot32("td,tc->dc", normed_all, dkey_value_low).astype(low)
        key_part = key_part.reshape(nz, MEMBERS, 2, piece, 2 * HEAD_SIZE)
        key_part = jnp.concatenate([key_part, router_rows], 3)
        key_own = lax.dynamic_index_in_dim(key_part, xi, 2, keepdims=False)
        key_other = lax.dynamic_index_in_dim(key_part, 1 - xi, 2, keepdims=False)
        return dnormed[0], dnormed[1].astype(low), key_own, key_other, key_gain_part

    moved, (dnormed_own, dnormed_send, key_own, key_other, key_gain_part), _ = step(
        [
            (query_sum2, "z", 2),
            (jnp.stack([query_planes[1][1], query_planes[3][1]]), "x"),
            (jnp.stack([near_last, output_far[1]]), "c"),
        ],
        project_keys_back,
        (dnormed, dkey_value[0], key_moves, key_value_weight),
    )
    query_z2, cross, output_back = moved
    query_sum1 = (query_planes[1][0].astype(wide) + cross[0].astype(wide)).astype(low)
    query_sum3 = (query_planes[3][0].astype(wide) + cross[1].astype(wide)).astype(low)

    def order_output(blocks):
        blocks = uncrossed(blocks)
        return [pick(blocks, around(k)) for k in range(nz)]

    moved, output_sends, _ = step(
        [
            (query_sum1, "z", 1),
            (query_sum3, "z", 3),
            (query_planes[0][1], "x"),
            (key_other, "x"),
            (dnormed_send, "c"),
        ],
        order_output,
        ([near_first, output_back[0], output_far[0], output_back[1]],),
    )
    query_z1, query_z3, cross, key_cross, near = moved
    dnormed_far = (dnormed_own[1] + near[1].astype(wide)).astype(low)
    key_sum = (key_own.astype(wide) + key_cross.astype(wide)).astype(low)

    def total_queries(own, cross, *moved):
        total = own.astype(wide) + cross.astype(wide) + sum(m.astype(wide) for m in moved)
        total = total.astype(low)
        parts = [pick(total, crossed[r]) for r in range(MEMBERS)]
        return parts[0], parts[1], jnp.stack(parts[2:])

    (output_z1, output_z3, other, gate1, down1), query_parts, _ = step(
        [
            (output_sends[1], "z", 1),
            (output_sends[3], "z", 3),
            (dnormed_far, "y"),
            (gate_send[gate_cut:], "x"),
            (down_send[down_cut:], "x"),
        ],
        total_queries,
        (query_planes[0][0], cross, query_z1, query_z2, query_z3),
    )
    dnormed = dnormed_own[0] + near[0].astype(wide) + other.astype(wide)
    dinput_norm, attention_gain_part = rms_back(inputs, inverse_attn, attention_gain, dnormed)
    small = [attention_gain_part, ffn_gain_part, query_gain_part, key_gain_part]
    small = jnp.concatenate(small).reshape(-1, 128)
    (*key_moves, small_x, query_far), d_tokens, _ = step(
        [(pick(key_sum, around(k)), "z", k) for k in range(1, nz)]
        + [(small, "x"), (query_parts[2], "y")],
        lambda a, b: (a + b).astype(low),
        (dmixed_attn, dinput_norm),
    )
    small = small + small_x
    key_total = pick(key_sum, zi).astype(wide)
    key_total = (key_total + sum(m.astype(wide) for m in key_moves)).astype(low)
    key_parts = [pick(key_total, crossed[r]) for r in range(MEMBERS)]

    def member_columns(parts):
        return uncrossed(parts).astype(wide).transpose(1, 0, 2)

    up_cut = up_send.shape[0] * 11 // 16
    (output_z2, up0, key_far, small_y, query_near), (down_grad, gate_grad), _ = step(
        [
            (output_sends[2], "z", 2),
            (up_send[:up_cut], "x"),
            (jnp.stack(key_parts[2:]), "y"),
            (small, "y"),
            (jnp.stack([query_parts[1], query_far[1]]), "c"),
        ],
        lambda down, downs, gate, gates: (joined(down, downs), joined(gate, gates)),
        (down_grad, [down0, down1], gate_grad, [gate0, gate1]),
    )
    small = small + small_y
    query_blocks = [query_parts[0], query_near[0], query_far[0], query_near[1]]
    (mixed_z3, up1, key_near, small_c), (query_grad, output_grad), _ = step(
        [
            (mixed_send3, "z", -3),
            (up_send[up_cut:], "x"),
            (jnp.stack([key_parts[1], key_far[1]]), "c"),
            (small, "c"),
        ],
        lambda blocks, own, *parts: (
            member_columns(blocks).reshape(piece, -1),
            own.astype(wide) + sum(part.astype(wide) for part in parts),
        ),
        (query_blocks, output_sends[0], output_z1, output_z2, output_z3),
    )
    small = small + small_c
    key_blocks = [key_parts[0], key_near[0], key_far[0], key_near[1]]

    def finish(up, ups, key_blocks, base, pair, back, far, z1, z2, z3):
        router = sum(block[piece : piece + extra_rows].astype(wide) for block in key_blocks)
        mixed = base + added(pair, back, 0) + far.astype(wide) + z1.astype(wide)
        mixed = mixed + z2.astype(wide) + z3.astype(wide)
        return (
            joined(up, ups),
            member_columns([block[:piece] for block in key_blocks]),
            router.reshape(piece, experts_all),
            mixed.astype(low),
        )

    small_z, results, _ = step(
        [(small, "z", k) for k in range(1, nz)],
        finish,
        (
            up_grad,
            [up0, up1],
            key_blocks,
            mixed_attn,
            mixed0,
            mixed_back0,
            mixed_far0,
            mixed_z1,
            mixed_z2,
            mixed_z3,
        ),
    )
    up_grad, key_grads, router_grad, mixed = results
    gains = (small + sum(small_z)).reshape(-1)
    key_grad = key_grads[..., :HEAD_SIZE].reshape(piece, -1)
    value_grad = key_grads[..., HEAD_SIZE:].reshape(piece, -1)
    return (
        mixed,
        d_tokens,
        gains[:model],
        gains[model : 2 * model],
        gains[2 * model : 2 * model + HEAD_SIZE],
        gains[2 * model + HEAD_SIZE :],
        query_grad,
        key_grad,
        value_grad,
        output_grad,
        router_grad,
        gate_grad,
        up_grad,
        down_grad,
    )


def solution(mesh):
    contexts, pairs = mesh.shape["ctx"], mesh.shape["fsdp"]
    planes = contexts // MEMBERS
    if planes == KEY_VALUE_HEADS and pairs * MEMBERS * KEY_VALUE_HEADS == QUERY_HEADS:
        layer, every, split = member_layer, ("z", "y", "c", "x"), ("z", "y", "c")
        pair = "x"
        mesh = Mesh(mesh.devices.reshape(planes, 2, 2, pairs), every)
    else:
        layer, every, split, pair = routed_layer, ("ctx", "fsdp"), "ctx", "fsdp"
    by_row = P(every, None)
    by_expert = P(split, pair, None)
    return jax.shard_map(
        layer,
        mesh=mesh,
        in_specs=(by_row,) * 3 + (P(),) * 4 + (by_row,) * 5 + (by_expert,) * 3,
        out_specs=(by_row,) * 2 + (P(),) * 4 + (by_row,) * 5 + (by_expert,) * 3,
        check_vma=False,
    )
```

```python
import functools
import math

import jax
import jax.numpy as jnp
from jax import lax
from jax.experimental import pallas as pl
from jax.experimental.pallas import tpu as pltpu
from jax.sharding import Mesh
from jax.sharding import PartitionSpec as P

QUERY_HEADS = 32
KEY_VALUE_HEADS = 4
HEAD_SIZE = 128
TOP = 8
LOCAL_SEQUENCES = 3


EPS = 1e-06
THETA = 1000000.0
NEGATIVE_LIMIT = -1e30


def shard_positions(device, context_count, block_len):
    within = jnp.arange(2 * block_len, dtype=jnp.int32)
    lower_pos = device * block_len + within
    upper_pos = (2 * context_count - 1 - device) * block_len + within - block_len
    return jnp.where(within < block_len, lower_pos, upper_pos)


def group_positions(first_dev, query_group_size, context_count, block_len):
    devices = first_dev + jnp.arange(query_group_size, dtype=jnp.int32)
    return jax.vmap(lambda device: shard_positions(device, context_count, block_len))(
        devices
    ).reshape(-1)


def rotary(positions, head_width):
    half_width = head_width // 2
    frequency = jnp.exp(
        -math.log(THETA) * (2.0 * jnp.arange(half_width, dtype=jnp.float32)) / head_width
    )
    angles = positions.astype(jnp.float32)[:, None] * frequency[None, :]
    angles = jnp.concatenate([angles, angles], -1)
    return (jnp.cos(angles)[:, None, :], jnp.sin(angles)[:, None, :])


def rope_apply(value_rows_list, cosine, sine_tab):
    half_width = value_rows_list.shape[-1] // 2
    turned = jnp.concatenate(
        [-value_rows_list[..., half_width:], value_rows_list[..., :half_width]], -1
    )
    return value_rows_list * cosine + turned * sine_tab


def rope_back(upstream, cosine, sine_tab):
    half_width = upstream.shape[-1] // 2
    moved_part = upstream * sine_tab
    return upstream * cosine + jnp.concatenate(
        [moved_part[..., half_width:], -moved_part[..., :half_width]], -1
    )


def rms_apply(value_rows_list, gain_vec):
    inverse = lax.rsqrt(jnp.mean(value_rows_list * value_rows_list, -1, keepdims=True) + EPS)
    return (value_rows_list * inverse * gain_vec, inverse)


def rms_back(value_rows_list, inverse, gain_vec, upstream):
    normalized_input = value_rows_list * inverse
    gain_part = jnp.sum((upstream * normalized_input).reshape(-1, value_rows_list.shape[-1]), 0)
    scaled = upstream * gain_vec
    back_part = inverse * (
        scaled - normalized_input * jnp.mean(scaled * normalized_input, -1, keepdims=True)
    )
    return (back_part, gain_part)


def arrange(blocks):
    query_group_size, seq_count, paired_rows, heads_kv, head_dim = blocks.shape
    return blocks.transpose(1, 0, 2, 3, 4).reshape(
        seq_count, query_group_size * paired_rows, heads_kv, head_dim
    )


def unarrange(rows_all, query_group_size):
    seq_count, width_all, heads_kv, head_dim = rows_all.shape
    return rows_all.reshape(
        seq_count, query_group_size, width_all // query_group_size, heads_kv, head_dim
    ).transpose(1, 0, 2, 3, 4)


def attend_group(state_now, queries, key_row_matrix, value_rows, query_pos, key_pos, score_scale):
    run_max, run_sum, run_acc = state_now
    scores = (
        jnp.einsum("skgqd,swkd->skgqw", queries, key_row_matrix, preferred_element_type=jnp.float32)
        * score_scale
    )
    allowed = key_pos[None, :] <= query_pos[:, None]
    new_max = jnp.maximum(run_max, jnp.max(jnp.where(allowed, scores, NEGATIVE_LIMIT), -1))
    weights_now = jnp.where(allowed, jnp.exp(scores - new_max[..., None]), 0.0)
    factor = jnp.exp(run_max - new_max)
    new_sum = run_sum * factor + jnp.sum(weights_now, -1)
    update = jnp.einsum(
        "skgqw,swkd->skgqd",
        weights_now.astype(jnp.bfloat16),
        value_rows,
        preferred_element_type=jnp.float32,
    )
    return (new_max, new_sum, run_acc * factor[..., None] + update)


def routed_layer(
    tokens,
    cotangent,
    expert_ids,
    attention_gain,
    ffn_gain,
    query_gain,
    key_gain,
    w_query,
    key_weight,
    value_weight,
    w_output,
    w_router,
    w_gate,
    w_up,
    w_down,
):
    context_count = lax.axis_size("ctx")
    ctx_here = lax.axis_index("ctx")
    token_per_device = tokens.shape[0]
    block_len = token_per_device // (2 * LOCAL_SEQUENCES)
    paired_rows = 2 * block_len
    query_groups = QUERY_HEADS // KEY_VALUE_HEADS
    score_scale = 1.0 / math.sqrt(HEAD_SIZE)
    experts_all = w_router.shape[1]
    exp_dev = w_gate.shape[0]
    cap_rows = token_per_device * TOP * 5 // (4 * experts_all)
    routes = token_per_device * TOP
    inputs = tokens.astype(jnp.float32)
    normed_attn, inverse_attn = rms_apply(inputs, attention_gain)
    normed_low = normed_attn.astype(jnp.bfloat16)
    query_all, key_all, value_all, output_all, router_all = (
        lax.all_gather(w_query, ("ctx", "fsdp"), axis=0, tiled=True),
        lax.all_gather(key_weight, ("ctx", "fsdp"), axis=0, tiled=True),
        lax.all_gather(value_weight, ("ctx", "fsdp"), axis=0, tiled=True),
        lax.all_gather(w_output, ("ctx", "fsdp"), axis=0, tiled=True),
        lax.all_gather(w_router, ("ctx", "fsdp"), axis=0, tiled=True),
    )
    local_pos = shard_positions(ctx_here, context_count, block_len)
    row_pos = jnp.tile(local_pos, LOCAL_SEQUENCES)
    cosine, sine_tab = rotary(row_pos, HEAD_SIZE)
    query_proj = jnp.dot(normed_low, query_all, preferred_element_type=jnp.float32).reshape(
        token_per_device, QUERY_HEADS, HEAD_SIZE
    )
    key_proj = jnp.dot(normed_low, key_all, preferred_element_type=jnp.float32).reshape(
        token_per_device, KEY_VALUE_HEADS, HEAD_SIZE
    )
    value_proj = jnp.dot(normed_low, value_all, preferred_element_type=jnp.float32).reshape(
        token_per_device, KEY_VALUE_HEADS, HEAD_SIZE
    )
    query_normed, query_inverse = rms_apply(query_proj, query_gain)
    key_normed, key_inverse = rms_apply(key_proj, key_gain)
    query_lower = rope_apply(query_normed, cosine, sine_tab).astype(jnp.bfloat16)
    key_low = rope_apply(key_normed, cosine, sine_tab).astype(jnp.bfloat16)
    value_low = value_proj.astype(jnp.bfloat16)
    query_head_rows = query_lower.reshape(
        LOCAL_SEQUENCES, paired_rows, KEY_VALUE_HEADS, query_groups, HEAD_SIZE
    ).transpose(0, 2, 3, 1, 4)
    initial = (
        jnp.full(
            (LOCAL_SEQUENCES, KEY_VALUE_HEADS, query_groups, paired_rows),
            NEGATIVE_LIMIT,
            jnp.float32,
        ),
        jnp.zeros((LOCAL_SEQUENCES, KEY_VALUE_HEADS, query_groups, paired_rows), jnp.float32),
        jnp.zeros(
            (LOCAL_SEQUENCES, KEY_VALUE_HEADS, query_groups, paired_rows, HEAD_SIZE), jnp.float32
        ),
    )
    key_every, value_every = (
        lax.all_gather(key_low, "ctx", axis=0, tiled=True),
        lax.all_gather(value_low, "ctx", axis=0, tiled=True),
    )
    shard_total_count = key_every.shape[0] // token_per_device
    fold_query_group_size = 4
    key_block_list = key_every.reshape(
        shard_total_count // fold_query_group_size,
        fold_query_group_size,
        LOCAL_SEQUENCES,
        paired_rows,
        KEY_VALUE_HEADS,
        HEAD_SIZE,
    )
    value_block_list = value_every.reshape(
        shard_total_count // fold_query_group_size,
        fold_query_group_size,
        LOCAL_SEQUENCES,
        paired_rows,
        KEY_VALUE_HEADS,
        HEAD_SIZE,
    )
    first_devs = 0 // token_per_device + fold_query_group_size * jnp.arange(
        shard_total_count // fold_query_group_size, dtype=jnp.int32
    )

    def one_group(state_in, loop_item):
        key_group, value_group, first_dev = loop_item
        key_pos = group_positions(first_dev, fold_query_group_size, context_count, block_len)
        return (
            attend_group(
                state_in,
                query_head_rows,
                arrange(key_group),
                arrange(value_group),
                local_pos,
                key_pos,
                score_scale,
            ),
            None,
        )

    state_out, unused = lax.scan(one_group, initial, (key_block_list, value_block_list, first_devs))
    run_max, run_sum, run_acc = state_out
    log_sum = run_max + jnp.log(run_sum)
    attended = run_acc / run_sum[..., None]
    attended_low = (
        attended.transpose(0, 3, 1, 2, 4)
        .reshape(token_per_device, QUERY_HEADS * HEAD_SIZE)
        .astype(jnp.bfloat16)
    )
    mixed_attn = inputs + jnp.dot(attended_low, output_all, preferred_element_type=jnp.float32)
    normed_ffn, inverse_ffn = rms_apply(mixed_attn, ffn_gain)
    ffn_low = normed_ffn.astype(jnp.bfloat16)
    logits = jnp.dot(ffn_low, router_all, preferred_element_type=jnp.float32)
    chosen = (expert_ids[..., None] == jnp.arange(experts_all, dtype=jnp.int32)).astype(jnp.float32)
    picked = jnp.einsum("tje,te->tj", chosen, logits, precision=lax.Precision.HIGHEST)
    gate_probs = jax.nn.softmax(picked, -1)
    flat_ids = expert_ids.reshape(-1)
    route_marks = (flat_ids[:, None] == jnp.arange(experts_all, dtype=jnp.int32)).astype(jnp.int32)
    route_ranks = jnp.sum((jnp.cumsum(route_marks, 0) - 1) * route_marks, -1)
    slot_of_route = flat_ids * cap_rows + route_ranks
    route_of_slot = (
        jnp.full((experts_all * cap_rows,), routes, jnp.int32)
        .at[slot_of_route]
        .set(jnp.arange(routes, dtype=jnp.int32))
    )
    padded = jnp.concatenate([ffn_low, jnp.zeros((1, ffn_low.shape[1]), jnp.bfloat16)], 0)
    outgoing = padded[route_of_slot // TOP].reshape(experts_all, cap_rows, -1)
    arrived = lax.all_to_all(outgoing, "ctx", split_axis=0, concat_axis=0, tiled=True)

    def to_experts(buffer):
        return (
            buffer.reshape(context_count, exp_dev, cap_rows, -1)
            .transpose(1, 0, 2, 3)
            .reshape(exp_dev, context_count * cap_rows, -1)
        )

    def from_experts(buffer):
        return (
            buffer.reshape(exp_dev, context_count, cap_rows, -1)
            .transpose(1, 0, 2, 3)
            .reshape(context_count * exp_dev, cap_rows, -1)
        )

    expert_rows = to_experts(arrived)
    gate_all, up_all, down_all = (
        lax.all_gather(w_gate, "fsdp", axis=1, tiled=True),
        lax.all_gather(w_up, "fsdp", axis=1, tiled=True),
        lax.all_gather(w_down, "fsdp", axis=1, tiled=True),
    )
    gate_part = jnp.einsum(
        "esd,edf->esf", expert_rows, gate_all, preferred_element_type=jnp.float32
    )
    up_part = jnp.einsum("esd,edf->esf", expert_rows, up_all, preferred_element_type=jnp.float32)
    sigmoid_gate = jax.nn.sigmoid(gate_part)
    silu_gate = gate_part * sigmoid_gate
    hidden_low = (silu_gate * up_part).astype(jnp.bfloat16)
    results = jnp.einsum(
        "esf,efd->esd", hidden_low, down_all, preferred_element_type=jnp.float32
    ).astype(jnp.bfloat16)
    returned = lax.all_to_all(from_experts(results), "ctx", split_axis=0, concat_axis=0, tiled=True)
    route_out = returned.reshape(experts_all * cap_rows, -1)[slot_of_route].reshape(
        token_per_device, TOP, -1
    )
    mixed = (mixed_attn + jnp.sum(gate_probs[..., None] * route_out, 1)).astype(jnp.bfloat16)
    query_back, key_back, value_back, output_back, router_back = (
        lax.all_gather(w_query, ("ctx", "fsdp"), axis=0, tiled=True),
        lax.all_gather(key_weight, ("ctx", "fsdp"), axis=0, tiled=True),
        lax.all_gather(value_weight, ("ctx", "fsdp"), axis=0, tiled=True),
        lax.all_gather(w_output, ("ctx", "fsdp"), axis=0, tiled=True),
        lax.all_gather(w_router, ("ctx", "fsdp"), axis=0, tiled=True),
    )
    upstream = cotangent.astype(jnp.float32)
    dgates = jnp.sum(upstream[:, None, :] * route_out, -1)
    dpicked = gate_probs * (dgates - jnp.sum(gate_probs * dgates, -1, keepdims=True))
    dlogits_low = jnp.einsum("tj,tje->te", dpicked, chosen, precision=lax.Precision.HIGHEST).astype(
        jnp.bfloat16
    )
    router_grad = jnp.einsum("td,te->de", ffn_low, dlogits_low, preferred_element_type=jnp.float32)
    dresults = (
        (gate_probs[..., None] * upstream[:, None, :]).astype(jnp.bfloat16).reshape(routes, -1)
    )
    dresults = jnp.concatenate([dresults, jnp.zeros((1, dresults.shape[1]), jnp.bfloat16)], 0)
    dreturned = lax.all_to_all(
        dresults[route_of_slot].reshape(experts_all, cap_rows, -1),
        "ctx",
        split_axis=0,
        concat_axis=0,
        tiled=True,
    )
    dresult_rows = to_experts(dreturned)
    dhidden = jnp.einsum("esd,efd->esf", dresult_rows, down_all, preferred_element_type=jnp.float32)
    down_grad = jnp.einsum(
        "esf,esd->efd", hidden_low, dresult_rows, preferred_element_type=jnp.float32
    )
    dsilu_gate = sigmoid_gate * (1.0 + gate_part * (1.0 - sigmoid_gate))
    dgate_low = (dhidden * up_part * dsilu_gate).astype(jnp.bfloat16)
    dup_low = (dhidden * silu_gate).astype(jnp.bfloat16)
    gate_grad = jnp.einsum(
        "esd,esf->edf", expert_rows, dgate_low, preferred_element_type=jnp.float32
    )
    up_grad = jnp.einsum("esd,esf->edf", expert_rows, dup_low, preferred_element_type=jnp.float32)
    dexpert_rows = (
        jnp.einsum("esf,edf->esd", dgate_low, gate_all, preferred_element_type=jnp.float32)
        + jnp.einsum("esf,edf->esd", dup_low, up_all, preferred_element_type=jnp.float32)
    ).astype(jnp.bfloat16)
    dsent_rows = lax.all_to_all(
        from_experts(dexpert_rows), "ctx", split_axis=0, concat_axis=0, tiled=True
    )
    droutes = dsent_rows.reshape(experts_all * cap_rows, -1)[slot_of_route].reshape(
        token_per_device, TOP, -1
    )
    dffn_rows = jnp.sum(droutes.astype(jnp.float32), 1) + jnp.einsum(
        "te,de->td", dlogits_low, router_back, preferred_element_type=jnp.float32
    )
    expert_sums = (
        lax.psum_scatter(
            gate_grad.astype(jnp.bfloat16), "fsdp", scatter_dimension=1, tiled=True
        ).astype(jnp.float32),
        lax.psum_scatter(
            up_grad.astype(jnp.bfloat16), "fsdp", scatter_dimension=1, tiled=True
        ).astype(jnp.float32),
        lax.psum_scatter(
            down_grad.astype(jnp.bfloat16), "fsdp", scatter_dimension=1, tiled=True
        ).astype(jnp.float32),
    )
    dmixed_norm, ffn_gain_part = rms_back(mixed_attn, inverse_ffn, ffn_gain, dffn_rows)
    dmixed_attn = upstream + dmixed_norm
    dattn_low = dmixed_attn.astype(jnp.bfloat16)
    output_grad = jnp.einsum(
        "tc,td->cd", attended_low, dattn_low, preferred_element_type=jnp.float32
    )
    attended_lower_grad = jnp.einsum(
        "td,cd->tc", dattn_low, output_back, preferred_element_type=jnp.float32
    ).astype(jnp.bfloat16)
    output_heads_grad = attended_lower_grad.reshape(
        LOCAL_SEQUENCES, paired_rows, KEY_VALUE_HEADS, query_groups, HEAD_SIZE
    ).transpose(0, 2, 3, 1, 4)
    delta_row = jnp.sum(output_heads_grad.astype(jnp.float32) * attended, -1)
    key_recomputed, value_recomputed = (key_every, value_every)

    def score_grads(key_group, value_group, first_dev, query_group_size):
        key_row_matrix = arrange(key_group)
        value_rows = arrange(value_group)
        key_pos = group_positions(first_dev, query_group_size, context_count, block_len)
        scores = (
            jnp.einsum(
                "skgqd,swkd->skgqw",
                query_head_rows,
                key_row_matrix,
                preferred_element_type=jnp.float32,
            )
            * score_scale
        )
        allowed = key_pos[None, :] <= local_pos[:, None]
        weights_now = jnp.where(allowed, jnp.exp(scores - log_sum[..., None]), 0.0)
        dweights = jnp.einsum(
            "skgqd,swkd->skgqw", output_heads_grad, value_rows, preferred_element_type=jnp.float32
        )
        dscores = (weights_now * (dweights - delta_row[..., None])).astype(jnp.bfloat16)
        return (key_row_matrix, weights_now, dscores)

    def key_terms(weights_now, dscores, query_group_size):
        dkey_rows = jnp.einsum(
            "skgqw,skgqd->swkd", dscores, query_head_rows, preferred_element_type=jnp.float32
        )
        dvalue_rows = jnp.einsum(
            "skgqw,skgqd->swkd",
            weights_now.astype(jnp.bfloat16),
            output_heads_grad,
            preferred_element_type=jnp.float32,
        )
        return (unarrange(dkey_rows, query_group_size), unarrange(dvalue_rows, query_group_size))

    query_group_size = 4
    loop_step_count = context_count // query_group_size
    key_block_list = key_recomputed.reshape(
        loop_step_count, query_group_size, LOCAL_SEQUENCES, paired_rows, KEY_VALUE_HEADS, HEAD_SIZE
    )
    value_block_list = value_recomputed.reshape(
        loop_step_count, query_group_size, LOCAL_SEQUENCES, paired_rows, KEY_VALUE_HEADS, HEAD_SIZE
    )
    first_devs = query_group_size * jnp.arange(loop_step_count, dtype=jnp.int32)

    def back_group(dquery_acc, loop_item):
        key_group, value_group, first_dev = loop_item
        key_row_matrix, weights_now, dscores = score_grads(
            key_group, value_group, first_dev, query_group_size
        )
        dquery_acc = dquery_acc + jnp.einsum(
            "skgqw,swkd->skgqd", dscores, key_row_matrix, preferred_element_type=jnp.float32
        )
        return (dquery_acc, key_terms(weights_now, dscores, query_group_size))

    dquery_heads, key_value_pieces = lax.scan(
        back_group,
        jnp.zeros(query_head_rows.shape, jnp.float32),
        (key_block_list, value_block_list, first_devs),
    )
    key_grad_every = key_value_pieces[0].reshape(
        context_count * token_per_device, KEY_VALUE_HEADS, HEAD_SIZE
    )
    value_grad_every = key_value_pieces[1].reshape(
        context_count * token_per_device, KEY_VALUE_HEADS, HEAD_SIZE
    )
    dkey_own, value_local_grad = (
        lax.psum_scatter(key_grad_every, "ctx", scatter_dimension=0, tiled=True),
        lax.psum_scatter(value_grad_every, "ctx", scatter_dimension=0, tiled=True),
    )
    dquery = (
        (dquery_heads * score_scale)
        .transpose(0, 3, 1, 2, 4)
        .reshape(token_per_device, QUERY_HEADS, HEAD_SIZE)
    )
    dquery_proj, query_gain_part = rms_back(
        query_proj, query_inverse, query_gain, rope_back(dquery, cosine, sine_tab)
    )
    key_projection_grad, key_gain_part = rms_back(
        key_proj, key_inverse, key_gain, rope_back(dkey_own * score_scale, cosine, sine_tab)
    )
    dquery_low = dquery_proj.reshape(token_per_device, QUERY_HEADS * HEAD_SIZE).astype(jnp.bfloat16)
    key_lower_grad = key_projection_grad.reshape(
        token_per_device, KEY_VALUE_HEADS * HEAD_SIZE
    ).astype(jnp.bfloat16)
    value_lower_grad = value_local_grad.reshape(
        token_per_device, KEY_VALUE_HEADS * HEAD_SIZE
    ).astype(jnp.bfloat16)
    query_grad = jnp.einsum("td,tc->dc", normed_low, dquery_low, preferred_element_type=jnp.float32)
    key_grad = jnp.einsum(
        "td,tc->dc", normed_low, key_lower_grad, preferred_element_type=jnp.float32
    )
    value_grad = jnp.einsum(
        "td,tc->dc", normed_low, value_lower_grad, preferred_element_type=jnp.float32
    )
    dnormed = jnp.einsum("tc,dc->td", dquery_low, query_back, preferred_element_type=jnp.float32)
    dnormed = dnormed + jnp.einsum(
        "tc,dc->td", key_lower_grad, key_back, preferred_element_type=jnp.float32
    )
    dnormed = dnormed + jnp.einsum(
        "tc,dc->td", value_lower_grad, value_back, preferred_element_type=jnp.float32
    )
    dinput_norm, attention_gain_part = rms_back(inputs, inverse_attn, attention_gain, dnormed)
    d_tokens = (dmixed_attn + dinput_norm).astype(jnp.bfloat16)
    gain_sums = lax.psum(
        (attention_gain_part, ffn_gain_part, query_gain_part, key_gain_part), ("ctx", "fsdp")
    )
    layer_sums = (
        lax.psum_scatter(query_grad, ("ctx", "fsdp"), scatter_dimension=0, tiled=True),
        lax.psum_scatter(key_grad, ("ctx", "fsdp"), scatter_dimension=0, tiled=True),
        lax.psum_scatter(value_grad, ("ctx", "fsdp"), scatter_dimension=0, tiled=True),
        lax.psum_scatter(output_grad, ("ctx", "fsdp"), scatter_dimension=0, tiled=True),
        lax.psum_scatter(router_grad, ("ctx", "fsdp"), scatter_dimension=0, tiled=True),
    )
    return (
        mixed,
        d_tokens,
        gain_sums[0],
        gain_sums[1],
        gain_sums[2],
        gain_sums[3],
        layer_sums[0],
        layer_sums[1],
        layer_sums[2],
        layer_sums[3],
        layer_sums[4],
        expert_sums[0],
        expert_sums[1],
        expert_sums[2],
    )


MEMBERS = 4


def shift(block, axis, step):
    count = lax.axis_size(axis)
    return lax.ppermute(block, axis, [(i, (i + step) % count) for i in range(count)])


def swap(block, axis):
    return lax.ppermute(block, axis, [(0, 1), (1, 0)])


def after(block, *earlier):
    return lax.optimization_barrier((block,) + earlier)[0]


class Steps:
    def __init__(self):
        self.mark = None

    def __call__(self, sends, work=None, given=(), join=()):
        blocks = tuple(send[0] for send in sends)
        mark = () if self.mark is None else (self.mark,)
        blocks, given, mark = lax.optimization_barrier((blocks, tuple(given), mark))
        moved = tuple(
            swap(block, send[1]) if len(send) == 2 else shift(block, send[1], send[2])
            for block, send in zip(blocks, sends)
        )
        done = () if work is None else work(*given)
        moved, done, join, mark = lax.optimization_barrier((moved, done, tuple(join), mark))
        self.mark = jax.tree.leaves((moved, done, join))[0]
        return moved, done, join


def pick(stack, index):
    return lax.dynamic_index_in_dim(stack, index, 0, keepdims=False)


def roped(raw, gain, cosine, sine):
    inverse = lax.rsqrt(jnp.mean(raw * raw, -1, keepdims=True) + EPS)
    scaled = raw * inverse * gain
    return scaled * cosine + pltpu.roll(scaled, HEAD_SIZE // 2, 1) * sine


def split_heads(ref, start, heads):
    size = ref.shape[2] // 2
    rows = ref[:, 0, start * size : (start + 1) * size, :]
    rows = rows.reshape(ref.shape[0] * size, ref.shape[3])
    return jnp.concatenate(
        [rows[:, i * HEAD_SIZE : (i + 1) * HEAD_SIZE] for i in range(heads)], 0
    )


def key_half(ref, k, start):
    size = ref.shape[3] // 2
    rows = ref[k, :, 0, start * size : (start + 1) * size, :]
    return rows.reshape(ref.shape[1] * size, HEAD_SIZE)


def twice(rows):
    return jnp.concatenate([rows, rows], 0)


ACROSS = (((1,), (1,)), ((), ()))
DOWN = (((0,), (0,)), ((), ()))


def score_blocks(z_here, queries, k_ref):
    nz = k_ref.shape[0]
    low_q, high_q = queries
    low_keys = jnp.concatenate([key_half(k_ref, k, 0) for k in range(nz)], 0)
    blocks = [(low_keys, high_q, None)]
    for k in range(1, nz):
        before = z_here >= k
        keys = jnp.where(before, key_half(k_ref, k, 0), key_half(k_ref, k, 1))
        blocks.append((keys, jnp.where(before, low_q, high_q), before))
    blocks.append((key_half(k_ref, 0, 0), low_q, None))
    blocks.append((key_half(k_ref, 0, 1), high_q, None))
    return blocks


def value_blocks(z_here, ref):
    nz = ref.shape[0]
    blocks = [jnp.concatenate([key_half(ref, k, 0) for k in range(nz)], 0)]
    for k in range(1, nz):
        blocks.append(jnp.where(z_here >= k, key_half(ref, k, 0), key_half(ref, k, 1)))
    return blocks + [key_half(ref, 0, 0), key_half(ref, 0, 1)]


def to_halves(parts, blocks):
    low_sum, high_sum = parts[-2], parts[0] + parts[-1]
    for part, (_, _, before) in zip(parts[1:-2], blocks[1:-2]):
        low_sum = low_sum + jnp.where(before, part, 0.0)
        high_sum = high_sum + jnp.where(before, 0.0, part)
    return low_sum, high_sum


def of_halves(low_row, high_row, blocks):
    rows = [high_row]
    rows += [jnp.where(before, low_row, high_row) for _, _, before in blocks[1:-2]]
    return rows + [low_row, high_row]


def weigh(blocks, mask_ref):
    exponent = math.log2(math.e) / math.sqrt(HEAD_SIZE)
    weights = []
    for keys, queries, _ in blocks:
        scores = lax.dot_general(keys, queries, ACROSS, preferred_element_type=jnp.float32)
        weights.append(jnp.exp2(scores * exponent))
    weights[-2] = weights[-2] * mask_ref[0]
    weights[-1] = weights[-1] * mask_ref[1]
    return weights


def attend_kernel(places_ref, q_ref, k_ref, v_ref, cos_ref, sin_ref, gain_ref, mask_ref, out_ref):
    count = q_ref.shape[3] // HEAD_SIZE
    size = q_ref.shape[2] // 2
    queries = []
    for half in range(2):
        raw = split_heads(q_ref, half, count)
        queries.append(
            roped(raw, gain_ref[...], twice(cos_ref[half]), twice(sin_ref[half])).astype(
                jnp.bfloat16
            )
        )
    z_here = places_ref[1]
    blocks = score_blocks(z_here, queries, k_ref)
    weights = weigh(blocks, mask_ref)
    totals = to_halves([jnp.sum(weight, 0, keepdims=True) for weight in weights], blocks)
    mixed = [
        lax.dot_general(
            values, weight.astype(jnp.bfloat16), DOWN, preferred_element_type=jnp.float32
        )
        for values, weight in zip(value_blocks(z_here, v_ref), weights)
    ]
    mixed = to_halves(mixed, blocks)
    for half in range(2):
        out = (mixed[half] / totals[half]).T.astype(jnp.bfloat16)
        rows = out.shape[0] // count
        for i in range(count):
            out_ref[:, 0, half * size : (half + 1) * size, i * HEAD_SIZE : (i + 1) * HEAD_SIZE] = (
                out[i * rows : (i + 1) * rows].reshape(-1, size, HEAD_SIZE)
            )


def attend_back_kernel(
    places_ref,
    q_ref,
    up_ref,
    k_ref,
    v_ref,
    cos_ref,
    sin_ref,
    gain_ref,
    mask_ref,
    dq_ref,
    dkv_ref,
    dgain_ref,
):
    nz = k_ref.shape[0]
    count = q_ref.shape[3] // HEAD_SIZE
    size = q_ref.shape[2] // 2
    low = jnp.bfloat16
    score_scale = 1.0 / math.sqrt(HEAD_SIZE)
    gain = gain_ref[...]
    z_here = places_ref[1]
    raws, queries, ups = [], [], []
    for half in range(2):
        raw = split_heads(q_ref, half, count)
        raws.append(raw)
        queries.append(roped(raw, gain, twice(cos_ref[half]), twice(sin_ref[half])).astype(low))
        ups.append(split_heads(up_ref, half, count))
    blocks = score_blocks(z_here, queries, k_ref)
    weights = weigh(blocks, mask_ref)
    totals = to_halves([jnp.sum(weight, 0, keepdims=True) for weight in weights], blocks)
    inverses = [1.0 / total for total in totals]
    block_ups = [ups[1]]
    block_ups += [jnp.where(before, ups[0], ups[1]) for _, _, before in blocks[1:-2]]
    block_ups += ups
    dprobs = [
        lax.dot_general(values, up, ACROSS, preferred_element_type=jnp.float32)
        for values, up in zip(value_blocks(z_here, v_ref), block_ups)
    ]
    probs = [
        weight * inverse
        for weight, inverse in zip(weights, of_halves(inverses[0], inverses[1], blocks))
    ]
    deltas = to_halves(
        [jnp.sum(p * d, 0, keepdims=True) for p, d in zip(probs, dprobs)], blocks
    )
    dscores = [
        (p * (d - delta)).astype(low)
        for p, d, delta in zip(probs, dprobs, of_halves(deltas[0], deltas[1], blocks))
    ]
    dvs = [
        jnp.dot(p.astype(low), up, preferred_element_type=jnp.float32)
        for p, up in zip(probs, block_ups)
    ]
    dks = [
        jnp.dot(d, block[1], preferred_element_type=jnp.float32) * score_scale
        for d, block in zip(dscores, blocks)
    ]
    dqs = [
        lax.dot_general(block[0], d, DOWN, preferred_element_type=jnp.float32)
        for d, block in zip(dscores, blocks)
    ]
    dqs = to_halves(dqs, blocks)
    each = dks[-1].shape[0]
    fresh = pl.program_id(1) == 0
    for k in range(nz):
        both = [
            jnp.concatenate([dk, dv], 1)
            for dk, dv in (
                (dks[0][k * each : (k + 1) * each], dvs[0][k * each : (k + 1) * each]),
                (dks[k], dvs[k]) if k > 0 else (dks[-2], dvs[-2]),
            )
        ]
        if k == 0:
            halves = (both[0] + both[1], jnp.concatenate([dks[-1], dvs[-1]], 1))
        else:
            before = z_here >= k
            halves = (
                both[0] + jnp.where(before, both[1], 0.0),
                jnp.where(before, 0.0, both[1]),
            )
        for half in range(2):
            part = slice(half * size, (half + 1) * size)
            earlier = jnp.where(fresh, 0.0, dkv_ref[k, :, 0, part, :])
            dkv_ref[k, :, 0, part, :] = earlier + halves[half].reshape(-1, size, 2 * HEAD_SIZE)

    gain_part = jnp.zeros((1, HEAD_SIZE), jnp.float32)
    for half in range(2):
        cosine, sine = twice(cos_ref[half]), twice(sin_ref[half])
        raw = raws[half]
        inverse = lax.rsqrt(jnp.mean(raw * raw, -1, keepdims=True) + EPS)
        unit = raw * inverse
        dq = dqs[half].T * score_scale
        turned = dq * cosine - pltpu.roll(dq, HEAD_SIZE // 2, 1) * sine
        gain_part = gain_part + jnp.sum(turned * unit, 0, keepdims=True)
        turned = turned * gain
        back = inverse * (turned - unit * jnp.mean(turned * unit, -1, keepdims=True))
        back = back.astype(low)
        rows = back.shape[0] // count
        for i in range(count):
            dq_ref[:, 0, half * size : (half + 1) * size, i * HEAD_SIZE : (i + 1) * HEAD_SIZE] = (
                back[i * rows : (i + 1) * rows].reshape(-1, size, HEAD_SIZE)
            )
    gain_part = jnp.concatenate([gain_part, jnp.zeros((7, HEAD_SIZE), jnp.float32)], 0)
    first = fresh & (pl.program_id(0) == 0)
    dgain_ref[...] = jnp.where(first, 0.0, dgain_ref[...]) + gain_part


def attention_specs(q, kv, mask):
    nz, members, sequences, paired, _ = kv.shape
    pair = q.shape[-1] // MEMBERS
    q_block = (members, 1, paired, pair)
    kv_block = (nz, members, 1, paired, HEAD_SIZE)
    own = pl.BlockSpec(q_block, lambda s, r, places: (0, s, 0, r ^ places[0]))
    relative = pl.BlockSpec(q_block, lambda s, r, places: (0, s, 0, r))
    key = pl.BlockSpec(kv_block, lambda s, r, places: (0, 0, s, 0, 0))
    value = pl.BlockSpec(kv_block, lambda s, r, places: (0, 0, s, 0, 1))
    both = pl.BlockSpec(
        (nz, members, 1, paired, 2 * HEAD_SIZE), lambda s, r, places: (0, 0, s, 0, 0)
    )
    fixed = lambda shape: pl.BlockSpec(shape, lambda s, r, places: (0,) * len(shape))
    table = fixed((2, members * paired // 2, HEAD_SIZE))
    tables = [table, table, fixed((1, HEAD_SIZE)), fixed(mask.shape)]
    return own, relative, key, value, both, fixed, tables


def attend(places, q, kv, cosine, sine, gain, mask):
    members, sequences, paired, width = q.shape
    own, relative, key, value, both, fixed, tables = attention_specs(q, kv, mask)
    elements = sequences * width // HEAD_SIZE * members * paired * kv.shape[0] * members * paired
    return pl.pallas_call(
        attend_kernel,
        grid_spec=pltpu.PrefetchScalarGridSpec(
            num_scalar_prefetch=1,
            grid=(sequences, MEMBERS),
            in_specs=[own, key, value] + tables,
            out_specs=relative,
        ),
        out_shape=jax.ShapeDtypeStruct(q.shape, jnp.bfloat16),
        compiler_params=pltpu.CompilerParams(vmem_limit_bytes=40 * 2**20),
        cost_estimate=pl.CostEstimate(
            flops=4 * elements * HEAD_SIZE, bytes_accessed=8 * 2**20, transcendentals=elements
        ),
    )(places, q, kv, kv, cosine, sine, gain, mask)


def attend_back(places, q, up, kv, cosine, sine, gain, mask):
    members, sequences, paired, width = q.shape
    own, relative, key, value, both, fixed, tables = attention_specs(q, kv, mask)
    elements = sequences * width // HEAD_SIZE * members * paired * kv.shape[0] * members * paired
    return pl.pallas_call(
        attend_back_kernel,
        grid_spec=pltpu.PrefetchScalarGridSpec(
            num_scalar_prefetch=1,
            grid=(sequences, MEMBERS),
            in_specs=[own, relative, key, value] + tables,
            out_specs=(own, both, fixed((8, HEAD_SIZE))),
        ),
        out_shape=(
            jax.ShapeDtypeStruct(q.shape, jnp.bfloat16),
            jax.ShapeDtypeStruct(kv.shape, jnp.float32),
            jax.ShapeDtypeStruct((8, HEAD_SIZE), jnp.float32),
        ),
        compiler_params=pltpu.CompilerParams(vmem_limit_bytes=40 * 2**20),
        cost_estimate=pl.CostEstimate(
            flops=10 * elements * HEAD_SIZE, bytes_accessed=16 * 2**20, transcendentals=elements
        ),
    )(places, q, up, kv, kv, cosine, sine, gain, mask)


def dot32(subscripts, left, right):
    return jnp.einsum(subscripts, left, right, preferred_element_type=jnp.float32)


def expert_kernel(*refs):
    scalars_ref, x_refs, c_refs = refs[0], refs[1:5], refs[5:9]
    rank_ref, chosen_ref, router_ref, gate_ref, up_ref, down_ref = refs[9:15]
    rows_ref, hidden_ref, dresults_ref, dgate_ref, dup_ref = refs[-9:-4]
    sent_refs, back_refs = refs[-4:-2], refs[-2:]
    low, wide = jnp.bfloat16, jnp.float32
    blocks = 2
    tokens, model = x_refs[0].shape
    opening = pl.program_id(0) == 0
    slots = rows_ref.shape[2]
    experts_all = router_ref.shape[0]
    across = (((1,), (1,)), ((), ()))
    down = (((0,), (0,)), ((), ()))
    own_expert = scalars_ref[0]
    places, picked, upstream, gates = [], [], [], []
    for block in range(blocks):
        rows = jnp.where(opening, x_refs[block][...], x_refs[2 + block][...])
        slot = lax.broadcasted_iota(jnp.int32, (slots, tokens), 0)
        place = jnp.where(slot == rank_ref[0, block], 1.0, 0.0)
        chosen = chosen_ref[0, block] > 0.5
        logits = lax.dot_general(router_ref[...], rows, across, preferred_element_type=wide)
        highest = jnp.max(jnp.where(chosen, logits, NEGATIVE_LIMIT), 0, keepdims=True)
        raised = jnp.where(chosen, jnp.exp(jnp.minimum(logits - highest, 0.0)), 0.0)
        expert = lax.broadcasted_iota(jnp.int32, (experts_all, tokens), 0)
        mine = jnp.sum(jnp.where(expert == own_expert, raised, 0.0), 0, keepdims=True)
        gate_row = mine / jnp.sum(raised, 0, keepdims=True)
        gates.append(jnp.sum(place * gate_row, 1, keepdims=True))
        place = place.astype(low)
        places.append(place)
        picked.append(jnp.dot(place, rows, preferred_element_type=wide).astype(low))
        cotangent = jnp.where(opening, c_refs[block][...], c_refs[2 + block][...])
        upstream.append(jnp.dot(place, cotangent, preferred_element_type=wide))
    rows = jnp.concatenate(picked, 0)
    upstream = jnp.concatenate(upstream, 0)
    gates = jnp.concatenate(gates, 0)
    gate_part = jnp.dot(rows, gate_ref[...], preferred_element_type=wide)
    up_part = jnp.dot(rows, up_ref[...], preferred_element_type=wide)
    sigmoid_gate = 1.0 / (1.0 + jnp.exp(-gate_part))
    silu_gate = gate_part * sigmoid_gate
    hidden = (silu_gate * up_part).astype(low)
    results = jnp.dot(hidden, down_ref[...], preferred_element_type=wide).astype(low).astype(wide)
    dgates = jnp.sum(upstream * results, 1, keepdims=True)
    scaled = (gates * results).astype(low)
    dresults = (gates * upstream).astype(low)
    dhidden = lax.dot_general(dresults, down_ref[...], across, preferred_element_type=wide)
    dsilu_gate = sigmoid_gate * (1.0 + gate_part * (1.0 - sigmoid_gate))
    dgate_low = (dhidden * up_part * dsilu_gate).astype(low)
    dup_low = (dhidden * silu_gate).astype(low)
    drows = lax.dot_general(dgate_low, gate_ref[...], across, preferred_element_type=wide)
    drows = drows + lax.dot_general(dup_low, up_ref[...], across, preferred_element_type=wide)
    drows = drows.astype(low)
    lane = lax.broadcasted_iota(jnp.int32, (blocks * slots, 128), 1)
    coarse = dgates.astype(low).astype(wide)
    extra = jnp.where(lane == own_expert, coarse, 0.0)
    extra = extra + jnp.where(lane == own_expert + experts_all, dgates - coarse, 0.0)
    extra = extra.astype(low)
    for block in range(blocks):
        part = slice(block * slots, (block + 1) * slots)
        sent_refs[block][0] = lax.dot_general(
            places[block], scaled[part], down, preferred_element_type=wide
        ).astype(low)
        back_refs[block][0, :, :model] = lax.dot_general(
            places[block], drows[part], down, preferred_element_type=wide
        ).astype(low)
        back_refs[block][0, :, model:] = lax.dot_general(
            places[block], extra[part], down, preferred_element_type=wide
        ).astype(low)
        rows_ref[0, block] = rows[part]
        hidden_ref[0, block] = hidden[part]
        dresults_ref[0, block] = dresults[part]
        dgate_ref[0, block] = dgate_low[part]
        dup_ref[0, block] = dup_low[part]


def experts(scalars, x_blocks, c_blocks, ranks, chosen, router, gate, up, down, slots, earlier):
    tokens, model = x_blocks[0].shape
    nz, members = ranks.shape[:2]
    hidden = gate.shape[1]
    low = jnp.bfloat16
    pair = members // 2
    experts_all = router.shape[0]
    whole = lambda array: pl.BlockSpec(
        array.shape, lambda a, s: (0, 0), pipeline_mode=pl.Buffered(1)
    )
    turn = lambda *tail: pl.BlockSpec((1, pair) + tail, lambda a, s: (s[1], a, 0, 0))
    in_specs = [
        *[whole(block) for block in x_blocks],
        *[whole(block) for block in c_blocks],
        turn(1, tokens),
        turn(experts_all, tokens),
        whole(router),
        whole(gate),
        whole(up),
        whole(down),
    ]
    shapes = [(slots, model), (slots, hidden), (slots, model)]
    shapes += [(slots, hidden), (slots, hidden)]
    out_shape = [jax.ShapeDtypeStruct((nz, members) + shape, low) for shape in shapes]
    out_specs = [turn(*shape) for shape in shapes]
    wide_model = model + 128
    for columns in (model, wide_model):
        out_shape += [jax.ShapeDtypeStruct((2, tokens, columns), low)] * 2
        out_specs += [pl.BlockSpec((1, tokens, columns), lambda a, s: (a, 0, 0))] * 2
    aliases = {}
    if earlier:
        in_specs = in_specs + [pl.BlockSpec(memory_space=pl.ANY)] * len(earlier)
        aliases = {15 + i: i for i in range(len(earlier))}
    return pl.pallas_call(
        expert_kernel,
        grid_spec=pltpu.PrefetchScalarGridSpec(
            num_scalar_prefetch=1, grid=(2,), in_specs=in_specs, out_specs=out_specs
        ),
        out_shape=out_shape,
        input_output_aliases=aliases,
        compiler_params=pltpu.CompilerParams(vmem_limit_bytes=58 * 2**20),
        cost_estimate=pl.CostEstimate(
            flops=12 * members * slots * model * hidden,
            bytes_accessed=40 * 2**20,
            transcendentals=2 * members * slots * hidden,
        ),
    )(scalars, *x_blocks, *c_blocks, ranks, chosen, router, gate, up, down, *earlier)


def dot32(subscripts, left, right):
    return jnp.einsum(subscripts, left, right, preferred_element_type=jnp.float32)


def member_layer(
    tokens,
    cotangent,
    expert_ids,
    attention_gain,
    ffn_gain,
    query_gain,
    key_gain,
    w_query,
    key_weight,
    value_weight,
    w_output,
    w_router,
    w_gate,
    w_up,
    w_down,
):
    low, wide = jnp.bfloat16, jnp.float32
    nz = lax.axis_size("z")
    zi, yi, ci, xi = (lax.axis_index(axis) for axis in ("z", "y", "c", "x"))
    member = 2 * yi + ci
    context_count = nz * MEMBERS
    rows, model = tokens.shape
    paired = rows // LOCAL_SEQUENCES
    block_len = paired // 2
    groups = QUERY_HEADS // KEY_VALUE_HEADS
    experts_all = w_router.shape[1]
    around = lambda k: lax.rem(zi + (k % nz), jnp.int32(nz))
    from_z = [around(-k) for k in range(nz)]
    crossed = [member ^ r for r in range(MEMBERS)]
    token_members = member ^ jnp.array([0, 2, 1, 3], jnp.int32)

    def uncrossed(blocks):
        for bit, odd in ((1, ci), (2, yi)):
            blocks = [jnp.where(odd == 0, blocks[r], blocks[r ^ bit]) for r in range(MEMBERS)]
        return jnp.stack(blocks)

    own_expert = zi * MEMBERS + member
    step = Steps()

    piece = w_query.shape[0]
    head_rows = w_output.shape[0]
    query_width = groups * HEAD_SIZE
    third = w_down.shape[1] // 3

    def make_tables(zi, token_members):
        own_pos = jax.vmap(lambda device: shard_positions(device, context_count, block_len))(
            zi * MEMBERS + token_members
        )
        cosine, sine_tab = rotary(own_pos.reshape(-1), HEAD_SIZE)
        row_cosine = cosine.reshape(MEMBERS, 1, paired, HEAD_SIZE)
        row_sine = sine_tab.reshape(MEMBERS, 1, paired, HEAD_SIZE)

        def halves(table):
            table = table.reshape(MEMBERS, 2, block_len, HEAD_SIZE).transpose(1, 0, 2, 3)
            return table.reshape(2, MEMBERS * block_len, HEAD_SIZE)

        half = HEAD_SIZE // 2
        signs = jnp.where(jnp.arange(HEAD_SIZE) < half, -1.0, 1.0)
        kernel_cosine, kernel_sine = halves(row_cosine), halves(row_sine * signs)
        half_pos = own_pos.reshape(MEMBERS, 2, block_len).transpose(1, 0, 2).reshape(2, -1)
        mask = (half_pos[:, :, None] <= half_pos[:, None, :]).astype(wide)
        mask = jnp.concatenate([mask, mask], 2)
        return row_cosine, row_sine, kernel_cosine, kernel_sine, mask

    def make_slots(packed):
        width_small = piece * experts_all
        flat = packed.reshape(nz * 8, -1)
        device = jnp.arange(nz * 8, dtype=jnp.int32)
        source = ((zi - device // 8) % nz) * 8 + ((device & 1) ^ xi) * 4
        source = source + (((device >> 1) & 1) ^ ci) * 2 + (((device >> 2) & 1) ^ yi)
        router = flat[:, :width_small][source].reshape(nz * 8, experts_all, piece)
        router = router.transpose(1, 0, 2).reshape(experts_all, model)
        ids_all = packed.reshape(nz, 2, 2, 2, -1)[:, 0, :, :, width_small:].transpose(0, 2, 1, 3)
        ids_all = ids_all.reshape(nz, MEMBERS, TOP, rows).astype(jnp.int32)
        named = jnp.any(ids_all == own_expert, 2)
        before = (
            jnp.arange(rows, dtype=jnp.int32)[:, None] <= jnp.arange(rows, dtype=jnp.int32)[None, :]
        )
        ranks = dot32("kjs,st->kjt", named.astype(low), before.astype(low)).astype(jnp.int32) - 1
        ranks = jnp.where(named, ranks, -1)[:, :, None, :]
        expert_column = jnp.arange(experts_all, dtype=jnp.int32)[:, None]
        chosen_all = jnp.any(ids_all[:, :, :, None, :] == expert_column, 2).astype(wide)
        return router, ranks, chosen_all

    cap_rows = rows * TOP * 5 // (4 * experts_all)
    slots = -(-cap_rows // 16) * 16

    def prepare(w_query, key_weight, value_weight, w_router, expert_ids):
        columns = jnp.concatenate(
            [w.reshape(piece, KEY_VALUE_HEADS, -1) for w in (w_query, key_weight, value_weight)],
            -1,
        ).transpose(1, 0, 2)
        packed = jnp.concatenate([w_router.T.reshape(-1), expert_ids.T.astype(low).reshape(-1)])
        parts = [pick(columns, crossed[r]) for r in range(MEMBERS)]
        return parts[0], parts[1], jnp.stack(parts[2:]), packed.reshape(-1, 128)

    (plane1,), (part0, part1, parts_far, packed), _ = step(
        [(w_output, "z", 1)],
        prepare,
        (w_query, key_weight, value_weight, w_router, expert_ids),
    )
    width = part0.shape[-1]
    inputs = tokens.astype(wide)

    def first_members(part0, part1, parts_far, tokens):
        far = swap(parts_far, "y")
        near = swap(jnp.stack([part1, far[1]]), "c")
        blocks = [part0, near[0], far[0], near[1]]
        return uncrossed(blocks), rms_apply(tokens.astype(wide), attention_gain)

    (plane3, *small), (ordered, (normed_attn, inverse_attn)), _ = step(
        [(w_output, "z", 3)] + [(packed, "z", k) for k in range(1, nz)],
        first_members,
        (part0, part1, parts_far, tokens),
    )
    packed = jnp.stack([packed] + small)
    normed_low = normed_attn.astype(low)
    held = [ordered]
    over_x = []
    (moved, cross, other, near, packed_far), _, _ = step(
        [
            (ordered, "z", 1),
            (ordered, "x"),
            (normed_low, "y"),
            (normed_low, "c"),
            (packed, "y"),
        ]
    )
    held.append(moved)
    over_x.append(cross)
    packed = jnp.stack([packed, packed_far], 1)
    (moved, cross, other_near, packed_near, down1), tables, _ = step(
        [
            (ordered, "z", 2),
            (held[1], "x"),
            (other, "c"),
            (packed, "c"),
            (w_down[0, third : 2 * third], "x"),
        ],
        make_tables,
        (zi, token_members),
    )
    row_cosine, row_sine, kernel_cosine, kernel_sine, mask = tables
    held.append(moved)
    over_x.append(cross)
    normed_all = jnp.concatenate([normed_low, other, near, other_near])
    packed = jnp.stack([packed, packed_near], 1)
    (moved, cross, c_near0, packed_cross), _, _ = step(
        [(ordered, "z", 3), (held[2], "x"), (cotangent, "c"), (packed, "x")]
    )
    packed = jnp.stack([packed, packed_cross], 1)
    held.append(moved)
    over_x.append(cross)
    cut = rows // 2
    gate_cut = w_gate.shape[1] * 5 // 16
    gate_next = w_gate.shape[1] * 9 // 16

    def cut_pieces(own, one, three, gate, down, cotangent):
        gates = (gate[:gate_cut], gate[gate_cut:gate_next], gate[gate_next:])
        halves = (cotangent[:cut], cotangent[cut:])
        return jnp.stack([own, one, one, three]), gates, down[2 * third :], halves

    (cross, plane2, c_far0, down0), (planes, gate_pieces, down_piece, c_halves), _ = step(
        [(held[3], "x"), (w_output, "z", 2), (cotangent, "y"), (w_down[0, :third], "x")],
        cut_pieces,
        (w_output, plane1, plane3, w_gate[0], w_down[0], cotangent),
    )
    over_x.append(cross)

    def assemble(start, stop):
        full = jnp.zeros((nz, MEMBERS, 2, piece, stop - start), low)
        for k in range(nz):
            full = lax.dynamic_update_slice(
                full, held[k][None, :, None, :, start:stop], (from_z[k], 0, xi, 0, 0)
            )
            full = lax.dynamic_update_slice(
                full, over_x[k][None, :, None, :, start:stop], (from_z[k], 0, 1 - xi, 0, 0)
            )
        return full.reshape(model, stop - start)

    query_weight = assemble(0, query_width)
    key_value_weight = assemble(query_width, width)

    def project_keys(normed_all, key_value_weight):
        raw = jnp.dot(normed_all, key_value_weight, preferred_element_type=wide)
        raw = raw.reshape(MEMBERS, LOCAL_SEQUENCES, paired, 2 * HEAD_SIZE)
        key_proj = raw[..., :HEAD_SIZE]
        key_normed, key_inverse = rms_apply(key_proj, key_gain)
        key_low = rope_apply(key_normed, row_cosine, row_sine).astype(low)
        value_low = raw[..., HEAD_SIZE:].astype(low)
        return key_proj, key_inverse, jnp.concatenate([key_low, value_low], -1)

    planes = lax.dynamic_update_index_in_dim(planes, plane2, 2, 0)
    wanted = [pick(planes, lax.rem(zi + nz - crossed[r], jnp.int32(nz))) for r in range(MEMBERS)]
    moved, (key_proj, key_inverse, key_value), _ = step(
        [
            (jnp.stack(wanted[2:]), "y"),
            (cotangent, "z", 1),
            (down_piece, "x"),
            (gate_pieces[0], "x"),
            (c_far0, "c"),
        ],
        project_keys,
        (normed_all, key_value_weight),
    )
    far, c1, down2, gate0, c_far_near0 = moved
    mine = jnp.stack([wanted[0], far[0]])

    def project_queries(normed_all, query_weight, pair):
        near = swap(pair, "c")
        return (
            near,
            swap(near[0], "x"),
            jnp.dot(normed_all, query_weight, preferred_element_type=wide),
        )

    moved, (near, cross_first, queries), _ = step(
        [(key_value, "z", k) for k in range(1, nz)] + [(mine, "x")],
        project_queries,
        (normed_all, query_weight, jnp.stack([wanted[1], far[1]])),
    )
    key_value = jnp.stack((key_value,) + moved[: nz - 1])
    cross_mine = moved[nz - 1]
    queries = queries.reshape(MEMBERS, LOCAL_SEQUENCES, paired, query_width)

    places = jnp.stack([member, zi]).astype(jnp.int32)
    gain_row = query_gain[None]
    (cross_last, c2_low, c_far1, gate1), attended, _ = step(
        [
            (near[1], "x"),
            (c_halves[0], "z", 2),
            (c1, "y"),
            (gate_pieces[1], "x"),
        ],
        attend,
        (places, queries, key_value, kernel_cosine, kernel_sine, gain_row, mask),
    )
    attended = attended.reshape(MEMBERS * rows, query_width)
    own_heads = jnp.stack([mine[0], near[0], mine[1], near[1]])
    other_heads = jnp.stack([cross_mine[0], cross_first, cross_mine[1], cross_last])
    output_weight = jnp.where(
        xi == 0, jnp.stack([own_heads, other_heads], 1), jnp.stack([other_heads, own_heads], 1)
    ).reshape(query_width, model)

    mixed_part = jnp.dot(attended, output_weight, preferred_element_type=wide)
    mixed_part = mixed_part.reshape(2, 2, rows, model)

    def summed_members(own, send):
        near = swap(send, "c")
        far = swap((own[1] + near[1].astype(wide)).astype(low), "y")
        return own[0] + near[0].astype(wide) + far.astype(wide)

    (gate2, c2_high, c_near1), mixed_sum, _ = step(
        [(gate_pieces[2], "x"), (c_halves[1], "z", 2), (c1, "c")],
        summed_members,
        (mixed_part[0], mixed_part[1].astype(low)),
    )
    c2 = jnp.concatenate([c2_low, c2_high])
    mixed_attn = inputs + mixed_sum
    normed_ffn, inverse_ffn = rms_apply(mixed_attn, ffn_gain)
    ffn_low = normed_ffn.astype(low)

    def whole(own, others):
        full = jnp.zeros((2,) + own.shape, low)
        full = lax.dynamic_update_slice(full, own[None], (xi, 0, 0))
        start = 0
        for other in others:
            full = lax.dynamic_update_slice(full, other[None], (1 - xi, start, 0))
            start += other.shape[0]
        return full.reshape(2 * own.shape[0], own.shape[1])

    def run_experts(k, x_blocks, c_blocks, kept, weights):
        scalars = jnp.stack([own_expert, jnp.int32(k)]).astype(jnp.int32)
        out = experts(
            scalars, x_blocks, c_blocks, ranks, chosen_all, router, *weights, slots, kept
        )
        return tuple(out[:-4]), out[-4:-2], out[-2:]

    def added(pair, back, a):
        return pair[0][a].astype(wide) + back[a].astype(wide)

    def both_rows(block):
        far = swap(block, "y")
        return far, swap(far, "c")

    moved, ((gate_all, down_all), (router, ranks, chosen_all)), _ = step(
        [
            (ffn_low, "z", 2),
            (w_up[0], "x"),
            (c2, "y"),
            (ffn_low, "y"),
            (c2, "c"),
        ],
        lambda owns, others, packed: (
            [whole(own, other) for own, other in zip(owns, others)],
            make_slots(packed),
        ),
        ([w_gate[0], w_down[0]], [[gate0, gate1, gate2], [down0, down1, down2]], packed),
    )
    x2, up_other, c_far2, y0, c_near2 = moved

    logits = dot32("td,ed->te", ffn_low, router)
    chosen = jnp.any(
        expert_ids[:, :, None] == jnp.arange(experts_all, dtype=jnp.int32)[None, None, :], 1
    )
    highest = jnp.max(jnp.where(chosen, logits, NEGATIVE_LIMIT), 1, keepdims=True)
    raised = jnp.where(chosen, jnp.exp(jnp.minimum(logits - highest, 0.0)), 0.0)
    gates = raised / jnp.sum(raised, 1, keepdims=True)

    (x1, c3_low, y2, n2, c_far_near2), up_all, _ = step(
        [
            (ffn_low, "z", 1),
            (c_halves[0], "z", 3),
            (x2, "y"),
            (x2, "c"),
            (c_far2, "c"),
        ],
        lambda own, other: whole(own, [other]),
        (w_up[0], up_other),
    )
    weights = [gate_all, up_all, down_all]
    (ny2, n0, ny0, c_far_near1), _, _ = step(
        [(y2, "c"), (ffn_low, "c"), (y0, "c"), (c_far1, "c")]
    )
    (x3, c3_high, y1, c_far3_low, n1), (kept, mixed2, rows2), _ = step(
        [
            (ffn_low, "z", 3),
            (c_halves[1], "z", 3),
            (x1, "y"),
            (c3_low, "y"),
            (x1, "c"),
        ],
        functools.partial(run_experts, 2),
        ([x2, n2, y2, ny2], [c2, c_near2, c_far2, c_far_near2], (), weights),
    )
    (ny1, n3), c3, _ = step(
        [(y1, "c"), (x3, "c")], lambda *halves: jnp.concatenate(halves), (c3_low, c3_high)
    )
    (y3, c_far3_high, c_near3, back2, mixed_back2), (kept, mixed1, rows1), _ = step(
        [(x3, "y"), (c3_high, "y"), (c3, "c"), (rows2[1], "c"), (mixed2[1], "c")],
        functools.partial(run_experts, 1),
        ([x1, n1, y1, ny1], [c1, c_near1, c_far1, c_far_near1], kept, weights),
    )
    c_far3 = jnp.concatenate([c_far3_low, c_far3_high])
    (ny3, c_far_near3), row_send2, _ = step(
        [(y3, "c"), (c_far3, "c")],
        lambda pair, back: added(pair, back, 1).astype(low),
        (rows2, back2),
    )
    (far2, mixed_far2, back1, mixed_back1), (kept, mixed3, rows3), _ = step(
        [
            (row_send2, "y"),
            (added(mixed2, mixed_back2, 1).astype(low), "y"),
            (rows1[1], "c"),
            (mixed1[1], "c"),
        ],
        functools.partial(run_experts, 3),
        ([x3, n3, y3, ny3], [c3, c_near3, c_far3, c_far_near3], kept, weights),
    )
    total2 = (added(rows2, back2, 0) + far2.astype(wide)).astype(low)
    (z2, far1, mixed_far1, back3, mixed_back3), (kept, mixed0, rows0), _ = step(
        [
            (total2, "z", -2),
            (added(rows1, back1, 1).astype(low), "y"),
            (added(mixed1, mixed_back1, 1).astype(low), "y"),
            (rows3[1], "c"),
            (mixed3[1], "c"),
        ],
        functools.partial(run_experts, 0),
        (
            [ffn_low, n0, y0, ny0],
            [cotangent, c_near0, c_far0, c_far_near0],
            kept,
            weights,
        ),
    )
    expert_rows, hidden_low, dresults, dgate_low, dup_low = (
        block.reshape(context_count * slots, -1) for block in kept
    )

    def halved(grad, sixteenths):
        size = grad.shape[0] // 2
        cut = size * sixteenths // 16
        own = lax.dynamic_slice_in_dim(grad, xi * size, size, 0)
        first = lax.dynamic_slice_in_dim(grad, (1 - xi) * size, cut, 0)
        rest = lax.dynamic_slice_in_dim(grad, (1 - xi) * size + cut, size - cut, 0)
        return own, first.astype(low), rest.astype(low)

    def joined(own, moved):
        return (own + jnp.concatenate(moved, 0).astype(wide))[None]

    total1 = (added(rows1, back1, 0) + far1.astype(wide)).astype(low)

    def total(pair, back, far):
        return (added(pair, back, 0) + far.astype(wide)).astype(low)

    (z1, far3, back0, mixed_back0), ((down_grad, down_first, down_rest), mixed_send1), _ = step(
        [
            (total1, "z", -1),
            (added(rows3, back3, 1).astype(low), "y"),
            (rows0[1], "c"),
            (mixed0[1], "c"),
        ],
        lambda rows, grad, *given: (halved(dot32("sf,sd->fd", rows, grad), 10), total(*given)),
        (hidden_low, dresults, mixed1, mixed_back1, mixed_far1),
    )
    total3 = (added(rows3, back3, 0) + far3.astype(wide)).astype(low)
    (z3, far0, down0), ((gate_grad, gate_first, gate_rest), mixed_send2), _ = step(
        [
            (total3, "z", -3),
            (added(rows0, back0, 1).astype(low), "y"),
            (down_first, "x"),
        ],
        lambda rows, grad, *given: (halved(dot32("sd,sf->df", rows, grad), 10), total(*given)),
        (expert_rows, dgate_low, mixed2, mixed_back2, mixed_far2),
    )
    returned = added(rows0, back0, 0) + far0.astype(wide) + z1.astype(wide)
    returned = returned + z2.astype(wide) + z3.astype(wide)
    dffn_routed = returned[:, :model]
    dgates = returned[:, model : model + experts_all]
    dgates = dgates + returned[:, model + experts_all : model + 2 * experts_all]
    dlogits = gates * (dgates - jnp.sum(gates * dgates, 1, keepdims=True))
    dlogits_low = dlogits.astype(low)
    router_rows = dot32("td,te->de", ffn_low, dlogits_low).astype(low)
    router_rows = router_rows.reshape(nz, MEMBERS, 2, -1, 2 * HEAD_SIZE)
    extra_rows = router_rows.shape[3]
    router_rows = jnp.pad(router_rows, ((0, 0),) * 3 + ((0, -extra_rows % 16), (0, 0)))

    upstream = cotangent.astype(wide)
    dffn_rows = dffn_routed + dot32("te,ed->td", dlogits_low, router)
    dmixed_norm, ffn_gain_part = rms_back(mixed_attn, inverse_ffn, ffn_gain, dffn_rows)
    dmixed_attn = upstream + dmixed_norm
    dattn_low = dmixed_attn.astype(low)
    moved, (up_grad, up_first, up_rest), _ = step(
        [
            (dattn_low, "y"),
            (dattn_low, "c"),
            (gate_first, "x"),
            (mixed_send1, "z", -1),
        ],
        lambda rows, grad: halved(dot32("sd,sf->df", rows, grad), 11),
        (expert_rows, dup_low),
    )
    other, near, gate0, mixed_z1 = moved
    (other_near,), (dattn_all,), _ = step(
        [(other, "c")],
        lambda *blocks: (jnp.concatenate(blocks),),
        (dattn_low, other, near, dattn_low),
    )
    dattn_all = lax.dynamic_update_slice_in_dim(dattn_all, other_near, 3 * rows, 0)

    output_part = dot32("tc,td->cd", attended, dattn_all).astype(low)
    output_part = output_part.reshape(MEMBERS, 2, head_rows, model)
    output_own = lax.dynamic_index_in_dim(output_part, xi, 1, keepdims=False)
    output_other = lax.dynamic_index_in_dim(output_part, 1 - xi, 1, keepdims=False)

    def planes_of(part):
        own = lax.dynamic_index_in_dim(part, xi, 2, keepdims=False)
        other = lax.dynamic_index_in_dim(part, 1 - xi, 2, keepdims=False)
        return [(pick(own, around(k)), pick(other, around(k))) for k in range(nz)]

    def attention_back(dattn_all, output_weight, *given):
        attended_grad = dot32("td,cd->tc", dattn_all, output_weight).astype(low)
        attended_grad = attended_grad.reshape(MEMBERS, LOCAL_SEQUENCES, paired, query_width)
        return attend_back(*given[:2], attended_grad, *given[2:])

    moved, attention_grads, _ = step(
        [
            (output_other[1:], "x"),
            (mixed_send2, "z", -2),
            (added(mixed3, mixed_back3, 1).astype(low), "y"),
            (added(mixed0, mixed_back0, 1).astype(low), "y"),
        ],
        attention_back,
        (
            dattn_all,
            output_weight,
            places,
            queries,
            key_value,
            kernel_cosine,
            kernel_sine,
            gain_row,
            mask,
        ),
    )
    cross_rest, mixed_z2, mixed_far3, mixed_far0 = moved
    dquery_low, dkey_value, query_gain_part = attention_grads
    query_gain_part = query_gain_part[0]
    dquery_low = dquery_low.reshape(MEMBERS * rows, query_width)
    query_part = dot32("td,tc->dc", normed_all, dquery_low).astype(low)
    query_planes = planes_of(query_part.reshape(nz, MEMBERS, 2, piece, query_width))
    output_far = (output_own[2:].astype(wide) + cross_rest[1:].astype(wide)).astype(low)

    def query_back(grad, weight, third):
        return dot32("tc,dc->td", grad, weight), total(*third)

    query_plane = query_planes[2][1].reshape(-1, query_width)
    first_head = [output_other[0][:, a : a + query_width] for a in range(0, model, query_width)]
    moved, (dnormed, mixed_send3), _ = step(
        [(dkey_value[k].astype(low), "z", -k) for k in range(1, nz)]
        + [(jnp.concatenate([query_plane] + first_head), "x"), (output_far, "y")],
        query_back,
        (dquery_low, query_weight, [mixed3, mixed_back3, mixed_far3]),
    )
    *key_moves, cross, output_far = moved
    plane_rows = query_plane.shape[0]
    cross_first = [
        cross[a : a + head_rows] for a in range(plane_rows, cross.shape[0], head_rows)
    ]
    cross_first = jnp.concatenate(cross_first, 1)
    cross = cross[:plane_rows].reshape(query_planes[2][0].shape)
    query_sum2 = (query_planes[2][0].astype(wide) + cross.astype(wide)).astype(low)
    near_first = (output_own[0].astype(wide) + cross_first.astype(wide)).astype(low)
    near_last = (output_own[1].astype(wide) + cross_rest[0].astype(wide)).astype(low)

    def project_keys_back(dnormed, dkey_value_own, moved, key_value_weight):
        dkey_value_own = dkey_value_own + sum(block.astype(wide) for block in moved)
        dkey, dvalue = dkey_value_own[..., :HEAD_SIZE], dkey_value_own[..., HEAD_SIZE:]
        dkey_proj, key_gain_part = rms_back(
            key_proj, key_inverse, key_gain, rope_back(dkey, row_cosine, row_sine)
        )
        dkey_value_low = jnp.concatenate([dkey_proj, dvalue], -1).astype(low)
        dkey_value_low = dkey_value_low.reshape(MEMBERS * rows, 2 * HEAD_SIZE)
        dnormed = dnormed + dot32("tc,dc->td", dkey_value_low, key_value_weight)
        dnormed = dnormed.reshape(2, 2, rows, model)
        key_part = dot32("td,tc->dc", normed_all, dkey_value_low).astype(low)
        key_part = key_part.reshape(nz, MEMBERS, 2, piece, 2 * HEAD_SIZE)
        key_part = jnp.concatenate([key_part, router_rows], 3)
        key_own = lax.dynamic_index_in_dim(key_part, xi, 2, keepdims=False)
        key_other = lax.dynamic_index_in_dim(key_part, 1 - xi, 2, keepdims=False)
        return dnormed[0], dnormed[1].astype(low), key_own, key_other, key_gain_part

    moved, (dnormed_own, dnormed_send, key_own, key_other, key_gain_part), _ = step(
        [
            (query_sum2, "z", 2),
            (jnp.stack([query_planes[1][1], query_planes[3][1]]), "x"),
            (jnp.stack([near_last, output_far[1]]), "c"),
        ],
        project_keys_back,
        (dnormed, dkey_value[0], key_moves, key_value_weight),
    )
    query_z2, cross, output_back = moved
    query_sum1 = (query_planes[1][0].astype(wide) + cross[0].astype(wide)).astype(low)
    query_sum3 = (query_planes[3][0].astype(wide) + cross[1].astype(wide)).astype(low)

    def order_output(blocks):
        blocks = uncrossed(blocks)
        return [pick(blocks, around(k)) for k in range(nz)]

    moved, output_sends, _ = step(
        [
            (query_sum1, "z", 1),
            (query_sum3, "z", 3),
            (query_planes[0][1], "x"),
            (key_other, "x"),
            (dnormed_send, "c"),
        ],
        order_output,
        ([near_first, output_back[0], output_far[0], output_back[1]],),
    )
    query_z1, query_z3, cross, key_cross, near = moved
    dnormed_far = (dnormed_own[1] + near[1].astype(wide)).astype(low)
    key_sum = (key_own.astype(wide) + key_cross.astype(wide)).astype(low)

    def total_queries(own, cross, *moved):
        total = own.astype(wide) + cross.astype(wide) + sum(m.astype(wide) for m in moved)
        total = total.astype(low)
        parts = [pick(total, crossed[r]) for r in range(MEMBERS)]
        return parts[0], parts[1], jnp.stack(parts[2:])

    (output_z1, output_z3, other, gate1, down1), query_parts, _ = step(
        [
            (output_sends[1], "z", 1),
            (output_sends[3], "z", 3),
            (dnormed_far, "y"),
            (gate_rest, "x"),
            (down_rest, "x"),
        ],
        total_queries,
        (query_planes[0][0], cross, query_z1, query_z2, query_z3),
    )
    dnormed = dnormed_own[0] + near[0].astype(wide) + other.astype(wide)
    dinput_norm, attention_gain_part = rms_back(inputs, inverse_attn, attention_gain, dnormed)
    small = [attention_gain_part, ffn_gain_part, query_gain_part, key_gain_part]
    small = jnp.concatenate(small).reshape(-1, 128)
    (*key_moves, small_x, query_far), d_tokens, _ = step(
        [(pick(key_sum, around(k)), "z", k) for k in range(1, nz)]
        + [(small, "x"), (query_parts[2], "y")],
        lambda a, b: (a + b).astype(low),
        (dmixed_attn, dinput_norm),
    )
    small = small + small_x
    key_total = pick(key_sum, zi).astype(wide)
    key_total = (key_total + sum(m.astype(wide) for m in key_moves)).astype(low)
    key_parts = [pick(key_total, crossed[r]) for r in range(MEMBERS)]

    def member_columns(parts):
        return uncrossed(parts).astype(wide).transpose(1, 0, 2)

    (output_z2, up0, key_far, small_y, query_near), (down_grad, gate_grad), _ = step(
        [
            (output_sends[2], "z", 2),
            (up_first, "x"),
            (jnp.stack(key_parts[2:]), "y"),
            (small, "y"),
            (jnp.stack([query_parts[1], query_far[1]]), "c"),
        ],
        lambda down, downs, gate, gates: (joined(down, downs), joined(gate, gates)),
        (down_grad, [down0, down1], gate_grad, [gate0, gate1]),
    )
    small = small + small_y
    query_blocks = [query_parts[0], query_near[0], query_far[0], query_near[1]]
    (mixed_z3, up1, key_near, small_c), (query_grad, output_grad), _ = step(
        [
            (mixed_send3, "z", -3),
            (up_rest, "x"),
            (jnp.stack([key_parts[1], key_far[1]]), "c"),
            (small, "c"),
        ],
        lambda blocks, own, *parts: (
            member_columns(blocks).reshape(piece, -1),
            own.astype(wide) + sum(part.astype(wide) for part in parts),
        ),
        (query_blocks, output_sends[0], output_z1, output_z2, output_z3),
    )
    small = small + small_c
    key_blocks = [key_parts[0], key_near[0], key_far[0], key_near[1]]

    def finish(up, ups, key_blocks, base, pair, back, far, z1, z2, z3):
        router = sum(block[piece : piece + extra_rows].astype(wide) for block in key_blocks)
        mixed = base + added(pair, back, 0) + far.astype(wide) + z1.astype(wide)
        mixed = mixed + z2.astype(wide) + z3.astype(wide)
        return (
            joined(up, ups),
            member_columns([block[:piece] for block in key_blocks]),
            router.reshape(piece, experts_all),
            mixed.astype(low),
        )

    small_z, results, _ = step(
        [(small, "z", k) for k in range(1, nz)],
        finish,
        (
            up_grad,
            [up0, up1],
            key_blocks,
            mixed_attn,
            mixed0,
            mixed_back0,
            mixed_far0,
            mixed_z1,
            mixed_z2,
            mixed_z3,
        ),
    )
    up_grad, key_grads, router_grad, mixed = results
    gains = (small + sum(small_z)).reshape(-1)
    key_grad = key_grads[..., :HEAD_SIZE].reshape(piece, -1)
    value_grad = key_grads[..., HEAD_SIZE:].reshape(piece, -1)
    return (
        mixed,
        d_tokens,
        gains[:model],
        gains[model : 2 * model],
        gains[2 * model : 2 * model + HEAD_SIZE],
        gains[2 * model + HEAD_SIZE :],
        query_grad,
        key_grad,
        value_grad,
        output_grad,
        router_grad,
        gate_grad,
        up_grad,
        down_grad,
    )


def solution(mesh):
    contexts, pairs = mesh.shape["ctx"], mesh.shape["fsdp"]
    planes = contexts // MEMBERS
    if planes == KEY_VALUE_HEADS and pairs * MEMBERS * KEY_VALUE_HEADS == QUERY_HEADS:
        layer, every, split = member_layer, ("z", "y", "c", "x"), ("z", "y", "c")
        pair = "x"
        mesh = Mesh(mesh.devices.reshape(planes, 2, 2, pairs), every)
    else:
        layer, every, split, pair = routed_layer, ("ctx", "fsdp"), "ctx", "fsdp"
    by_row = P(every, None)
    by_expert = P(split, pair, None)
    return jax.shard_map(
        layer,
        mesh=mesh,
        in_specs=(by_row,) * 3 + (P(),) * 4 + (by_row,) * 5 + (by_expert,) * 3,
        out_specs=(by_row,) * 2 + (P(),) * 4 + (by_row,) * 5 + (by_expert,) * 3,
        check_vma=False,
    )
```

```python
import functools
import math

import jax
import jax.numpy as jnp
from jax import lax
from jax.experimental import pallas as pl
from jax.experimental.pallas import tpu as pltpu
from jax.sharding import Mesh
from jax.sharding import PartitionSpec as P

QUERY_HEADS = 32
KEY_VALUE_HEADS = 4
HEAD_SIZE = 128
TOP = 8
LOCAL_SEQUENCES = 3


EPS = 1e-06
THETA = 1000000.0
NEGATIVE_LIMIT = -1e30


def shard_positions(device, context_count, block_len):
    within = jnp.arange(2 * block_len, dtype=jnp.int32)
    lower_pos = device * block_len + within
    upper_pos = (2 * context_count - 1 - device) * block_len + within - block_len
    return jnp.where(within < block_len, lower_pos, upper_pos)


def group_positions(first_dev, query_group_size, context_count, block_len):
    devices = first_dev + jnp.arange(query_group_size, dtype=jnp.int32)
    return jax.vmap(lambda device: shard_positions(device, context_count, block_len))(
        devices
    ).reshape(-1)


def rotary(positions, head_width):
    half_width = head_width // 2
    frequency = jnp.exp(
        -math.log(THETA) * (2.0 * jnp.arange(half_width, dtype=jnp.float32)) / head_width
    )
    angles = positions.astype(jnp.float32)[:, None] * frequency[None, :]
    angles = jnp.concatenate([angles, angles], -1)
    return (jnp.cos(angles)[:, None, :], jnp.sin(angles)[:, None, :])


def rope_apply(value_rows_list, cosine, sine_tab):
    half_width = value_rows_list.shape[-1] // 2
    turned = jnp.concatenate(
        [-value_rows_list[..., half_width:], value_rows_list[..., :half_width]], -1
    )
    return value_rows_list * cosine + turned * sine_tab


def rope_back(upstream, cosine, sine_tab):
    half_width = upstream.shape[-1] // 2
    moved_part = upstream * sine_tab
    return upstream * cosine + jnp.concatenate(
        [moved_part[..., half_width:], -moved_part[..., :half_width]], -1
    )


def rms_apply(value_rows_list, gain_vec):
    inverse = lax.rsqrt(jnp.mean(value_rows_list * value_rows_list, -1, keepdims=True) + EPS)
    return (value_rows_list * inverse * gain_vec, inverse)


def rms_back(value_rows_list, inverse, gain_vec, upstream):
    normalized_input = value_rows_list * inverse
    gain_part = jnp.sum((upstream * normalized_input).reshape(-1, value_rows_list.shape[-1]), 0)
    scaled = upstream * gain_vec
    back_part = inverse * (
        scaled - normalized_input * jnp.mean(scaled * normalized_input, -1, keepdims=True)
    )
    return (back_part, gain_part)


def arrange(blocks):
    query_group_size, seq_count, paired_rows, heads_kv, head_dim = blocks.shape
    return blocks.transpose(1, 0, 2, 3, 4).reshape(
        seq_count, query_group_size * paired_rows, heads_kv, head_dim
    )


def unarrange(rows_all, query_group_size):
    seq_count, width_all, heads_kv, head_dim = rows_all.shape
    return rows_all.reshape(
        seq_count, query_group_size, width_all // query_group_size, heads_kv, head_dim
    ).transpose(1, 0, 2, 3, 4)


def attend_group(state_now, queries, key_row_matrix, value_rows, query_pos, key_pos, score_scale):
    run_max, run_sum, run_acc = state_now
    scores = (
        jnp.einsum("skgqd,swkd->skgqw", queries, key_row_matrix, preferred_element_type=jnp.float32)
        * score_scale
    )
    allowed = key_pos[None, :] <= query_pos[:, None]
    new_max = jnp.maximum(run_max, jnp.max(jnp.where(allowed, scores, NEGATIVE_LIMIT), -1))
    weights_now = jnp.where(allowed, jnp.exp(scores - new_max[..., None]), 0.0)
    factor = jnp.exp(run_max - new_max)
    new_sum = run_sum * factor + jnp.sum(weights_now, -1)
    update = jnp.einsum(
        "skgqw,swkd->skgqd",
        weights_now.astype(jnp.bfloat16),
        value_rows,
        preferred_element_type=jnp.float32,
    )
    return (new_max, new_sum, run_acc * factor[..., None] + update)


def routed_layer(
    tokens,
    cotangent,
    expert_ids,
    attention_gain,
    ffn_gain,
    query_gain,
    key_gain,
    w_query,
    key_weight,
    value_weight,
    w_output,
    w_router,
    w_gate,
    w_up,
    w_down,
):
    context_count = lax.axis_size("ctx")
    ctx_here = lax.axis_index("ctx")
    token_per_device = tokens.shape[0]
    block_len = token_per_device // (2 * LOCAL_SEQUENCES)
    paired_rows = 2 * block_len
    query_groups = QUERY_HEADS // KEY_VALUE_HEADS
    score_scale = 1.0 / math.sqrt(HEAD_SIZE)
    experts_all = w_router.shape[1]
    exp_dev = w_gate.shape[0]
    cap_rows = token_per_device * TOP * 5 // (4 * experts_all)
    routes = token_per_device * TOP
    inputs = tokens.astype(jnp.float32)
    normed_attn, inverse_attn = rms_apply(inputs, attention_gain)
    normed_low = normed_attn.astype(jnp.bfloat16)
    query_all, key_all, value_all, output_all, router_all = (
        lax.all_gather(w_query, ("ctx", "fsdp"), axis=0, tiled=True),
        lax.all_gather(key_weight, ("ctx", "fsdp"), axis=0, tiled=True),
        lax.all_gather(value_weight, ("ctx", "fsdp"), axis=0, tiled=True),
        lax.all_gather(w_output, ("ctx", "fsdp"), axis=0, tiled=True),
        lax.all_gather(w_router, ("ctx", "fsdp"), axis=0, tiled=True),
    )
    local_pos = shard_positions(ctx_here, context_count, block_len)
    row_pos = jnp.tile(local_pos, LOCAL_SEQUENCES)
    cosine, sine_tab = rotary(row_pos, HEAD_SIZE)
    query_proj = jnp.dot(normed_low, query_all, preferred_element_type=jnp.float32).reshape(
        token_per_device, QUERY_HEADS, HEAD_SIZE
    )
    key_proj = jnp.dot(normed_low, key_all, preferred_element_type=jnp.float32).reshape(
        token_per_device, KEY_VALUE_HEADS, HEAD_SIZE
    )
    value_proj = jnp.dot(normed_low, value_all, preferred_element_type=jnp.float32).reshape(
        token_per_device, KEY_VALUE_HEADS, HEAD_SIZE
    )
    query_normed, query_inverse = rms_apply(query_proj, query_gain)
    key_normed, key_inverse = rms_apply(key_proj, key_gain)
    query_lower = rope_apply(query_normed, cosine, sine_tab).astype(jnp.bfloat16)
    key_low = rope_apply(key_normed, cosine, sine_tab).astype(jnp.bfloat16)
    value_low = value_proj.astype(jnp.bfloat16)
    query_head_rows = query_lower.reshape(
        LOCAL_SEQUENCES, paired_rows, KEY_VALUE_HEADS, query_groups, HEAD_SIZE
    ).transpose(0, 2, 3, 1, 4)
    initial = (
        jnp.full(
            (LOCAL_SEQUENCES, KEY_VALUE_HEADS, query_groups, paired_rows),
            NEGATIVE_LIMIT,
            jnp.float32,
        ),
        jnp.zeros((LOCAL_SEQUENCES, KEY_VALUE_HEADS, query_groups, paired_rows), jnp.float32),
        jnp.zeros(
            (LOCAL_SEQUENCES, KEY_VALUE_HEADS, query_groups, paired_rows, HEAD_SIZE), jnp.float32
        ),
    )
    key_every, value_every = (
        lax.all_gather(key_low, "ctx", axis=0, tiled=True),
        lax.all_gather(value_low, "ctx", axis=0, tiled=True),
    )
    shard_total_count = key_every.shape[0] // token_per_device
    fold_query_group_size = 4
    key_block_list = key_every.reshape(
        shard_total_count // fold_query_group_size,
        fold_query_group_size,
        LOCAL_SEQUENCES,
        paired_rows,
        KEY_VALUE_HEADS,
        HEAD_SIZE,
    )
    value_block_list = value_every.reshape(
        shard_total_count // fold_query_group_size,
        fold_query_group_size,
        LOCAL_SEQUENCES,
        paired_rows,
        KEY_VALUE_HEADS,
        HEAD_SIZE,
    )
    first_devs = 0 // token_per_device + fold_query_group_size * jnp.arange(
        shard_total_count // fold_query_group_size, dtype=jnp.int32
    )

    def one_group(state_in, loop_item):
        key_group, value_group, first_dev = loop_item
        key_pos = group_positions(first_dev, fold_query_group_size, context_count, block_len)
        return (
            attend_group(
                state_in,
                query_head_rows,
                arrange(key_group),
                arrange(value_group),
                local_pos,
                key_pos,
                score_scale,
            ),
            None,
        )

    state_out, unused = lax.scan(one_group, initial, (key_block_list, value_block_list, first_devs))
    run_max, run_sum, run_acc = state_out
    log_sum = run_max + jnp.log(run_sum)
    attended = run_acc / run_sum[..., None]
    attended_low = (
        attended.transpose(0, 3, 1, 2, 4)
        .reshape(token_per_device, QUERY_HEADS * HEAD_SIZE)
        .astype(jnp.bfloat16)
    )
    mixed_attn = inputs + jnp.dot(attended_low, output_all, preferred_element_type=jnp.float32)
    normed_ffn, inverse_ffn = rms_apply(mixed_attn, ffn_gain)
    ffn_low = normed_ffn.astype(jnp.bfloat16)
    logits = jnp.dot(ffn_low, router_all, preferred_element_type=jnp.float32)
    chosen = (expert_ids[..., None] == jnp.arange(experts_all, dtype=jnp.int32)).astype(jnp.float32)
    picked = jnp.einsum("tje,te->tj", chosen, logits, precision=lax.Precision.HIGHEST)
    gate_probs = jax.nn.softmax(picked, -1)
    flat_ids = expert_ids.reshape(-1)
    route_marks = (flat_ids[:, None] == jnp.arange(experts_all, dtype=jnp.int32)).astype(jnp.int32)
    route_ranks = jnp.sum((jnp.cumsum(route_marks, 0) - 1) * route_marks, -1)
    slot_of_route = flat_ids * cap_rows + route_ranks
    route_of_slot = (
        jnp.full((experts_all * cap_rows,), routes, jnp.int32)
        .at[slot_of_route]
        .set(jnp.arange(routes, dtype=jnp.int32))
    )
    padded = jnp.concatenate([ffn_low, jnp.zeros((1, ffn_low.shape[1]), jnp.bfloat16)], 0)
    outgoing = padded[route_of_slot // TOP].reshape(experts_all, cap_rows, -1)
    arrived = lax.all_to_all(outgoing, "ctx", split_axis=0, concat_axis=0, tiled=True)

    def to_experts(buffer):
        return (
            buffer.reshape(context_count, exp_dev, cap_rows, -1)
            .transpose(1, 0, 2, 3)
            .reshape(exp_dev, context_count * cap_rows, -1)
        )

    def from_experts(buffer):
        return (
            buffer.reshape(exp_dev, context_count, cap_rows, -1)
            .transpose(1, 0, 2, 3)
            .reshape(context_count * exp_dev, cap_rows, -1)
        )

    expert_rows = to_experts(arrived)
    gate_all, up_all, down_all = (
        lax.all_gather(w_gate, "fsdp", axis=1, tiled=True),
        lax.all_gather(w_up, "fsdp", axis=1, tiled=True),
        lax.all_gather(w_down, "fsdp", axis=1, tiled=True),
    )
    gate_part = jnp.einsum(
        "esd,edf->esf", expert_rows, gate_all, preferred_element_type=jnp.float32
    )
    up_part = jnp.einsum("esd,edf->esf", expert_rows, up_all, preferred_element_type=jnp.float32)
    sigmoid_gate = jax.nn.sigmoid(gate_part)
    silu_gate = gate_part * sigmoid_gate
    hidden_low = (silu_gate * up_part).astype(jnp.bfloat16)
    results = jnp.einsum(
        "esf,efd->esd", hidden_low, down_all, preferred_element_type=jnp.float32
    ).astype(jnp.bfloat16)
    returned = lax.all_to_all(from_experts(results), "ctx", split_axis=0, concat_axis=0, tiled=True)
    route_out = returned.reshape(experts_all * cap_rows, -1)[slot_of_route].reshape(
        token_per_device, TOP, -1
    )
    mixed = (mixed_attn + jnp.sum(gate_probs[..., None] * route_out, 1)).astype(jnp.bfloat16)
    query_back, key_back, value_back, output_back, router_back = (
        lax.all_gather(w_query, ("ctx", "fsdp"), axis=0, tiled=True),
        lax.all_gather(key_weight, ("ctx", "fsdp"), axis=0, tiled=True),
        lax.all_gather(value_weight, ("ctx", "fsdp"), axis=0, tiled=True),
        lax.all_gather(w_output, ("ctx", "fsdp"), axis=0, tiled=True),
        lax.all_gather(w_router, ("ctx", "fsdp"), axis=0, tiled=True),
    )
    upstream = cotangent.astype(jnp.float32)
    dgates = jnp.sum(upstream[:, None, :] * route_out, -1)
    dpicked = gate_probs * (dgates - jnp.sum(gate_probs * dgates, -1, keepdims=True))
    dlogits_low = jnp.einsum("tj,tje->te", dpicked, chosen, precision=lax.Precision.HIGHEST).astype(
        jnp.bfloat16
    )
    router_grad = jnp.einsum("td,te->de", ffn_low, dlogits_low, preferred_element_type=jnp.float32)
    dresults = (
        (gate_probs[..., None] * upstream[:, None, :]).astype(jnp.bfloat16).reshape(routes, -1)
    )
    dresults = jnp.concatenate([dresults, jnp.zeros((1, dresults.shape[1]), jnp.bfloat16)], 0)
    dreturned = lax.all_to_all(
        dresults[route_of_slot].reshape(experts_all, cap_rows, -1),
        "ctx",
        split_axis=0,
        concat_axis=0,
        tiled=True,
    )
    dresult_rows = to_experts(dreturned)
    dhidden = jnp.einsum("esd,efd->esf", dresult_rows, down_all, preferred_element_type=jnp.float32)
    down_grad = jnp.einsum(
        "esf,esd->efd", hidden_low, dresult_rows, preferred_element_type=jnp.float32
    )
    dsilu_gate = sigmoid_gate * (1.0 + gate_part * (1.0 - sigmoid_gate))
    dgate_low = (dhidden * up_part * dsilu_gate).astype(jnp.bfloat16)
    dup_low = (dhidden * silu_gate).astype(jnp.bfloat16)
    gate_grad = jnp.einsum(
        "esd,esf->edf", expert_rows, dgate_low, preferred_element_type=jnp.float32
    )
    up_grad = jnp.einsum("esd,esf->edf", expert_rows, dup_low, preferred_element_type=jnp.float32)
    dexpert_rows = (
        jnp.einsum("esf,edf->esd", dgate_low, gate_all, preferred_element_type=jnp.float32)
        + jnp.einsum("esf,edf->esd", dup_low, up_all, preferred_element_type=jnp.float32)
    ).astype(jnp.bfloat16)
    dsent_rows = lax.all_to_all(
        from_experts(dexpert_rows), "ctx", split_axis=0, concat_axis=0, tiled=True
    )
    droutes = dsent_rows.reshape(experts_all * cap_rows, -1)[slot_of_route].reshape(
        token_per_device, TOP, -1
    )
    dffn_rows = jnp.sum(droutes.astype(jnp.float32), 1) + jnp.einsum(
        "te,de->td", dlogits_low, router_back, preferred_element_type=jnp.float32
    )
    expert_sums = (
        lax.psum_scatter(
            gate_grad.astype(jnp.bfloat16), "fsdp", scatter_dimension=1, tiled=True
        ).astype(jnp.float32),
        lax.psum_scatter(
            up_grad.astype(jnp.bfloat16), "fsdp", scatter_dimension=1, tiled=True
        ).astype(jnp.float32),
        lax.psum_scatter(
            down_grad.astype(jnp.bfloat16), "fsdp", scatter_dimension=1, tiled=True
        ).astype(jnp.float32),
    )
    dmixed_norm, ffn_gain_part = rms_back(mixed_attn, inverse_ffn, ffn_gain, dffn_rows)
    dmixed_attn = upstream + dmixed_norm
    dattn_low = dmixed_attn.astype(jnp.bfloat16)
    output_grad = jnp.einsum(
        "tc,td->cd", attended_low, dattn_low, preferred_element_type=jnp.float32
    )
    attended_lower_grad = jnp.einsum(
        "td,cd->tc", dattn_low, output_back, preferred_element_type=jnp.float32
    ).astype(jnp.bfloat16)
    output_heads_grad = attended_lower_grad.reshape(
        LOCAL_SEQUENCES, paired_rows, KEY_VALUE_HEADS, query_groups, HEAD_SIZE
    ).transpose(0, 2, 3, 1, 4)
    delta_row = jnp.sum(output_heads_grad.astype(jnp.float32) * attended, -1)
    key_recomputed, value_recomputed = (key_every, value_every)

    def score_grads(key_group, value_group, first_dev, query_group_size):
        key_row_matrix = arrange(key_group)
        value_rows = arrange(value_group)
        key_pos = group_positions(first_dev, query_group_size, context_count, block_len)
        scores = (
            jnp.einsum(
                "skgqd,swkd->skgqw",
                query_head_rows,
                key_row_matrix,
                preferred_element_type=jnp.float32,
            )
            * score_scale
        )
        allowed = key_pos[None, :] <= local_pos[:, None]
        weights_now = jnp.where(allowed, jnp.exp(scores - log_sum[..., None]), 0.0)
        dweights = jnp.einsum(
            "skgqd,swkd->skgqw", output_heads_grad, value_rows, preferred_element_type=jnp.float32
        )
        dscores = (weights_now * (dweights - delta_row[..., None])).astype(jnp.bfloat16)
        return (key_row_matrix, weights_now, dscores)

    def key_terms(weights_now, dscores, query_group_size):
        dkey_rows = jnp.einsum(
            "skgqw,skgqd->swkd", dscores, query_head_rows, preferred_element_type=jnp.float32
        )
        dvalue_rows = jnp.einsum(
            "skgqw,skgqd->swkd",
            weights_now.astype(jnp.bfloat16),
            output_heads_grad,
            preferred_element_type=jnp.float32,
        )
        return (unarrange(dkey_rows, query_group_size), unarrange(dvalue_rows, query_group_size))

    query_group_size = 4
    loop_step_count = context_count // query_group_size
    key_block_list = key_recomputed.reshape(
        loop_step_count, query_group_size, LOCAL_SEQUENCES, paired_rows, KEY_VALUE_HEADS, HEAD_SIZE
    )
    value_block_list = value_recomputed.reshape(
        loop_step_count, query_group_size, LOCAL_SEQUENCES, paired_rows, KEY_VALUE_HEADS, HEAD_SIZE
    )
    first_devs = query_group_size * jnp.arange(loop_step_count, dtype=jnp.int32)

    def back_group(dquery_acc, loop_item):
        key_group, value_group, first_dev = loop_item
        key_row_matrix, weights_now, dscores = score_grads(
            key_group, value_group, first_dev, query_group_size
        )
        dquery_acc = dquery_acc + jnp.einsum(
            "skgqw,swkd->skgqd", dscores, key_row_matrix, preferred_element_type=jnp.float32
        )
        return (dquery_acc, key_terms(weights_now, dscores, query_group_size))

    dquery_heads, key_value_pieces = lax.scan(
        back_group,
        jnp.zeros(query_head_rows.shape, jnp.float32),
        (key_block_list, value_block_list, first_devs),
    )
    key_grad_every = key_value_pieces[0].reshape(
        context_count * token_per_device, KEY_VALUE_HEADS, HEAD_SIZE
    )
    value_grad_every = key_value_pieces[1].reshape(
        context_count * token_per_device, KEY_VALUE_HEADS, HEAD_SIZE
    )
    dkey_own, value_local_grad = (
        lax.psum_scatter(key_grad_every, "ctx", scatter_dimension=0, tiled=True),
        lax.psum_scatter(value_grad_every, "ctx", scatter_dimension=0, tiled=True),
    )
    dquery = (
        (dquery_heads * score_scale)
        .transpose(0, 3, 1, 2, 4)
        .reshape(token_per_device, QUERY_HEADS, HEAD_SIZE)
    )
    dquery_proj, query_gain_part = rms_back(
        query_proj, query_inverse, query_gain, rope_back(dquery, cosine, sine_tab)
    )
    key_projection_grad, key_gain_part = rms_back(
        key_proj, key_inverse, key_gain, rope_back(dkey_own * score_scale, cosine, sine_tab)
    )
    dquery_low = dquery_proj.reshape(token_per_device, QUERY_HEADS * HEAD_SIZE).astype(jnp.bfloat16)
    key_lower_grad = key_projection_grad.reshape(
        token_per_device, KEY_VALUE_HEADS * HEAD_SIZE
    ).astype(jnp.bfloat16)
    value_lower_grad = value_local_grad.reshape(
        token_per_device, KEY_VALUE_HEADS * HEAD_SIZE
    ).astype(jnp.bfloat16)
    query_grad = jnp.einsum("td,tc->dc", normed_low, dquery_low, preferred_element_type=jnp.float32)
    key_grad = jnp.einsum(
        "td,tc->dc", normed_low, key_lower_grad, preferred_element_type=jnp.float32
    )
    value_grad = jnp.einsum(
        "td,tc->dc", normed_low, value_lower_grad, preferred_element_type=jnp.float32
    )
    dnormed = jnp.einsum("tc,dc->td", dquery_low, query_back, preferred_element_type=jnp.float32)
    dnormed = dnormed + jnp.einsum(
        "tc,dc->td", key_lower_grad, key_back, preferred_element_type=jnp.float32
    )
    dnormed = dnormed + jnp.einsum(
        "tc,dc->td", value_lower_grad, value_back, preferred_element_type=jnp.float32
    )
    dinput_norm, attention_gain_part = rms_back(inputs, inverse_attn, attention_gain, dnormed)
    d_tokens = (dmixed_attn + dinput_norm).astype(jnp.bfloat16)
    gain_sums = lax.psum(
        (attention_gain_part, ffn_gain_part, query_gain_part, key_gain_part), ("ctx", "fsdp")
    )
    layer_sums = (
        lax.psum_scatter(query_grad, ("ctx", "fsdp"), scatter_dimension=0, tiled=True),
        lax.psum_scatter(key_grad, ("ctx", "fsdp"), scatter_dimension=0, tiled=True),
        lax.psum_scatter(value_grad, ("ctx", "fsdp"), scatter_dimension=0, tiled=True),
        lax.psum_scatter(output_grad, ("ctx", "fsdp"), scatter_dimension=0, tiled=True),
        lax.psum_scatter(router_grad, ("ctx", "fsdp"), scatter_dimension=0, tiled=True),
    )
    return (
        mixed,
        d_tokens,
        gain_sums[0],
        gain_sums[1],
        gain_sums[2],
        gain_sums[3],
        layer_sums[0],
        layer_sums[1],
        layer_sums[2],
        layer_sums[3],
        layer_sums[4],
        expert_sums[0],
        expert_sums[1],
        expert_sums[2],
    )


MEMBERS = 4


def shift(block, axis, step):
    count = lax.axis_size(axis)
    return lax.ppermute(block, axis, [(i, (i + step) % count) for i in range(count)])


def swap(block, axis):
    return lax.ppermute(block, axis, [(0, 1), (1, 0)])


def after(block, *earlier):
    return lax.optimization_barrier((block,) + earlier)[0]


class Steps:
    def __init__(self):
        self.mark = None

    def __call__(self, sends, work=None, given=(), join=()):
        blocks = tuple(send[0] for send in sends)
        mark = () if self.mark is None else (self.mark,)
        blocks, given, mark = lax.optimization_barrier((blocks, tuple(given), mark))
        moved = tuple(
            swap(block, send[1]) if len(send) == 2 else shift(block, send[1], send[2])
            for block, send in zip(blocks, sends)
        )
        done = () if work is None else work(*given)
        moved, done, join, mark = lax.optimization_barrier((moved, done, tuple(join), mark))
        self.mark = jax.tree.leaves((moved, done, join))[0]
        return moved, done, join


def pick(stack, index):
    return lax.dynamic_index_in_dim(stack, index, 0, keepdims=False)


def roped(raw, gain, cosine, sine):
    inverse = lax.rsqrt(jnp.mean(raw * raw, -1, keepdims=True) + EPS)
    scaled = raw * inverse * gain
    return scaled * cosine + pltpu.roll(scaled, HEAD_SIZE // 2, 1) * sine


def split_heads(ref, start, heads):
    size = ref.shape[2] // 2
    rows = ref[:, 0, start * size : (start + 1) * size, :]
    rows = rows.reshape(ref.shape[0] * size, ref.shape[3])
    return jnp.concatenate(
        [rows[:, i * HEAD_SIZE : (i + 1) * HEAD_SIZE] for i in range(heads)], 0
    )


def key_half(ref, k, start):
    size = ref.shape[3] // 2
    rows = ref[k, :, 0, start * size : (start + 1) * size, :]
    return rows.reshape(ref.shape[1] * size, HEAD_SIZE)


def twice(rows):
    return jnp.concatenate([rows, rows], 0)


ACROSS = (((1,), (1,)), ((), ()))
DOWN = (((0,), (0,)), ((), ()))


def score_blocks(z_here, queries, k_ref):
    nz = k_ref.shape[0]
    low_q, high_q = queries
    low_keys = jnp.concatenate([key_half(k_ref, k, 0) for k in range(nz)], 0)
    blocks = [(low_keys, high_q, None)]
    for k in range(1, nz):
        before = z_here >= k
        keys = jnp.where(before, key_half(k_ref, k, 0), key_half(k_ref, k, 1))
        blocks.append((keys, jnp.where(before, low_q, high_q), before))
    blocks.append((key_half(k_ref, 0, 0), low_q, None))
    blocks.append((key_half(k_ref, 0, 1), high_q, None))
    return blocks


def value_blocks(z_here, ref):
    nz = ref.shape[0]
    blocks = [jnp.concatenate([key_half(ref, k, 0) for k in range(nz)], 0)]
    for k in range(1, nz):
        blocks.append(jnp.where(z_here >= k, key_half(ref, k, 0), key_half(ref, k, 1)))
    return blocks + [key_half(ref, 0, 0), key_half(ref, 0, 1)]


def to_halves(parts, blocks):
    low_sum, high_sum = parts[-2], parts[0] + parts[-1]
    for part, (_, _, before) in zip(parts[1:-2], blocks[1:-2]):
        low_sum = low_sum + jnp.where(before, part, 0.0)
        high_sum = high_sum + jnp.where(before, 0.0, part)
    return low_sum, high_sum


def of_halves(low_row, high_row, blocks):
    rows = [high_row]
    rows += [jnp.where(before, low_row, high_row) for _, _, before in blocks[1:-2]]
    return rows + [low_row, high_row]


def weigh(blocks, mask_ref):
    exponent = math.log2(math.e) / math.sqrt(HEAD_SIZE)
    weights = []
    for keys, queries, _ in blocks:
        scores = lax.dot_general(keys, queries, ACROSS, preferred_element_type=jnp.float32)
        weights.append(jnp.exp2(scores * exponent))
    weights[-2] = weights[-2] * mask_ref[0]
    weights[-1] = weights[-1] * mask_ref[1]
    return weights


def attend_kernel(places_ref, q_ref, k_ref, v_ref, cos_ref, sin_ref, gain_ref, mask_ref, out_ref):
    count = q_ref.shape[3] // HEAD_SIZE
    size = q_ref.shape[2] // 2
    queries = []
    for half in range(2):
        raw = split_heads(q_ref, half, count)
        queries.append(
            roped(raw, gain_ref[...], twice(cos_ref[half]), twice(sin_ref[half])).astype(
                jnp.bfloat16
            )
        )
    z_here = places_ref[1]
    blocks = score_blocks(z_here, queries, k_ref)
    weights = weigh(blocks, mask_ref)
    totals = to_halves([jnp.sum(weight, 0, keepdims=True) for weight in weights], blocks)
    mixed = [
        lax.dot_general(
            values, weight.astype(jnp.bfloat16), DOWN, preferred_element_type=jnp.float32
        )
        for values, weight in zip(value_blocks(z_here, v_ref), weights)
    ]
    mixed = to_halves(mixed, blocks)
    for half in range(2):
        out = (mixed[half] / totals[half]).T.astype(jnp.bfloat16)
        rows = out.shape[0] // count
        for i in range(count):
            out_ref[:, 0, half * size : (half + 1) * size, i * HEAD_SIZE : (i + 1) * HEAD_SIZE] = (
                out[i * rows : (i + 1) * rows].reshape(-1, size, HEAD_SIZE)
            )


def attend_back_kernel(
    places_ref,
    q_ref,
    up_ref,
    k_ref,
    v_ref,
    cos_ref,
    sin_ref,
    gain_ref,
    mask_ref,
    dq_ref,
    dkv_ref,
    dgain_ref,
):
    nz = k_ref.shape[0]
    count = q_ref.shape[3] // HEAD_SIZE
    size = q_ref.shape[2] // 2
    low = jnp.bfloat16
    score_scale = 1.0 / math.sqrt(HEAD_SIZE)
    gain = gain_ref[...]
    z_here = places_ref[1]
    raws, queries, ups = [], [], []
    for half in range(2):
        raw = split_heads(q_ref, half, count)
        raws.append(raw)
        queries.append(roped(raw, gain, twice(cos_ref[half]), twice(sin_ref[half])).astype(low))
        ups.append(split_heads(up_ref, half, count))
    blocks = score_blocks(z_here, queries, k_ref)
    weights = weigh(blocks, mask_ref)
    totals = to_halves([jnp.sum(weight, 0, keepdims=True) for weight in weights], blocks)
    inverses = [1.0 / total for total in totals]
    block_ups = [ups[1]]
    block_ups += [jnp.where(before, ups[0], ups[1]) for _, _, before in blocks[1:-2]]
    block_ups += ups
    dprobs = [
        lax.dot_general(values, up, ACROSS, preferred_element_type=jnp.float32)
        for values, up in zip(value_blocks(z_here, v_ref), block_ups)
    ]
    probs = [
        weight * inverse
        for weight, inverse in zip(weights, of_halves(inverses[0], inverses[1], blocks))
    ]
    deltas = to_halves(
        [jnp.sum(p * d, 0, keepdims=True) for p, d in zip(probs, dprobs)], blocks
    )
    dscores = [
        (p * (d - delta)).astype(low)
        for p, d, delta in zip(probs, dprobs, of_halves(deltas[0], deltas[1], blocks))
    ]
    dvs = [
        jnp.dot(p.astype(low), up, preferred_element_type=jnp.float32)
        for p, up in zip(probs, block_ups)
    ]
    dks = [
        jnp.dot(d, block[1], preferred_element_type=jnp.float32) * score_scale
        for d, block in zip(dscores, blocks)
    ]
    dqs = [
        lax.dot_general(block[0], d, DOWN, preferred_element_type=jnp.float32)
        for d, block in zip(dscores, blocks)
    ]
    dqs = to_halves(dqs, blocks)
    each = dks[-1].shape[0]
    fresh = pl.program_id(1) == 0
    for k in range(nz):
        both = [
            jnp.concatenate([dk, dv], 1)
            for dk, dv in (
                (dks[0][k * each : (k + 1) * each], dvs[0][k * each : (k + 1) * each]),
                (dks[k], dvs[k]) if k > 0 else (dks[-2], dvs[-2]),
            )
        ]
        if k == 0:
            halves = (both[0] + both[1], jnp.concatenate([dks[-1], dvs[-1]], 1))
        else:
            before = z_here >= k
            halves = (
                both[0] + jnp.where(before, both[1], 0.0),
                jnp.where(before, 0.0, both[1]),
            )
        for half in range(2):
            part = slice(half * size, (half + 1) * size)
            earlier = jnp.where(fresh, 0.0, dkv_ref[k, :, 0, part, :])
            dkv_ref[k, :, 0, part, :] = earlier + halves[half].reshape(-1, size, 2 * HEAD_SIZE)

    gain_part = jnp.zeros((1, HEAD_SIZE), jnp.float32)
    for half in range(2):
        cosine, sine = twice(cos_ref[half]), twice(sin_ref[half])
        raw = raws[half]
        inverse = lax.rsqrt(jnp.mean(raw * raw, -1, keepdims=True) + EPS)
        unit = raw * inverse
        dq = dqs[half].T * score_scale
        turned = dq * cosine - pltpu.roll(dq, HEAD_SIZE // 2, 1) * sine
        gain_part = gain_part + jnp.sum(turned * unit, 0, keepdims=True)
        turned = turned * gain
        back = inverse * (turned - unit * jnp.mean(turned * unit, -1, keepdims=True))
        back = back.astype(low)
        rows = back.shape[0] // count
        for i in range(count):
            dq_ref[:, 0, half * size : (half + 1) * size, i * HEAD_SIZE : (i + 1) * HEAD_SIZE] = (
                back[i * rows : (i + 1) * rows].reshape(-1, size, HEAD_SIZE)
            )
    gain_part = jnp.concatenate([gain_part, jnp.zeros((7, HEAD_SIZE), jnp.float32)], 0)
    first = fresh & (pl.program_id(0) == 0)
    dgain_ref[...] = jnp.where(first, 0.0, dgain_ref[...]) + gain_part


def attention_specs(q, kv, mask):
    nz, members, sequences, paired, _ = kv.shape
    pair = q.shape[-1] // MEMBERS
    q_block = (members, 1, paired, pair)
    kv_block = (nz, members, 1, paired, HEAD_SIZE)
    own = pl.BlockSpec(q_block, lambda s, r, places: (0, s, 0, r ^ places[0]))
    relative = pl.BlockSpec(q_block, lambda s, r, places: (0, s, 0, r))
    key = pl.BlockSpec(kv_block, lambda s, r, places: (0, 0, s, 0, 0))
    value = pl.BlockSpec(kv_block, lambda s, r, places: (0, 0, s, 0, 1))
    both = pl.BlockSpec(
        (nz, members, 1, paired, 2 * HEAD_SIZE), lambda s, r, places: (0, 0, s, 0, 0)
    )
    fixed = lambda shape: pl.BlockSpec(shape, lambda s, r, places: (0,) * len(shape))
    table = fixed((2, members * paired // 2, HEAD_SIZE))
    tables = [table, table, fixed((1, HEAD_SIZE)), fixed(mask.shape)]
    return own, relative, key, value, both, fixed, tables


def attend(places, q, kv, cosine, sine, gain, mask):
    members, sequences, paired, width = q.shape
    own, relative, key, value, both, fixed, tables = attention_specs(q, kv, mask)
    elements = sequences * width // HEAD_SIZE * members * paired * kv.shape[0] * members * paired
    return pl.pallas_call(
        attend_kernel,
        grid_spec=pltpu.PrefetchScalarGridSpec(
            num_scalar_prefetch=1,
            grid=(sequences, MEMBERS),
            in_specs=[own, key, value] + tables,
            out_specs=relative,
        ),
        out_shape=jax.ShapeDtypeStruct(q.shape, jnp.bfloat16),
        compiler_params=pltpu.CompilerParams(vmem_limit_bytes=40 * 2**20),
        cost_estimate=pl.CostEstimate(
            flops=4 * elements * HEAD_SIZE, bytes_accessed=8 * 2**20, transcendentals=elements
        ),
    )(places, q, kv, kv, cosine, sine, gain, mask)


def attend_back(places, q, up, kv, cosine, sine, gain, mask):
    members, sequences, paired, width = q.shape
    own, relative, key, value, both, fixed, tables = attention_specs(q, kv, mask)
    elements = sequences * width // HEAD_SIZE * members * paired * kv.shape[0] * members * paired
    return pl.pallas_call(
        attend_back_kernel,
        grid_spec=pltpu.PrefetchScalarGridSpec(
            num_scalar_prefetch=1,
            grid=(sequences, MEMBERS),
            in_specs=[own, relative, key, value] + tables,
            out_specs=(own, both, fixed((8, HEAD_SIZE))),
        ),
        out_shape=(
            jax.ShapeDtypeStruct(q.shape, jnp.bfloat16),
            jax.ShapeDtypeStruct(kv.shape, jnp.float32),
            jax.ShapeDtypeStruct((8, HEAD_SIZE), jnp.float32),
        ),
        compiler_params=pltpu.CompilerParams(vmem_limit_bytes=40 * 2**20),
        cost_estimate=pl.CostEstimate(
            flops=10 * elements * HEAD_SIZE, bytes_accessed=16 * 2**20, transcendentals=elements
        ),
    )(places, q, up, kv, kv, cosine, sine, gain, mask)


def dot32(subscripts, left, right):
    return jnp.einsum(subscripts, left, right, preferred_element_type=jnp.float32)


def expert_kernel(*refs):
    scalars_ref, x_refs, c_refs = refs[0], refs[1:5], refs[5:9]
    rank_ref, chosen_ref, router_ref, gate_ref, up_ref, down_ref = refs[9:15]
    rows_ref, hidden_ref, dresults_ref, dgate_ref, dup_ref = refs[-9:-4]
    sent_refs, back_refs = refs[-4:-2], refs[-2:]
    low, wide = jnp.bfloat16, jnp.float32
    blocks = 2
    tokens, model = x_refs[0].shape
    opening = pl.program_id(0) == 0
    slots = rows_ref.shape[2]
    experts_all = router_ref.shape[0]
    across = (((1,), (1,)), ((), ()))
    down = (((0,), (0,)), ((), ()))
    own_expert = scalars_ref[0]
    places, picked, upstream, gates = [], [], [], []
    for block in range(blocks):
        rows = jnp.where(opening, x_refs[block][...], x_refs[2 + block][...])
        slot = lax.broadcasted_iota(jnp.int32, (slots, tokens), 0)
        place = jnp.where(slot == rank_ref[0, block], 1.0, 0.0)
        chosen = chosen_ref[0, block] > 0.5
        logits = lax.dot_general(router_ref[...], rows, across, preferred_element_type=wide)
        highest = jnp.max(jnp.where(chosen, logits, NEGATIVE_LIMIT), 0, keepdims=True)
        raised = jnp.where(chosen, jnp.exp(jnp.minimum(logits - highest, 0.0)), 0.0)
        expert = lax.broadcasted_iota(jnp.int32, (experts_all, tokens), 0)
        mine = jnp.sum(jnp.where(expert == own_expert, raised, 0.0), 0, keepdims=True)
        gate_row = mine / jnp.sum(raised, 0, keepdims=True)
        gates.append(jnp.sum(place * gate_row, 1, keepdims=True))
        place = place.astype(low)
        places.append(place)
        picked.append(jnp.dot(place, rows, preferred_element_type=wide).astype(low))
        cotangent = jnp.where(opening, c_refs[block][...], c_refs[2 + block][...])
        upstream.append(jnp.dot(place, cotangent, preferred_element_type=wide))
    rows = jnp.concatenate(picked, 0)
    upstream = jnp.concatenate(upstream, 0)
    gates = jnp.concatenate(gates, 0)
    gate_part = jnp.dot(rows, gate_ref[...], preferred_element_type=wide)
    up_part = jnp.dot(rows, up_ref[...], preferred_element_type=wide)
    sigmoid_gate = 1.0 / (1.0 + jnp.exp(-gate_part))
    silu_gate = gate_part * sigmoid_gate
    hidden = (silu_gate * up_part).astype(low)
    results = jnp.dot(hidden, down_ref[...], preferred_element_type=wide).astype(low).astype(wide)
    dgates = jnp.sum(upstream * results, 1, keepdims=True)
    scaled = (gates * results).astype(low)
    dresults = (gates * upstream).astype(low)
    dhidden = lax.dot_general(dresults, down_ref[...], across, preferred_element_type=wide)
    dsilu_gate = sigmoid_gate * (1.0 + gate_part * (1.0 - sigmoid_gate))
    dgate_low = (dhidden * up_part * dsilu_gate).astype(low)
    dup_low = (dhidden * silu_gate).astype(low)
    drows = lax.dot_general(dgate_low, gate_ref[...], across, preferred_element_type=wide)
    drows = drows + lax.dot_general(dup_low, up_ref[...], across, preferred_element_type=wide)
    drows = drows.astype(low)
    lane = lax.broadcasted_iota(jnp.int32, (blocks * slots, 128), 1)
    coarse = dgates.astype(low).astype(wide)
    extra = jnp.where(lane == own_expert, coarse, 0.0)
    extra = extra + jnp.where(lane == own_expert + experts_all, dgates - coarse, 0.0)
    extra = extra.astype(low)
    for block in range(blocks):
        part = slice(block * slots, (block + 1) * slots)
        sent_refs[block][0] = lax.dot_general(
            places[block], scaled[part], down, preferred_element_type=wide
        ).astype(low)
        back_refs[block][0, :, :model] = lax.dot_general(
            places[block], drows[part], down, preferred_element_type=wide
        ).astype(low)
        back_refs[block][0, :, model:] = lax.dot_general(
            places[block], extra[part], down, preferred_element_type=wide
        ).astype(low)
        rows_ref[0, block] = rows[part]
        hidden_ref[0, block] = hidden[part]
        dresults_ref[0, block] = dresults[part]
        dgate_ref[0, block] = dgate_low[part]
        dup_ref[0, block] = dup_low[part]


def experts(scalars, x_blocks, c_blocks, ranks, chosen, router, gate, up, down, slots, earlier):
    tokens, model = x_blocks[0].shape
    nz, members = ranks.shape[:2]
    hidden = gate.shape[1]
    low = jnp.bfloat16
    pair = members // 2
    experts_all = router.shape[0]
    whole = lambda array: pl.BlockSpec(
        array.shape, lambda a, s: (0, 0), pipeline_mode=pl.Buffered(1)
    )
    turn = lambda *tail: pl.BlockSpec((1, pair) + tail, lambda a, s: (s[1], a, 0, 0))
    in_specs = [
        *[whole(block) for block in x_blocks],
        *[whole(block) for block in c_blocks],
        turn(1, tokens),
        turn(experts_all, tokens),
        whole(router),
        whole(gate),
        whole(up),
        whole(down),
    ]
    shapes = [(slots, model), (slots, hidden), (slots, model)]
    shapes += [(slots, hidden), (slots, hidden)]
    out_shape = [jax.ShapeDtypeStruct((nz, members) + shape, low) for shape in shapes]
    out_specs = [turn(*shape) for shape in shapes]
    wide_model = model + 128
    for columns in (model, wide_model):
        out_shape += [jax.ShapeDtypeStruct((2, tokens, columns), low)] * 2
        out_specs += [pl.BlockSpec((1, tokens, columns), lambda a, s: (a, 0, 0))] * 2
    aliases = {}
    if earlier:
        in_specs = in_specs + [pl.BlockSpec(memory_space=pl.ANY)] * len(earlier)
        aliases = {15 + i: i for i in range(len(earlier))}
    return pl.pallas_call(
        expert_kernel,
        grid_spec=pltpu.PrefetchScalarGridSpec(
            num_scalar_prefetch=1, grid=(2,), in_specs=in_specs, out_specs=out_specs
        ),
        out_shape=out_shape,
        input_output_aliases=aliases,
        compiler_params=pltpu.CompilerParams(vmem_limit_bytes=58 * 2**20),
        cost_estimate=pl.CostEstimate(
            flops=12 * members * slots * model * hidden,
            bytes_accessed=40 * 2**20,
            transcendentals=2 * members * slots * hidden,
        ),
    )(scalars, *x_blocks, *c_blocks, ranks, chosen, router, gate, up, down, *earlier)


def dot32(subscripts, left, right):
    return jnp.einsum(subscripts, left, right, preferred_element_type=jnp.float32)


def member_layer(
    tokens,
    cotangent,
    expert_ids,
    attention_gain,
    ffn_gain,
    query_gain,
    key_gain,
    w_query,
    key_weight,
    value_weight,
    w_output,
    w_router,
    w_gate,
    w_up,
    w_down,
):
    low, wide = jnp.bfloat16, jnp.float32
    nz = lax.axis_size("z")
    zi, yi, ci, xi = (lax.axis_index(axis) for axis in ("z", "y", "c", "x"))
    member = 2 * yi + ci
    context_count = nz * MEMBERS
    rows, model = tokens.shape
    paired = rows // LOCAL_SEQUENCES
    block_len = paired // 2
    groups = QUERY_HEADS // KEY_VALUE_HEADS
    experts_all = w_router.shape[1]
    around = lambda k: lax.rem(zi + (k % nz), jnp.int32(nz))
    from_z = [around(-k) for k in range(nz)]
    crossed = [member ^ r for r in range(MEMBERS)]
    token_members = member ^ jnp.array([0, 2, 1, 3], jnp.int32)

    def uncrossed(blocks):
        for bit, odd in ((1, ci), (2, yi)):
            blocks = [jnp.where(odd == 0, blocks[r], blocks[r ^ bit]) for r in range(MEMBERS)]
        return jnp.stack(blocks)

    own_expert = zi * MEMBERS + member
    step = Steps()

    piece = w_query.shape[0]
    head_rows = w_output.shape[0]
    query_width = groups * HEAD_SIZE
    third = w_down.shape[1] // 3

    def make_tables(zi, token_members):
        own_pos = jax.vmap(lambda device: shard_positions(device, context_count, block_len))(
            zi * MEMBERS + token_members
        )
        cosine, sine_tab = rotary(own_pos.reshape(-1), HEAD_SIZE)
        row_cosine = cosine.reshape(MEMBERS, 1, paired, HEAD_SIZE)
        row_sine = sine_tab.reshape(MEMBERS, 1, paired, HEAD_SIZE)

        def halves(table):
            table = table.reshape(MEMBERS, 2, block_len, HEAD_SIZE).transpose(1, 0, 2, 3)
            return table.reshape(2, MEMBERS * block_len, HEAD_SIZE)

        half = HEAD_SIZE // 2
        signs = jnp.where(jnp.arange(HEAD_SIZE) < half, -1.0, 1.0)
        kernel_cosine, kernel_sine = halves(row_cosine), halves(row_sine * signs)
        half_pos = own_pos.reshape(MEMBERS, 2, block_len).transpose(1, 0, 2).reshape(2, -1)
        mask = (half_pos[:, :, None] <= half_pos[:, None, :]).astype(wide)
        mask = jnp.concatenate([mask, mask], 2)
        return row_cosine, row_sine, kernel_cosine, kernel_sine, mask

    def make_slots(packed):
        width_small = piece * experts_all
        flat = packed.reshape(nz * 8, -1)
        device = jnp.arange(nz * 8, dtype=jnp.int32)
        source = ((zi - device // 8) % nz) * 8 + ((device & 1) ^ xi) * 4
        source = source + (((device >> 1) & 1) ^ ci) * 2 + (((device >> 2) & 1) ^ yi)
        router = flat[:, :width_small][source].reshape(nz * 8, experts_all, piece)
        router = router.transpose(1, 0, 2).reshape(experts_all, model)
        ids_all = packed.reshape(nz, 2, 2, 2, -1)[:, 0, :, :, width_small:].transpose(0, 2, 1, 3)
        ids_all = ids_all.reshape(nz, MEMBERS, TOP, rows).astype(jnp.int32)
        named = jnp.any(ids_all == own_expert, 2)
        before = (
            jnp.arange(rows, dtype=jnp.int32)[:, None] <= jnp.arange(rows, dtype=jnp.int32)[None, :]
        )
        ranks = dot32("kjs,st->kjt", named.astype(low), before.astype(low)).astype(jnp.int32) - 1
        ranks = jnp.where(named, ranks, -1)[:, :, None, :]
        expert_column = jnp.arange(experts_all, dtype=jnp.int32)[:, None]
        chosen_all = jnp.any(ids_all[:, :, :, None, :] == expert_column, 2).astype(wide)
        return router, ranks, chosen_all

    cap_rows = rows * TOP * 5 // (4 * experts_all)
    slots = -(-cap_rows // 16) * 16

    def prepare(w_query, key_weight, value_weight, w_router, expert_ids):
        columns = jnp.concatenate(
            [w.reshape(piece, KEY_VALUE_HEADS, -1) for w in (w_query, key_weight, value_weight)],
            -1,
        ).transpose(1, 0, 2)
        packed = jnp.concatenate([w_router.T.reshape(-1), expert_ids.T.astype(low).reshape(-1)])
        parts = [pick(columns, crossed[r]) for r in range(MEMBERS)]
        return parts[0], parts[1], jnp.stack(parts[2:]), packed.reshape(-1, 128)

    (plane1,), (part0, part1, parts_far, packed), _ = step(
        [(w_output, "z", 1)],
        prepare,
        (w_query, key_weight, value_weight, w_router, expert_ids),
    )
    width = part0.shape[-1]
    inputs = tokens.astype(wide)

    def first_members(part0, part1, parts_far, tokens):
        far = swap(parts_far, "y")
        near = swap(jnp.stack([part1, far[1]]), "c")
        blocks = [part0, near[0], far[0], near[1]]
        return uncrossed(blocks), rms_apply(tokens.astype(wide), attention_gain)

    (plane3, *small), (ordered, (normed_attn, inverse_attn)), _ = step(
        [(w_output, "z", 3)] + [(packed, "z", k) for k in range(1, nz)],
        first_members,
        (part0, part1, parts_far, tokens),
    )
    packed = jnp.stack([packed] + small)
    normed_low = normed_attn.astype(low)
    held = [ordered]
    over_x = []
    (moved, cross, other, near, packed_far), _, _ = step(
        [
            (ordered, "z", 1),
            (ordered, "x"),
            (normed_low, "y"),
            (normed_low, "c"),
            (packed, "y"),
        ]
    )
    held.append(moved)
    over_x.append(cross)
    packed = jnp.stack([packed, packed_far], 1)
    (moved, cross, other_near, packed_near, down1), tables, _ = step(
        [
            (ordered, "z", 2),
            (held[1], "x"),
            (other, "c"),
            (packed, "c"),
            (w_down[0, third : 2 * third], "x"),
        ],
        make_tables,
        (zi, token_members),
    )
    row_cosine, row_sine, kernel_cosine, kernel_sine, mask = tables
    held.append(moved)
    over_x.append(cross)
    normed_all = jnp.concatenate([normed_low, other, near, other_near])
    packed = jnp.stack([packed, packed_near], 1)
    (moved, cross, c_near0, packed_cross), _, _ = step(
        [(ordered, "z", 3), (held[2], "x"), (cotangent, "c"), (packed, "x")]
    )
    packed = jnp.stack([packed, packed_cross], 1)
    held.append(moved)
    over_x.append(cross)
    cut = rows // 2
    gate_cut = w_gate.shape[1] * 5 // 16
    gate_next = w_gate.shape[1] * 9 // 16

    def cut_pieces(own, one, three, gate, down, cotangent):
        gates = (gate[:gate_cut], gate[gate_cut:gate_next], gate[gate_next:])
        halves = (cotangent[:cut], cotangent[cut:])
        return jnp.stack([own, one, one, three]), gates, down[2 * third :], halves

    (cross, plane2, c_far0, down0), (planes, gate_pieces, down_piece, c_halves), _ = step(
        [(held[3], "x"), (w_output, "z", 2), (cotangent, "y"), (w_down[0, :third], "x")],
        cut_pieces,
        (w_output, plane1, plane3, w_gate[0], w_down[0], cotangent),
    )
    over_x.append(cross)

    def assemble(start, stop):
        full = jnp.zeros((nz, MEMBERS, 2, piece, stop - start), low)
        for k in range(nz):
            full = lax.dynamic_update_slice(
                full, held[k][None, :, None, :, start:stop], (from_z[k], 0, xi, 0, 0)
            )
            full = lax.dynamic_update_slice(
                full, over_x[k][None, :, None, :, start:stop], (from_z[k], 0, 1 - xi, 0, 0)
            )
        return full.reshape(model, stop - start)

    query_weight = assemble(0, query_width)
    key_value_weight = assemble(query_width, width)

    def project_keys(normed_all, key_value_weight):
        raw = jnp.dot(normed_all, key_value_weight, preferred_element_type=wide)
        raw = raw.reshape(MEMBERS, LOCAL_SEQUENCES, paired, 2 * HEAD_SIZE)
        key_proj = raw[..., :HEAD_SIZE]
        key_normed, key_inverse = rms_apply(key_proj, key_gain)
        key_low = rope_apply(key_normed, row_cosine, row_sine).astype(low)
        value_low = raw[..., HEAD_SIZE:].astype(low)
        return key_proj, key_inverse, jnp.concatenate([key_low, value_low], -1)

    planes = lax.dynamic_update_index_in_dim(planes, plane2, 2, 0)
    wanted = [pick(planes, lax.rem(zi + nz - crossed[r], jnp.int32(nz))) for r in range(MEMBERS)]
    moved, (key_proj, key_inverse, key_value), _ = step(
        [
            (jnp.stack(wanted[2:]), "y"),
            (cotangent, "z", 1),
            (down_piece, "x"),
            (gate_pieces[0], "x"),
            (c_far0, "c"),
        ],
        project_keys,
        (normed_all, key_value_weight),
    )
    far, c1, down2, gate0, c_far_near0 = moved
    mine = jnp.stack([wanted[0], far[0]])

    def project_queries(normed_all, query_weight, pair):
        near = swap(pair, "c")
        return (
            near,
            swap(near[0], "x"),
            jnp.dot(normed_all, query_weight, preferred_element_type=wide),
        )

    moved, (near, cross_first, queries), _ = step(
        [(key_value, "z", k) for k in range(1, nz)] + [(mine, "x")],
        project_queries,
        (normed_all, query_weight, jnp.stack([wanted[1], far[1]])),
    )
    key_value = jnp.stack((key_value,) + moved[: nz - 1])
    cross_mine = moved[nz - 1]
    queries = queries.reshape(MEMBERS, LOCAL_SEQUENCES, paired, query_width)

    places = jnp.stack([member, zi]).astype(jnp.int32)
    gain_row = query_gain[None]
    (cross_last, c2_low, c_far1, gate1), attended, _ = step(
        [
            (near[1], "x"),
            (c_halves[0], "z", 2),
            (c1, "y"),
            (gate_pieces[1], "x"),
        ],
        attend,
        (places, queries, key_value, kernel_cosine, kernel_sine, gain_row, mask),
    )
    attended = attended.reshape(MEMBERS * rows, query_width)
    own_heads = jnp.stack([mine[0], near[0], mine[1], near[1]])
    other_heads = jnp.stack([cross_mine[0], cross_first, cross_mine[1], cross_last])
    output_weight = jnp.where(
        xi == 0, jnp.stack([own_heads, other_heads], 1), jnp.stack([other_heads, own_heads], 1)
    ).reshape(query_width, model)

    mixed_part = jnp.dot(attended, output_weight, preferred_element_type=wide)
    mixed_part = mixed_part.reshape(2, 2, rows, model)

    def summed_members(own, send):
        near = swap(send, "c")
        far = swap((own[1] + near[1].astype(wide)).astype(low), "y")
        return own[0] + near[0].astype(wide) + far.astype(wide)

    (gate2, c2_high, c_near1), mixed_sum, _ = step(
        [(gate_pieces[2], "x"), (c_halves[1], "z", 2), (c1, "c")],
        summed_members,
        (mixed_part[0], mixed_part[1].astype(low)),
    )
    c2 = jnp.concatenate([c2_low, c2_high])
    mixed_attn = inputs + mixed_sum
    normed_ffn, inverse_ffn = rms_apply(mixed_attn, ffn_gain)
    ffn_low = normed_ffn.astype(low)

    def whole(own, others):
        full = jnp.zeros((2,) + own.shape, low)
        full = lax.dynamic_update_slice(full, own[None], (xi, 0, 0))
        start = 0
        for other in others:
            full = lax.dynamic_update_slice(full, other[None], (1 - xi, start, 0))
            start += other.shape[0]
        return full.reshape(2 * own.shape[0], own.shape[1])

    def run_experts(k, x_blocks, c_blocks, kept, weights):
        scalars = jnp.stack([own_expert, jnp.int32(k)]).astype(jnp.int32)
        out = experts(
            scalars, x_blocks, c_blocks, ranks, chosen_all, router, *weights, slots, kept
        )
        return tuple(out[:-4]), out[-4:-2], out[-2:]

    def added(pair, back, a):
        return pair[0][a].astype(wide) + back[a].astype(wide)

    def both_rows(block):
        far = swap(block, "y")
        return far, swap(far, "c")

    moved, ((gate_all, down_all), (router, ranks, chosen_all)), _ = step(
        [
            (ffn_low, "z", 2),
            (w_up[0], "x"),
            (c2, "y"),
            (ffn_low, "y"),
            (c2, "c"),
        ],
        lambda owns, others, packed: (
            [whole(own, other) for own, other in zip(owns, others)],
            make_slots(packed),
        ),
        ([w_gate[0], w_down[0]], [[gate0, gate1, gate2], [down0, down1, down2]], packed),
    )
    x2, up_other, c_far2, y0, c_near2 = moved

    logits = dot32("td,ed->te", ffn_low, router)
    chosen = jnp.any(
        expert_ids[:, :, None] == jnp.arange(experts_all, dtype=jnp.int32)[None, None, :], 1
    )
    highest = jnp.max(jnp.where(chosen, logits, NEGATIVE_LIMIT), 1, keepdims=True)
    raised = jnp.where(chosen, jnp.exp(jnp.minimum(logits - highest, 0.0)), 0.0)
    gates = raised / jnp.sum(raised, 1, keepdims=True)

    (x1, c3_low, y2, n2, c_far_near2), up_all, _ = step(
        [
            (ffn_low, "z", 1),
            (c_halves[0], "z", 3),
            (x2, "y"),
            (x2, "c"),
            (c_far2, "c"),
        ],
        lambda own, other: whole(own, [other]),
        (w_up[0], up_other),
    )
    weights = [gate_all, up_all, down_all]
    (ny2, n0, ny0, c_far_near1), _, _ = step(
        [(y2, "c"), (ffn_low, "c"), (y0, "c"), (c_far1, "c")]
    )
    (x3, c3_high, y1, c_far3_low, n1), (kept, mixed2, rows2), _ = step(
        [
            (ffn_low, "z", 3),
            (c_halves[1], "z", 3),
            (x1, "y"),
            (c3_low, "y"),
            (x1, "c"),
        ],
        functools.partial(run_experts, 2),
        ([x2, n2, y2, ny2], [c2, c_near2, c_far2, c_far_near2], (), weights),
    )
    (ny1, n3), c3, _ = step(
        [(y1, "c"), (x3, "c")], lambda *halves: jnp.concatenate(halves), (c3_low, c3_high)
    )
    def core_sums(*pairs):
        backs = [swap(pair[1], "c") for pair in pairs]
        return backs, [added(pair, back, 1).astype(low) for pair, back in zip(pairs, backs)]

    def sums_and_experts(pairs, k, *given):
        return core_sums(*pairs), run_experts(k, *given)

    (y3, c_far3_high, c_near3), (sums, (kept, mixed1, rows1)), _ = step(
        [(x3, "y"), (c3_high, "y"), (c3, "c")],
        lambda pairs, *given: sums_and_experts(pairs, 1, *given),
        (
            [rows2, mixed2],
            [x1, n1, y1, ny1],
            [c1, c_near1, c_far1, c_far_near1],
            kept,
            weights,
        ),
    )
    (back2, mixed_back2), (row_send2, mixed_far_send2) = sums
    c_far3 = jnp.concatenate([c_far3_low, c_far3_high])
    (ny3, c_far_near3), _, _ = step([(y3, "c"), (c_far3, "c")])
    (far2, mixed_far2), (sums, (kept, mixed3, rows3)), _ = step(
        [(row_send2, "y"), (mixed_far_send2, "y")],
        lambda pairs, *given: sums_and_experts(pairs, 3, *given),
        (
            [rows1, mixed1],
            [x3, n3, y3, ny3],
            [c3, c_near3, c_far3, c_far_near3],
            kept,
            weights,
        ),
    )
    (back1, mixed_back1), (row_send1, mixed_far_send1) = sums
    total2 = (added(rows2, back2, 0) + far2.astype(wide)).astype(low)
    (z2, far1, mixed_far1), (sums, (kept, mixed0, rows0)), _ = step(
        [(total2, "z", -2), (row_send1, "y"), (mixed_far_send1, "y")],
        lambda pairs, *given: sums_and_experts(pairs, 0, *given),
        (
            [rows3, mixed3],
            [ffn_low, n0, y0, ny0],
            [cotangent, c_near0, c_far0, c_far_near0],
            kept,
            weights,
        ),
    )
    (back3, mixed_back3), (row_send3, mixed_far_send3) = sums
    expert_rows, hidden_low, dresults, dgate_low, dup_low = (
        block.reshape(context_count * slots, -1) for block in kept
    )

    def halved(grad, sixteenths):
        size = grad.shape[0] // 2
        cut = size * sixteenths // 16
        own = lax.dynamic_slice_in_dim(grad, xi * size, size, 0)
        first = lax.dynamic_slice_in_dim(grad, (1 - xi) * size, cut, 0)
        rest = lax.dynamic_slice_in_dim(grad, (1 - xi) * size + cut, size - cut, 0)
        return own, first.astype(low), rest.astype(low)

    def joined(own, moved):
        return (own + jnp.concatenate(moved, 0).astype(wide))[None]

    total1 = (added(rows1, back1, 0) + far1.astype(wide)).astype(low)

    def total(pair, back, far):
        return (added(pair, back, 0) + far.astype(wide)).astype(low)

    (z1, far3), (sums, (down_grad, down_first, down_rest), mixed_send1), _ = step(
        [(total1, "z", -1), (row_send3, "y")],
        lambda pairs, rows, grad, *given: (
            core_sums(*pairs),
            halved(dot32("sf,sd->fd", rows, grad), 10),
            total(*given),
        ),
        ([rows0, mixed0], hidden_low, dresults, mixed1, mixed_back1, mixed_far1),
    )
    (back0, mixed_back0), (row_send0, mixed_far_send0) = sums
    total3 = (added(rows3, back3, 0) + far3.astype(wide)).astype(low)
    (z3, far0, down0), ((gate_grad, gate_first, gate_rest), mixed_send2), _ = step(
        [
            (total3, "z", -3),
            (row_send0, "y"),
            (down_first, "x"),
        ],
        lambda rows, grad, *given: (halved(dot32("sd,sf->df", rows, grad), 10), total(*given)),
        (expert_rows, dgate_low, mixed2, mixed_back2, mixed_far2),
    )
    returned = added(rows0, back0, 0) + far0.astype(wide) + z1.astype(wide)
    returned = returned + z2.astype(wide) + z3.astype(wide)
    dffn_routed = returned[:, :model]
    dgates = returned[:, model : model + experts_all]
    dgates = dgates + returned[:, model + experts_all : model + 2 * experts_all]
    dlogits = gates * (dgates - jnp.sum(gates * dgates, 1, keepdims=True))
    dlogits_low = dlogits.astype(low)
    router_rows = dot32("td,te->de", ffn_low, dlogits_low).astype(low)
    router_rows = router_rows.reshape(nz, MEMBERS, 2, -1, 2 * HEAD_SIZE)
    extra_rows = router_rows.shape[3]
    router_rows = jnp.pad(router_rows, ((0, 0),) * 3 + ((0, -extra_rows % 16), (0, 0)))

    upstream = cotangent.astype(wide)
    dffn_rows = dffn_routed + dot32("te,ed->td", dlogits_low, router)
    dmixed_norm, ffn_gain_part = rms_back(mixed_attn, inverse_ffn, ffn_gain, dffn_rows)
    dmixed_attn = upstream + dmixed_norm
    dattn_low = dmixed_attn.astype(low)
    moved, (up_grad, up_first, up_rest), _ = step(
        [
            (dattn_low, "y"),
            (dattn_low, "c"),
            (gate_first, "x"),
            (mixed_send1, "z", -1),
        ],
        lambda rows, grad: halved(dot32("sd,sf->df", rows, grad), 11),
        (expert_rows, dup_low),
    )
    other, near, gate0, mixed_z1 = moved
    (other_near,), (dattn_all,), _ = step(
        [(other, "c")],
        lambda *blocks: (jnp.concatenate(blocks),),
        (dattn_low, other, near, dattn_low),
    )
    dattn_all = lax.dynamic_update_slice_in_dim(dattn_all, other_near, 3 * rows, 0)

    output_part = dot32("tc,td->cd", attended, dattn_all).astype(low)
    output_part = output_part.reshape(MEMBERS, 2, head_rows, model)
    output_own = lax.dynamic_index_in_dim(output_part, xi, 1, keepdims=False)
    output_other = lax.dynamic_index_in_dim(output_part, 1 - xi, 1, keepdims=False)

    def planes_of(part):
        own = lax.dynamic_index_in_dim(part, xi, 2, keepdims=False)
        other = lax.dynamic_index_in_dim(part, 1 - xi, 2, keepdims=False)
        return [(pick(own, around(k)), pick(other, around(k))) for k in range(nz)]

    def attention_back(dattn_all, output_weight, normed_all, head, *given):
        attended_grad = dot32("td,cd->tc", dattn_all, output_weight).astype(low)
        attended_grad = attended_grad.reshape(MEMBERS, LOCAL_SEQUENCES, paired, query_width)
        dquery, dkey_value, gain_part = attend_back(*given[:2], attended_grad, *given[2:])
        dquery = dquery.reshape(MEMBERS * rows, query_width)
        part = dot32("td,tc->dc", normed_all, dquery).astype(low)
        plane = pick(part.reshape(nz, MEMBERS, 2, piece, query_width), around(2))
        plane = lax.dynamic_index_in_dim(plane, 1 - xi, 1, keepdims=False)
        plane = [plane.reshape(-1, query_width)]
        plane += [head[:, a : a + query_width] for a in range(0, model, query_width)]
        return dquery, dkey_value, gain_part, part, jnp.concatenate(plane)

    moved, attention_grads, _ = step(
        [
            (output_other[1:], "x"),
            (mixed_send2, "z", -2),
            (mixed_far_send3, "y"),
            (mixed_far_send0, "y"),
        ],
        attention_back,
        (
            dattn_all,
            output_weight,
            normed_all,
            output_other[0],
            places,
            queries,
            key_value,
            kernel_cosine,
            kernel_sine,
            gain_row,
            mask,
        ),
    )
    cross_rest, mixed_z2, mixed_far3, mixed_far0 = moved
    dquery_low, dkey_value, query_gain_part, query_part, query_and_head = attention_grads
    query_gain_part = query_gain_part[0]
    query_planes = planes_of(query_part.reshape(nz, MEMBERS, 2, piece, query_width))
    output_far = (output_own[2:].astype(wide) + cross_rest[1:].astype(wide)).astype(low)

    def query_back(grad, weight, third, own, other):
        near = (own.astype(wide) + other.astype(wide)).astype(low)
        return dot32("tc,dc->td", grad, weight), total(*third), near

    moved, (dnormed, mixed_send3, near_last), _ = step(
        [(dkey_value[k].astype(low), "z", -k) for k in range(1, nz)]
        + [(query_and_head, "x"), (output_far, "y")],
        query_back,
        (
            dquery_low,
            query_weight,
            [mixed3, mixed_back3, mixed_far3],
            output_own[1],
            cross_rest[0],
        ),
    )
    *key_moves, cross, output_far = moved
    plane_rows = MEMBERS * piece
    cross_first = [
        cross[a : a + head_rows] for a in range(plane_rows, cross.shape[0], head_rows)
    ]
    cross_first = jnp.concatenate(cross_first, 1)
    cross = cross[:plane_rows].reshape(query_planes[2][0].shape)
    query_sum2 = (query_planes[2][0].astype(wide) + cross.astype(wide)).astype(low)
    near_first = (output_own[0].astype(wide) + cross_first.astype(wide)).astype(low)

    def project_keys_back(dnormed, dkey_value_own, moved, key_value_weight):
        dkey_value_own = dkey_value_own + sum(block.astype(wide) for block in moved)
        dkey, dvalue = dkey_value_own[..., :HEAD_SIZE], dkey_value_own[..., HEAD_SIZE:]
        dkey_proj, key_gain_part = rms_back(
            key_proj, key_inverse, key_gain, rope_back(dkey, row_cosine, row_sine)
        )
        dkey_value_low = jnp.concatenate([dkey_proj, dvalue], -1).astype(low)
        dkey_value_low = dkey_value_low.reshape(MEMBERS * rows, 2 * HEAD_SIZE)
        dnormed = dnormed + dot32("tc,dc->td", dkey_value_low, key_value_weight)
        dnormed = dnormed.reshape(2, 2, rows, model)
        key_part = dot32("td,tc->dc", normed_all, dkey_value_low).astype(low)
        key_part = key_part.reshape(nz, MEMBERS, 2, piece, 2 * HEAD_SIZE)
        key_part = jnp.concatenate([key_part, router_rows], 3)
        key_own = lax.dynamic_index_in_dim(key_part, xi, 2, keepdims=False)
        key_other = lax.dynamic_index_in_dim(key_part, 1 - xi, 2, keepdims=False)
        return dnormed[0], dnormed[1].astype(low), key_own, key_other, key_gain_part

    moved, (dnormed_own, dnormed_send, key_own, key_other, key_gain_part), _ = step(
        [
            (query_sum2, "z", 2),
            (jnp.stack([query_planes[1][1], query_planes[3][1]]), "x"),
            (jnp.stack([near_last, output_far[1]]), "c"),
        ],
        project_keys_back,
        (dnormed, dkey_value[0], key_moves, key_value_weight),
    )
    query_z2, cross, output_back = moved
    query_sum1 = (query_planes[1][0].astype(wide) + cross[0].astype(wide)).astype(low)
    query_sum3 = (query_planes[3][0].astype(wide) + cross[1].astype(wide)).astype(low)

    def order_output(blocks):
        blocks = uncrossed(blocks)
        return [pick(blocks, around(k)) for k in range(nz)]

    moved, output_sends, _ = step(
        [
            (query_sum1, "z", 1),
            (query_sum3, "z", 3),
            (query_planes[0][1], "x"),
            (key_other, "x"),
            (dnormed_send, "c"),
        ],
        order_output,
        ([near_first, output_back[0], output_far[0], output_back[1]],),
    )
    query_z1, query_z3, cross, key_cross, near = moved
    dnormed_far = (dnormed_own[1] + near[1].astype(wide)).astype(low)
    key_sum = (key_own.astype(wide) + key_cross.astype(wide)).astype(low)

    def total_queries(own, cross, *moved):
        total = own.astype(wide) + cross.astype(wide) + sum(m.astype(wide) for m in moved)
        total = total.astype(low)
        parts = [pick(total, crossed[r]) for r in range(MEMBERS)]
        return parts[0], parts[1], jnp.stack(parts[2:])

    (output_z1, output_z3, other, gate1, down1), query_parts, _ = step(
        [
            (output_sends[1], "z", 1),
            (output_sends[3], "z", 3),
            (dnormed_far, "y"),
            (gate_rest, "x"),
            (down_rest, "x"),
        ],
        total_queries,
        (query_planes[0][0], cross, query_z1, query_z2, query_z3),
    )
    dnormed = dnormed_own[0] + near[0].astype(wide) + other.astype(wide)
    dinput_norm, attention_gain_part = rms_back(inputs, inverse_attn, attention_gain, dnormed)
    small = [attention_gain_part, ffn_gain_part, query_gain_part, key_gain_part]
    small = jnp.concatenate(small).reshape(-1, 128)
    (*key_moves, small_x, query_far), d_tokens, _ = step(
        [(pick(key_sum, around(k)), "z", k) for k in range(1, nz)]
        + [(small, "x"), (query_parts[2], "y")],
        lambda a, b: (a + b).astype(low),
        (dmixed_attn, dinput_norm),
    )
    small = small + small_x
    key_total = pick(key_sum, zi).astype(wide)
    key_total = (key_total + sum(m.astype(wide) for m in key_moves)).astype(low)
    key_parts = [pick(key_total, crossed[r]) for r in range(MEMBERS)]

    def member_columns(parts):
        return uncrossed(parts).astype(wide).transpose(1, 0, 2)

    (output_z2, up0, key_far, small_y, query_near), (down_grad, gate_grad), _ = step(
        [
            (output_sends[2], "z", 2),
            (up_first, "x"),
            (jnp.stack(key_parts[2:]), "y"),
            (small, "y"),
            (jnp.stack([query_parts[1], query_far[1]]), "c"),
        ],
        lambda down, downs, gate, gates: (joined(down, downs), joined(gate, gates)),
        (down_grad, [down0, down1], gate_grad, [gate0, gate1]),
    )
    small = small + small_y
    query_blocks = [query_parts[0], query_near[0], query_far[0], query_near[1]]
    (mixed_z3, up1, key_near, small_c), (query_grad, output_grad), _ = step(
        [
            (mixed_send3, "z", -3),
            (up_rest, "x"),
            (jnp.stack([key_parts[1], key_far[1]]), "c"),
            (small, "c"),
        ],
        lambda blocks, own, *parts: (
            member_columns(blocks).reshape(piece, -1),
            own.astype(wide) + sum(part.astype(wide) for part in parts),
        ),
        (query_blocks, output_sends[0], output_z1, output_z2, output_z3),
    )
    small = small + small_c
    key_blocks = [key_parts[0], key_near[0], key_far[0], key_near[1]]

    def finish(up, ups, key_blocks, base, pair, back, far, z1, z2, z3):
        router = sum(block[piece : piece + extra_rows].astype(wide) for block in key_blocks)
        mixed = base + added(pair, back, 0) + far.astype(wide) + z1.astype(wide)
        mixed = mixed + z2.astype(wide) + z3.astype(wide)
        return (
            joined(up, ups),
            member_columns([block[:piece] for block in key_blocks]),
            router.reshape(piece, experts_all),
            mixed.astype(low),
        )

    small_z, results, _ = step(
        [(small, "z", k) for k in range(1, nz)],
        finish,
        (
            up_grad,
            [up0, up1],
            key_blocks,
            mixed_attn,
            mixed0,
            mixed_back0,
            mixed_far0,
            mixed_z1,
            mixed_z2,
            mixed_z3,
        ),
    )
    up_grad, key_grads, router_grad, mixed = results
    gains = (small + sum(small_z)).reshape(-1)
    key_grad = key_grads[..., :HEAD_SIZE].reshape(piece, -1)
    value_grad = key_grads[..., HEAD_SIZE:].reshape(piece, -1)
    return (
        mixed,
        d_tokens,
        gains[:model],
        gains[model : 2 * model],
        gains[2 * model : 2 * model + HEAD_SIZE],
        gains[2 * model + HEAD_SIZE :],
        query_grad,
        key_grad,
        value_grad,
        output_grad,
        router_grad,
        gate_grad,
        up_grad,
        down_grad,
    )


def solution(mesh):
    contexts, pairs = mesh.shape["ctx"], mesh.shape["fsdp"]
    planes = contexts // MEMBERS
    if planes == KEY_VALUE_HEADS and pairs * MEMBERS * KEY_VALUE_HEADS == QUERY_HEADS:
        layer, every, split = member_layer, ("z", "y", "c", "x"), ("z", "y", "c")
        pair = "x"
        mesh = Mesh(mesh.devices.reshape(planes, 2, 2, pairs), every)
    else:
        layer, every, split, pair = routed_layer, ("ctx", "fsdp"), "ctx", "fsdp"
    by_row = P(every, None)
    by_expert = P(split, pair, None)
    return jax.shard_map(
        layer,
        mesh=mesh,
        in_specs=(by_row,) * 3 + (P(),) * 4 + (by_row,) * 5 + (by_expert,) * 3,
        out_specs=(by_row,) * 2 + (P(),) * 4 + (by_row,) * 5 + (by_expert,) * 3,
        check_vma=False,
    )
```

```python
import functools
import math

import jax
import jax.numpy as jnp
from jax import lax
from jax.experimental import pallas as pl
from jax.experimental.pallas import tpu as pltpu
from jax.sharding import Mesh
from jax.sharding import PartitionSpec as P

QUERY_HEADS = 32
KEY_VALUE_HEADS = 4
HEAD_SIZE = 128
TOP = 8
LOCAL_SEQUENCES = 3


EPS = 1e-06
THETA = 1000000.0
NEGATIVE_LIMIT = -1e30


def shard_positions(device, context_count, block_len):
    within = jnp.arange(2 * block_len, dtype=jnp.int32)
    lower_pos = device * block_len + within
    upper_pos = (2 * context_count - 1 - device) * block_len + within - block_len
    return jnp.where(within < block_len, lower_pos, upper_pos)


def group_positions(first_dev, query_group_size, context_count, block_len):
    devices = first_dev + jnp.arange(query_group_size, dtype=jnp.int32)
    return jax.vmap(lambda device: shard_positions(device, context_count, block_len))(
        devices
    ).reshape(-1)


def rotary(positions, head_width):
    half_width = head_width // 2
    frequency = jnp.exp(
        -math.log(THETA) * (2.0 * jnp.arange(half_width, dtype=jnp.float32)) / head_width
    )
    angles = positions.astype(jnp.float32)[:, None] * frequency[None, :]
    angles = jnp.concatenate([angles, angles], -1)
    return (jnp.cos(angles)[:, None, :], jnp.sin(angles)[:, None, :])


def rope_apply(value_rows_list, cosine, sine_tab):
    half_width = value_rows_list.shape[-1] // 2
    turned = jnp.concatenate(
        [-value_rows_list[..., half_width:], value_rows_list[..., :half_width]], -1
    )
    return value_rows_list * cosine + turned * sine_tab


def rope_back(upstream, cosine, sine_tab):
    half_width = upstream.shape[-1] // 2
    moved_part = upstream * sine_tab
    return upstream * cosine + jnp.concatenate(
        [moved_part[..., half_width:], -moved_part[..., :half_width]], -1
    )


def rms_apply(value_rows_list, gain_vec):
    inverse = lax.rsqrt(jnp.mean(value_rows_list * value_rows_list, -1, keepdims=True) + EPS)
    return (value_rows_list * inverse * gain_vec, inverse)


def rms_back(value_rows_list, inverse, gain_vec, upstream):
    normalized_input = value_rows_list * inverse
    gain_part = jnp.sum((upstream * normalized_input).reshape(-1, value_rows_list.shape[-1]), 0)
    scaled = upstream * gain_vec
    back_part = inverse * (
        scaled - normalized_input * jnp.mean(scaled * normalized_input, -1, keepdims=True)
    )
    return (back_part, gain_part)


def arrange(blocks):
    query_group_size, seq_count, paired_rows, heads_kv, head_dim = blocks.shape
    return blocks.transpose(1, 0, 2, 3, 4).reshape(
        seq_count, query_group_size * paired_rows, heads_kv, head_dim
    )


def unarrange(rows_all, query_group_size):
    seq_count, width_all, heads_kv, head_dim = rows_all.shape
    return rows_all.reshape(
        seq_count, query_group_size, width_all // query_group_size, heads_kv, head_dim
    ).transpose(1, 0, 2, 3, 4)


def attend_group(state_now, queries, key_row_matrix, value_rows, query_pos, key_pos, score_scale):
    run_max, run_sum, run_acc = state_now
    scores = (
        jnp.einsum("skgqd,swkd->skgqw", queries, key_row_matrix, preferred_element_type=jnp.float32)
        * score_scale
    )
    allowed = key_pos[None, :] <= query_pos[:, None]
    new_max = jnp.maximum(run_max, jnp.max(jnp.where(allowed, scores, NEGATIVE_LIMIT), -1))
    weights_now = jnp.where(allowed, jnp.exp(scores - new_max[..., None]), 0.0)
    factor = jnp.exp(run_max - new_max)
    new_sum = run_sum * factor + jnp.sum(weights_now, -1)
    update = jnp.einsum(
        "skgqw,swkd->skgqd",
        weights_now.astype(jnp.bfloat16),
        value_rows,
        preferred_element_type=jnp.float32,
    )
    return (new_max, new_sum, run_acc * factor[..., None] + update)


def routed_layer(
    tokens,
    cotangent,
    expert_ids,
    attention_gain,
    ffn_gain,
    query_gain,
    key_gain,
    w_query,
    key_weight,
    value_weight,
    w_output,
    w_router,
    w_gate,
    w_up,
    w_down,
):
    context_count = lax.axis_size("ctx")
    ctx_here = lax.axis_index("ctx")
    token_per_device = tokens.shape[0]
    block_len = token_per_device // (2 * LOCAL_SEQUENCES)
    paired_rows = 2 * block_len
    query_groups = QUERY_HEADS // KEY_VALUE_HEADS
    score_scale = 1.0 / math.sqrt(HEAD_SIZE)
    experts_all = w_router.shape[1]
    exp_dev = w_gate.shape[0]
    cap_rows = token_per_device * TOP * 5 // (4 * experts_all)
    routes = token_per_device * TOP
    inputs = tokens.astype(jnp.float32)
    normed_attn, inverse_attn = rms_apply(inputs, attention_gain)
    normed_low = normed_attn.astype(jnp.bfloat16)
    query_all, key_all, value_all, output_all, router_all = (
        lax.all_gather(w_query, ("ctx", "fsdp"), axis=0, tiled=True),
        lax.all_gather(key_weight, ("ctx", "fsdp"), axis=0, tiled=True),
        lax.all_gather(value_weight, ("ctx", "fsdp"), axis=0, tiled=True),
        lax.all_gather(w_output, ("ctx", "fsdp"), axis=0, tiled=True),
        lax.all_gather(w_router, ("ctx", "fsdp"), axis=0, tiled=True),
    )
    local_pos = shard_positions(ctx_here, context_count, block_len)
    row_pos = jnp.tile(local_pos, LOCAL_SEQUENCES)
    cosine, sine_tab = rotary(row_pos, HEAD_SIZE)
    query_proj = jnp.dot(normed_low, query_all, preferred_element_type=jnp.float32).reshape(
        token_per_device, QUERY_HEADS, HEAD_SIZE
    )
    key_proj = jnp.dot(normed_low, key_all, preferred_element_type=jnp.float32).reshape(
        token_per_device, KEY_VALUE_HEADS, HEAD_SIZE
    )
    value_proj = jnp.dot(normed_low, value_all, preferred_element_type=jnp.float32).reshape(
        token_per_device, KEY_VALUE_HEADS, HEAD_SIZE
    )
    query_normed, query_inverse = rms_apply(query_proj, query_gain)
    key_normed, key_inverse = rms_apply(key_proj, key_gain)
    query_lower = rope_apply(query_normed, cosine, sine_tab).astype(jnp.bfloat16)
    key_low = rope_apply(key_normed, cosine, sine_tab).astype(jnp.bfloat16)
    value_low = value_proj.astype(jnp.bfloat16)
    query_head_rows = query_lower.reshape(
        LOCAL_SEQUENCES, paired_rows, KEY_VALUE_HEADS, query_groups, HEAD_SIZE
    ).transpose(0, 2, 3, 1, 4)
    initial = (
        jnp.full(
            (LOCAL_SEQUENCES, KEY_VALUE_HEADS, query_groups, paired_rows),
            NEGATIVE_LIMIT,
            jnp.float32,
        ),
        jnp.zeros((LOCAL_SEQUENCES, KEY_VALUE_HEADS, query_groups, paired_rows), jnp.float32),
        jnp.zeros(
            (LOCAL_SEQUENCES, KEY_VALUE_HEADS, query_groups, paired_rows, HEAD_SIZE), jnp.float32
        ),
    )
    key_every, value_every = (
        lax.all_gather(key_low, "ctx", axis=0, tiled=True),
        lax.all_gather(value_low, "ctx", axis=0, tiled=True),
    )
    shard_total_count = key_every.shape[0] // token_per_device
    fold_query_group_size = 4
    key_block_list = key_every.reshape(
        shard_total_count // fold_query_group_size,
        fold_query_group_size,
        LOCAL_SEQUENCES,
        paired_rows,
        KEY_VALUE_HEADS,
        HEAD_SIZE,
    )
    value_block_list = value_every.reshape(
        shard_total_count // fold_query_group_size,
        fold_query_group_size,
        LOCAL_SEQUENCES,
        paired_rows,
        KEY_VALUE_HEADS,
        HEAD_SIZE,
    )
    first_devs = 0 // token_per_device + fold_query_group_size * jnp.arange(
        shard_total_count // fold_query_group_size, dtype=jnp.int32
    )

    def one_group(state_in, loop_item):
        key_group, value_group, first_dev = loop_item
        key_pos = group_positions(first_dev, fold_query_group_size, context_count, block_len)
        return (
            attend_group(
                state_in,
                query_head_rows,
                arrange(key_group),
                arrange(value_group),
                local_pos,
                key_pos,
                score_scale,
            ),
            None,
        )

    state_out, unused = lax.scan(one_group, initial, (key_block_list, value_block_list, first_devs))
    run_max, run_sum, run_acc = state_out
    log_sum = run_max + jnp.log(run_sum)
    attended = run_acc / run_sum[..., None]
    attended_low = (
        attended.transpose(0, 3, 1, 2, 4)
        .reshape(token_per_device, QUERY_HEADS * HEAD_SIZE)
        .astype(jnp.bfloat16)
    )
    mixed_attn = inputs + jnp.dot(attended_low, output_all, preferred_element_type=jnp.float32)
    normed_ffn, inverse_ffn = rms_apply(mixed_attn, ffn_gain)
    ffn_low = normed_ffn.astype(jnp.bfloat16)
    logits = jnp.dot(ffn_low, router_all, preferred_element_type=jnp.float32)
    chosen = (expert_ids[..., None] == jnp.arange(experts_all, dtype=jnp.int32)).astype(jnp.float32)
    picked = jnp.einsum("tje,te->tj", chosen, logits, precision=lax.Precision.HIGHEST)
    gate_probs = jax.nn.softmax(picked, -1)
    flat_ids = expert_ids.reshape(-1)
    route_marks = (flat_ids[:, None] == jnp.arange(experts_all, dtype=jnp.int32)).astype(jnp.int32)
    route_ranks = jnp.sum((jnp.cumsum(route_marks, 0) - 1) * route_marks, -1)
    slot_of_route = flat_ids * cap_rows + route_ranks
    route_of_slot = (
        jnp.full((experts_all * cap_rows,), routes, jnp.int32)
        .at[slot_of_route]
        .set(jnp.arange(routes, dtype=jnp.int32))
    )
    padded = jnp.concatenate([ffn_low, jnp.zeros((1, ffn_low.shape[1]), jnp.bfloat16)], 0)
    outgoing = padded[route_of_slot // TOP].reshape(experts_all, cap_rows, -1)
    arrived = lax.all_to_all(outgoing, "ctx", split_axis=0, concat_axis=0, tiled=True)

    def to_experts(buffer):
        return (
            buffer.reshape(context_count, exp_dev, cap_rows, -1)
            .transpose(1, 0, 2, 3)
            .reshape(exp_dev, context_count * cap_rows, -1)
        )

    def from_experts(buffer):
        return (
            buffer.reshape(exp_dev, context_count, cap_rows, -1)
            .transpose(1, 0, 2, 3)
            .reshape(context_count * exp_dev, cap_rows, -1)
        )

    expert_rows = to_experts(arrived)
    gate_all, up_all, down_all = (
        lax.all_gather(w_gate, "fsdp", axis=1, tiled=True),
        lax.all_gather(w_up, "fsdp", axis=1, tiled=True),
        lax.all_gather(w_down, "fsdp", axis=1, tiled=True),
    )
    gate_part = jnp.einsum(
        "esd,edf->esf", expert_rows, gate_all, preferred_element_type=jnp.float32
    )
    up_part = jnp.einsum("esd,edf->esf", expert_rows, up_all, preferred_element_type=jnp.float32)
    sigmoid_gate = jax.nn.sigmoid(gate_part)
    silu_gate = gate_part * sigmoid_gate
    hidden_low = (silu_gate * up_part).astype(jnp.bfloat16)
    results = jnp.einsum(
        "esf,efd->esd", hidden_low, down_all, preferred_element_type=jnp.float32
    ).astype(jnp.bfloat16)
    returned = lax.all_to_all(from_experts(results), "ctx", split_axis=0, concat_axis=0, tiled=True)
    route_out = returned.reshape(experts_all * cap_rows, -1)[slot_of_route].reshape(
        token_per_device, TOP, -1
    )
    mixed = (mixed_attn + jnp.sum(gate_probs[..., None] * route_out, 1)).astype(jnp.bfloat16)
    query_back, key_back, value_back, output_back, router_back = (
        lax.all_gather(w_query, ("ctx", "fsdp"), axis=0, tiled=True),
        lax.all_gather(key_weight, ("ctx", "fsdp"), axis=0, tiled=True),
        lax.all_gather(value_weight, ("ctx", "fsdp"), axis=0, tiled=True),
        lax.all_gather(w_output, ("ctx", "fsdp"), axis=0, tiled=True),
        lax.all_gather(w_router, ("ctx", "fsdp"), axis=0, tiled=True),
    )
    upstream = cotangent.astype(jnp.float32)
    dgates = jnp.sum(upstream[:, None, :] * route_out, -1)
    dpicked = gate_probs * (dgates - jnp.sum(gate_probs * dgates, -1, keepdims=True))
    dlogits_low = jnp.einsum("tj,tje->te", dpicked, chosen, precision=lax.Precision.HIGHEST).astype(
        jnp.bfloat16
    )
    router_grad = jnp.einsum("td,te->de", ffn_low, dlogits_low, preferred_element_type=jnp.float32)
    dresults = (
        (gate_probs[..., None] * upstream[:, None, :]).astype(jnp.bfloat16).reshape(routes, -1)
    )
    dresults = jnp.concatenate([dresults, jnp.zeros((1, dresults.shape[1]), jnp.bfloat16)], 0)
    dreturned = lax.all_to_all(
        dresults[route_of_slot].reshape(experts_all, cap_rows, -1),
        "ctx",
        split_axis=0,
        concat_axis=0,
        tiled=True,
    )
    dresult_rows = to_experts(dreturned)
    dhidden = jnp.einsum("esd,efd->esf", dresult_rows, down_all, preferred_element_type=jnp.float32)
    down_grad = jnp.einsum(
        "esf,esd->efd", hidden_low, dresult_rows, preferred_element_type=jnp.float32
    )
    dsilu_gate = sigmoid_gate * (1.0 + gate_part * (1.0 - sigmoid_gate))
    dgate_low = (dhidden * up_part * dsilu_gate).astype(jnp.bfloat16)
    dup_low = (dhidden * silu_gate).astype(jnp.bfloat16)
    gate_grad = jnp.einsum(
        "esd,esf->edf", expert_rows, dgate_low, preferred_element_type=jnp.float32
    )
    up_grad = jnp.einsum("esd,esf->edf", expert_rows, dup_low, preferred_element_type=jnp.float32)
    dexpert_rows = (
        jnp.einsum("esf,edf->esd", dgate_low, gate_all, preferred_element_type=jnp.float32)
        + jnp.einsum("esf,edf->esd", dup_low, up_all, preferred_element_type=jnp.float32)
    ).astype(jnp.bfloat16)
    dsent_rows = lax.all_to_all(
        from_experts(dexpert_rows), "ctx", split_axis=0, concat_axis=0, tiled=True
    )
    droutes = dsent_rows.reshape(experts_all * cap_rows, -1)[slot_of_route].reshape(
        token_per_device, TOP, -1
    )
    dffn_rows = jnp.sum(droutes.astype(jnp.float32), 1) + jnp.einsum(
        "te,de->td", dlogits_low, router_back, preferred_element_type=jnp.float32
    )
    expert_sums = (
        lax.psum_scatter(
            gate_grad.astype(jnp.bfloat16), "fsdp", scatter_dimension=1, tiled=True
        ).astype(jnp.float32),
        lax.psum_scatter(
            up_grad.astype(jnp.bfloat16), "fsdp", scatter_dimension=1, tiled=True
        ).astype(jnp.float32),
        lax.psum_scatter(
            down_grad.astype(jnp.bfloat16), "fsdp", scatter_dimension=1, tiled=True
        ).astype(jnp.float32),
    )
    dmixed_norm, ffn_gain_part = rms_back(mixed_attn, inverse_ffn, ffn_gain, dffn_rows)
    dmixed_attn = upstream + dmixed_norm
    dattn_low = dmixed_attn.astype(jnp.bfloat16)
    output_grad = jnp.einsum(
        "tc,td->cd", attended_low, dattn_low, preferred_element_type=jnp.float32
    )
    attended_lower_grad = jnp.einsum(
        "td,cd->tc", dattn_low, output_back, preferred_element_type=jnp.float32
    ).astype(jnp.bfloat16)
    output_heads_grad = attended_lower_grad.reshape(
        LOCAL_SEQUENCES, paired_rows, KEY_VALUE_HEADS, query_groups, HEAD_SIZE
    ).transpose(0, 2, 3, 1, 4)
    delta_row = jnp.sum(output_heads_grad.astype(jnp.float32) * attended, -1)
    key_recomputed, value_recomputed = (key_every, value_every)

    def score_grads(key_group, value_group, first_dev, query_group_size):
        key_row_matrix = arrange(key_group)
        value_rows = arrange(value_group)
        key_pos = group_positions(first_dev, query_group_size, context_count, block_len)
        scores = (
            jnp.einsum(
                "skgqd,swkd->skgqw",
                query_head_rows,
                key_row_matrix,
                preferred_element_type=jnp.float32,
            )
            * score_scale
        )
        allowed = key_pos[None, :] <= local_pos[:, None]
        weights_now = jnp.where(allowed, jnp.exp(scores - log_sum[..., None]), 0.0)
        dweights = jnp.einsum(
            "skgqd,swkd->skgqw", output_heads_grad, value_rows, preferred_element_type=jnp.float32
        )
        dscores = (weights_now * (dweights - delta_row[..., None])).astype(jnp.bfloat16)
        return (key_row_matrix, weights_now, dscores)

    def key_terms(weights_now, dscores, query_group_size):
        dkey_rows = jnp.einsum(
            "skgqw,skgqd->swkd", dscores, query_head_rows, preferred_element_type=jnp.float32
        )
        dvalue_rows = jnp.einsum(
            "skgqw,skgqd->swkd",
            weights_now.astype(jnp.bfloat16),
            output_heads_grad,
            preferred_element_type=jnp.float32,
        )
        return (unarrange(dkey_rows, query_group_size), unarrange(dvalue_rows, query_group_size))

    query_group_size = 4
    loop_step_count = context_count // query_group_size
    key_block_list = key_recomputed.reshape(
        loop_step_count, query_group_size, LOCAL_SEQUENCES, paired_rows, KEY_VALUE_HEADS, HEAD_SIZE
    )
    value_block_list = value_recomputed.reshape(
        loop_step_count, query_group_size, LOCAL_SEQUENCES, paired_rows, KEY_VALUE_HEADS, HEAD_SIZE
    )
    first_devs = query_group_size * jnp.arange(loop_step_count, dtype=jnp.int32)

    def back_group(dquery_acc, loop_item):
        key_group, value_group, first_dev = loop_item
        key_row_matrix, weights_now, dscores = score_grads(
            key_group, value_group, first_dev, query_group_size
        )
        dquery_acc = dquery_acc + jnp.einsum(
            "skgqw,swkd->skgqd", dscores, key_row_matrix, preferred_element_type=jnp.float32
        )
        return (dquery_acc, key_terms(weights_now, dscores, query_group_size))

    dquery_heads, key_value_pieces = lax.scan(
        back_group,
        jnp.zeros(query_head_rows.shape, jnp.float32),
        (key_block_list, value_block_list, first_devs),
    )
    key_grad_every = key_value_pieces[0].reshape(
        context_count * token_per_device, KEY_VALUE_HEADS, HEAD_SIZE
    )
    value_grad_every = key_value_pieces[1].reshape(
        context_count * token_per_device, KEY_VALUE_HEADS, HEAD_SIZE
    )
    dkey_own, value_local_grad = (
        lax.psum_scatter(key_grad_every, "ctx", scatter_dimension=0, tiled=True),
        lax.psum_scatter(value_grad_every, "ctx", scatter_dimension=0, tiled=True),
    )
    dquery = (
        (dquery_heads * score_scale)
        .transpose(0, 3, 1, 2, 4)
        .reshape(token_per_device, QUERY_HEADS, HEAD_SIZE)
    )
    dquery_proj, query_gain_part = rms_back(
        query_proj, query_inverse, query_gain, rope_back(dquery, cosine, sine_tab)
    )
    key_projection_grad, key_gain_part = rms_back(
        key_proj, key_inverse, key_gain, rope_back(dkey_own * score_scale, cosine, sine_tab)
    )
    dquery_low = dquery_proj.reshape(token_per_device, QUERY_HEADS * HEAD_SIZE).astype(jnp.bfloat16)
    key_lower_grad = key_projection_grad.reshape(
        token_per_device, KEY_VALUE_HEADS * HEAD_SIZE
    ).astype(jnp.bfloat16)
    value_lower_grad = value_local_grad.reshape(
        token_per_device, KEY_VALUE_HEADS * HEAD_SIZE
    ).astype(jnp.bfloat16)
    query_grad = jnp.einsum("td,tc->dc", normed_low, dquery_low, preferred_element_type=jnp.float32)
    key_grad = jnp.einsum(
        "td,tc->dc", normed_low, key_lower_grad, preferred_element_type=jnp.float32
    )
    value_grad = jnp.einsum(
        "td,tc->dc", normed_low, value_lower_grad, preferred_element_type=jnp.float32
    )
    dnormed = jnp.einsum("tc,dc->td", dquery_low, query_back, preferred_element_type=jnp.float32)
    dnormed = dnormed + jnp.einsum(
        "tc,dc->td", key_lower_grad, key_back, preferred_element_type=jnp.float32
    )
    dnormed = dnormed + jnp.einsum(
        "tc,dc->td", value_lower_grad, value_back, preferred_element_type=jnp.float32
    )
    dinput_norm, attention_gain_part = rms_back(inputs, inverse_attn, attention_gain, dnormed)
    d_tokens = (dmixed_attn + dinput_norm).astype(jnp.bfloat16)
    gain_sums = lax.psum(
        (attention_gain_part, ffn_gain_part, query_gain_part, key_gain_part), ("ctx", "fsdp")
    )
    layer_sums = (
        lax.psum_scatter(query_grad, ("ctx", "fsdp"), scatter_dimension=0, tiled=True),
        lax.psum_scatter(key_grad, ("ctx", "fsdp"), scatter_dimension=0, tiled=True),
        lax.psum_scatter(value_grad, ("ctx", "fsdp"), scatter_dimension=0, tiled=True),
        lax.psum_scatter(output_grad, ("ctx", "fsdp"), scatter_dimension=0, tiled=True),
        lax.psum_scatter(router_grad, ("ctx", "fsdp"), scatter_dimension=0, tiled=True),
    )
    return (
        mixed,
        d_tokens,
        gain_sums[0],
        gain_sums[1],
        gain_sums[2],
        gain_sums[3],
        layer_sums[0],
        layer_sums[1],
        layer_sums[2],
        layer_sums[3],
        layer_sums[4],
        expert_sums[0],
        expert_sums[1],
        expert_sums[2],
    )


MEMBERS = 4


def shift(block, axis, step):
    count = lax.axis_size(axis)
    return lax.ppermute(block, axis, [(i, (i + step) % count) for i in range(count)])


def swap(block, axis):
    return lax.ppermute(block, axis, [(0, 1), (1, 0)])


def after(block, *earlier):
    return lax.optimization_barrier((block,) + earlier)[0]


class Steps:
    def __init__(self):
        self.mark = None

    def __call__(self, sends, work=None, given=(), join=()):
        blocks = tuple(send[0] for send in sends)
        mark = () if self.mark is None else (self.mark,)
        blocks, given, mark = lax.optimization_barrier((blocks, tuple(given), mark))
        moved = tuple(
            swap(block, send[1]) if len(send) == 2 else shift(block, send[1], send[2])
            for block, send in zip(blocks, sends)
        )
        done = () if work is None else work(*given)
        moved, done, join, mark = lax.optimization_barrier((moved, done, tuple(join), mark))
        self.mark = jax.tree.leaves((moved, done, join))[0]
        return moved, done, join


def pick(stack, index):
    return lax.dynamic_index_in_dim(stack, index, 0, keepdims=False)


def roped(raw, gain, cosine, sine):
    inverse = lax.rsqrt(jnp.mean(raw * raw, -1, keepdims=True) + EPS)
    scaled = raw * inverse * gain
    return scaled * cosine + pltpu.roll(scaled, HEAD_SIZE // 2, 1) * sine


def split_heads(ref, start, heads):
    size = ref.shape[2] // 2
    rows = ref[:, 0, start * size : (start + 1) * size, :]
    rows = rows.reshape(ref.shape[0] * size, ref.shape[3])
    return jnp.concatenate(
        [rows[:, i * HEAD_SIZE : (i + 1) * HEAD_SIZE] for i in range(heads)], 0
    )


def key_half(ref, k, start):
    size = ref.shape[3] // 2
    rows = ref[k, :, 0, start * size : (start + 1) * size, :]
    return rows.reshape(ref.shape[1] * size, HEAD_SIZE)


def twice(rows):
    return jnp.concatenate([rows, rows], 0)


ACROSS = (((1,), (1,)), ((), ()))
DOWN = (((0,), (0,)), ((), ()))


def score_blocks(z_here, queries, k_ref):
    nz = k_ref.shape[0]
    low_q, high_q = queries
    low_keys = jnp.concatenate([key_half(k_ref, k, 0) for k in range(nz)], 0)
    blocks = [(low_keys, high_q, None)]
    for k in range(1, nz):
        before = z_here >= k
        keys = jnp.where(before, key_half(k_ref, k, 0), key_half(k_ref, k, 1))
        blocks.append((keys, jnp.where(before, low_q, high_q), before))
    blocks.append((key_half(k_ref, 0, 0), low_q, None))
    blocks.append((key_half(k_ref, 0, 1), high_q, None))
    return blocks


def value_blocks(z_here, ref):
    nz = ref.shape[0]
    blocks = [jnp.concatenate([key_half(ref, k, 0) for k in range(nz)], 0)]
    for k in range(1, nz):
        blocks.append(jnp.where(z_here >= k, key_half(ref, k, 0), key_half(ref, k, 1)))
    return blocks + [key_half(ref, 0, 0), key_half(ref, 0, 1)]


def to_halves(parts, blocks):
    low_sum, high_sum = parts[-2], parts[0] + parts[-1]
    for part, (_, _, before) in zip(parts[1:-2], blocks[1:-2]):
        low_sum = low_sum + jnp.where(before, part, 0.0)
        high_sum = high_sum + jnp.where(before, 0.0, part)
    return low_sum, high_sum


def of_halves(low_row, high_row, blocks):
    rows = [high_row]
    rows += [jnp.where(before, low_row, high_row) for _, _, before in blocks[1:-2]]
    return rows + [low_row, high_row]


def weigh(blocks, mask_ref):
    exponent = math.log2(math.e) / math.sqrt(HEAD_SIZE)
    weights = []
    for keys, queries, _ in blocks:
        scores = lax.dot_general(keys, queries, ACROSS, preferred_element_type=jnp.float32)
        weights.append(jnp.exp2(scores * exponent))
    weights[-2] = weights[-2] * mask_ref[0]
    weights[-1] = weights[-1] * mask_ref[1]
    return weights


def attend_kernel(places_ref, q_ref, k_ref, v_ref, cos_ref, sin_ref, gain_ref, mask_ref, out_ref):
    count = q_ref.shape[3] // HEAD_SIZE
    size = q_ref.shape[2] // 2
    queries = []
    for half in range(2):
        raw = split_heads(q_ref, half, count)
        queries.append(
            roped(raw, gain_ref[...], twice(cos_ref[half]), twice(sin_ref[half])).astype(
                jnp.bfloat16
            )
        )
    z_here = places_ref[1]
    blocks = score_blocks(z_here, queries, k_ref)
    weights = weigh(blocks, mask_ref)
    totals = to_halves([jnp.sum(weight, 0, keepdims=True) for weight in weights], blocks)
    mixed = [
        lax.dot_general(
            values, weight.astype(jnp.bfloat16), DOWN, preferred_element_type=jnp.float32
        )
        for values, weight in zip(value_blocks(z_here, v_ref), weights)
    ]
    mixed = to_halves(mixed, blocks)
    for half in range(2):
        out = (mixed[half] / totals[half]).T.astype(jnp.bfloat16)
        rows = out.shape[0] // count
        for i in range(count):
            out_ref[:, 0, half * size : (half + 1) * size, i * HEAD_SIZE : (i + 1) * HEAD_SIZE] = (
                out[i * rows : (i + 1) * rows].reshape(-1, size, HEAD_SIZE)
            )


def attend_back_kernel(
    places_ref,
    q_ref,
    up_ref,
    k_ref,
    v_ref,
    cos_ref,
    sin_ref,
    gain_ref,
    mask_ref,
    dq_ref,
    dkv_ref,
    dgain_ref,
):
    nz = k_ref.shape[0]
    count = q_ref.shape[3] // HEAD_SIZE
    size = q_ref.shape[2] // 2
    low = jnp.bfloat16
    score_scale = 1.0 / math.sqrt(HEAD_SIZE)
    gain = gain_ref[...]
    z_here = places_ref[1]
    raws, queries, ups = [], [], []
    for half in range(2):
        raw = split_heads(q_ref, half, count)
        raws.append(raw)
        queries.append(roped(raw, gain, twice(cos_ref[half]), twice(sin_ref[half])).astype(low))
        ups.append(split_heads(up_ref, half, count))
    blocks = score_blocks(z_here, queries, k_ref)
    weights = weigh(blocks, mask_ref)
    totals = to_halves([jnp.sum(weight, 0, keepdims=True) for weight in weights], blocks)
    inverses = [1.0 / total for total in totals]
    block_ups = [ups[1]]
    block_ups += [jnp.where(before, ups[0], ups[1]) for _, _, before in blocks[1:-2]]
    block_ups += ups
    dprobs = [
        lax.dot_general(values, up, ACROSS, preferred_element_type=jnp.float32)
        for values, up in zip(value_blocks(z_here, v_ref), block_ups)
    ]
    probs = [
        weight * inverse
        for weight, inverse in zip(weights, of_halves(inverses[0], inverses[1], blocks))
    ]
    deltas = to_halves(
        [jnp.sum(p * d, 0, keepdims=True) for p, d in zip(probs, dprobs)], blocks
    )
    dscores = [
        (p * (d - delta)).astype(low)
        for p, d, delta in zip(probs, dprobs, of_halves(deltas[0], deltas[1], blocks))
    ]
    dvs = [
        jnp.dot(p.astype(low), up, preferred_element_type=jnp.float32)
        for p, up in zip(probs, block_ups)
    ]
    dks = [
        jnp.dot(d, block[1], preferred_element_type=jnp.float32) * score_scale
        for d, block in zip(dscores, blocks)
    ]
    dqs = [
        lax.dot_general(block[0], d, DOWN, preferred_element_type=jnp.float32)
        for d, block in zip(dscores, blocks)
    ]
    dqs = to_halves(dqs, blocks)
    each = dks[-1].shape[0]
    fresh = pl.program_id(1) == 0
    for k in range(nz):
        both = [
            jnp.concatenate([dk, dv], 1)
            for dk, dv in (
                (dks[0][k * each : (k + 1) * each], dvs[0][k * each : (k + 1) * each]),
                (dks[k], dvs[k]) if k > 0 else (dks[-2], dvs[-2]),
            )
        ]
        if k == 0:
            halves = (both[0] + both[1], jnp.concatenate([dks[-1], dvs[-1]], 1))
        else:
            before = z_here >= k
            halves = (
                both[0] + jnp.where(before, both[1], 0.0),
                jnp.where(before, 0.0, both[1]),
            )
        for half in range(2):
            part = slice(half * size, (half + 1) * size)
            earlier = jnp.where(fresh, 0.0, dkv_ref[k, :, 0, part, :])
            dkv_ref[k, :, 0, part, :] = earlier + halves[half].reshape(-1, size, 2 * HEAD_SIZE)

    gain_part = jnp.zeros((1, HEAD_SIZE), jnp.float32)
    for half in range(2):
        cosine, sine = twice(cos_ref[half]), twice(sin_ref[half])
        raw = raws[half]
        inverse = lax.rsqrt(jnp.mean(raw * raw, -1, keepdims=True) + EPS)
        unit = raw * inverse
        dq = dqs[half].T * score_scale
        turned = dq * cosine - pltpu.roll(dq, HEAD_SIZE // 2, 1) * sine
        gain_part = gain_part + jnp.sum(turned * unit, 0, keepdims=True)
        turned = turned * gain
        back = inverse * (turned - unit * jnp.mean(turned * unit, -1, keepdims=True))
        back = back.astype(low)
        rows = back.shape[0] // count
        for i in range(count):
            dq_ref[:, 0, half * size : (half + 1) * size, i * HEAD_SIZE : (i + 1) * HEAD_SIZE] = (
                back[i * rows : (i + 1) * rows].reshape(-1, size, HEAD_SIZE)
            )
    gain_part = jnp.concatenate([gain_part, jnp.zeros((7, HEAD_SIZE), jnp.float32)], 0)
    first = fresh & (pl.program_id(0) == 0)
    dgain_ref[...] = jnp.where(first, 0.0, dgain_ref[...]) + gain_part


def attention_specs(q, kv, mask):
    nz, members, sequences, paired, _ = kv.shape
    pair = q.shape[-1] // MEMBERS
    q_block = (members, 1, paired, pair)
    kv_block = (nz, members, 1, paired, HEAD_SIZE)
    own = pl.BlockSpec(q_block, lambda s, r, places: (0, s, 0, r ^ places[0]))
    relative = pl.BlockSpec(q_block, lambda s, r, places: (0, s, 0, r))
    key = pl.BlockSpec(kv_block, lambda s, r, places: (0, 0, s, 0, 0))
    value = pl.BlockSpec(kv_block, lambda s, r, places: (0, 0, s, 0, 1))
    both = pl.BlockSpec(
        (nz, members, 1, paired, 2 * HEAD_SIZE), lambda s, r, places: (0, 0, s, 0, 0)
    )
    fixed = lambda shape: pl.BlockSpec(shape, lambda s, r, places: (0,) * len(shape))
    table = fixed((2, members * paired // 2, HEAD_SIZE))
    tables = [table, table, fixed((1, HEAD_SIZE)), fixed(mask.shape)]
    return own, relative, key, value, both, fixed, tables


def attend(places, q, kv, cosine, sine, gain, mask):
    members, sequences, paired, width = q.shape
    own, relative, key, value, both, fixed, tables = attention_specs(q, kv, mask)
    elements = sequences * width // HEAD_SIZE * members * paired * kv.shape[0] * members * paired
    return pl.pallas_call(
        attend_kernel,
        grid_spec=pltpu.PrefetchScalarGridSpec(
            num_scalar_prefetch=1,
            grid=(sequences, MEMBERS),
            in_specs=[own, key, value] + tables,
            out_specs=relative,
        ),
        out_shape=jax.ShapeDtypeStruct(q.shape, jnp.bfloat16),
        compiler_params=pltpu.CompilerParams(vmem_limit_bytes=40 * 2**20),
        cost_estimate=pl.CostEstimate(
            flops=4 * elements * HEAD_SIZE, bytes_accessed=8 * 2**20, transcendentals=elements
        ),
    )(places, q, kv, kv, cosine, sine, gain, mask)


def attend_back(places, q, up, kv, cosine, sine, gain, mask):
    members, sequences, paired, width = q.shape
    own, relative, key, value, both, fixed, tables = attention_specs(q, kv, mask)
    elements = sequences * width // HEAD_SIZE * members * paired * kv.shape[0] * members * paired
    return pl.pallas_call(
        attend_back_kernel,
        grid_spec=pltpu.PrefetchScalarGridSpec(
            num_scalar_prefetch=1,
            grid=(sequences, MEMBERS),
            in_specs=[own, relative, key, value] + tables,
            out_specs=(own, both, fixed((8, HEAD_SIZE))),
        ),
        out_shape=(
            jax.ShapeDtypeStruct(q.shape, jnp.bfloat16),
            jax.ShapeDtypeStruct(kv.shape, jnp.float32),
            jax.ShapeDtypeStruct((8, HEAD_SIZE), jnp.float32),
        ),
        compiler_params=pltpu.CompilerParams(vmem_limit_bytes=40 * 2**20),
        cost_estimate=pl.CostEstimate(
            flops=10 * elements * HEAD_SIZE, bytes_accessed=16 * 2**20, transcendentals=elements
        ),
    )(places, q, up, kv, kv, cosine, sine, gain, mask)


def dot32(subscripts, left, right):
    return jnp.einsum(subscripts, left, right, preferred_element_type=jnp.float32)


def expert_kernel(*refs):
    scalars_ref, x_refs, c_refs = refs[0], refs[1:5], refs[5:9]
    rank_ref, chosen_ref, router_ref, gate_ref, up_ref, down_ref = refs[9:15]
    rows_ref, hidden_ref, dresults_ref, dgate_ref, dup_ref = refs[-9:-4]
    sent_refs, back_refs = refs[-4:-2], refs[-2:]
    low, wide = jnp.bfloat16, jnp.float32
    blocks = 2
    tokens, model = x_refs[0].shape
    opening = pl.program_id(0) == 0
    slots = rows_ref.shape[2]
    experts_all = router_ref.shape[0]
    across = (((1,), (1,)), ((), ()))
    down = (((0,), (0,)), ((), ()))
    own_expert = scalars_ref[0]
    places, picked, upstream, gates = [], [], [], []
    for block in range(blocks):
        rows = jnp.where(opening, x_refs[block][...], x_refs[2 + block][...])
        slot = lax.broadcasted_iota(jnp.int32, (slots, tokens), 0)
        place = jnp.where(slot == rank_ref[0, block], 1.0, 0.0)
        chosen = chosen_ref[0, block] > 0.5
        logits = lax.dot_general(router_ref[...], rows, across, preferred_element_type=wide)
        highest = jnp.max(jnp.where(chosen, logits, NEGATIVE_LIMIT), 0, keepdims=True)
        raised = jnp.where(chosen, jnp.exp(jnp.minimum(logits - highest, 0.0)), 0.0)
        expert = lax.broadcasted_iota(jnp.int32, (experts_all, tokens), 0)
        mine = jnp.sum(jnp.where(expert == own_expert, raised, 0.0), 0, keepdims=True)
        gate_row = mine / jnp.sum(raised, 0, keepdims=True)
        gates.append(jnp.sum(place * gate_row, 1, keepdims=True))
        place = place.astype(low)
        places.append(place)
        picked.append(jnp.dot(place, rows, preferred_element_type=wide).astype(low))
        cotangent = jnp.where(opening, c_refs[block][...], c_refs[2 + block][...])
        upstream.append(jnp.dot(place, cotangent, preferred_element_type=wide))
    rows = jnp.concatenate(picked, 0)
    upstream = jnp.concatenate(upstream, 0)
    gates = jnp.concatenate(gates, 0)
    gate_part = jnp.dot(rows, gate_ref[...], preferred_element_type=wide)
    up_part = jnp.dot(rows, up_ref[...], preferred_element_type=wide)
    sigmoid_gate = 1.0 / (1.0 + jnp.exp(-gate_part))
    silu_gate = gate_part * sigmoid_gate
    hidden = (silu_gate * up_part).astype(low)
    results = jnp.dot(hidden, down_ref[...], preferred_element_type=wide).astype(low).astype(wide)
    dgates = jnp.sum(upstream * results, 1, keepdims=True)
    scaled = (gates * results).astype(low)
    dresults = (gates * upstream).astype(low)
    dhidden = lax.dot_general(dresults, down_ref[...], across, preferred_element_type=wide)
    dsilu_gate = sigmoid_gate * (1.0 + gate_part * (1.0 - sigmoid_gate))
    dgate_low = (dhidden * up_part * dsilu_gate).astype(low)
    dup_low = (dhidden * silu_gate).astype(low)
    drows = lax.dot_general(dgate_low, gate_ref[...], across, preferred_element_type=wide)
    drows = drows + lax.dot_general(dup_low, up_ref[...], across, preferred_element_type=wide)
    drows = drows.astype(low)
    lane = lax.broadcasted_iota(jnp.int32, (blocks * slots, 128), 1)
    coarse = dgates.astype(low).astype(wide)
    extra = jnp.where(lane == own_expert, coarse, 0.0)
    extra = extra + jnp.where(lane == own_expert + experts_all, dgates - coarse, 0.0)
    extra = extra.astype(low)
    for block in range(blocks):
        part = slice(block * slots, (block + 1) * slots)
        sent_refs[block][0] = lax.dot_general(
            places[block], scaled[part], down, preferred_element_type=wide
        ).astype(low)
        back_refs[block][0, :, :model] = lax.dot_general(
            places[block], drows[part], down, preferred_element_type=wide
        ).astype(low)
        back_refs[block][0, :, model:] = lax.dot_general(
            places[block], extra[part], down, preferred_element_type=wide
        ).astype(low)
        rows_ref[0, block] = rows[part]
        hidden_ref[0, block] = hidden[part]
        dresults_ref[0, block] = dresults[part]
        dgate_ref[0, block] = dgate_low[part]
        dup_ref[0, block] = dup_low[part]


def experts(scalars, x_blocks, c_blocks, ranks, chosen, router, gate, up, down, slots, earlier):
    tokens, model = x_blocks[0].shape
    nz, members = ranks.shape[:2]
    hidden = gate.shape[1]
    low = jnp.bfloat16
    pair = members // 2
    experts_all = router.shape[0]
    whole = lambda array: pl.BlockSpec(
        array.shape, lambda a, s: (0, 0), pipeline_mode=pl.Buffered(1)
    )
    turn = lambda *tail: pl.BlockSpec((1, pair) + tail, lambda a, s: (s[1], a, 0, 0))
    in_specs = [
        *[whole(block) for block in x_blocks],
        *[whole(block) for block in c_blocks],
        turn(1, tokens),
        turn(experts_all, tokens),
        whole(router),
        whole(gate),
        whole(up),
        whole(down),
    ]
    shapes = [(slots, model), (slots, hidden), (slots, model)]
    shapes += [(slots, hidden), (slots, hidden)]
    out_shape = [jax.ShapeDtypeStruct((nz, members) + shape, low) for shape in shapes]
    out_specs = [turn(*shape) for shape in shapes]
    wide_model = model + 128
    for columns in (model, wide_model):
        out_shape += [jax.ShapeDtypeStruct((2, tokens, columns), low)] * 2
        out_specs += [pl.BlockSpec((1, tokens, columns), lambda a, s: (a, 0, 0))] * 2
    aliases = {}
    if earlier:
        in_specs = in_specs + [pl.BlockSpec(memory_space=pl.ANY)] * len(earlier)
        aliases = {15 + i: i for i in range(len(earlier))}
    return pl.pallas_call(
        expert_kernel,
        grid_spec=pltpu.PrefetchScalarGridSpec(
            num_scalar_prefetch=1, grid=(2,), in_specs=in_specs, out_specs=out_specs
        ),
        out_shape=out_shape,
        input_output_aliases=aliases,
        compiler_params=pltpu.CompilerParams(vmem_limit_bytes=58 * 2**20),
        cost_estimate=pl.CostEstimate(
            flops=12 * members * slots * model * hidden,
            bytes_accessed=40 * 2**20,
            transcendentals=2 * members * slots * hidden,
        ),
    )(scalars, *x_blocks, *c_blocks, ranks, chosen, router, gate, up, down, *earlier)


def dot32(subscripts, left, right):
    return jnp.einsum(subscripts, left, right, preferred_element_type=jnp.float32)


def member_layer(
    tokens,
    cotangent,
    expert_ids,
    attention_gain,
    ffn_gain,
    query_gain,
    key_gain,
    w_query,
    key_weight,
    value_weight,
    w_output,
    w_router,
    w_gate,
    w_up,
    w_down,
):
    low, wide = jnp.bfloat16, jnp.float32
    nz = lax.axis_size("z")
    zi, yi, ci, xi = (lax.axis_index(axis) for axis in ("z", "y", "c", "x"))
    member = 2 * yi + ci
    context_count = nz * MEMBERS
    rows, model = tokens.shape
    paired = rows // LOCAL_SEQUENCES
    block_len = paired // 2
    groups = QUERY_HEADS // KEY_VALUE_HEADS
    experts_all = w_router.shape[1]
    around = lambda k: lax.rem(zi + (k % nz), jnp.int32(nz))
    from_z = [around(-k) for k in range(nz)]
    crossed = [member ^ r for r in range(MEMBERS)]
    token_members = member ^ jnp.array([0, 2, 1, 3], jnp.int32)

    def uncrossed(blocks):
        for bit, odd in ((1, ci), (2, yi)):
            blocks = [jnp.where(odd == 0, blocks[r], blocks[r ^ bit]) for r in range(MEMBERS)]
        return jnp.stack(blocks)

    own_expert = zi * MEMBERS + member
    step = Steps()

    piece = w_query.shape[0]
    head_rows = w_output.shape[0]
    query_width = groups * HEAD_SIZE
    third = w_down.shape[1] // 3

    def make_tables(zi, token_members):
        own_pos = jax.vmap(lambda device: shard_positions(device, context_count, block_len))(
            zi * MEMBERS + token_members
        )
        cosine, sine_tab = rotary(own_pos.reshape(-1), HEAD_SIZE)
        row_cosine = cosine.reshape(MEMBERS, 1, paired, HEAD_SIZE)
        row_sine = sine_tab.reshape(MEMBERS, 1, paired, HEAD_SIZE)

        def halves(table):
            table = table.reshape(MEMBERS, 2, block_len, HEAD_SIZE).transpose(1, 0, 2, 3)
            return table.reshape(2, MEMBERS * block_len, HEAD_SIZE)

        half = HEAD_SIZE // 2
        signs = jnp.where(jnp.arange(HEAD_SIZE) < half, -1.0, 1.0)
        kernel_cosine, kernel_sine = halves(row_cosine), halves(row_sine * signs)
        half_pos = own_pos.reshape(MEMBERS, 2, block_len).transpose(1, 0, 2).reshape(2, -1)
        mask = (half_pos[:, :, None] <= half_pos[:, None, :]).astype(wide)
        mask = jnp.concatenate([mask, mask], 2)
        return row_cosine, row_sine, kernel_cosine, kernel_sine, mask

    def make_slots(packed):
        width_small = piece * experts_all
        flat = packed.reshape(nz * 8, -1)
        device = jnp.arange(nz * 8, dtype=jnp.int32)
        source = ((zi - device // 8) % nz) * 8 + ((device & 1) ^ xi) * 4
        source = source + (((device >> 1) & 1) ^ ci) * 2 + (((device >> 2) & 1) ^ yi)
        router = flat[:, :width_small][source].reshape(nz * 8, experts_all, piece)
        router = router.transpose(1, 0, 2).reshape(experts_all, model)
        ids_all = packed.reshape(nz, 2, 2, 2, -1)[:, 0, :, :, width_small:].transpose(0, 2, 1, 3)
        ids_all = ids_all.reshape(nz, MEMBERS, TOP, rows).astype(jnp.int32)
        named = jnp.any(ids_all == own_expert, 2)
        before = (
            jnp.arange(rows, dtype=jnp.int32)[:, None] <= jnp.arange(rows, dtype=jnp.int32)[None, :]
        )
        ranks = dot32("kjs,st->kjt", named.astype(low), before.astype(low)).astype(jnp.int32) - 1
        ranks = jnp.where(named, ranks, -1)[:, :, None, :]
        expert_column = jnp.arange(experts_all, dtype=jnp.int32)[:, None]
        chosen_all = jnp.any(ids_all[:, :, :, None, :] == expert_column, 2).astype(wide)
        return router, ranks, chosen_all

    cap_rows = rows * TOP * 5 // (4 * experts_all)
    slots = -(-cap_rows // 16) * 16

    def prepare(w_query, key_weight, value_weight, w_router, expert_ids):
        columns = jnp.concatenate(
            [w.reshape(piece, KEY_VALUE_HEADS, -1) for w in (w_query, key_weight, value_weight)],
            -1,
        ).transpose(1, 0, 2)
        packed = jnp.concatenate([w_router.T.reshape(-1), expert_ids.T.astype(low).reshape(-1)])
        parts = [pick(columns, crossed[r]) for r in range(MEMBERS)]
        return parts[0], parts[1], jnp.stack(parts[2:]), packed.reshape(-1, 128)

    (plane1,), (part0, part1, parts_far, packed), _ = step(
        [(w_output, "z", 1)],
        prepare,
        (w_query, key_weight, value_weight, w_router, expert_ids),
    )
    width = part0.shape[-1]
    inputs = tokens.astype(wide)

    def first_members(part0, part1, parts_far, tokens):
        far = swap(parts_far, "y")
        near = swap(jnp.stack([part1, far[1]]), "c")
        blocks = [part0, near[0], far[0], near[1]]
        return uncrossed(blocks), rms_apply(tokens.astype(wide), attention_gain)

    (plane3, *small), (ordered, (normed_attn, inverse_attn)), _ = step(
        [(w_output, "z", 3)] + [(packed, "z", k) for k in range(1, nz)],
        first_members,
        (part0, part1, parts_far, tokens),
    )
    packed = jnp.stack([packed] + small)
    normed_low = normed_attn.astype(low)
    held = [ordered]
    over_x = []
    (moved, cross, other, near), _, _ = step(
        [
            (ordered, "z", 1),
            (ordered, "x"),
            (normed_low, "y"),
            (normed_low, "c"),
        ]
    )
    held.append(moved)
    over_x.append(cross)
    (moved, cross, other_near, packed_far, down1), tables, _ = step(
        [
            (ordered, "z", 2),
            (held[1], "x"),
            (other, "c"),
            (packed, "y"),
            (w_down[0, third : 2 * third], "x"),
        ],
        make_tables,
        (zi, token_members),
    )
    row_cosine, row_sine, kernel_cosine, kernel_sine, mask = tables
    held.append(moved)
    over_x.append(cross)
    normed_all = jnp.concatenate([normed_low, other, near, other_near])
    packed = jnp.stack([packed, packed_far], 1)
    (moved, cross, c_near0, packed_near), _, _ = step(
        [(ordered, "z", 3), (held[2], "x"), (cotangent, "c"), (packed, "c")]
    )
    packed = jnp.stack([packed, packed_near], 1)
    held.append(moved)
    over_x.append(cross)
    cut = rows // 2
    gate_cut = w_gate.shape[1] * 5 // 16
    gate_next = w_gate.shape[1] * 9 // 16

    def cut_pieces(own, one, three, gate, down, cotangent):
        gates = (gate[:gate_cut], gate[gate_cut:gate_next], gate[gate_next:])
        halves = (cotangent[:cut], cotangent[cut:])
        return jnp.stack([own, one, one, three]), gates, down[2 * third :], halves

    moved, (planes, gate_pieces, down_piece, c_halves), _ = step(
        [
            (held[3], "x"),
            (w_output, "z", 2),
            (cotangent, "y"),
            (w_down[0, :third], "x"),
            (packed, "x"),
        ],
        cut_pieces,
        (w_output, plane1, plane3, w_gate[0], w_down[0], cotangent),
    )
    cross, plane2, c_far0, down0, packed_cross = moved
    packed = jnp.stack([packed, packed_cross], 1)
    over_x.append(cross)

    def assemble(start, stop):
        full = jnp.zeros((nz, MEMBERS, 2, piece, stop - start), low)
        for k in range(nz):
            full = lax.dynamic_update_slice(
                full, held[k][None, :, None, :, start:stop], (from_z[k], 0, xi, 0, 0)
            )
            full = lax.dynamic_update_slice(
                full, over_x[k][None, :, None, :, start:stop], (from_z[k], 0, 1 - xi, 0, 0)
            )
        return full.reshape(model, stop - start)

    query_weight = assemble(0, query_width)
    key_value_weight = assemble(query_width, width)

    def project_keys(normed_all, key_value_weight):
        raw = jnp.dot(normed_all, key_value_weight, preferred_element_type=wide)
        raw = raw.reshape(MEMBERS, LOCAL_SEQUENCES, paired, 2 * HEAD_SIZE)
        key_proj = raw[..., :HEAD_SIZE]
        key_normed, key_inverse = rms_apply(key_proj, key_gain)
        key_low = rope_apply(key_normed, row_cosine, row_sine).astype(low)
        value_low = raw[..., HEAD_SIZE:].astype(low)
        return key_proj, key_inverse, jnp.concatenate([key_low, value_low], -1)

    planes = lax.dynamic_update_index_in_dim(planes, plane2, 2, 0)
    wanted = [pick(planes, lax.rem(zi + nz - crossed[r], jnp.int32(nz))) for r in range(MEMBERS)]
    moved, (key_proj, key_inverse, key_value), _ = step(
        [
            (jnp.stack(wanted[2:]), "y"),
            (cotangent, "z", 1),
            (down_piece, "x"),
            (gate_pieces[0], "x"),
            (c_far0, "c"),
        ],
        project_keys,
        (normed_all, key_value_weight),
    )
    far, c1, down2, gate0, c_far_near0 = moved
    mine = jnp.stack([wanted[0], far[0]])

    def project_queries(normed_all, query_weight, pair):
        near = swap(pair, "c")
        return (
            near,
            swap(near[0], "x"),
            jnp.dot(normed_all, query_weight, preferred_element_type=wide),
        )

    moved, (near, cross_first, queries), _ = step(
        [(key_value, "z", k) for k in range(1, nz)] + [(mine, "x")],
        project_queries,
        (normed_all, query_weight, jnp.stack([wanted[1], far[1]])),
    )
    key_value = jnp.stack((key_value,) + moved[: nz - 1])
    cross_mine = moved[nz - 1]
    queries = queries.reshape(MEMBERS, LOCAL_SEQUENCES, paired, query_width)

    places = jnp.stack([member, zi]).astype(jnp.int32)
    gain_row = query_gain[None]
    (cross_last, c2_low, c_far1, gate1), attended, _ = step(
        [
            (near[1], "x"),
            (c_halves[0], "z", 2),
            (c1, "y"),
            (gate_pieces[1], "x"),
        ],
        attend,
        (places, queries, key_value, kernel_cosine, kernel_sine, gain_row, mask),
    )
    attended = attended.reshape(MEMBERS * rows, query_width)
    own_heads = jnp.stack([mine[0], near[0], mine[1], near[1]])
    other_heads = jnp.stack([cross_mine[0], cross_first, cross_mine[1], cross_last])
    output_weight = jnp.where(
        xi == 0, jnp.stack([own_heads, other_heads], 1), jnp.stack([other_heads, own_heads], 1)
    ).reshape(query_width, model)

    mixed_part = jnp.dot(attended, output_weight, preferred_element_type=wide)
    mixed_part = mixed_part.reshape(2, 2, rows, model)

    def summed_members(own, send):
        near = swap(send, "c")
        far = swap((own[1] + near[1].astype(wide)).astype(low), "y")
        return own[0] + near[0].astype(wide) + far.astype(wide)

    (gate2, c2_high, c_near1), mixed_sum, _ = step(
        [(gate_pieces[2], "x"), (c_halves[1], "z", 2), (c1, "c")],
        summed_members,
        (mixed_part[0], mixed_part[1].astype(low)),
    )
    c2 = jnp.concatenate([c2_low, c2_high])
    mixed_attn = inputs + mixed_sum
    normed_ffn, inverse_ffn = rms_apply(mixed_attn, ffn_gain)
    ffn_low = normed_ffn.astype(low)

    def whole(own, others):
        full = jnp.zeros((2,) + own.shape, low)
        full = lax.dynamic_update_slice(full, own[None], (xi, 0, 0))
        start = 0
        for other in others:
            full = lax.dynamic_update_slice(full, other[None], (1 - xi, start, 0))
            start += other.shape[0]
        return full.reshape(2 * own.shape[0], own.shape[1])

    def run_experts(k, x_blocks, c_blocks, kept, weights):
        scalars = jnp.stack([own_expert, jnp.int32(k)]).astype(jnp.int32)
        out = experts(
            scalars, x_blocks, c_blocks, ranks, chosen_all, router, *weights, slots, kept
        )
        return tuple(out[:-4]), out[-4:-2], out[-2:]

    def added(pair, back, a):
        return pair[0][a].astype(wide) + back[a].astype(wide)

    def both_rows(block):
        far = swap(block, "y")
        return far, swap(far, "c")

    moved, ((gate_all, down_all), (router, ranks, chosen_all)), _ = step(
        [
            (ffn_low, "z", 2),
            (w_up[0], "x"),
            (c2, "y"),
            (ffn_low, "y"),
            (c2, "c"),
        ],
        lambda owns, others, packed: (
            [whole(own, other) for own, other in zip(owns, others)],
            make_slots(packed),
        ),
        ([w_gate[0], w_down[0]], [[gate0, gate1, gate2], [down0, down1, down2]], packed),
    )
    x2, up_other, c_far2, y0, c_near2 = moved

    logits = dot32("td,ed->te", ffn_low, router)
    chosen = jnp.any(
        expert_ids[:, :, None] == jnp.arange(experts_all, dtype=jnp.int32)[None, None, :], 1
    )
    highest = jnp.max(jnp.where(chosen, logits, NEGATIVE_LIMIT), 1, keepdims=True)
    raised = jnp.where(chosen, jnp.exp(jnp.minimum(logits - highest, 0.0)), 0.0)
    gates = raised / jnp.sum(raised, 1, keepdims=True)

    (x1, c3_low, y2, n2, c_far_near2), up_all, _ = step(
        [
            (ffn_low, "z", 1),
            (c_halves[0], "z", 3),
            (x2, "y"),
            (x2, "c"),
            (c_far2, "c"),
        ],
        lambda own, other: whole(own, [other]),
        (w_up[0], up_other),
    )
    weights = [gate_all, up_all, down_all]
    (ny2, n0, ny0, c_far_near1), _, _ = step(
        [(y2, "c"), (ffn_low, "c"), (y0, "c"), (c_far1, "c")]
    )
    (x3, c3_high, y1, c_far3_low, n1), (kept, mixed2, rows2), _ = step(
        [
            (ffn_low, "z", 3),
            (c_halves[1], "z", 3),
            (x1, "y"),
            (c3_low, "y"),
            (x1, "c"),
        ],
        functools.partial(run_experts, 2),
        ([x2, n2, y2, ny2], [c2, c_near2, c_far2, c_far_near2], (), weights),
    )
    (ny1, n3), c3, _ = step(
        [(y1, "c"), (x3, "c")], lambda *halves: jnp.concatenate(halves), (c3_low, c3_high)
    )
    def core_sums(*pairs):
        backs = [swap(pair[1], "c") for pair in pairs]
        return backs, [added(pair, back, 1).astype(low) for pair, back in zip(pairs, backs)]

    def sums_and_experts(pairs, k, *given):
        return core_sums(*pairs), run_experts(k, *given)

    (y3, c_far3_high, c_near3), (sums, (kept, mixed1, rows1)), _ = step(
        [(x3, "y"), (c3_high, "y"), (c3, "c")],
        lambda pairs, *given: sums_and_experts(pairs, 1, *given),
        (
            [rows2, mixed2],
            [x1, n1, y1, ny1],
            [c1, c_near1, c_far1, c_far_near1],
            kept,
            weights,
        ),
    )
    (back2, mixed_back2), (row_send2, mixed_far_send2) = sums
    c_far3 = jnp.concatenate([c_far3_low, c_far3_high])
    (ny3, c_far_near3), _, _ = step([(y3, "c"), (c_far3, "c")])
    (far2, mixed_far2), (sums, (kept, mixed3, rows3)), _ = step(
        [(row_send2, "y"), (mixed_far_send2, "y")],
        lambda pairs, *given: sums_and_experts(pairs, 3, *given),
        (
            [rows1, mixed1],
            [x3, n3, y3, ny3],
            [c3, c_near3, c_far3, c_far_near3],
            kept,
            weights,
        ),
    )
    (back1, mixed_back1), (row_send1, mixed_far_send1) = sums
    total2 = (added(rows2, back2, 0) + far2.astype(wide)).astype(low)
    (z2, far1, mixed_far1), (sums, (kept, mixed0, rows0)), _ = step(
        [(total2, "z", -2), (row_send1, "y"), (mixed_far_send1, "y")],
        lambda pairs, *given: sums_and_experts(pairs, 0, *given),
        (
            [rows3, mixed3],
            [ffn_low, n0, y0, ny0],
            [cotangent, c_near0, c_far0, c_far_near0],
            kept,
            weights,
        ),
    )
    (back3, mixed_back3), (row_send3, mixed_far_send3) = sums
    expert_rows, hidden_low, dresults, dgate_low, dup_low = (
        block.reshape(context_count * slots, -1) for block in kept
    )

    def halved(grad, sixteenths):
        size = grad.shape[0] // 2
        cut = size * sixteenths // 16
        own = lax.dynamic_slice_in_dim(grad, xi * size, size, 0)
        first = lax.dynamic_slice_in_dim(grad, (1 - xi) * size, cut, 0)
        rest = lax.dynamic_slice_in_dim(grad, (1 - xi) * size + cut, size - cut, 0)
        return own, first.astype(low), rest.astype(low)

    def joined(own, moved):
        return (own + jnp.concatenate(moved, 0).astype(wide))[None]

    total1 = (added(rows1, back1, 0) + far1.astype(wide)).astype(low)

    def total(pair, back, far):
        return (added(pair, back, 0) + far.astype(wide)).astype(low)

    (z1, far3), (sums, (down_grad, down_first, down_rest), mixed_send1), _ = step(
        [(total1, "z", -1), (row_send3, "y")],
        lambda pairs, rows, grad, *given: (
            core_sums(*pairs),
            halved(dot32("sf,sd->fd", rows, grad), 10),
            total(*given),
        ),
        ([rows0, mixed0], hidden_low, dresults, mixed1, mixed_back1, mixed_far1),
    )
    (back0, mixed_back0), (row_send0, mixed_far_send0) = sums
    total3 = (added(rows3, back3, 0) + far3.astype(wide)).astype(low)
    (z3, far0, down0), ((gate_grad, gate_first, gate_rest), mixed_send2), _ = step(
        [
            (total3, "z", -3),
            (row_send0, "y"),
            (down_first, "x"),
        ],
        lambda rows, grad, *given: (halved(dot32("sd,sf->df", rows, grad), 10), total(*given)),
        (expert_rows, dgate_low, mixed2, mixed_back2, mixed_far2),
    )
    returned = added(rows0, back0, 0) + far0.astype(wide) + z1.astype(wide)
    returned = returned + z2.astype(wide) + z3.astype(wide)
    dffn_routed = returned[:, :model]
    dgates = returned[:, model : model + experts_all]
    dgates = dgates + returned[:, model + experts_all : model + 2 * experts_all]
    dlogits = gates * (dgates - jnp.sum(gates * dgates, 1, keepdims=True))
    dlogits_low = dlogits.astype(low)
    router_rows = dot32("td,te->de", ffn_low, dlogits_low).astype(low)
    router_rows = router_rows.reshape(nz, MEMBERS, 2, -1, 2 * HEAD_SIZE)
    extra_rows = router_rows.shape[3]
    router_rows = jnp.pad(router_rows, ((0, 0),) * 3 + ((0, -extra_rows % 16), (0, 0)))

    upstream = cotangent.astype(wide)
    dffn_rows = dffn_routed + dot32("te,ed->td", dlogits_low, router)
    dmixed_norm, ffn_gain_part = rms_back(mixed_attn, inverse_ffn, ffn_gain, dffn_rows)
    dmixed_attn = upstream + dmixed_norm
    dattn_low = dmixed_attn.astype(low)
    moved, (up_grad, up_first, up_rest), _ = step(
        [
            (dattn_low, "y"),
            (dattn_low, "c"),
            (gate_first, "x"),
            (mixed_send1, "z", -1),
        ],
        lambda rows, grad: halved(dot32("sd,sf->df", rows, grad), 11),
        (expert_rows, dup_low),
    )
    other, near, gate0, mixed_z1 = moved
    (other_near,), (dattn_all,), _ = step(
        [(other, "c")],
        lambda *blocks: (jnp.concatenate(blocks),),
        (dattn_low, other, near, dattn_low),
    )
    dattn_all = lax.dynamic_update_slice_in_dim(dattn_all, other_near, 3 * rows, 0)

    output_part = dot32("tc,td->cd", attended, dattn_all).astype(low)
    output_part = output_part.reshape(MEMBERS, 2, head_rows, model)
    output_own = lax.dynamic_index_in_dim(output_part, xi, 1, keepdims=False)
    output_other = lax.dynamic_index_in_dim(output_part, 1 - xi, 1, keepdims=False)

    def planes_of(part):
        own = lax.dynamic_index_in_dim(part, xi, 2, keepdims=False)
        other = lax.dynamic_index_in_dim(part, 1 - xi, 2, keepdims=False)
        return [(pick(own, around(k)), pick(other, around(k))) for k in range(nz)]

    def attention_back(dattn_all, output_weight, normed_all, head, *given):
        attended_grad = dot32("td,cd->tc", dattn_all, output_weight).astype(low)
        attended_grad = attended_grad.reshape(MEMBERS, LOCAL_SEQUENCES, paired, query_width)
        dquery, dkey_value, gain_part = attend_back(*given[:2], attended_grad, *given[2:])
        dquery = dquery.reshape(MEMBERS * rows, query_width)
        part = dot32("td,tc->dc", normed_all, dquery).astype(low)
        plane = pick(part.reshape(nz, MEMBERS, 2, piece, query_width), around(2))
        plane = lax.dynamic_index_in_dim(plane, 1 - xi, 1, keepdims=False)
        plane = [plane.reshape(-1, query_width)]
        plane += [head[:, a : a + query_width] for a in range(0, model, query_width)]
        return dquery, dkey_value, gain_part, part, jnp.concatenate(plane)

    moved, attention_grads, _ = step(
        [
            (output_other[1:], "x"),
            (mixed_send2, "z", -2),
            (mixed_far_send3, "y"),
            (mixed_far_send0, "y"),
        ],
        attention_back,
        (
            dattn_all,
            output_weight,
            normed_all,
            output_other[0],
            places,
            queries,
            key_value,
            kernel_cosine,
            kernel_sine,
            gain_row,
            mask,
        ),
    )
    cross_rest, mixed_z2, mixed_far3, mixed_far0 = moved
    dquery_low, dkey_value, query_gain_part, query_part, query_and_head = attention_grads
    query_gain_part = query_gain_part[0]
    query_planes = planes_of(query_part.reshape(nz, MEMBERS, 2, piece, query_width))
    output_far = (output_own[2:].astype(wide) + cross_rest[1:].astype(wide)).astype(low)

    def query_back(grad, weight, third, own, other):
        near = (own.astype(wide) + other.astype(wide)).astype(low)
        return dot32("tc,dc->td", grad, weight), total(*third), near

    moved, (dnormed, mixed_send3, near_last), _ = step(
        [(dkey_value[k].astype(low), "z", -k) for k in range(1, nz)]
        + [(query_and_head, "x"), (output_far, "y")],
        query_back,
        (
            dquery_low,
            query_weight,
            [mixed3, mixed_back3, mixed_far3],
            output_own[1],
            cross_rest[0],
        ),
    )
    *key_moves, cross, output_far = moved
    plane_rows = MEMBERS * piece
    cross_first = [
        cross[a : a + head_rows] for a in range(plane_rows, cross.shape[0], head_rows)
    ]
    cross_first = jnp.concatenate(cross_first, 1)
    cross = cross[:plane_rows].reshape(query_planes[2][0].shape)
    query_sum2 = (query_planes[2][0].astype(wide) + cross.astype(wide)).astype(low)
    near_first = (output_own[0].astype(wide) + cross_first.astype(wide)).astype(low)

    def project_keys_back(dnormed, dkey_value_own, moved, key_value_weight):
        dkey_value_own = dkey_value_own + sum(block.astype(wide) for block in moved)
        dkey, dvalue = dkey_value_own[..., :HEAD_SIZE], dkey_value_own[..., HEAD_SIZE:]
        dkey_proj, key_gain_part = rms_back(
            key_proj, key_inverse, key_gain, rope_back(dkey, row_cosine, row_sine)
        )
        dkey_value_low = jnp.concatenate([dkey_proj, dvalue], -1).astype(low)
        dkey_value_low = dkey_value_low.reshape(MEMBERS * rows, 2 * HEAD_SIZE)
        dnormed = dnormed + dot32("tc,dc->td", dkey_value_low, key_value_weight)
        dnormed = dnormed.reshape(2, 2, rows, model)
        key_part = dot32("td,tc->dc", normed_all, dkey_value_low).astype(low)
        key_part = key_part.reshape(nz, MEMBERS, 2, piece, 2 * HEAD_SIZE)
        key_part = jnp.concatenate([key_part, router_rows], 3)
        key_own = lax.dynamic_index_in_dim(key_part, xi, 2, keepdims=False)
        key_other = lax.dynamic_index_in_dim(key_part, 1 - xi, 2, keepdims=False)
        return dnormed[0], dnormed[1].astype(low), key_own, key_other, key_gain_part

    moved, (dnormed_own, dnormed_send, key_own, key_other, key_gain_part), _ = step(
        [
            (query_sum2, "z", 2),
            (jnp.stack([query_planes[1][1], query_planes[3][1]]), "x"),
            (jnp.stack([near_last, output_far[1]]), "c"),
        ],
        project_keys_back,
        (dnormed, dkey_value[0], key_moves, key_value_weight),
    )
    query_z2, cross, output_back = moved
    query_sum1 = (query_planes[1][0].astype(wide) + cross[0].astype(wide)).astype(low)
    query_sum3 = (query_planes[3][0].astype(wide) + cross[1].astype(wide)).astype(low)

    def order_output(blocks):
        blocks = uncrossed(blocks)
        return [pick(blocks, around(k)) for k in range(nz)]

    moved, output_sends, _ = step(
        [
            (query_sum1, "z", 1),
            (query_sum3, "z", 3),
            (query_planes[0][1], "x"),
            (key_other, "x"),
            (dnormed_send, "c"),
        ],
        order_output,
        ([near_first, output_back[0], output_far[0], output_back[1]],),
    )
    query_z1, query_z3, cross, key_cross, near = moved
    dnormed_far = (dnormed_own[1] + near[1].astype(wide)).astype(low)
    key_sum = (key_own.astype(wide) + key_cross.astype(wide)).astype(low)

    def total_queries(own, cross, *moved):
        total = own.astype(wide) + cross.astype(wide) + sum(m.astype(wide) for m in moved)
        total = total.astype(low)
        parts = [pick(total, crossed[r]) for r in range(MEMBERS)]
        return parts[0], parts[1], jnp.stack(parts[2:])

    (output_z1, output_z3, other, gate1, down1), query_parts, _ = step(
        [
            (output_sends[1], "z", 1),
            (output_sends[3], "z", 3),
            (dnormed_far, "y"),
            (gate_rest, "x"),
            (down_rest, "x"),
        ],
        total_queries,
        (query_planes[0][0], cross, query_z1, query_z2, query_z3),
    )
    dnormed = dnormed_own[0] + near[0].astype(wide) + other.astype(wide)
    dinput_norm, attention_gain_part = rms_back(inputs, inverse_attn, attention_gain, dnormed)
    small = [attention_gain_part, ffn_gain_part, query_gain_part, key_gain_part]
    small = jnp.concatenate(small).reshape(-1, 128)
    (*key_moves, small_x, query_far), d_tokens, _ = step(
        [(pick(key_sum, around(k)), "z", k) for k in range(1, nz)]
        + [(small, "x"), (query_parts[2], "y")],
        lambda a, b: (a + b).astype(low),
        (dmixed_attn, dinput_norm),
    )
    small = small + small_x
    key_total = pick(key_sum, zi).astype(wide)
    key_total = (key_total + sum(m.astype(wide) for m in key_moves)).astype(low)
    key_parts = [pick(key_total, crossed[r]) for r in range(MEMBERS)]

    def member_columns(parts):
        return uncrossed(parts).astype(wide).transpose(1, 0, 2)

    (output_z2, up0, key_far, small_y, query_near), (down_grad, gate_grad), _ = step(
        [
            (output_sends[2], "z", 2),
            (up_first, "x"),
            (jnp.stack(key_parts[2:]), "y"),
            (small, "y"),
            (jnp.stack([query_parts[1], query_far[1]]), "c"),
        ],
        lambda down, downs, gate, gates: (joined(down, downs), joined(gate, gates)),
        (down_grad, [down0, down1], gate_grad, [gate0, gate1]),
    )
    small = small + small_y
    query_blocks = [query_parts[0], query_near[0], query_far[0], query_near[1]]
    (mixed_z3, up1, key_near, small_c), (query_grad, output_grad), _ = step(
        [
            (mixed_send3, "z", -3),
            (up_rest, "x"),
            (jnp.stack([key_parts[1], key_far[1]]), "c"),
            (small, "c"),
        ],
        lambda blocks, own, *parts: (
            member_columns(blocks).reshape(piece, -1),
            own.astype(wide) + sum(part.astype(wide) for part in parts),
        ),
        (query_blocks, output_sends[0], output_z1, output_z2, output_z3),
    )
    small = small + small_c
    key_blocks = [key_parts[0], key_near[0], key_far[0], key_near[1]]

    def finish(up, ups, key_blocks, base, pair, back, far, z1, z2, z3):
        router = sum(block[piece : piece + extra_rows].astype(wide) for block in key_blocks)
        mixed = base + added(pair, back, 0) + far.astype(wide) + z1.astype(wide)
        mixed = mixed + z2.astype(wide) + z3.astype(wide)
        return (
            joined(up, ups),
            member_columns([block[:piece] for block in key_blocks]),
            router.reshape(piece, experts_all),
            mixed.astype(low),
        )

    small_z, results, _ = step(
        [(small, "z", k) for k in range(1, nz)],
        finish,
        (
            up_grad,
            [up0, up1],
            key_blocks,
            mixed_attn,
            mixed0,
            mixed_back0,
            mixed_far0,
            mixed_z1,
            mixed_z2,
            mixed_z3,
        ),
    )
    up_grad, key_grads, router_grad, mixed = results
    gains = (small + sum(small_z)).reshape(-1)
    key_grad = key_grads[..., :HEAD_SIZE].reshape(piece, -1)
    value_grad = key_grads[..., HEAD_SIZE:].reshape(piece, -1)
    return (
        mixed,
        d_tokens,
        gains[:model],
        gains[model : 2 * model],
        gains[2 * model : 2 * model + HEAD_SIZE],
        gains[2 * model + HEAD_SIZE :],
        query_grad,
        key_grad,
        value_grad,
        output_grad,
        router_grad,
        gate_grad,
        up_grad,
        down_grad,
    )


def solution(mesh):
    contexts, pairs = mesh.shape["ctx"], mesh.shape["fsdp"]
    planes = contexts // MEMBERS
    if planes == KEY_VALUE_HEADS and pairs * MEMBERS * KEY_VALUE_HEADS == QUERY_HEADS:
        layer, every, split = member_layer, ("z", "y", "c", "x"), ("z", "y", "c")
        pair = "x"
        mesh = Mesh(mesh.devices.reshape(planes, 2, 2, pairs), every)
    else:
        layer, every, split, pair = routed_layer, ("ctx", "fsdp"), "ctx", "fsdp"
    by_row = P(every, None)
    by_expert = P(split, pair, None)
    return jax.shard_map(
        layer,
        mesh=mesh,
        in_specs=(by_row,) * 3 + (P(),) * 4 + (by_row,) * 5 + (by_expert,) * 3,
        out_specs=(by_row,) * 2 + (P(),) * 4 + (by_row,) * 5 + (by_expert,) * 3,
        check_vma=False,
    )
```
